32 devices in a mesh: sub: 8 (over z, y), blk: 4 (over x, core).
Axes of the slice: x: 2, y: 2, z: 4, core: 2. Of those that a mesh axis runs over, the one named last changes fastest.
Arguments:
- right_side: float32 [8, 4, 96, 32], P('sub', 'blk')
- stiffness: bfloat16 [8, 4, 48, 9216], P('sub', 'blk'), may hold values from -1 to 7, as said below
- block_pairs: int32 [8, 4, 2, 16], P('sub', 'blk'), may hold values from 0 to 31, as said below
- trace_rows: int32 [8, 4, 128, 128], P('sub', 'blk'), may hold values from 0 to 3071
- partner_face: int32 [8, 4, 64], P('sub', 'blk'), may hold values from 0 to 63, each once within a row
- owner_list: int32 [8, 4, 4], P('sub', 'blk'), may hold values from 0 to 3, as said below
- mortar_weight: float32 [8, 4, 4, 16, 128], P('sub', 'blk'), may hold values from 0.1 to 1
Outputs:
- solution_field: float32 [8, 4, 96, 32], P('sub', 'blk')
- residual: float32 [8, 4, 96, 32], P('sub', 'blk')
The draws below stay inside these ranges and needn't reach their ends.
Inputs may be any that keep to these rules, and one draw needn't show every extreme that they name: `block_pairs`: on each subdomain every block row 0 to 31 appears exactly once among the 2 rows. `owner_list`: for each subdomain the 4 face groups go to distinct owners, and within a group every owner receives exactly one face group from each subdomain slot. The assembled stiffness K is symmetric positive definite.
All inputs are finite; a program needn't handle non-finite values.
Results may differ from the reference program's by a relative error of at most 0.005.
Values sent between devices are 32-bit elements; how exact they have to be, the bound alone decides.
No kernel may reach another device: no remote copies, remote signals or barrier semaphores. Data moves between devices by JAX's collectives and lax.ppermute only.
A program may use at most 64 MiB of HBM per device.

```python
import math
import jax
import jax.numpy as jnp
from jax import lax

BS = 96
NB = 32
FACE_DOF = 128
GROUP_FACES = 16
ITERS = 2
FE = 64
N_SUB = 8
N_BLK = 4


def draw_right_side(key, part):
    key = jax.random.fold_in(key, 11)
    key_base, key_rows, key_cols = jax.random.split(key, 3)
    shape = (N_SUB, N_BLK, BS, NB)
    base = jax.random.normal(key_base, shape, jnp.float32)
    growth = 3.0
    row_scale = jnp.power(10.0, jax.random.uniform(key_rows, (1, 1, BS, 1), jnp.float32))
    col_scale = jnp.power(10.0, jax.random.uniform(key_cols, (1, 1, 1, NB), jnp.float32))
    place = jnp.arange(N_SUB, dtype=jnp.float32)[:, None] * N_BLK + jnp.arange(N_BLK, dtype=jnp.float32)[None, :]
    place = place / max(N_SUB * N_BLK - 1, 1)
    device_scale = jnp.power(growth, place)
    return base * row_scale * col_scale * device_scale[:, :, None, None]


def draw_stiffness(key, part):
    key = jax.random.fold_in(key, 12)
    key_sym, key_diag, key_pair = jax.random.split(key, 3)
    half = 1.0 / BS
    raw = jax.random.uniform(key_sym, (N_SUB, N_BLK, NB, BS, BS), jnp.float32, -half, half)
    symmetric = raw + jnp.swapaxes(raw, 3, 4)
    identity = (jnp.arange(BS)[:, None] == jnp.arange(BS)[None, :]).astype(jnp.float32)[None, None, None, :, :]
    diag_value = jax.random.uniform(key_diag, (N_SUB, N_BLK, NB, BS, 1), jnp.float32, 3.5, 7.0)
    own_blocks = symmetric * (1.0 - identity) + identity * diag_value
    paired = jax.random.uniform(key_pair, (N_SUB, N_BLK, NB // 2, BS, BS), jnp.float32, -half, half)
    joined = jnp.concatenate([own_blocks, paired], axis=2)
    return joined.reshape(N_SUB, N_BLK, NB + NB // 2, BS * BS).astype(jnp.bfloat16)


def draw_block_pairs(key, part):
    key = jax.random.fold_in(key, 13)
    keys = jax.random.split(key, N_SUB * N_BLK)
    orders = jax.vmap(lambda single: jax.random.permutation(single, NB))(keys)
    return orders.astype(jnp.int32).reshape(N_SUB, N_BLK, 2, NB // 2)


def draw_owner_list(key, part):
    key = jax.random.fold_in(key, 14)
    keys = jax.random.split(key, N_SUB)

    def latin(single):
        key_cols, key_rows = jax.random.split(single)
        column_order = jax.random.permutation(key_cols, N_BLK).astype(jnp.int32)
        row_order = jax.random.permutation(key_rows, N_BLK).astype(jnp.int32)
        return (row_order[:, None] + column_order[None, :]) % N_BLK
    return jax.vmap(latin)(keys).astype(jnp.int32)


def place_ends(entries, rng, low, high):
    longest = entries.shape.index(max(entries.shape))
    spots = []
    for shift in (0, 1):
        where = [jax.random.randint(jax.random.fold_in(rng, axis), (), 0, length) for axis, length in enumerate(entries.shape)]
        where[longest] = (where[longest] + shift) % entries.shape[longest]
        spots.append(tuple(where))
    return entries.at[spots[0]].set(low).at[spots[1]].set(high)


def levels(rng, extent, pieces, low, top_value):
    factor_of, own = 1.0, jax.random.fold_in(rng, 6)
    for position, blocks in pieces:
        steps = jnp.exp(jax.random.uniform(jax.random.fold_in(own, position), (blocks,), jnp.float32, low / len(pieces), top_value / len(pieces)))
        factor_of = factor_of * jnp.repeat(steps, extent[position] // blocks).reshape([-1 if axis == position else 1 for axis in range(len(extent))])
    return factor_of


def setup_inputs(seed: int = 0) -> dict:
    key_of = jax.random.split(jax.random.key(seed), 8)
    return {
        "right_side": draw_right_side(jax.random.fold_in(key_of[7], 71), 0),
        "stiffness": draw_stiffness(jax.random.fold_in(key_of[7], 71), 0),
        "block_pairs": draw_block_pairs(jax.random.fold_in(key_of[7], 71), 0),
        "trace_rows": place_ends(jax.random.randint(key_of[3], (N_SUB, N_BLK, 2 * FE, FACE_DOF), 0, BS * NB), jax.random.fold_in(key_of[3], 1), 0, (BS * NB) - 1).astype(jnp.int32),
        "partner_face": jax.vmap(lambda own: jax.random.permutation(own, FE))(jax.random.split(key_of[4], N_SUB * N_BLK)).reshape((N_SUB, N_BLK, FE)).astype(jnp.int32),
        "owner_list": draw_owner_list(jax.random.fold_in(key_of[7], 71), 0),
        "mortar_weight": jnp.clip(jnp.exp(math.log(1.0) - 2.3025851 * jax.random.uniform(key_of[6], (N_SUB, N_BLK, N_BLK, GROUP_FACES, FACE_DOF), jnp.float32) ** levels(key_of[6], (N_SUB, N_BLK, N_BLK, GROUP_FACES, FACE_DOF), ((0, 8), (1, 4)), -0.2, 0.2)), 0.1, 1.0),
    }


HIGH = lax.Precision.HIGHEST


def local_stiffness(vector, blocks, pair_rows):
    width = vector.shape[1]
    size = vector.shape[0]
    widened = blocks.reshape(blocks.shape[0], size, size).astype(jnp.float32)
    first_end = pair_rows[0]
    other_end = pair_rows[1]
    result = jnp.einsum("iab,bi->ai", widened[:width], vector, precision=HIGH)
    to_first = jnp.einsum("pab,bp->ap", widened[width:], vector[:, other_end], precision=HIGH)
    to_other = jnp.einsum("pab,ap->bp", widened[width:], vector[:, first_end], precision=HIGH)
    return result.at[:, first_end].add(to_first).at[:, other_end].add(to_other)


def inverse_order(order):
    count = order.shape[0]
    return jnp.zeros_like(order).at[order].set(jnp.arange(count, dtype=jnp.int32))


def take_traces(vector, face_rows):
    return vector.reshape(-1)[face_rows]


def spread_values(face_rows, values):
    total = jnp.zeros((BS * NB,), jnp.float32)
    return total.at[face_rows.reshape(-1)].add(values.reshape(-1)).reshape(BS, NB)


def operate(vector, stiffness, block_pairs, trace_rows, partner_face, owner_list, mortar_weight):
    flat_vec = vector.reshape(N_SUB * N_BLK, BS, NB)
    flat_blocks = stiffness.reshape(N_SUB * N_BLK, NB + NB // 2, BS * BS)
    flat_pairs = block_pairs.reshape(N_SUB * N_BLK, 2, NB // 2)
    product = lax.map(lambda items: local_stiffness(items[0], items[1], items[2]), (flat_vec, flat_blocks, flat_pairs))
    product = product.reshape(N_SUB, N_BLK, BS, NB)
    traces = jax.vmap(jax.vmap(take_traces))(vector, trace_rows)
    faces = partner_face.shape[2]
    east = traces[:, :, :faces]
    west = traces[:, :, faces:]
    beyond = jnp.roll(west, -1, axis=0)
    partner = jax.vmap(jax.vmap(lambda rows, order: rows[order]))(beyond, partner_face)
    jump = east - partner
    swapped = jnp.swapaxes(mortar_weight, 1, 2)
    chosen = jnp.take_along_axis(swapped, owner_list[:, :, :, None, None], axis=2)
    scaled = chosen.reshape(N_SUB, N_BLK, faces, FACE_DOF) * jump
    handed = jax.vmap(jax.vmap(lambda rows, order: rows[inverse_order(order)]))(scaled, partner_face)
    before = jnp.roll(handed, 1, axis=0)
    values = jnp.concatenate([scaled, -before], axis=2)
    coupled = jax.vmap(jax.vmap(spread_values))(trace_rows, values)
    return product + coupled


def reference(right_side, stiffness, block_pairs, trace_rows, partner_face, owner_list, mortar_weight):
    solution_field = jnp.zeros_like(right_side)
    residual = right_side
    direction = right_side
    norm_now = jnp.sum(residual * residual)
    for iteration in range(ITERS):
        image = operate(direction, stiffness, block_pairs, trace_rows, partner_face, owner_list, mortar_weight)
        alpha = norm_now / jnp.sum(direction * image)
        solution_field = solution_field + alpha * direction
        residual = residual - alpha * image
        if iteration + 1 < ITERS:
            norm_next = jnp.sum(residual * residual)
            direction = residual + (norm_next / norm_now) * direction
            norm_now = norm_next
    return solution_field, residual
```

```python
import functools

import jax
import jax.numpy as jnp
from jax import lax
from jax.experimental import pallas as pl
from jax.experimental.pallas import tpu as pltpu
from jax.sharding import PartitionSpec as P

LANES = 128
SUBLANES = 8
VMEM = pl.BlockSpec(memory_space=pltpu.VMEM)
SMEM = pl.BlockSpec(memory_space=pltpu.SMEM)
PARAMS = pltpu.CompilerParams(vmem_limit_bytes=32 * 1024 * 1024)
F32 = jnp.float32
BF16 = jnp.bfloat16


def call(body, outs, inputs, scratch=(), flops=1_000_000):
    return pl.pallas_call(
        body,
        out_shape=outs,
        in_specs=[spec for _, spec in inputs],
        out_specs=[VMEM] * len(outs),
        scratch_shapes=list(scratch),
        compiler_params=PARAMS,
        cost_estimate=pl.CostEstimate(
            flops=flops, bytes_accessed=1_000_000, transcendentals=0
        ),
    )(*[value for value, _ in inputs])


def shape(rows, dtype=F32):
    return jax.ShapeDtypeStruct((rows, LANES), dtype)


def halves(value):
    high = value.astype(BF16).astype(F32)
    return high, value - high


def gather_traces(field, rows_ref, east_ref, west_ref):
    block_rows = field.shape[0]
    faces = east_ref.shape[0]
    spread = [
        jnp.broadcast_to(field[i : i + 1, :], (SUBLANES, LANES)) for i in range(block_rows)
    ]

    def step(target, base, k):
        index = rows_ref[pl.ds(pl.multiple_of(base + k * SUBLANES, SUBLANES), SUBLANES), :]
        dof = index // block_rows
        row = index % block_rows
        taken = jnp.zeros((SUBLANES, LANES), F32)
        for i in range(block_rows):
            here = jnp.take_along_axis(spread[i], dof, axis=1, mode="promise_in_bounds")
            taken = jnp.where(row == i, here, taken)
        target[pl.ds(pl.multiple_of(k * SUBLANES, SUBLANES), SUBLANES), :] = taken

    for target, base in ((east_ref, 0), (west_ref, faces)):

        def body(k, _, target=target, base=base):
            step(target, base, k)
            return 0

        lax.fori_loop(0, faces // SUBLANES, body, 0)


def first_kernel(partner_ref, field_ref, rows_ref, aligned_ref, padded_ref, east_ref, west_ref):
    faces = east_ref.shape[0]
    size = field_ref.shape[1]
    aligned_ref[faces:, :] = rows_ref[faces:, :]

    def move(f, _):
        aligned_ref[pl.ds(partner_ref[f], 1), :] = rows_ref[pl.ds(f, 1), :]
        return 0

    lax.fori_loop(0, faces, move, 0, unroll=8)
    padded_ref[...] = jnp.zeros_like(padded_ref)
    padded_ref[:, :size] = field_ref[...]
    gather_traces(padded_ref[...], aligned_ref, east_ref, west_ref)


def weight_kernel(partner_ref, owner_ref, arrived_ref, out_ref):
    groups, per_group, _ = arrived_ref.shape
    for g in range(groups):
        owner = owner_ref[g]
        for k in range(per_group):
            out_ref[pl.ds(partner_ref[g * per_group + k], 1), :] = arrived_ref[
                owner, pl.ds(k, 1), :
            ]


def stiffness_kernel(pairs_ref, blocks_ref, field_ref, out_ref, pieces, sums):
    block_rows = field_ref.shape[0]
    size = blocks_ref.shape[1]
    count = pairs_ref.shape[1]
    high, low = halves(field_ref[...])
    pieces[...] = jnp.zeros_like(pieces)
    pieces[pl.ds(0, block_rows, stride=SUBLANES), :] = high
    pieces[pl.ds(1, block_rows, stride=SUBLANES), :] = low

    def times(row, block, contract):
        left = pieces[pl.ds(pl.multiple_of(row * SUBLANES, SUBLANES), SUBLANES), :]
        return lax.dot_general(
            left[:, :size].astype(BF16),
            block,
            (((1,), (contract,)), ((), ())),
            preferred_element_type=F32,
        )

    def add(row, value):
        place = pl.ds(pl.multiple_of(row * SUBLANES, SUBLANES), SUBLANES)
        sums[place, :size] = sums[place, :size] + value

    sums[...] = jnp.zeros_like(sums)
    for i in range(block_rows):
        sums[i * SUBLANES : (i + 1) * SUBLANES, :size] = times(i, blocks_ref[i], 1)
    for p in range(count):
        first = pairs_ref[0, p]
        other = pairs_ref[1, p]
        block = blocks_ref[block_rows + p]
        add(first, times(other, block, 1))
        add(other, times(first, block, 0))
    out_ref[...] = (
        sums[pl.ds(0, block_rows, stride=SUBLANES), :]
        + sums[pl.ds(1, block_rows, stride=SUBLANES), :]
    )


def spread_jumps(block_rows, size, aligned_ref, weights, own, arrived):
    faces = own[0].shape[0]
    dof_of = lax.broadcasted_iota(jnp.int32, (size, LANES), 0)
    row_of = lax.broadcasted_iota(jnp.int32, (block_rows, LANES), 0)

    def step(k, total, side):
        place = pl.ds(pl.multiple_of(k * SUBLANES, SUBLANES), SUBLANES)
        lam = weights[side][place, :] * (own[side][place, :] - arrived[side][place, :])
        high, low = halves(lam)
        index = aligned_ref[pl.ds(pl.multiple_of(side * faces + k * SUBLANES, SUBLANES), SUBLANES), :]
        dof = index // block_rows
        row = index % block_rows
        left = []
        right = []
        for f in range(SUBLANES):
            here = row_of == row[f : f + 1, :]
            left.append(
                jnp.concatenate(
                    [
                        jnp.where(here, high[f : f + 1, :], 0.0),
                        jnp.where(here, low[f : f + 1, :], 0.0),
                    ],
                    axis=0,
                ).astype(BF16)
            )
            right.append(jnp.where(dof_of == dof[f : f + 1, :], 1.0, 0.0).astype(BF16))
        return total + lax.dot_general(
            jnp.concatenate(left, axis=1),
            jnp.concatenate(right, axis=1),
            (((1,), (1,)), ((), ())),
            preferred_element_type=F32,
        )

    total = jnp.zeros((2 * block_rows, size), F32)
    for side in (0, 1):
        total = lax.fori_loop(
            0, faces // SUBLANES, functools.partial(step, side=side), total
        )
    return total[:block_rows] + total[block_rows:]


def middle_kernel(
    size,
    aligned_ref,
    product_ref,
    weight_east_ref,
    weight_west_ref,
    east_ref,
    west_ref,
    from_next_ref,
    from_last_ref,
    image_ref,
    next_east_ref,
    next_west_ref,
):
    block_rows = product_ref.shape[0]
    coupled = spread_jumps(
        block_rows,
        size,
        aligned_ref,
        (weight_east_ref, weight_west_ref),
        (east_ref, west_ref),
        (from_next_ref, from_last_ref),
    )
    image_ref[...] = product_ref[...]
    image_ref[:, :size] = image_ref[:, :size] + coupled
    gather_traces(image_ref[...], aligned_ref, next_east_ref, next_west_ref)


def total_of(value):
    return jnp.sum(jnp.sum(value, axis=0, keepdims=True), axis=1, keepdims=True)


def last_kernel(
    size,
    aligned_ref,
    product_ref,
    weight_east_ref,
    weight_west_ref,
    east_ref,
    west_ref,
    from_next_ref,
    from_last_ref,
    field_ref,
    image_ref,
    second_ref,
    sums_ref,
):
    block_rows = product_ref.shape[0]
    coupled = spread_jumps(
        block_rows,
        size,
        aligned_ref,
        (weight_east_ref, weight_west_ref),
        (east_ref, west_ref),
        (from_next_ref, from_last_ref),
    )
    second_ref[...] = product_ref[...]
    second_ref[:, :size] = second_ref[:, :size] + coupled
    field = field_ref[...]
    image = image_ref[...]
    second = second_ref[...]
    lane = lax.broadcasted_iota(jnp.int32, (1, LANES), 1)
    row = jnp.zeros((1, LANES), F32)
    for k, product in enumerate(
        (field * field, field * image, image * image, field * second, image * second)
    ):
        row = jnp.where(lane == k, total_of(product), row)
    sums_ref[...] = jnp.broadcast_to(row[None], sums_ref.shape)


def final_kernel(field_ref, image_ref, second_ref, sums_ref, solution_ref, residual_ref):
    size = solution_ref.shape[1]
    row = jnp.sum(sums_ref[...], axis=0)
    lane = lax.broadcasted_iota(jnp.int32, (1, LANES), 1)

    def entry(k):
        return jnp.sum(jnp.where(lane == k, row, 0.0), axis=1, keepdims=True)

    bb, bq, qq, bw, qw = (entry(k) for k in range(5))
    field = field_ref[:, :size]
    image = image_ref[:, :size]
    second = second_ref[:, :size]
    alpha = bb / bq
    norm = bb - alpha * (2.0 * bq - alpha * qq)
    beta = norm / bb
    grown = 1.0 + beta
    energy = grown * (grown * bq - alpha * (bw + qq)) + alpha * alpha * qw
    alpha_next = norm / energy
    residual = field - alpha * image
    direction = residual + beta * field
    moved = (image - alpha * second) + beta * image
    solution_ref[...] = alpha * field + alpha_next * direction
    residual_ref[...] = residual - alpha_next * moved


def from_behind(value, axis, steps):
    count = lax.axis_size(axis)
    pairs = [(source, (source + steps) % count) for source in range(count)]
    return lax.ppermute(value, axis, pairs)


def on_device(
    right_side, stiffness, block_pairs, trace_rows, partner_face, owner_list, mortar_weight
):
    field = right_side[0, 0].T
    block_rows, size = field.shape
    stored = stiffness[0, 0]
    blocks = stored.reshape(stored.shape[0], size, size)
    pairs = block_pairs[0, 0]
    rows = trace_rows[0, 0]
    partner = partner_face[0, 0]
    owners = owner_list[0, 0]
    faces = partner.shape[0]
    groups = owners.shape[0]
    devices = lax.axis_size("sub") * lax.axis_size("blk")

    held = lax.all_to_all(mortar_weight[0, 0], "blk", split_axis=0, concat_axis=0, tiled=True)
    aligned, padded, east, west = call(
        first_kernel,
        [shape(2 * faces, jnp.int32), shape(block_rows), shape(faces), shape(faces)],
        [(partner, SMEM), (field, VMEM), (rows, VMEM)],
    )
    from_last = from_behind(east, "sub", 1)
    from_next = from_behind(west, "sub", -1)
    (weight_east,) = call(
        weight_kernel,
        [shape(faces)],
        [(partner, SMEM), (owners, SMEM), (held, VMEM)],
    )
    weight_west = from_behind(weight_east, "sub", 1)

    def stiff(vector):
        (product,) = call(
            stiffness_kernel,
            [shape(block_rows)],
            [(pairs, SMEM), (blocks, VMEM), (vector, VMEM)],
            scratch=[pltpu.VMEM((block_rows * SUBLANES, LANES), F32)] * 2,
        )
        return product

    product = stiff(padded)
    image, next_east, next_west = call(
        functools.partial(middle_kernel, size),
        [shape(block_rows), shape(faces), shape(faces)],
        [
            (value, VMEM)
            for value in (
                aligned, product, weight_east, weight_west, east, west, from_next, from_last
            )
        ],
    )
    second_last = from_behind(next_east, "sub", 1)
    second_next = from_behind(next_west, "sub", -1)
    product = stiff(image)
    second, sums = call(
        functools.partial(last_kernel, size),
        [shape(block_rows), jax.ShapeDtypeStruct((devices, 1, LANES), F32)],
        [
            (value, VMEM)
            for value in (
                aligned,
                product,
                weight_east,
                weight_west,
                next_east,
                next_west,
                second_next,
                second_last,
                padded,
                image,
            )
        ],
    )
    sums = lax.all_to_all(sums, ("sub", "blk"), split_axis=0, concat_axis=0, tiled=True)
    solution_field, residual = call(
        final_kernel,
        [jax.ShapeDtypeStruct((block_rows, size), F32)] * 2,
        [(padded, VMEM), (image, VMEM), (second, VMEM), (sums, VMEM)],
    )
    return (solution_field.T[None, None], residual.T[None, None])


def solution(mesh):
    in_specs = (
        P("sub", "blk", None, None),
        P("sub", "blk", None, None),
        P("sub", "blk", None, None),
        P("sub", "blk", None, None),
        P("sub", "blk", None),
        P("sub", "blk", None),
        P("sub", "blk", None, None, None),
    )
    out_specs = (P("sub", "blk", None, None), P("sub", "blk", None, None))
    return jax.shard_map(
        on_device, mesh=mesh, in_specs=in_specs, out_specs=out_specs, check_vma=False
    )
```

```python
import functools

import jax
import jax.numpy as jnp
from jax import lax
from jax.experimental import pallas as pl
from jax.experimental.pallas import tpu as pltpu
from jax.sharding import PartitionSpec as P

LANES = 128
SUBLANES = 8
VMEM = pl.BlockSpec(memory_space=pltpu.VMEM)
SMEM = pl.BlockSpec(memory_space=pltpu.SMEM)
PARAMS = pltpu.CompilerParams(vmem_limit_bytes=32 * 1024 * 1024)
F32 = jnp.float32
BF16 = jnp.bfloat16


def call(body, outs, inputs, scratch=(), flops=1_000_000):
    return pl.pallas_call(
        body,
        out_shape=outs,
        in_specs=[spec for _, spec in inputs],
        out_specs=[VMEM] * len(outs),
        scratch_shapes=list(scratch),
        compiler_params=PARAMS,
        cost_estimate=pl.CostEstimate(
            flops=flops, bytes_accessed=1_000_000, transcendentals=0
        ),
    )(*[value for value, _ in inputs])


def shape(rows, dtype=F32):
    return jax.ShapeDtypeStruct((rows, LANES), dtype)


def halves(value):
    high = value.astype(BF16).astype(F32)
    return high, value - high


def gather_traces(field, rows_ref, east_ref, west_ref):
    block_rows = field.shape[0]
    faces = east_ref.shape[0]
    spread = [
        jnp.broadcast_to(field[i : i + 1, :], (SUBLANES, LANES)) for i in range(block_rows)
    ]

    def step(target, base, k):
        index = rows_ref[pl.ds(pl.multiple_of(base + k * SUBLANES, SUBLANES), SUBLANES), :]
        dof = index // block_rows
        row = index % block_rows
        taken = jnp.zeros((SUBLANES, LANES), F32)
        for i in range(block_rows):
            here = jnp.take_along_axis(spread[i], dof, axis=1, mode="promise_in_bounds")
            taken = jnp.where(row == i, here, taken)
        target[pl.ds(pl.multiple_of(k * SUBLANES, SUBLANES), SUBLANES), :] = taken

    for target, base in ((east_ref, 0), (west_ref, faces)):

        def body(k, _, target=target, base=base):
            step(target, base, k)
            return 0

        lax.fori_loop(0, faces // SUBLANES, body, 0, unroll=4)


def first_kernel(partner_ref, field_ref, rows_ref, aligned_ref, padded_ref, east_ref, west_ref):
    faces = east_ref.shape[0]
    size = field_ref.shape[1]
    aligned_ref[faces:, :] = rows_ref[faces:, :]

    def move(f, _):
        aligned_ref[pl.ds(partner_ref[f], 1), :] = rows_ref[pl.ds(f, 1), :]
        return 0

    lax.fori_loop(0, faces, move, 0, unroll=8)
    padded_ref[...] = jnp.zeros_like(padded_ref)
    padded_ref[:, :size] = field_ref[...]
    gather_traces(padded_ref[...], aligned_ref, east_ref, west_ref)


def weight_kernel(partner_ref, owner_ref, place_ref, arrived_ref, out_ref):
    _, groups, per_group, _ = arrived_ref.shape
    place = place_ref[0]
    for g in range(groups):
        owner = owner_ref[g]
        for k in range(per_group):
            out_ref[pl.ds(partner_ref[g * per_group + k], 1), :] = arrived_ref[
                owner, place, pl.ds(k, 1), :
            ]


def stiffness_kernel(pairs_ref, blocks_ref, field_ref, out_ref, pieces, sums):
    block_rows = field_ref.shape[0]
    size = blocks_ref.shape[1]
    count = pairs_ref.shape[1]
    high, low = halves(field_ref[...])
    pieces[...] = jnp.zeros_like(pieces)
    pieces[pl.ds(0, block_rows, stride=SUBLANES), :] = high
    pieces[pl.ds(1, block_rows, stride=SUBLANES), :] = low

    def times(row, block, contract):
        left = pieces[pl.ds(pl.multiple_of(row * SUBLANES, SUBLANES), SUBLANES), :]
        return lax.dot_general(
            left[:, :size].astype(BF16),
            block,
            (((1,), (contract,)), ((), ())),
            preferred_element_type=F32,
        )

    def add(row, value):
        place = pl.ds(pl.multiple_of(row * SUBLANES, SUBLANES), SUBLANES)
        sums[place, :size] = sums[place, :size] + value

    sums[...] = jnp.zeros_like(sums)
    for i in range(block_rows):
        sums[i * SUBLANES : (i + 1) * SUBLANES, :size] = times(i, blocks_ref[i], 1)
    for p in range(count):
        first = pairs_ref[0, p]
        other = pairs_ref[1, p]
        block = blocks_ref[block_rows + p]
        add(first, times(other, block, 1))
        add(other, times(first, block, 0))
    out_ref[...] = (
        sums[pl.ds(0, block_rows, stride=SUBLANES), :]
        + sums[pl.ds(1, block_rows, stride=SUBLANES), :]
    )


def spread_jumps(block_rows, size, aligned_ref, weights, own, arrived):
    faces = own[0].shape[0]
    dof_of = lax.broadcasted_iota(jnp.int32, (size, LANES), 0)
    row_of = lax.broadcasted_iota(jnp.int32, (block_rows, LANES), 0)

    def step(k, total, side):
        place = pl.ds(pl.multiple_of(k * SUBLANES, SUBLANES), SUBLANES)
        lam = weights[side][place, :] * (own[side][place, :] - arrived[side][place, :])
        high, low = halves(lam)
        index = aligned_ref[pl.ds(pl.multiple_of(side * faces + k * SUBLANES, SUBLANES), SUBLANES), :]
        dof = index // block_rows
        row = index % block_rows
        left = []
        right = []
        for f in range(SUBLANES):
            here = row_of == row[f : f + 1, :]
            left.append(
                jnp.concatenate(
                    [
                        jnp.where(here, high[f : f + 1, :], 0.0),
                        jnp.where(here, low[f : f + 1, :], 0.0),
                    ],
                    axis=0,
                ).astype(BF16)
            )
            right.append(jnp.where(dof_of == dof[f : f + 1, :], 1.0, 0.0).astype(BF16))
        return total + lax.dot_general(
            jnp.concatenate(left, axis=1),
            jnp.concatenate(right, axis=1),
            (((1,), (1,)), ((), ())),
            preferred_element_type=F32,
        )

    total = jnp.zeros((2 * block_rows, size), F32)
    for side in (0, 1):
        total = lax.fori_loop(
            0, faces // SUBLANES, functools.partial(step, side=side), total, unroll=2
        )
    return total[:block_rows] + total[block_rows:]


def middle_kernel(
    size,
    aligned_ref,
    product_ref,
    weight_east_ref,
    weight_west_ref,
    east_ref,
    west_ref,
    from_next_ref,
    from_last_ref,
    image_ref,
    next_east_ref,
    next_west_ref,
):
    block_rows = product_ref.shape[0]
    coupled = spread_jumps(
        block_rows,
        size,
        aligned_ref,
        (weight_east_ref, weight_west_ref),
        (east_ref, west_ref),
        (from_next_ref, from_last_ref),
    )
    image_ref[...] = product_ref[...]
    image_ref[:, :size] = image_ref[:, :size] + coupled
    gather_traces(image_ref[...], aligned_ref, next_east_ref, next_west_ref)


def total_of(value):
    return jnp.sum(jnp.sum(value, axis=0, keepdims=True), axis=1, keepdims=True)


def last_kernel(
    size,
    aligned_ref,
    product_ref,
    weight_east_ref,
    weight_west_ref,
    east_ref,
    west_ref,
    from_next_ref,
    from_last_ref,
    field_ref,
    image_ref,
    second_ref,
    sums_ref,
):
    block_rows = product_ref.shape[0]
    coupled = spread_jumps(
        block_rows,
        size,
        aligned_ref,
        (weight_east_ref, weight_west_ref),
        (east_ref, west_ref),
        (from_next_ref, from_last_ref),
    )
    second_ref[...] = product_ref[...]
    second_ref[:, :size] = second_ref[:, :size] + coupled
    field = field_ref[...]
    image = image_ref[...]
    second = second_ref[...]
    lane = lax.broadcasted_iota(jnp.int32, (1, LANES), 1)
    row = jnp.zeros((1, LANES), F32)
    for k, product in enumerate(
        (field * field, field * image, image * image, field * second, image * second)
    ):
        row = jnp.where(lane == k, total_of(product), row)
    sums_ref[...] = row


def final_kernel(field_ref, image_ref, second_ref, sums_ref, solution_ref, residual_ref):
    size = solution_ref.shape[1]
    row = jnp.sum(sums_ref[...], axis=0)
    lane = lax.broadcasted_iota(jnp.int32, (1, LANES), 1)

    def entry(k):
        return jnp.sum(jnp.where(lane == k, row, 0.0), axis=1, keepdims=True)

    bb, bq, qq, bw, qw = (entry(k) for k in range(5))
    field = field_ref[:, :size]
    image = image_ref[:, :size]
    second = second_ref[:, :size]
    alpha = bb / bq
    norm = bb - alpha * (2.0 * bq - alpha * qq)
    beta = norm / bb
    grown = 1.0 + beta
    energy = grown * (grown * bq - alpha * (bw + qq)) + alpha * alpha * qw
    alpha_next = norm / energy
    residual = field - alpha * image
    direction = residual + beta * field
    moved = (image - alpha * second) + beta * image
    solution_ref[...] = alpha * field + alpha_next * direction
    residual_ref[...] = residual - alpha_next * moved


def from_behind(value, axis, steps):
    count = lax.axis_size(axis)
    pairs = [(source, (source + steps) % count) for source in range(count)]
    return lax.ppermute(value, axis, pairs)


def on_device(
    right_side, stiffness, block_pairs, trace_rows, partner_face, owner_list, mortar_weight
):
    field = right_side[0, 0].T
    block_rows, size = field.shape
    stored = stiffness[0, 0]
    blocks = stored.reshape(stored.shape[0], size, size)
    pairs = block_pairs[0, 0]
    rows = trace_rows[0, 0]
    partner = partner_face[0, 0]
    owners = owner_list[0, 0]
    faces = partner.shape[0]
    groups = owners.shape[0]

    held = lax.all_gather(mortar_weight[0, 0], "blk")
    place = lax.axis_index("blk").astype(jnp.int32).reshape(1)
    aligned, padded, east, west = call(
        first_kernel,
        [shape(2 * faces, jnp.int32), shape(block_rows), shape(faces), shape(faces)],
        [(partner, SMEM), (field, VMEM), (rows, VMEM)],
    )
    from_last = from_behind(east, "sub", 1)
    from_next = from_behind(west, "sub", -1)
    (weight_east,) = call(
        weight_kernel,
        [shape(faces)],
        [(partner, SMEM), (owners, SMEM), (place, SMEM), (held, VMEM)],
    )
    weight_west = from_behind(weight_east, "sub", 1)

    def stiff(vector):
        (product,) = call(
            stiffness_kernel,
            [shape(block_rows)],
            [(pairs, SMEM), (blocks, VMEM), (vector, VMEM)],
            scratch=[pltpu.VMEM((block_rows * SUBLANES, LANES), F32)] * 2,
        )
        return product

    product = stiff(padded)
    image, next_east, next_west = call(
        functools.partial(middle_kernel, size),
        [shape(block_rows), shape(faces), shape(faces)],
        [
            (value, VMEM)
            for value in (
                aligned, product, weight_east, weight_west, east, west, from_next, from_last
            )
        ],
    )
    second_last = from_behind(next_east, "sub", 1)
    second_next = from_behind(next_west, "sub", -1)
    product = stiff(image)
    second, sums = call(
        functools.partial(last_kernel, size),
        [shape(block_rows), shape(1)],
        [
            (value, VMEM)
            for value in (
                aligned,
                product,
                weight_east,
                weight_west,
                next_east,
                next_west,
                second_next,
                second_last,
                padded,
                image,
            )
        ],
    )
    sums = lax.all_gather(sums, ("sub", "blk"))
    solution_field, residual = call(
        final_kernel,
        [jax.ShapeDtypeStruct((block_rows, size), F32)] * 2,
        [(padded, VMEM), (image, VMEM), (second, VMEM), (sums, VMEM)],
    )
    return (solution_field.T[None, None], residual.T[None, None])


def solution(mesh):
    in_specs = (
        P("sub", "blk", None, None),
        P("sub", "blk", None, None),
        P("sub", "blk", None, None),
        P("sub", "blk", None, None),
        P("sub", "blk", None),
        P("sub", "blk", None),
        P("sub", "blk", None, None, None),
    )
    out_specs = (P("sub", "blk", None, None), P("sub", "blk", None, None))
    return jax.shard_map(
        on_device, mesh=mesh, in_specs=in_specs, out_specs=out_specs, check_vma=False
    )
```

```python
import functools

import jax
import jax.numpy as jnp
from jax import lax
from jax.experimental import pallas as pl
from jax.experimental.pallas import tpu as pltpu
from jax.sharding import PartitionSpec as P

LANES = 128
SUBLANES = 8
VMEM = pl.BlockSpec(memory_space=pltpu.VMEM)
HBM = pl.BlockSpec(memory_space=pltpu.HBM)
SMEM = pl.BlockSpec(memory_space=pltpu.SMEM)
PARAMS = pltpu.CompilerParams(vmem_limit_bytes=32 * 1024 * 1024)
F32 = jnp.float32
BF16 = jnp.bfloat16


def call(body, outs, inputs, scratch=(), flops=1_000_000):
    return pl.pallas_call(
        body,
        out_shape=outs,
        in_specs=[spec for _, spec in inputs],
        out_specs=[VMEM] * len(outs),
        scratch_shapes=list(scratch),
        compiler_params=PARAMS,
        cost_estimate=pl.CostEstimate(
            flops=flops, bytes_accessed=1_000_000, transcendentals=0
        ),
    )(*[value for value, _ in inputs])


def shape(rows, dtype=F32):
    return jax.ShapeDtypeStruct((rows, LANES), dtype)


def halves(value):
    high = value.astype(BF16).astype(F32)
    return high, value - high


def gather_traces(field, rows_ref, traces_refs):
    block_rows = field.shape[0]
    spread = [
        jnp.broadcast_to(field[i : i + 1, :], (SUBLANES, LANES)) for i in range(block_rows)
    ]
    faces = rows_ref.shape[0] // len(traces_refs)
    for side, target in enumerate(traces_refs):

        def step(k, _, target=target, side=side):
            index = rows_ref[tile(side * faces // SUBLANES + k), :]
            dof, row = split(index, block_rows)
            taken = jnp.zeros((SUBLANES, LANES), F32)
            for i in range(block_rows):
                here = jnp.take_along_axis(spread[i], dof, axis=1, mode="promise_in_bounds")
                taken = jnp.where(row == i, here, taken)
            target[tile(k), :] = taken
            return 0

        lax.fori_loop(0, faces // SUBLANES, step, 0, unroll=4)


def tile(k):
    return pl.ds(pl.multiple_of(k * SUBLANES, SUBLANES), SUBLANES)


def split(index, block_rows):
    if block_rows & (block_rows - 1) == 0:
        shift = block_rows.bit_length() - 1
        return index >> shift, index & (block_rows - 1)
    return lax.div(index, block_rows), lax.rem(index, block_rows)


def first_kernel(
    partner_hbm,
    owner_hbm,
    rows_hbm,
    field_hbm,
    aligned_ref,
    padded_ref,
    chosen_ref,
    side_a_ref,
    side_b_ref,
    partner_ref,
    owner_ref,
    rows_ref,
    field_ref,
    sems,
):
    copies = [
        pltpu.make_async_copy(source, target, sems.at[k])
        for k, (source, target) in enumerate(
            (
                (partner_hbm, partner_ref),
                (owner_hbm, owner_ref),
                (rows_hbm, rows_ref),
                (field_hbm, field_ref),
            )
        )
    ]
    for copy in copies:
        copy.start()
    faces = side_a_ref.shape[0]
    per_group = faces // owner_ref.shape[0]
    size = field_ref.shape[1]
    parity = lax.rem(lax.axis_index("sub"), 2)
    east = pl.multiple_of((1 - parity) * faces, faces)
    west = pl.multiple_of(parity * faces, faces)
    padded_ref[...] = jnp.zeros_like(padded_ref)
    lane = lax.broadcasted_iota(jnp.int32, (1, chosen_ref.shape[1]), 1)
    for copy in copies:
        copy.wait()
    aligned_ref[pl.ds(west, faces), :] = rows_ref[faces:, :]
    for f in range(faces):
        place = partner_ref[f]
        source = owner_ref[f // per_group] * per_group + f % per_group
        aligned_ref[pl.ds(east + place, 1), :] = rows_ref[f : f + 1, :]
        chosen_ref[pl.ds(place, 1), :] = jnp.where(lane == source, 1.0, 0.0)
    padded_ref[:, :size] = field_ref[...]
    gather_traces(padded_ref[...], aligned_ref, (side_a_ref, side_b_ref))


def message_kernel(held_ref, chosen_ref, side_a_ref, side_b_ref, to_a_ref, to_b_ref):
    faces = side_a_ref.shape[0]
    own = jnp.dot(
        chosen_ref[...],
        held_ref[...],
        precision=lax.Precision.HIGHEST,
        preferred_element_type=F32,
    )
    for side, target in ((side_a_ref, to_a_ref), (side_b_ref, to_b_ref)):
        target[:faces, :] = side[...]
        target[faces:, :] = own


def stiffness_kernel(pairs_ref, blocks_ref, field_ref, out_ref, pieces, sums):
    block_rows = field_ref.shape[0]
    size = blocks_ref.shape[1]
    count = pairs_ref.shape[1]
    high, low = halves(field_ref[...])
    pieces[...] = jnp.zeros_like(pieces)
    pieces[pl.ds(0, block_rows, stride=SUBLANES), :] = high
    pieces[pl.ds(1, block_rows, stride=SUBLANES), :] = low

    def times(row, block, contract):
        left = pieces[pl.ds(pl.multiple_of(row * SUBLANES, SUBLANES), SUBLANES), :]
        return lax.dot_general(
            left[:, :size].astype(BF16),
            block,
            (((1,), (contract,)), ((), ())),
            preferred_element_type=F32,
        )

    def add(row, value):
        place = pl.ds(pl.multiple_of(row * SUBLANES, SUBLANES), SUBLANES)
        sums[place, :size] = sums[place, :size] + value

    sums[...] = jnp.zeros_like(sums)
    for i in range(block_rows):
        sums[i * SUBLANES : (i + 1) * SUBLANES, :size] = times(i, blocks_ref[i], 1)
    for p in range(count):
        first = pairs_ref[0, p]
        other = pairs_ref[1, p]
        block = blocks_ref[block_rows + p]
        add(first, times(other, block, 1))
        add(other, times(first, block, 0))
    out_ref[...] = (
        sums[pl.ds(0, block_rows, stride=SUBLANES), :]
        + sums[pl.ds(1, block_rows, stride=SUBLANES), :]
    )


def spread_jumps(block_rows, size, aligned_ref, weights_ref, own, arrived):
    faces = weights_ref.shape[0] // 2
    dof_of = lax.broadcasted_iota(jnp.int32, (size, LANES), 0)
    row_of = lax.broadcasted_iota(jnp.int32, (block_rows, LANES), 0)

    def step(k, total, side):
        place = tile(side * faces // SUBLANES + k)
        lam = weights_ref[place, :] * (own[side][tile(k), :] - arrived[side][tile(k), :])
        high, low = halves(lam)
        dof, row = split(aligned_ref[place, :], block_rows)
        left = []
        right = []
        for f in range(SUBLANES):
            here = row_of == row[f : f + 1, :]
            left.append(
                jnp.concatenate(
                    [
                        jnp.where(here, high[f : f + 1, :], 0.0),
                        jnp.where(here, low[f : f + 1, :], 0.0),
                    ],
                    axis=0,
                ).astype(BF16)
            )
            right.append(jnp.where(dof_of == dof[f : f + 1, :], 1.0, 0.0).astype(BF16))
        return total + lax.dot_general(
            jnp.concatenate(left, axis=1),
            jnp.concatenate(right, axis=1),
            (((1,), (1,)), ((), ())),
            preferred_element_type=F32,
        )

    total = jnp.zeros((2 * block_rows, size), F32)
    for side in (0, 1):
        total = lax.fori_loop(
            0, faces // SUBLANES, functools.partial(step, side=side), total, unroll=2
        )
    return total[:block_rows] + total[block_rows:]


def middle_kernel(
    size,
    aligned_ref,
    product_ref,
    to_a_ref,
    to_b_ref,
    from_a_ref,
    from_b_ref,
    image_ref,
    weights_ref,
    side_a_ref,
    side_b_ref,
):
    block_rows = product_ref.shape[0]
    faces = side_a_ref.shape[0]
    odd = lax.rem(lax.axis_index("sub"), 2) == 1
    weights_ref[:faces, :] = jnp.where(odd, to_a_ref[faces:, :], from_a_ref[faces:, :])
    weights_ref[faces:, :] = jnp.where(odd, from_b_ref[faces:, :], to_a_ref[faces:, :])
    coupled = spread_jumps(
        block_rows,
        size,
        aligned_ref,
        weights_ref,
        (to_a_ref, to_b_ref),
        (from_a_ref, from_b_ref),
    )
    image_ref[...] = product_ref[...]
    image_ref[:, :size] = image_ref[:, :size] + coupled
    gather_traces(image_ref[...], aligned_ref, (side_a_ref, side_b_ref))


def total_of(value):
    return jnp.sum(jnp.sum(value, axis=0, keepdims=True), axis=1, keepdims=True)


def last_kernel(
    size,
    aligned_ref,
    product_ref,
    weights_ref,
    side_a_ref,
    side_b_ref,
    from_a_ref,
    from_b_ref,
    field_ref,
    image_ref,
    second_ref,
    sums_ref,
):
    block_rows = product_ref.shape[0]
    coupled = spread_jumps(
        block_rows,
        size,
        aligned_ref,
        weights_ref,
        (side_a_ref, side_b_ref),
        (from_a_ref, from_b_ref),
    )
    second_ref[...] = product_ref[...]
    second_ref[:, :size] = second_ref[:, :size] + coupled
    field = field_ref[...]
    image = image_ref[...]
    second = second_ref[...]
    lane = lax.broadcasted_iota(jnp.int32, (1, LANES), 1)
    row = jnp.zeros((1, LANES), F32)
    for k, product in enumerate(
        (field * field, field * image, image * image, field * second, image * second)
    ):
        row = jnp.where(lane == k, total_of(product), row)
    sums_ref[...] = jnp.broadcast_to(row[None], sums_ref.shape)


def final_kernel(field_ref, image_ref, second_ref, sums_ref, solution_ref, residual_ref):
    size = solution_ref.shape[1]
    row = jnp.sum(sums_ref[...], axis=0)
    lane = lax.broadcasted_iota(jnp.int32, (1, LANES), 1)

    def entry(k):
        return jnp.sum(jnp.where(lane == k, row, 0.0), axis=1, keepdims=True)

    bb, bq, qq, bw, qw = (entry(k) for k in range(5))
    field = field_ref[:, :size]
    image = image_ref[:, :size]
    second = second_ref[:, :size]
    alpha = bb / bq
    norm = bb - alpha * (2.0 * bq - alpha * qq)
    beta = norm / bb
    grown = 1.0 + beta
    energy = grown * (grown * bq - alpha * (bw + qq)) + alpha * alpha * qw
    alpha_next = norm / energy
    residual = field - alpha * image
    direction = residual + beta * field
    moved = (image - alpha * second) + beta * image
    solution_ref[...] = alpha * field + alpha_next * direction
    residual_ref[...] = residual - alpha_next * moved


def swap(value, odd):
    count = lax.axis_size("sub")
    pairs = []
    for first in range(odd, count, 2):
        second = (first + 1) % count
        pairs += [(first, second), (second, first)]
    return lax.ppermute(value, "sub", pairs)


def on_device(
    right_side, stiffness, block_pairs, trace_rows, partner_face, owner_list, mortar_weight
):
    field = right_side[0, 0].T
    block_rows, size = field.shape
    stored = stiffness[0, 0]
    blocks = stored.reshape(stored.shape[0], size, size)
    pairs = block_pairs[0, 0]
    rows = trace_rows[0, 0]
    partner = partner_face[0, 0]
    owners = owner_list[0, 0]
    faces = partner.shape[0]
    devices = lax.axis_size("sub") * lax.axis_size("blk")

    held = lax.all_to_all(mortar_weight[0, 0], "blk", split_axis=0, concat_axis=0, tiled=True)
    aligned, padded, chosen, side_a, side_b = call(
        first_kernel,
        [
            shape(2 * faces, jnp.int32),
            shape(block_rows),
            jax.ShapeDtypeStruct((faces, faces), F32),
            shape(faces),
            shape(faces),
        ],
        [(partner, HBM), (owners, HBM), (rows, HBM), (field, HBM)],
        scratch=[
            pltpu.SMEM(partner.shape, jnp.int32),
            pltpu.SMEM(owners.shape, jnp.int32),
            pltpu.VMEM(rows.shape, jnp.int32),
            pltpu.VMEM(field.shape, F32),
            pltpu.SemaphoreType.DMA((4,)),
        ],
    )
    to_a, to_b = call(
        message_kernel,
        [shape(2 * faces)] * 2,
        [(value, VMEM) for value in (held.reshape(faces, LANES), chosen, side_a, side_b)],
    )
    from_a = swap(to_a, 1)
    from_b = swap(to_b, 0)

    def stiff(vector):
        (product,) = call(
            stiffness_kernel,
            [shape(block_rows)],
            [(pairs, SMEM), (blocks, VMEM), (vector, VMEM)],
            scratch=[pltpu.VMEM((block_rows * SUBLANES, LANES), F32)] * 2,
        )
        return product

    image, weights, side_a, side_b = call(
        functools.partial(middle_kernel, size),
        [shape(block_rows), shape(2 * faces), shape(faces), shape(faces)],
        [(value, VMEM) for value in (aligned, stiff(padded), to_a, to_b, from_a, from_b)],
    )
    from_a = swap(side_a, 1)
    from_b = swap(side_b, 0)
    second, sums = call(
        functools.partial(last_kernel, size),
        [shape(block_rows), jax.ShapeDtypeStruct((devices, 1, LANES), F32)],
        [
            (value, VMEM)
            for value in (
                aligned, stiff(image), weights, side_a, side_b, from_a, from_b, padded, image
            )
        ],
    )
    sums = lax.all_to_all(sums, ("sub", "blk"), split_axis=0, concat_axis=0, tiled=True)
    solution_field, residual = call(
        final_kernel,
        [jax.ShapeDtypeStruct((block_rows, size), F32)] * 2,
        [(padded, VMEM), (image, VMEM), (second, VMEM), (sums, VMEM)],
    )
    return (solution_field.T[None, None], residual.T[None, None])


def solution(mesh):
    in_specs = (
        P("sub", "blk", None, None),
        P("sub", "blk", None, None),
        P("sub", "blk", None, None),
        P("sub", "blk", None, None),
        P("sub", "blk", None),
        P("sub", "blk", None),
        P("sub", "blk", None, None, None),
    )
    out_specs = (P("sub", "blk", None, None), P("sub", "blk", None, None))
    return jax.shard_map(
        on_device, mesh=mesh, in_specs=in_specs, out_specs=out_specs, check_vma=False
    )
```

```python
import functools

import jax
import jax.numpy as jnp
from jax import lax
from jax.experimental import pallas as pl
from jax.experimental.pallas import tpu as pltpu
from jax.sharding import PartitionSpec as P

LANES = 128
SUBLANES = 8
VMEM = pl.BlockSpec(memory_space=pltpu.VMEM)
HBM = pl.BlockSpec(memory_space=pltpu.HBM)
SMEM = pl.BlockSpec(memory_space=pltpu.SMEM)
PARAMS = pltpu.CompilerParams(vmem_limit_bytes=32 * 1024 * 1024)
F32 = jnp.float32
BF16 = jnp.bfloat16


def call(body, outs, inputs, scratch=(), flops=1_000_000):
    return pl.pallas_call(
        body,
        out_shape=outs,
        in_specs=[spec for _, spec in inputs],
        out_specs=[VMEM] * len(outs),
        scratch_shapes=list(scratch),
        compiler_params=PARAMS,
        cost_estimate=pl.CostEstimate(
            flops=flops, bytes_accessed=1_000_000, transcendentals=0
        ),
    )(*[value for value, _ in inputs])


def shape(rows, dtype=F32):
    return jax.ShapeDtypeStruct((rows, LANES), dtype)


def halves(value):
    high = value.astype(BF16).astype(F32)
    return high, value - high


def gather_traces(field, rows_ref, traces_refs):
    block_rows = field.shape[0]
    spread = [
        jnp.broadcast_to(field[i : i + 1, :], (SUBLANES, LANES)) for i in range(block_rows)
    ]
    faces = rows_ref.shape[0] // len(traces_refs)
    for side, target in enumerate(traces_refs):

        def step(k, _, target=target, side=side):
            index = rows_ref[tile(side * faces // SUBLANES + k), :]
            dof, row = split(index, block_rows)
            taken = jnp.zeros((SUBLANES, LANES), F32)
            for i in range(block_rows):
                here = jnp.take_along_axis(spread[i], dof, axis=1, mode="promise_in_bounds")
                taken = jnp.where(row == i, here, taken)
            target[tile(k), :] = taken
            return 0

        lax.fori_loop(0, faces // SUBLANES, step, 0, unroll=4)


def tile(k):
    return pl.ds(pl.multiple_of(k * SUBLANES, SUBLANES), SUBLANES)


def split(index, block_rows):
    if block_rows & (block_rows - 1) == 0:
        shift = block_rows.bit_length() - 1
        return index >> shift, index & (block_rows - 1)
    return lax.div(index, block_rows), lax.rem(index, block_rows)


def first_kernel(
    partner_hbm,
    owner_hbm,
    rows_hbm,
    field_hbm,
    aligned_ref,
    padded_ref,
    chosen_ref,
    side_a_ref,
    side_b_ref,
    partner_ref,
    owner_ref,
    rows_ref,
    field_ref,
    sems,
):
    copies = [
        pltpu.make_async_copy(source, target, sems.at[k])
        for k, (source, target) in enumerate(
            (
                (partner_hbm, partner_ref),
                (owner_hbm, owner_ref),
                (rows_hbm, rows_ref),
                (field_hbm, field_ref),
            )
        )
    ]
    for copy in copies:
        copy.start()
    faces = side_a_ref.shape[0]
    per_group = faces // owner_ref.shape[0]
    size = field_ref.shape[1]
    parity = lax.rem(lax.axis_index("sub"), 2)
    east = pl.multiple_of((1 - parity) * faces, faces)
    west = pl.multiple_of(parity * faces, faces)
    padded_ref[...] = jnp.zeros_like(padded_ref)
    lane = lax.broadcasted_iota(jnp.int32, (1, chosen_ref.shape[1]), 1)
    for copy in copies:
        copy.wait()
    aligned_ref[pl.ds(west, faces), :] = rows_ref[faces:, :]
    for f in range(faces):
        place = partner_ref[f]
        source = owner_ref[f // per_group] * per_group + f % per_group
        aligned_ref[pl.ds(east + place, 1), :] = rows_ref[f : f + 1, :]
        chosen_ref[pl.ds(place, 1), :] = jnp.where(lane == source, 1.0, 0.0)
    padded_ref[:, :size] = field_ref[...]
    gather_traces(padded_ref[...], aligned_ref, (side_a_ref, side_b_ref))


def message_kernel(held_ref, chosen_ref, side_a_ref, side_b_ref, to_a_ref, to_b_ref):
    faces = side_a_ref.shape[0]
    own = jnp.dot(
        chosen_ref[...],
        held_ref[...],
        precision=lax.Precision.HIGHEST,
        preferred_element_type=F32,
    )
    for side, target in ((side_a_ref, to_a_ref), (side_b_ref, to_b_ref)):
        target[:faces, :] = side[...]
        target[faces:, :] = own


def stiffness_kernel(pairs_ref, blocks_ref, field_ref, out_ref, pieces, sums):
    block_rows = field_ref.shape[0]
    size = blocks_ref.shape[1]
    count = pairs_ref.shape[1]
    high, low = halves(field_ref[...])
    pieces[...] = jnp.zeros_like(pieces)
    pieces[pl.ds(0, block_rows, stride=SUBLANES), :] = high
    pieces[pl.ds(1, block_rows, stride=SUBLANES), :] = low

    def times(row, block, contract):
        left = pieces[pl.ds(pl.multiple_of(row * SUBLANES, SUBLANES), SUBLANES), :]
        return lax.dot_general(
            left[:, :size].astype(BF16),
            block,
            (((1,), (contract,)), ((), ())),
            preferred_element_type=F32,
        )

    def add(row, value):
        place = pl.ds(pl.multiple_of(row * SUBLANES, SUBLANES), SUBLANES)
        sums[place, :size] = sums[place, :size] + value

    sums[...] = jnp.zeros_like(sums)
    for i in range(block_rows):
        sums[i * SUBLANES : (i + 1) * SUBLANES, :size] = times(i, blocks_ref[i], 1)
    for p in range(count):
        first = pairs_ref[0, p]
        other = pairs_ref[1, p]
        block = blocks_ref[block_rows + p]
        add(first, times(other, block, 1))
        add(other, times(first, block, 0))
    out_ref[...] = (
        sums[pl.ds(0, block_rows, stride=SUBLANES), :]
        + sums[pl.ds(1, block_rows, stride=SUBLANES), :]
    )


def spread_jumps(block_rows, size, aligned_ref, weights_ref, own, arrived):
    faces = weights_ref.shape[0] // 2
    dof_of = lax.broadcasted_iota(jnp.int32, (size, LANES), 0)
    row_of = lax.broadcasted_iota(jnp.int32, (block_rows, LANES), 0)

    def step(k, total, side):
        place = tile(side * faces // SUBLANES + k)
        lam = weights_ref[place, :] * (own[side][tile(k), :] - arrived[side][tile(k), :])
        high, low = halves(lam)
        dof, row = split(aligned_ref[place, :], block_rows)
        left = []
        right = []
        for f in range(SUBLANES):
            here = row_of == row[f : f + 1, :]
            left.append(
                jnp.concatenate(
                    [
                        jnp.where(here, high[f : f + 1, :], 0.0),
                        jnp.where(here, low[f : f + 1, :], 0.0),
                    ],
                    axis=0,
                ).astype(BF16)
            )
            right.append(jnp.where(dof_of == dof[f : f + 1, :], 1.0, 0.0).astype(BF16))
        return total + lax.dot_general(
            jnp.concatenate(left, axis=1),
            jnp.concatenate(right, axis=1),
            (((1,), (1,)), ((), ())),
            preferred_element_type=F32,
        )

    total = jnp.zeros((2 * block_rows, size), F32)
    for side in (0, 1):
        total = lax.fori_loop(
            0, faces // SUBLANES, functools.partial(step, side=side), total, unroll=2
        )
    return total[:block_rows] + total[block_rows:]


def middle_kernel(
    size,
    aligned_ref,
    product_ref,
    to_a_ref,
    to_b_ref,
    from_a_ref,
    from_b_ref,
    image_ref,
    weights_ref,
    side_a_ref,
    side_b_ref,
):
    block_rows = product_ref.shape[0]
    faces = side_a_ref.shape[0]
    odd = lax.rem(lax.axis_index("sub"), 2) == 1
    weights_ref[:faces, :] = jnp.where(odd, to_a_ref[faces:, :], from_a_ref[faces:, :])
    weights_ref[faces:, :] = jnp.where(odd, from_b_ref[faces:, :], to_a_ref[faces:, :])
    coupled = spread_jumps(
        block_rows,
        size,
        aligned_ref,
        weights_ref,
        (to_a_ref, to_b_ref),
        (from_a_ref, from_b_ref),
    )
    image_ref[...] = product_ref[...]
    image_ref[:, :size] = image_ref[:, :size] + coupled
    gather_traces(image_ref[...], aligned_ref, (side_a_ref, side_b_ref))


def sums_kernel(
    product_ref,
    weights_ref,
    side_a_ref,
    side_b_ref,
    from_a_ref,
    from_b_ref,
    first_a_ref,
    first_b_ref,
    field_ref,
    image_ref,
    sums_ref,
):
    faces = side_a_ref.shape[0]
    field = field_ref[...]
    image = image_ref[...]
    product = product_ref[...]
    with_field = jnp.sum(field * product, axis=0, keepdims=True)
    with_image = jnp.sum(image * product, axis=0, keepdims=True)
    for place, own, arrived, first in (
        (slice(0, faces), side_a_ref, from_a_ref, first_a_ref),
        (slice(faces, 2 * faces), side_b_ref, from_b_ref, first_b_ref),
    ):
        lam = weights_ref[place, :] * (own[...] - arrived[...])
        with_field += jnp.sum(lam * first[:faces, :], axis=0, keepdims=True)
        with_image += jnp.sum(lam * own[...], axis=0, keepdims=True)
    lane = lax.broadcasted_iota(jnp.int32, (1, LANES), 1)
    row = jnp.zeros((1, LANES), F32)
    for k, part in enumerate(
        (
            jnp.sum(field * field, axis=0, keepdims=True),
            jnp.sum(field * image, axis=0, keepdims=True),
            jnp.sum(image * image, axis=0, keepdims=True),
            with_field,
            with_image,
        )
    ):
        row = jnp.where(lane == k, jnp.sum(part, axis=1, keepdims=True), row)
    sums_ref[...] = jnp.broadcast_to(row[None], sums_ref.shape)


def second_kernel(
    size,
    aligned_ref,
    product_ref,
    weights_ref,
    side_a_ref,
    side_b_ref,
    from_a_ref,
    from_b_ref,
    second_ref,
):
    second_ref[...] = product_ref[...]
    second_ref[:, :size] = second_ref[:, :size] + spread_jumps(
        product_ref.shape[0],
        size,
        aligned_ref,
        weights_ref,
        (side_a_ref, side_b_ref),
        (from_a_ref, from_b_ref),
    )


def final_kernel(field_ref, image_ref, second_ref, sums_ref, solution_ref, residual_ref):
    size = solution_ref.shape[1]
    row = jnp.sum(sums_ref[...], axis=0)
    lane = lax.broadcasted_iota(jnp.int32, (1, LANES), 1)

    def entry(k):
        return jnp.sum(jnp.where(lane == k, row, 0.0), axis=1, keepdims=True)

    bb, bq, qq, bw, qw = (entry(k) for k in range(5))
    field = field_ref[:, :size]
    image = image_ref[:, :size]
    second = second_ref[:, :size]
    alpha = bb / bq
    norm = bb - alpha * (2.0 * bq - alpha * qq)
    beta = norm / bb
    grown = 1.0 + beta
    energy = grown * (grown * bq - alpha * (bw + qq)) + alpha * alpha * qw
    alpha_next = norm / energy
    residual = field - alpha * image
    direction = residual + beta * field
    moved = (image - alpha * second) + beta * image
    solution_ref[...] = alpha * field + alpha_next * direction
    residual_ref[...] = residual - alpha_next * moved


def swap(value, odd):
    count = lax.axis_size("sub")
    pairs = []
    for first in range(odd, count, 2):
        second = (first + 1) % count
        pairs += [(first, second), (second, first)]
    return lax.ppermute(value, "sub", pairs)


def on_device(
    right_side, stiffness, block_pairs, trace_rows, partner_face, owner_list, mortar_weight
):
    field = right_side[0, 0].T
    block_rows, size = field.shape
    stored = stiffness[0, 0]
    blocks = stored.reshape(stored.shape[0], size, size)
    pairs = block_pairs[0, 0]
    rows = trace_rows[0, 0]
    partner = partner_face[0, 0]
    owners = owner_list[0, 0]
    faces = partner.shape[0]
    devices = lax.axis_size("sub") * lax.axis_size("blk")

    held = lax.all_to_all(mortar_weight[0, 0], "blk", split_axis=0, concat_axis=0, tiled=True)
    aligned, padded, chosen, side_a, side_b = call(
        first_kernel,
        [
            shape(2 * faces, jnp.int32),
            shape(block_rows),
            jax.ShapeDtypeStruct((faces, faces), F32),
            shape(faces),
            shape(faces),
        ],
        [(partner, HBM), (owners, HBM), (rows, HBM), (field, HBM)],
        scratch=[
            pltpu.SMEM(partner.shape, jnp.int32),
            pltpu.SMEM(owners.shape, jnp.int32),
            pltpu.VMEM(rows.shape, jnp.int32),
            pltpu.VMEM(field.shape, F32),
            pltpu.SemaphoreType.DMA((4,)),
        ],
    )
    to_a, to_b = call(
        message_kernel,
        [shape(2 * faces)] * 2,
        [(value, VMEM) for value in (held.reshape(faces, LANES), chosen, side_a, side_b)],
    )
    from_a = swap(to_a, 1)
    from_b = swap(to_b, 0)

    def stiff(vector):
        (product,) = call(
            stiffness_kernel,
            [shape(block_rows)],
            [(pairs, SMEM), (blocks, VMEM), (vector, VMEM)],
            scratch=[pltpu.VMEM((block_rows * SUBLANES, LANES), F32)] * 2,
        )
        return product

    image, weights, side_a, side_b = call(
        functools.partial(middle_kernel, size),
        [shape(block_rows), shape(2 * faces), shape(faces), shape(faces)],
        [(value, VMEM) for value in (aligned, stiff(padded), to_a, to_b, from_a, from_b)],
    )
    from_a = swap(side_a, 1)
    from_b = swap(side_b, 0)
    product = stiff(image)
    jumps = (weights, side_a, side_b, from_a, from_b)
    (sums,) = call(
        sums_kernel,
        [jax.ShapeDtypeStruct((devices, 1, LANES), F32)],
        [(value, VMEM) for value in (product, *jumps, to_a, to_b, padded, image)],
    )
    (second,) = call(
        functools.partial(second_kernel, size),
        [shape(block_rows)],
        [(value, VMEM) for value in (aligned, product, *jumps)],
        flops=1_000_000_000,
    )
    sums = lax.all_to_all(sums, ("sub", "blk"), split_axis=0, concat_axis=0, tiled=True)
    solution_field, residual = call(
        final_kernel,
        [jax.ShapeDtypeStruct((block_rows, size), F32)] * 2,
        [(padded, VMEM), (image, VMEM), (second, VMEM), (sums, VMEM)],
    )
    return (solution_field.T[None, None], residual.T[None, None])


def solution(mesh):
    in_specs = (
        P("sub", "blk", None, None),
        P("sub", "blk", None, None),
        P("sub", "blk", None, None),
        P("sub", "blk", None, None),
        P("sub", "blk", None),
        P("sub", "blk", None),
        P("sub", "blk", None, None, None),
    )
    out_specs = (P("sub", "blk", None, None), P("sub", "blk", None, None))
    return jax.shard_map(
        on_device, mesh=mesh, in_specs=in_specs, out_specs=out_specs, check_vma=False
    )
```

```python
import functools

import jax
import jax.numpy as jnp
from jax import lax
from jax.experimental import pallas as pl
from jax.experimental.pallas import tpu as pltpu
from jax.sharding import PartitionSpec as P

LANES = 128
SUBLANES = 8
VMEM = pl.BlockSpec(memory_space=pltpu.VMEM)
SMEM = pl.BlockSpec(memory_space=pltpu.SMEM)
PARAMS = pltpu.CompilerParams(vmem_limit_bytes=32 * 1024 * 1024)
F32 = jnp.float32
BF16 = jnp.bfloat16


def call(body, outs, inputs, scratch=(), flops=1_000_000):
    return pl.pallas_call(
        body,
        out_shape=outs,
        in_specs=[spec for _, spec in inputs],
        out_specs=[VMEM] * len(outs),
        scratch_shapes=list(scratch),
        compiler_params=PARAMS,
        cost_estimate=pl.CostEstimate(
            flops=flops, bytes_accessed=1_000_000, transcendentals=0
        ),
    )(*[value for value, _ in inputs])


def shape(rows, dtype=F32):
    return jax.ShapeDtypeStruct((rows, LANES), dtype)


def halves(value):
    high = value.astype(BF16).astype(F32)
    return high, value - high


def gather_traces(field, rows_ref, traces_refs):
    block_rows = field.shape[0]
    spread = [
        jnp.broadcast_to(field[i : i + 1, :], (SUBLANES, LANES)) for i in range(block_rows)
    ]
    faces = rows_ref.shape[0] // len(traces_refs)
    for side, target in enumerate(traces_refs):

        def step(k, _, target=target, side=side):
            index = rows_ref[tile(side * faces // SUBLANES + k), :]
            dof, row = split(index, block_rows)
            taken = jnp.zeros((SUBLANES, LANES), F32)
            for i in range(block_rows):
                here = jnp.take_along_axis(spread[i], dof, axis=1, mode="promise_in_bounds")
                taken = jnp.where(row == i, here, taken)
            target[tile(k), :] = taken
            return 0

        lax.fori_loop(0, faces // SUBLANES, step, 0, unroll=4)


def tile(k):
    return pl.ds(pl.multiple_of(k * SUBLANES, SUBLANES), SUBLANES)


def split(index, block_rows):
    if block_rows & (block_rows - 1) == 0:
        shift = block_rows.bit_length() - 1
        return index >> shift, index & (block_rows - 1)
    return lax.div(index, block_rows), lax.rem(index, block_rows)


def one_hot(place, count):
    row = lax.broadcasted_iota(jnp.int32, (count, place.shape[1]), 0)
    return jnp.where(row == place, 1.0, 0.0)


def exact_dot(left, right):
    return jnp.dot(
        left, right, precision=lax.Precision.HIGHEST, preferred_element_type=F32
    )


def first_kernel(
    groups, packed_ref, aligned_ref, padded_ref, chosen_ref, side_a_ref, side_b_ref
):
    faces = side_a_ref.shape[0]
    block_rows = padded_ref.shape[0]
    per_group = faces // groups
    parity = lax.rem(lax.axis_index("sub"), 2)
    east = pl.multiple_of((1 - parity) * faces, faces)
    west = pl.multiple_of(parity * faces, faces)
    padded_ref[...] = packed_ref[2 * faces : 2 * faces + block_rows, :]
    tail = packed_ref[2 * faces + block_rows :, :].astype(jnp.int32)
    partner = tail[:1, :faces]
    face = lax.broadcasted_iota(jnp.int32, (1, faces), 1)
    source = jnp.zeros((1, faces), jnp.int32)
    for g in range(groups):
        inside = face - g * per_group
        source = jnp.where(
            (inside >= 0) & (inside < per_group), tail[1:2, g : g + 1] * per_group + inside, source
        )
    order = one_hot(partner, faces)
    aligned_ref[pl.ds(west, faces), :] = packed_ref[faces : 2 * faces, :].astype(jnp.int32)
    aligned_ref[pl.ds(east, faces), :] = exact_dot(order, packed_ref[:faces, :]).astype(jnp.int32)
    chosen_ref[...] = lax.dot_general(
        order.astype(BF16),
        one_hot(source, faces).astype(BF16),
        (((1,), (1,)), ((), ())),
        preferred_element_type=F32,
    )
    gather_traces(padded_ref[...], aligned_ref, (side_a_ref, side_b_ref))


def message_kernel(held_ref, chosen_ref, side_a_ref, side_b_ref, to_a_ref, to_b_ref):
    faces = side_a_ref.shape[0]
    own = exact_dot(chosen_ref[...], held_ref[...])
    for side, target in ((side_a_ref, to_a_ref), (side_b_ref, to_b_ref)):
        target[:faces, :] = side[...]
        target[faces:, :] = own


def stiffness_kernel(pairs_ref, blocks_ref, field_ref, out_ref, pieces, sums):
    block_rows = field_ref.shape[0]
    size = blocks_ref.shape[1]
    count = pairs_ref.shape[1]
    high, low = halves(field_ref[...])
    pieces[...] = jnp.zeros_like(pieces)
    pieces[pl.ds(0, block_rows, stride=SUBLANES), :] = high
    pieces[pl.ds(1, block_rows, stride=SUBLANES), :] = low

    def times(row, block, contract):
        left = pieces[pl.ds(pl.multiple_of(row * SUBLANES, SUBLANES), SUBLANES), :]
        return lax.dot_general(
            left[:, :size].astype(BF16),
            block,
            (((1,), (contract,)), ((), ())),
            preferred_element_type=F32,
        )

    def add(row, value):
        place = pl.ds(pl.multiple_of(row * SUBLANES, SUBLANES), SUBLANES)
        sums[place, :size] = sums[place, :size] + value

    sums[...] = jnp.zeros_like(sums)
    for i in range(block_rows):
        sums[i * SUBLANES : (i + 1) * SUBLANES, :size] = times(i, blocks_ref[i], 1)
    for p in range(count):
        first = pairs_ref[0, p]
        other = pairs_ref[1, p]
        block = blocks_ref[block_rows + p]
        add(first, times(other, block, 1))
        add(other, times(first, block, 0))
    out_ref[...] = (
        sums[pl.ds(0, block_rows, stride=SUBLANES), :]
        + sums[pl.ds(1, block_rows, stride=SUBLANES), :]
    )


def spread_jumps(block_rows, size, aligned_ref, weights_ref, own, arrived):
    faces = weights_ref.shape[0] // 2
    dof_of = lax.broadcasted_iota(jnp.int32, (size, LANES), 0)
    row_of = lax.broadcasted_iota(jnp.int32, (block_rows, LANES), 0)

    def step(k, total, side):
        place = tile(side * faces // SUBLANES + k)
        lam = weights_ref[place, :] * (own[side][tile(k), :] - arrived[side][tile(k), :])
        high, low = halves(lam)
        dof, row = split(aligned_ref[place, :], block_rows)
        left = []
        right = []
        for f in range(SUBLANES):
            here = row_of == row[f : f + 1, :]
            left.append(
                jnp.concatenate(
                    [
                        jnp.where(here, high[f : f + 1, :], 0.0),
                        jnp.where(here, low[f : f + 1, :], 0.0),
                    ],
                    axis=0,
                ).astype(BF16)
            )
            right.append(jnp.where(dof_of == dof[f : f + 1, :], 1.0, 0.0).astype(BF16))
        return total + lax.dot_general(
            jnp.concatenate(left, axis=1),
            jnp.concatenate(right, axis=1),
            (((1,), (1,)), ((), ())),
            preferred_element_type=F32,
        )

    total = jnp.zeros((2 * block_rows, size), F32)
    for side in (0, 1):
        total = lax.fori_loop(
            0, faces // SUBLANES, functools.partial(step, side=side), total, unroll=2
        )
    return total[:block_rows] + total[block_rows:]


def middle_kernel(
    size,
    aligned_ref,
    product_ref,
    to_a_ref,
    to_b_ref,
    from_a_ref,
    from_b_ref,
    image_ref,
    weights_ref,
    side_a_ref,
    side_b_ref,
):
    block_rows = product_ref.shape[0]
    faces = side_a_ref.shape[0]
    odd = lax.rem(lax.axis_index("sub"), 2) == 1
    weights_ref[:faces, :] = jnp.where(odd, to_a_ref[faces:, :], from_a_ref[faces:, :])
    weights_ref[faces:, :] = jnp.where(odd, from_b_ref[faces:, :], to_a_ref[faces:, :])
    coupled = spread_jumps(
        block_rows,
        size,
        aligned_ref,
        weights_ref,
        (to_a_ref, to_b_ref),
        (from_a_ref, from_b_ref),
    )
    image_ref[...] = product_ref[...]
    image_ref[:, :size] = image_ref[:, :size] + coupled
    gather_traces(image_ref[...], aligned_ref, (side_a_ref, side_b_ref))


def sums_kernel(
    product_ref,
    weights_ref,
    side_a_ref,
    side_b_ref,
    from_a_ref,
    from_b_ref,
    first_a_ref,
    first_b_ref,
    field_ref,
    image_ref,
    sums_ref,
):
    faces = side_a_ref.shape[0]
    field = field_ref[...]
    image = image_ref[...]
    product = product_ref[...]
    with_field = jnp.sum(field * product, axis=0, keepdims=True)
    with_image = jnp.sum(image * product, axis=0, keepdims=True)
    for place, own, arrived, first in (
        (slice(0, faces), side_a_ref, from_a_ref, first_a_ref),
        (slice(faces, 2 * faces), side_b_ref, from_b_ref, first_b_ref),
    ):
        lam = weights_ref[place, :] * (own[...] - arrived[...])
        with_field += jnp.sum(lam * first[:faces, :], axis=0, keepdims=True)
        with_image += jnp.sum(lam * own[...], axis=0, keepdims=True)
    lane = lax.broadcasted_iota(jnp.int32, (1, LANES), 1)
    row = jnp.zeros((1, LANES), F32)
    for k, part in enumerate(
        (
            jnp.sum(field * field, axis=0, keepdims=True),
            jnp.sum(field * image, axis=0, keepdims=True),
            jnp.sum(image * image, axis=0, keepdims=True),
            with_field,
            with_image,
        )
    ):
        row = jnp.where(lane == k, jnp.sum(part, axis=1, keepdims=True), row)
    sums_ref[...] = jnp.broadcast_to(row[None], sums_ref.shape)


def second_kernel(
    size,
    aligned_ref,
    product_ref,
    weights_ref,
    side_a_ref,
    side_b_ref,
    from_a_ref,
    from_b_ref,
    second_ref,
):
    second_ref[...] = product_ref[...]
    second_ref[:, :size] = second_ref[:, :size] + spread_jumps(
        product_ref.shape[0],
        size,
        aligned_ref,
        weights_ref,
        (side_a_ref, side_b_ref),
        (from_a_ref, from_b_ref),
    )


def final_kernel(field_ref, image_ref, second_ref, sums_ref, solution_ref, residual_ref):
    size = solution_ref.shape[1]
    row = jnp.sum(sums_ref[...], axis=0)
    lane = lax.broadcasted_iota(jnp.int32, (1, LANES), 1)

    def entry(k):
        return jnp.sum(jnp.where(lane == k, row, 0.0), axis=1, keepdims=True)

    bb, bq, qq, bw, qw = (entry(k) for k in range(5))
    field = field_ref[:, :size]
    image = image_ref[:, :size]
    second = second_ref[:, :size]
    alpha = bb / bq
    norm = bb - alpha * (2.0 * bq - alpha * qq)
    beta = norm / bb
    grown = 1.0 + beta
    energy = grown * (grown * bq - alpha * (bw + qq)) + alpha * alpha * qw
    alpha_next = norm / energy
    residual = field - alpha * image
    direction = residual + beta * field
    moved = (image - alpha * second) + beta * image
    solution_ref[...] = alpha * field + alpha_next * direction
    residual_ref[...] = residual - alpha_next * moved


def swap(value, odd):
    count = lax.axis_size("sub")
    pairs = []
    for first in range(odd, count, 2):
        second = (first + 1) % count
        pairs += [(first, second), (second, first)]
    return lax.ppermute(value, "sub", pairs)


def on_device(
    right_side, stiffness, block_pairs, trace_rows, partner_face, owner_list, mortar_weight
):
    field = right_side[0, 0].T
    block_rows, size = field.shape
    stored = stiffness[0, 0]
    blocks = stored.reshape(stored.shape[0], size, size)
    pairs = block_pairs[0, 0]
    rows = trace_rows[0, 0]
    partner = partner_face[0, 0]
    owners = owner_list[0, 0]
    faces = partner.shape[0]
    devices = lax.axis_size("sub") * lax.axis_size("blk")

    held = lax.all_to_all(mortar_weight[0, 0], "blk", split_axis=0, concat_axis=0, tiled=True)
    last = 2 * faces + block_rows

    def placed(value, first):
        below = last + SUBLANES - first - value.shape[0]
        return jnp.pad(value, ((first, below), (0, LANES - value.shape[1])))

    indices = placed(rows, 0) + placed(partner_face[0], last) + placed(owner_list[0], last + 1)
    packed = indices.astype(F32) + placed(field, 2 * faces)
    aligned, padded, chosen, side_a, side_b = call(
        functools.partial(first_kernel, owners.shape[0]),
        [
            shape(2 * faces, jnp.int32),
            shape(block_rows),
            jax.ShapeDtypeStruct((faces, faces), F32),
            shape(faces),
            shape(faces),
        ],
        [(packed, VMEM)],
    )
    to_a, to_b = call(
        message_kernel,
        [shape(2 * faces)] * 2,
        [(value, VMEM) for value in (held.reshape(faces, LANES), chosen, side_a, side_b)],
    )
    from_a = swap(to_a, 1)
    from_b = swap(to_b, 0)

    def stiff(vector):
        (product,) = call(
            stiffness_kernel,
            [shape(block_rows)],
            [(pairs, SMEM), (blocks, VMEM), (vector, VMEM)],
            scratch=[pltpu.VMEM((block_rows * SUBLANES, LANES), F32)] * 2,
        )
        return product

    image, weights, side_a, side_b = call(
        functools.partial(middle_kernel, size),
        [shape(block_rows), shape(2 * faces), shape(faces), shape(faces)],
        [(value, VMEM) for value in (aligned, stiff(padded), to_a, to_b, from_a, from_b)],
    )
    from_a = swap(side_a, 1)
    from_b = swap(side_b, 0)
    product = stiff(image)
    jumps = (weights, side_a, side_b, from_a, from_b)
    (sums,) = call(
        sums_kernel,
        [jax.ShapeDtypeStruct((devices, 1, LANES), F32)],
        [(value, VMEM) for value in (product, *jumps, to_a, to_b, padded, image)],
    )
    (second,) = call(
        functools.partial(second_kernel, size),
        [shape(block_rows)],
        [(value, VMEM) for value in (aligned, product, *jumps)],
        flops=1_000_000_000,
    )
    sums = lax.all_to_all(sums, ("sub", "blk"), split_axis=0, concat_axis=0, tiled=True)
    solution_field, residual = call(
        final_kernel,
        [jax.ShapeDtypeStruct((block_rows, size), F32)] * 2,
        [(padded, VMEM), (image, VMEM), (second, VMEM), (sums, VMEM)],
    )
    return (solution_field.T[None, None], residual.T[None, None])


def solution(mesh):
    in_specs = (
        P("sub", "blk", None, None),
        P("sub", "blk", None, None),
        P("sub", "blk", None, None),
        P("sub", "blk", None, None),
        P("sub", "blk", None),
        P("sub", "blk", None),
        P("sub", "blk", None, None, None),
    )
    out_specs = (P("sub", "blk", None, None), P("sub", "blk", None, None))
    return jax.shard_map(
        on_device, mesh=mesh, in_specs=in_specs, out_specs=out_specs, check_vma=False
    )
```

```python
import functools
import math

import jax
import jax.numpy as jnp
from jax import lax
from jax.experimental import pallas as pl
from jax.experimental.pallas import tpu as pltpu
from jax.sharding import PartitionSpec as P

LANES = 128
SUBLANES = 8
VMEM = pl.BlockSpec(memory_space=pltpu.VMEM)
SMEM = pl.BlockSpec(memory_space=pltpu.SMEM)
PARAMS = pltpu.CompilerParams(vmem_limit_bytes=32 * 1024 * 1024)
F32 = jnp.float32
BF16 = jnp.bfloat16


def call(body, outs, inputs, scratch=(), flops=1_000_000):
    return pl.pallas_call(
        body,
        out_shape=outs,
        in_specs=[spec for _, spec in inputs],
        out_specs=[VMEM] * len(outs),
        scratch_shapes=list(scratch),
        compiler_params=PARAMS,
        cost_estimate=pl.CostEstimate(
            flops=flops, bytes_accessed=1_000_000, transcendentals=0
        ),
    )(*[value for value, _ in inputs])


def shape(rows, dtype=F32):
    return jax.ShapeDtypeStruct((rows, LANES), dtype)


def halves(value):
    high = value.astype(BF16).astype(F32)
    return high, value - high


def gather_traces(field, rows_ref, traces_refs):
    block_rows = field.shape[0]
    spread = [
        jnp.broadcast_to(field[i : i + 1, :], (SUBLANES, LANES)) for i in range(block_rows)
    ]
    faces = rows_ref.shape[0] // len(traces_refs)
    for side, target in enumerate(traces_refs):

        def step(k, _, target=target, side=side):
            index = rows_ref[tile(side * faces // SUBLANES + k), :]
            dof, row = split(index, block_rows)
            taken = jnp.zeros((SUBLANES, LANES), F32)
            for i in range(block_rows):
                here = jnp.take_along_axis(spread[i], dof, axis=1, mode="promise_in_bounds")
                taken = jnp.where(row == i, here, taken)
            target[tile(k), :] = taken
            return 0

        lax.fori_loop(0, faces // SUBLANES, step, 0, unroll=4)


def tile(k):
    return pl.ds(pl.multiple_of(k * SUBLANES, SUBLANES), SUBLANES)


def split(index, block_rows):
    if block_rows & (block_rows - 1) == 0:
        shift = block_rows.bit_length() - 1
        return index >> shift, index & (block_rows - 1)
    return lax.div(index, block_rows), lax.rem(index, block_rows)


def one_hot(place, count):
    row = lax.broadcasted_iota(jnp.int32, (count, place.shape[1]), 0)
    return jnp.where(row == place, 1.0, 0.0)


def exact_dot(left, right):
    return jnp.dot(
        left, right, precision=lax.Precision.HIGHEST, preferred_element_type=F32
    )


def first_kernel(
    groups, packed_ref, aligned_ref, padded_ref, chosen_ref, side_a_ref, side_b_ref
):
    faces = side_a_ref.shape[0]
    block_rows = padded_ref.shape[0]
    per_group = faces // groups
    parity = lax.rem(lax.axis_index("sub"), 2)
    east = pl.multiple_of((1 - parity) * faces, faces)
    west = pl.multiple_of(parity * faces, faces)
    padded_ref[...] = packed_ref[2 * faces : 2 * faces + block_rows, :]
    tail = packed_ref[2 * faces + block_rows :, :].astype(jnp.int32)
    partner = tail[:1, :faces]
    face = lax.broadcasted_iota(jnp.int32, (1, faces), 1)
    source = jnp.zeros((1, faces), jnp.int32)
    for g in range(groups):
        inside = face - g * per_group
        source = jnp.where(
            (inside >= 0) & (inside < per_group), tail[1:2, g : g + 1] * per_group + inside, source
        )
    order = one_hot(partner, faces)
    aligned_ref[pl.ds(west, faces), :] = packed_ref[faces : 2 * faces, :].astype(jnp.int32)
    aligned_ref[pl.ds(east, faces), :] = exact_dot(order, packed_ref[:faces, :]).astype(jnp.int32)
    chosen_ref[...] = lax.dot_general(
        order.astype(BF16),
        one_hot(source, faces).astype(BF16),
        (((1,), (1,)), ((), ())),
        preferred_element_type=F32,
    )
    gather_traces(padded_ref[...], aligned_ref, (side_a_ref, side_b_ref))


def message_kernel(held_ref, chosen_ref, side_a_ref, side_b_ref, to_a_ref, to_b_ref):
    faces = side_a_ref.shape[0]
    own = exact_dot(chosen_ref[...], held_ref[...])
    for side, target in ((side_a_ref, to_a_ref), (side_b_ref, to_b_ref)):
        target[:faces, :] = side[...]
        target[faces:, :] = own


def stiffness_kernel(size, pairs_ref, blocks_ref, field_ref, out_ref, ends, mixed):
    block_rows = field_ref.shape[0]
    count = pairs_ref.shape[1]
    width = math.lcm(size, LANES)
    tiles = width // LANES
    segments = width // size
    for p in range(count):
        ends[p : p + 1, :] = field_ref[pl.ds(pairs_ref[1, p], 1), :]
        ends[count + p : count + p + 1, :] = field_ref[pl.ds(pairs_ref[0, p], 1), :]
    right = jnp.concatenate([field_ref[...], ends[:count, :]], axis=0)
    left = ends[count:, :]

    def place(position):
        segment = sum(jnp.where(position >= k * size, 1, 0) for k in range(1, segments))
        return segment, position - segment * size

    def lanes_of(value, index):
        slabs = [
            jnp.take_along_axis(
                value[k : k + SUBLANES, :], index, axis=1, mode="promise_in_bounds"
            )
            for k in range(0, value.shape[0], SUBLANES)
        ]
        return jnp.concatenate(slabs, axis=0)

    lane = lax.broadcasted_iota(jnp.int32, (SUBLANES, LANES), 1)
    places = [place(lane + t * LANES) for t in range(tiles)]
    repeated = jnp.concatenate([lanes_of(right, inside) for _, inside in places], axis=1)
    segment, inside = place(lax.broadcasted_iota(jnp.int32, (width, LANES), 0))
    column = lax.broadcasted_iota(jnp.int32, (width, LANES), 1)
    add_segments = jnp.where(segment == column % segments, 1.0, 0.0).astype(BF16)
    fold = jnp.where(inside == column, 1.0, 0.0)
    dof_group = lax.broadcasted_iota(jnp.int32, (block_rows + count, LANES), 1) // segments

    def step(g, carry):
        total, turned = carry
        stored = blocks_ref[:, pl.ds(pl.multiple_of(g * width, LANES), width)].astype(F32)
        product = stored * repeated
        high = product.astype(BF16)
        low = (product - high.astype(F32)).astype(BF16)
        sums = jnp.dot(
            jnp.concatenate([high, low], axis=0), add_segments, preferred_element_type=F32
        )
        sums = sums[: block_rows + count] + sums[block_rows + count :]
        total = jnp.where(dof_group == g, sums, total)
        across = [lanes_of(left, g * segments + segment) for segment, _ in places]
        turned = turned + stored[block_rows:] * jnp.concatenate(across, axis=1)
        return total, turned

    total, turned = lax.fori_loop(
        0,
        size // segments,
        step,
        (jnp.zeros((block_rows + count, LANES), F32), jnp.zeros((count, width), F32)),
        unroll=4,
    )
    ends[:count, :] = total[block_rows:]
    ends[count:, :] = exact_dot(turned, fold)
    for p in range(count):
        mixed[pl.ds(pairs_ref[0, p], 1), :] = ends[p : p + 1, :]
        mixed[pl.ds(pairs_ref[1, p], 1), :] = ends[count + p : count + p + 1, :]
    out_ref[...] = total[:block_rows] + mixed[...]


def spread_jumps(block_rows, size, aligned_ref, weights_ref, own, arrived):
    faces = weights_ref.shape[0] // 2
    dof_of = lax.broadcasted_iota(jnp.int32, (size, LANES), 0).astype(F32).astype(BF16)
    row_of = lax.broadcasted_iota(jnp.int32, (block_rows, LANES), 0).astype(F32).astype(BF16)
    none = jnp.zeros((), BF16)
    one = jnp.ones((), BF16)

    def widened(value, f, rows):
        slab = jnp.broadcast_to(value[f : f + 1, :], (2 * SUBLANES, LANES)).astype(BF16)
        return jnp.concatenate([slab] * (rows // (2 * SUBLANES)), axis=0)

    def step(k, total, side):
        place = tile(side * faces // SUBLANES + k)
        lam = weights_ref[place, :] * (own[side][tile(k), :] - arrived[side][tile(k), :])
        high, low = halves(lam)
        dof, row = split(aligned_ref[place, :], block_rows)
        dof = dof.astype(F32)
        row = row.astype(F32)
        left = []
        right = []
        for f in range(SUBLANES):
            here = row_of == widened(row, f, block_rows)
            left.append(
                jnp.concatenate(
                    [
                        jnp.where(here, widened(high, f, block_rows), none),
                        jnp.where(here, widened(low, f, block_rows), none),
                    ],
                    axis=0,
                )
            )
            right.append(jnp.where(dof_of == widened(dof, f, size), one, none))
        return total + lax.dot_general(
            jnp.concatenate(left, axis=1),
            jnp.concatenate(right, axis=1),
            (((1,), (1,)), ((), ())),
            preferred_element_type=F32,
        )

    total = jnp.zeros((2 * block_rows, size), F32)
    for side in (0, 1):
        total = lax.fori_loop(
            0, faces // SUBLANES, functools.partial(step, side=side), total, unroll=2
        )
    return total[:block_rows] + total[block_rows:]


def middle_kernel(
    size,
    aligned_ref,
    product_ref,
    to_a_ref,
    to_b_ref,
    from_a_ref,
    from_b_ref,
    image_ref,
    weights_ref,
    side_a_ref,
    side_b_ref,
):
    block_rows = product_ref.shape[0]
    faces = side_a_ref.shape[0]
    odd = lax.rem(lax.axis_index("sub"), 2) == 1
    weights_ref[:faces, :] = jnp.where(odd, to_a_ref[faces:, :], from_a_ref[faces:, :])
    weights_ref[faces:, :] = jnp.where(odd, from_b_ref[faces:, :], to_a_ref[faces:, :])
    coupled = spread_jumps(
        block_rows,
        size,
        aligned_ref,
        weights_ref,
        (to_a_ref, to_b_ref),
        (from_a_ref, from_b_ref),
    )
    image_ref[...] = product_ref[...]
    image_ref[:, :size] = image_ref[:, :size] + coupled
    gather_traces(image_ref[...], aligned_ref, (side_a_ref, side_b_ref))


def sums_kernel(
    product_ref,
    weights_ref,
    side_a_ref,
    side_b_ref,
    from_a_ref,
    from_b_ref,
    first_a_ref,
    first_b_ref,
    field_ref,
    image_ref,
    sums_ref,
):
    faces = side_a_ref.shape[0]
    field = field_ref[...]
    image = image_ref[...]
    product = product_ref[...]
    with_field = jnp.sum(field * product, axis=0, keepdims=True)
    with_image = jnp.sum(image * product, axis=0, keepdims=True)
    for place, own, arrived, first in (
        (slice(0, faces), side_a_ref, from_a_ref, first_a_ref),
        (slice(faces, 2 * faces), side_b_ref, from_b_ref, first_b_ref),
    ):
        lam = weights_ref[place, :] * (own[...] - arrived[...])
        with_field += jnp.sum(lam * first[:faces, :], axis=0, keepdims=True)
        with_image += jnp.sum(lam * own[...], axis=0, keepdims=True)
    lane = lax.broadcasted_iota(jnp.int32, (1, LANES), 1)
    row = jnp.zeros((1, LANES), F32)
    for k, part in enumerate(
        (
            jnp.sum(field * field, axis=0, keepdims=True),
            jnp.sum(field * image, axis=0, keepdims=True),
            jnp.sum(image * image, axis=0, keepdims=True),
            with_field,
            with_image,
        )
    ):
        row = jnp.where(lane == k, jnp.sum(part, axis=1, keepdims=True), row)
    sums_ref[...] = jnp.broadcast_to(row[None], sums_ref.shape)


def second_kernel(
    size,
    aligned_ref,
    product_ref,
    weights_ref,
    side_a_ref,
    side_b_ref,
    from_a_ref,
    from_b_ref,
    second_ref,
):
    second_ref[...] = product_ref[...]
    second_ref[:, :size] = second_ref[:, :size] + spread_jumps(
        product_ref.shape[0],
        size,
        aligned_ref,
        weights_ref,
        (side_a_ref, side_b_ref),
        (from_a_ref, from_b_ref),
    )


def final_kernel(field_ref, image_ref, second_ref, sums_ref, solution_ref, residual_ref):
    size = solution_ref.shape[1]
    row = jnp.sum(sums_ref[...], axis=0)
    lane = lax.broadcasted_iota(jnp.int32, (1, LANES), 1)

    def entry(k):
        return jnp.sum(jnp.where(lane == k, row, 0.0), axis=1, keepdims=True)

    bb, bq, qq, bw, qw = (entry(k) for k in range(5))
    field = field_ref[:, :size]
    image = image_ref[:, :size]
    second = second_ref[:, :size]
    alpha = bb / bq
    norm = bb - alpha * (2.0 * bq - alpha * qq)
    beta = norm / bb
    grown = 1.0 + beta
    energy = grown * (grown * bq - alpha * (bw + qq)) + alpha * alpha * qw
    alpha_next = norm / energy
    residual = field - alpha * image
    direction = residual + beta * field
    moved = (image - alpha * second) + beta * image
    solution_ref[...] = alpha * field + alpha_next * direction
    residual_ref[...] = residual - alpha_next * moved


def swap(value, odd):
    count = lax.axis_size("sub")
    pairs = []
    for first in range(odd, count, 2):
        second = (first + 1) % count
        pairs += [(first, second), (second, first)]
    return lax.ppermute(value, "sub", pairs)


def on_device(
    right_side, stiffness, block_pairs, trace_rows, partner_face, owner_list, mortar_weight
):
    field = right_side[0, 0].T
    block_rows, size = field.shape
    blocks = stiffness[0, 0]
    pairs = block_pairs[0, 0]
    rows = trace_rows[0, 0]
    partner = partner_face[0, 0]
    owners = owner_list[0, 0]
    faces = partner.shape[0]
    devices = lax.axis_size("sub") * lax.axis_size("blk")

    held = lax.all_to_all(mortar_weight[0, 0], "blk", split_axis=0, concat_axis=0, tiled=True)
    last = 2 * faces + block_rows

    def placed(value, first):
        below = last + SUBLANES - first - value.shape[0]
        return jnp.pad(value, ((first, below), (0, LANES - value.shape[1])))

    indices = placed(rows, 0) + placed(partner_face[0], last) + placed(owner_list[0], last + 1)
    packed = indices.astype(F32) + placed(field, 2 * faces)
    aligned, padded, chosen, side_a, side_b = call(
        functools.partial(first_kernel, owners.shape[0]),
        [
            shape(2 * faces, jnp.int32),
            shape(block_rows),
            jax.ShapeDtypeStruct((faces, faces), F32),
            shape(faces),
            shape(faces),
        ],
        [(packed, VMEM)],
    )
    to_a, to_b = call(
        message_kernel,
        [shape(2 * faces)] * 2,
        [(value, VMEM) for value in (held.reshape(faces, LANES), chosen, side_a, side_b)],
    )
    from_a = swap(to_a, 1)
    from_b = swap(to_b, 0)

    def stiff(vector):
        (product,) = call(
            functools.partial(stiffness_kernel, size),
            [shape(block_rows)],
            [(pairs, SMEM), (blocks, VMEM), (vector, VMEM)],
            scratch=[
                pltpu.VMEM((2 * pairs.shape[1], LANES), F32),
                pltpu.VMEM((block_rows, LANES), F32),
            ],
        )
        return product

    image, weights, side_a, side_b = call(
        functools.partial(middle_kernel, size),
        [shape(block_rows), shape(2 * faces), shape(faces), shape(faces)],
        [(value, VMEM) for value in (aligned, stiff(padded), to_a, to_b, from_a, from_b)],
    )
    from_a = swap(side_a, 1)
    from_b = swap(side_b, 0)
    product = stiff(image)
    jumps = (weights, side_a, side_b, from_a, from_b)
    (sums,) = call(
        sums_kernel,
        [jax.ShapeDtypeStruct((devices, 1, LANES), F32)],
        [(value, VMEM) for value in (product, *jumps, to_a, to_b, padded, image)],
    )
    (second,) = call(
        functools.partial(second_kernel, size),
        [shape(block_rows)],
        [(value, VMEM) for value in (aligned, product, *jumps)],
        flops=1_000_000_000,
    )
    sums = lax.all_to_all(sums, ("sub", "blk"), split_axis=0, concat_axis=0, tiled=True)
    solution_field, residual = call(
        final_kernel,
        [jax.ShapeDtypeStruct((block_rows, size), F32)] * 2,
        [(padded, VMEM), (image, VMEM), (second, VMEM), (sums, VMEM)],
    )
    return (solution_field.T[None, None], residual.T[None, None])


def solution(mesh):
    in_specs = (
        P("sub", "blk", None, None),
        P("sub", "blk", None, None),
        P("sub", "blk", None, None),
        P("sub", "blk", None, None),
        P("sub", "blk", None),
        P("sub", "blk", None),
        P("sub", "blk", None, None, None),
    )
    out_specs = (P("sub", "blk", None, None), P("sub", "blk", None, None))
    return jax.shard_map(
        on_device, mesh=mesh, in_specs=in_specs, out_specs=out_specs, check_vma=False
    )
```

```python
import functools
import math

import jax
import jax.numpy as jnp
from jax import lax
from jax.experimental import pallas as pl
from jax.experimental.pallas import tpu as pltpu
from jax.sharding import PartitionSpec as P

LANES = 128
SUBLANES = 8
VMEM = pl.BlockSpec(memory_space=pltpu.VMEM)
HBM = pl.BlockSpec(memory_space=pltpu.HBM)
F32 = jnp.float32
BF16 = jnp.bfloat16


def call(body, outs, inputs, scratch=(), flops=1_000_000, moved=1_000_000, limit=32 * 1024 * 1024):
    return pl.pallas_call(
        body,
        out_shape=outs,
        in_specs=[spec for _, spec in inputs],
        out_specs=[VMEM] * len(outs),
        scratch_shapes=list(scratch),
        compiler_params=pltpu.CompilerParams(vmem_limit_bytes=limit),
        cost_estimate=pl.CostEstimate(
            flops=flops, bytes_accessed=moved, transcendentals=0
        ),
    )(*[value for value, _ in inputs])


def shape(rows, dtype=F32):
    return jax.ShapeDtypeStruct((rows, LANES), dtype)


def halves(value):
    high = value.astype(BF16).astype(F32)
    return high, value - high


def gather_traces(field, rows_ref, rows_first, target):
    block_rows = field.shape[0]
    spread = [
        jnp.broadcast_to(field[i : i + 1, :], (SUBLANES, LANES)) for i in range(block_rows)
    ]
    for k in range(target.shape[0] // SUBLANES):
        index = rows_ref[rows_first + k * SUBLANES : rows_first + (k + 1) * SUBLANES, :]
        dof, row = split(index, block_rows)
        taken = jnp.zeros((SUBLANES, LANES), F32)
        for i in range(block_rows):
            here = jnp.take_along_axis(spread[i], dof, axis=1, mode="promise_in_bounds")
            taken = jnp.where(row == i, here, taken)
        target[k * SUBLANES : (k + 1) * SUBLANES, :] = taken


def tile(k):
    return pl.ds(pl.multiple_of(k * SUBLANES, SUBLANES), SUBLANES)


def split(index, block_rows):
    if block_rows & (block_rows - 1) == 0:
        shift = block_rows.bit_length() - 1
        return index >> shift, index & (block_rows - 1)
    return lax.div(index, block_rows), lax.rem(index, block_rows)


def one_hot(place, count):
    row = lax.broadcasted_iota(jnp.int32, (count, place.shape[1]), 0)
    return jnp.where(row == place, 1.0, 0.0)


def exact_dot(left, right):
    return jnp.dot(
        left, right, precision=lax.Precision.HIGHEST, preferred_element_type=F32
    )


def first_kernel(
    groups, packed_ref, aligned_ref, padded_ref, chosen_ref, side_a_ref
):
    faces = side_a_ref.shape[0]
    block_rows = padded_ref.shape[0]
    per_group = faces // groups
    parity = lax.rem(lax.axis_index("sub"), 2)
    east = pl.multiple_of((1 - parity) * faces, faces)
    west = pl.multiple_of(parity * faces, faces)
    padded_ref[...] = packed_ref[2 * faces : 2 * faces + block_rows, :]
    tail = packed_ref[2 * faces + block_rows :, :].astype(jnp.int32)
    partner = tail[:1, :faces]
    face = lax.broadcasted_iota(jnp.int32, (1, faces), 1)
    source = jnp.zeros((1, faces), jnp.int32)
    for g in range(groups):
        inside = face - g * per_group
        source = jnp.where(
            (inside >= 0) & (inside < per_group), tail[1:2, g : g + 1] * per_group + inside, source
        )
    order = one_hot(partner, faces)
    aligned_ref[pl.ds(west, faces), :] = packed_ref[faces : 2 * faces, :].astype(jnp.int32)
    aligned_ref[pl.ds(east, faces), :] = exact_dot(order, packed_ref[:faces, :]).astype(jnp.int32)
    chosen_ref[...] = lax.dot_general(
        order.astype(BF16),
        one_hot(source, faces).astype(BF16),
        (((1,), (1,)), ((), ())),
        preferred_element_type=F32,
    )
    gather_traces(padded_ref[...], aligned_ref, 0, side_a_ref)


def far_message_kernel(held_ref, chosen_ref, side_a_ref, to_a_ref):
    faces = side_a_ref.shape[0]
    to_a_ref[:faces, :] = side_a_ref[...]
    to_a_ref[faces : 2 * faces, :] = exact_dot(chosen_ref[...], held_ref[...])
    to_a_ref[2 * faces :, :] = jnp.zeros_like(to_a_ref[2 * faces :, :])


def near_message_kernel(aligned_ref, padded_ref, to_a_ref, to_b_ref):
    faces = to_b_ref.shape[0] // 2
    to_b_ref[faces:, :] = to_a_ref[faces : 2 * faces, :]
    gather_traces(padded_ref[...], aligned_ref, faces, to_b_ref.at[:faces, :])


def near_traces_kernel(aligned_ref, image_ref, side_b_ref):
    gather_traces(image_ref[...], aligned_ref, side_b_ref.shape[0], side_b_ref)


def stiffness_kernel(
    size, count, pieces, packed_ref, field_ref, blocks_hbm, out_ref, blocks_ref, sems
):
    block_rows = field_ref.shape[0]
    width = math.lcm(size, LANES)
    tiles = width // LANES
    segments = width // size
    groups = size // segments // pieces
    copies = []
    for k in range(pieces):
        part = slice(k * groups * width, (k + 1) * groups * width)
        copies.append(
            pltpu.make_async_copy(blocks_hbm.at[:, part], blocks_ref.at[:, part], sems.at[k])
        )
        copies[-1].start()

    def place(position):
        segment = sum(jnp.where(position >= k * size, 1, 0) for k in range(1, segments))
        return segment, position - segment * size

    def lanes_of(value, index):
        slabs = [
            jnp.take_along_axis(
                value[k : k + SUBLANES, :], index, axis=1, mode="promise_in_bounds"
            )
            for k in range(0, value.shape[0], SUBLANES)
        ]
        return jnp.concatenate(slabs, axis=0)

    tail = packed_ref[packed_ref.shape[0] - SUBLANES :, :].astype(jnp.int32)
    first_of, other_of = (one_hot(tail[k : k + 1, :count], block_rows) for k in (2, 3))
    field = field_ref[...]
    left, other = (
        lax.dot_general(
            ends,
            field,
            (((0,), (0,)), ((), ())),
            precision=lax.Precision.HIGHEST,
            preferred_element_type=F32,
        )
        for ends in (first_of, other_of)
    )
    right = jnp.concatenate([field, other], axis=0)
    lane = lax.broadcasted_iota(jnp.int32, (SUBLANES, LANES), 1)
    places = [place(lane + t * LANES) for t in range(tiles)]
    repeated = jnp.concatenate([lanes_of(right, inside) for _, inside in places], axis=1)
    segment, inside = place(lax.broadcasted_iota(jnp.int32, (width, LANES), 0))
    column = lax.broadcasted_iota(jnp.int32, (width, LANES), 1)
    add_segments = jnp.where(segment == column % segments, 1.0, 0.0).astype(BF16)
    fold = jnp.where(inside == column, 1.0, 0.0)
    rows = block_rows + count
    dof_group = lax.broadcasted_iota(jnp.int32, (rows, LANES), 1) // segments
    total = jnp.zeros((rows, LANES), F32)
    turned = jnp.zeros((count, width), F32)
    for k in range(pieces):
        copies[k].wait()
        stack = []
        for g in range(k * groups, (k + 1) * groups):
            stored = blocks_ref[:, g * width : (g + 1) * width].astype(F32)
            product = stored * repeated
            high = product.astype(BF16)
            stack += [high, (product - high.astype(F32)).astype(BF16)]
            across = [lanes_of(left, g * segments + segment) for segment, _ in places]
            turned = turned + stored[block_rows:] * jnp.concatenate(across, axis=1)
        sums = jnp.dot(
            jnp.concatenate(stack, axis=0), add_segments, preferred_element_type=F32
        )
        for n in range(groups):
            both = sums[2 * n * rows : 2 * (n + 1) * rows]
            total = jnp.where(dof_group == k * groups + n, both[:rows] + both[rows:], total)
    out_ref[...] = (
        total[:block_rows]
        + exact_dot(first_of, total[block_rows:])
        + exact_dot(other_of, exact_dot(turned, fold))
    )


def spread_jumps(size, faces, rows_ref, rows_first, weights_ref, own_ref, arrived_ref, block_rows):
    dof_of = lax.broadcasted_iota(jnp.int32, (size, LANES), 0).astype(F32).astype(BF16)
    row_of = lax.broadcasted_iota(jnp.int32, (block_rows, LANES), 0).astype(F32).astype(BF16)
    none = jnp.zeros((), BF16)
    one = jnp.ones((), BF16)

    def widened(value, f, rows):
        slab = jnp.broadcast_to(value[f : f + 1, :], (2 * SUBLANES, LANES)).astype(BF16)
        return jnp.concatenate([slab] * (rows // (2 * SUBLANES)), axis=0)

    def step(k, total):
        lam = weights_ref[tile(k), :] * (own_ref[tile(k), :] - arrived_ref[tile(k), :])
        high, low = halves(lam)
        dof, row = split(rows_ref[tile(rows_first // SUBLANES + k), :], block_rows)
        dof = dof.astype(F32)
        row = row.astype(F32)
        left = []
        right = []
        for f in range(SUBLANES):
            here = row_of == widened(row, f, block_rows)
            left.append(
                jnp.concatenate(
                    [
                        jnp.where(here, widened(high, f, block_rows), none),
                        jnp.where(here, widened(low, f, block_rows), none),
                    ],
                    axis=0,
                )
            )
            right.append(jnp.where(dof_of == widened(dof, f, size), one, none))
        return total + lax.dot_general(
            jnp.concatenate(left, axis=1),
            jnp.concatenate(right, axis=1),
            (((1,), (1,)), ((), ())),
            preferred_element_type=F32,
        )

    total = lax.fori_loop(
        0, faces // SUBLANES, step, jnp.zeros((2 * block_rows, size), F32), unroll=8
    )
    return total[:block_rows] + total[block_rows:]


def near_kernel(size, aligned_ref, product_ref, to_ref, from_ref, partial_ref, weights_ref):
    block_rows = product_ref.shape[0]
    faces = weights_ref.shape[0]
    odd = lax.rem(lax.axis_index("sub"), 2) == 1
    weights_ref[...] = jnp.where(odd, from_ref[faces:, :], to_ref[faces:, :])
    partial_ref[...] = product_ref[...]
    partial_ref[:, :size] = partial_ref[:, :size] + spread_jumps(
        size, faces, aligned_ref, faces, weights_ref, to_ref, from_ref, block_rows
    )


def far_kernel(
    size,
    aligned_ref,
    partial_ref,
    to_ref,
    from_ref,
    image_ref,
    weights_ref,
    side_a_ref,
):
    block_rows = partial_ref.shape[0]
    faces = weights_ref.shape[0]
    odd = lax.rem(lax.axis_index("sub"), 2) == 1
    weights_ref[...] = jnp.where(
        odd, to_ref[faces : 2 * faces, :], from_ref[faces : 2 * faces, :]
    )
    image_ref[...] = partial_ref[...]
    image_ref[:, :size] = image_ref[:, :size] + spread_jumps(
        size, faces, aligned_ref, 0, weights_ref, to_ref, from_ref, block_rows
    )
    gather_traces(image_ref[...], aligned_ref, 0, side_a_ref.at[:faces, :])
    side_a_ref[faces:, :] = jnp.zeros_like(side_a_ref[faces:, :])


def column_sums(value):
    return jnp.sum(value, axis=0, keepdims=True)


def jump_sums(weights_ref, own_ref, arrived_ref, first_ref):
    faces = slice(0, weights_ref.shape[0])
    own = own_ref[faces, :]
    lam = weights_ref[...] * (own - arrived_ref[faces, :])
    return column_sums(lam * first_ref[faces, :]), column_sums(lam * own)


def near_sums_kernel(
    product_ref, weights_ref, own_ref, arrived_ref, first_ref, field_ref, image_ref, rows_ref
):
    field = field_ref[...]
    image = image_ref[...]
    product = product_ref[...]
    with_field, with_image = jump_sums(weights_ref, own_ref, arrived_ref, first_ref)
    parts = [
        column_sums(field * field),
        column_sums(field * image),
        column_sums(image * image),
        column_sums(field * product) + with_field,
        column_sums(image * product) + with_image,
    ]
    parts += [jnp.zeros_like(parts[0])] * (SUBLANES - len(parts))
    rows_ref[...] = jnp.concatenate(parts, axis=0)


def sums_kernel(rows_ref, weights_ref, own_ref, arrived_ref, first_ref, sums_ref):
    with_field, with_image = jump_sums(weights_ref, own_ref, arrived_ref, first_ref)
    row = lax.broadcasted_iota(jnp.int32, (SUBLANES, LANES), 0)
    rows = rows_ref[...] + jnp.where(row == 3, with_field, jnp.where(row == 4, with_image, 0.0))
    lane = lax.broadcasted_iota(jnp.int32, (SUBLANES, LANES), 1)
    whole = jnp.sum(rows, axis=1, keepdims=True)
    packed = column_sums(jnp.where(lane == row, whole, 0.0))
    sums_ref[...] = jnp.broadcast_to(packed[None], sums_ref.shape)


def second_kernel(
    size,
    aligned_ref,
    product_ref,
    weights_a_ref,
    weights_b_ref,
    side_a_ref,
    side_b_ref,
    from_a_ref,
    from_b_ref,
    second_ref,
):
    block_rows = product_ref.shape[0]
    faces = weights_a_ref.shape[0]
    second_ref[...] = product_ref[...]
    second_ref[:, :size] = (
        second_ref[:, :size]
        + spread_jumps(
            size, faces, aligned_ref, 0, weights_a_ref, side_a_ref, from_a_ref, block_rows
        )
        + spread_jumps(
            size, faces, aligned_ref, faces, weights_b_ref, side_b_ref, from_b_ref, block_rows
        )
    )


def final_kernel(field_ref, image_ref, second_ref, sums_ref, solution_ref, residual_ref):
    size = solution_ref.shape[1]
    row = jnp.sum(sums_ref[...], axis=0)
    lane = lax.broadcasted_iota(jnp.int32, (1, LANES), 1)

    def entry(k):
        return jnp.sum(jnp.where(lane == k, row, 0.0), axis=1, keepdims=True)

    bb, bq, qq, bw, qw = (entry(k) for k in range(5))
    field = field_ref[:, :size]
    image = image_ref[:, :size]
    second = second_ref[:, :size]
    alpha = bb / bq
    norm = bb - alpha * (2.0 * bq - alpha * qq)
    beta = norm / bb
    grown = 1.0 + beta
    energy = grown * (grown * bq - alpha * (bw + qq)) + alpha * alpha * qw
    alpha_next = norm / energy
    residual = field - alpha * image
    direction = residual + beta * field
    moved = (image - alpha * second) + beta * image
    solution_ref[...] = alpha * field + alpha_next * direction
    residual_ref[...] = residual - alpha_next * moved


def swap(value, odd):
    count = lax.axis_size("sub")
    pairs = []
    for first in range(odd, count, 2):
        second = (first + 1) % count
        pairs += [(first, second), (second, first)]
    return lax.ppermute(value, "sub", pairs)


def on_device(
    right_side, stiffness, block_pairs, trace_rows, partner_face, owner_list, mortar_weight
):
    field = right_side[0, 0].T
    block_rows, size = field.shape
    blocks = stiffness[0, 0]
    pairs = block_pairs[0, 0]
    rows = trace_rows[0, 0]
    partner = partner_face[0, 0]
    owners = owner_list[0, 0]
    faces = partner.shape[0]
    devices = lax.axis_size("sub") * lax.axis_size("blk")

    held = lax.all_to_all(mortar_weight[0, 0], "blk", split_axis=0, concat_axis=0, tiled=True)
    last = 2 * faces + block_rows

    def placed(value, first):
        below = last + SUBLANES - first - value.shape[0]
        return jnp.pad(value, ((first, below), (0, LANES - value.shape[1])))

    indices = (
        placed(rows, 0)
        + placed(partner_face[0], last)
        + placed(owner_list[0], last + 1)
        + placed(pairs, last + 2)
    )
    packed = indices.astype(F32) + placed(field, 2 * faces)
    aligned, padded, chosen, side_a = call(
        functools.partial(first_kernel, owners.shape[0]),
        [
            shape(2 * faces, jnp.int32),
            shape(block_rows),
            jax.ShapeDtypeStruct((faces, faces), F32),
            shape(faces),
        ],
        [(packed, VMEM)],
    )
    (to_a,) = call(
        far_message_kernel,
        [shape(2 * faces + SUBLANES)],
        [(value, VMEM) for value in (held.reshape(faces, LANES), chosen, side_a)],
    )
    from_a = swap(to_a, 1)
    (to_b,) = call(
        near_message_kernel,
        [shape(2 * faces)],
        [(value, VMEM) for value in (aligned, padded, to_a)],
    )
    from_b = swap(to_b, 0)
    pieces = next(k for k in (6, 4, 3, 2, 1) if size * size // math.lcm(size, LANES) % k == 0)

    def stiff(vector):
        (product,) = call(
            functools.partial(stiffness_kernel, size, pairs.shape[1], pieces),
            [shape(block_rows)],
            [(packed, VMEM), (vector, VMEM), (blocks, HBM)],
            scratch=[pltpu.VMEM(blocks.shape, BF16), pltpu.SemaphoreType.DMA((pieces,))],
            limit=66_300_000,
        )
        return product

    partial, weights_b = call(
        functools.partial(near_kernel, size),
        [shape(block_rows), shape(faces)],
        [(value, VMEM) for value in (aligned, stiff(padded), to_b, from_b)],
        flops=1,
        moved=1,
    )
    image, weights_a, side_a = call(
        functools.partial(far_kernel, size),
        [shape(block_rows), shape(faces), shape(faces + SUBLANES)],
        [(value, VMEM) for value in (aligned, partial, to_a, from_a)],
    )
    from_a = swap(side_a, 1)
    (side_b,) = call(
        near_traces_kernel, [shape(faces)], [(aligned, VMEM), (image, VMEM)]
    )
    from_b = swap(side_b, 0)
    product = stiff(image)
    (sums,) = call(
        near_sums_kernel,
        [shape(SUBLANES)],
        [(value, VMEM) for value in (product, weights_b, side_b, from_b, to_b, padded, image)],
        flops=1,
        moved=1,
    )
    (sums,) = call(
        sums_kernel,
        [jax.ShapeDtypeStruct((devices, 1, LANES), F32)],
        [(value, VMEM) for value in (sums, weights_a, side_a, from_a, to_a)],
    )
    (second,) = call(
        functools.partial(second_kernel, size),
        [shape(block_rows)],
        [
            (value, VMEM)
            for value in (
                aligned, product, weights_a, weights_b, side_a, side_b, from_a, from_b
            )
        ],
        flops=1_000_000_000,
    )
    sums = lax.all_to_all(sums, ("sub", "blk"), split_axis=0, concat_axis=0, tiled=True)
    solution_field, residual = call(
        final_kernel,
        [jax.ShapeDtypeStruct((block_rows, size), F32)] * 2,
        [(padded, VMEM), (image, VMEM), (second, VMEM), (sums, VMEM)],
    )
    return (solution_field.T[None, None], residual.T[None, None])


def solution(mesh):
    in_specs = (
        P("sub", "blk", None, None),
        P("sub", "blk", None, None),
        P("sub", "blk", None, None),
        P("sub", "blk", None, None),
        P("sub", "blk", None),
        P("sub", "blk", None),
        P("sub", "blk", None, None, None),
    )
    out_specs = (P("sub", "blk", None, None), P("sub", "blk", None, None))
    return jax.shard_map(
        on_device, mesh=mesh, in_specs=in_specs, out_specs=out_specs, check_vma=False
    )
```

```python
import functools

import jax
import jax.numpy as jnp
from jax import lax
from jax.experimental import pallas as pl
from jax.experimental.pallas import tpu as pltpu
from jax.sharding import PartitionSpec as P

LANES = 128
SUBLANES = 8
VMEM = pl.BlockSpec(memory_space=pltpu.VMEM)
SMEM = pl.BlockSpec(memory_space=pltpu.SMEM)
F32 = jnp.float32
BF16 = jnp.bfloat16


def call(body, outs, inputs, scratch=(), flops=1_000_000, moved=1_000_000):
    return pl.pallas_call(
        body,
        out_shape=outs,
        in_specs=[spec for _, spec in inputs],
        out_specs=[VMEM] * len(outs),
        scratch_shapes=list(scratch),
        compiler_params=pltpu.CompilerParams(vmem_limit_bytes=32 * 1024 * 1024),
        cost_estimate=pl.CostEstimate(
            flops=flops, bytes_accessed=moved, transcendentals=0
        ),
    )(*[value for value, _ in inputs])


def shape(rows, dtype=F32):
    return jax.ShapeDtypeStruct((rows, LANES), dtype)


def halves(value):
    high = value.astype(BF16).astype(F32)
    return high, value - high


def gather_traces(field, rows_ref, rows_first, target):
    block_rows = field.shape[0]
    spread = [
        jnp.broadcast_to(field[i : i + 1, :], (SUBLANES, LANES)) for i in range(block_rows)
    ]
    for k in range(target.shape[0] // SUBLANES):
        index = rows_ref[rows_first + k * SUBLANES : rows_first + (k + 1) * SUBLANES, :]
        dof, row = split(index, block_rows)
        taken = jnp.zeros((SUBLANES, LANES), F32)
        for i in range(block_rows):
            here = jnp.take_along_axis(spread[i], dof, axis=1, mode="promise_in_bounds")
            taken = jnp.where(row == i, here, taken)
        target[k * SUBLANES : (k + 1) * SUBLANES, :] = taken


def tile(k):
    return pl.ds(pl.multiple_of(k * SUBLANES, SUBLANES), SUBLANES)


def split(index, block_rows):
    if block_rows & (block_rows - 1) == 0:
        shift = block_rows.bit_length() - 1
        return index >> shift, index & (block_rows - 1)
    return lax.div(index, block_rows), lax.rem(index, block_rows)


def one_hot(place, count):
    row = lax.broadcasted_iota(jnp.int32, (count, place.shape[1]), 0)
    return jnp.where(row == place, 1.0, 0.0)


def exact_dot(left, right):
    return jnp.dot(
        left, right, precision=lax.Precision.HIGHEST, preferred_element_type=F32
    )


def first_kernel(
    groups, packed_ref, aligned_ref, padded_ref, chosen_ref, side_a_ref
):
    faces = side_a_ref.shape[0]
    block_rows = padded_ref.shape[0]
    per_group = faces // groups
    parity = lax.rem(lax.axis_index("sub"), 2)
    east = pl.multiple_of((1 - parity) * faces, faces)
    west = pl.multiple_of(parity * faces, faces)
    padded_ref[...] = packed_ref[2 * faces : 2 * faces + block_rows, :]
    tail = packed_ref[2 * faces + block_rows :, :].astype(jnp.int32)
    partner = tail[:1, :faces]
    face = lax.broadcasted_iota(jnp.int32, (1, faces), 1)
    source = jnp.zeros((1, faces), jnp.int32)
    for g in range(groups):
        inside = face - g * per_group
        source = jnp.where(
            (inside >= 0) & (inside < per_group), tail[1:2, g : g + 1] * per_group + inside, source
        )
    order = one_hot(partner, faces)
    aligned_ref[pl.ds(west, faces), :] = packed_ref[faces : 2 * faces, :].astype(jnp.int32)
    aligned_ref[pl.ds(east, faces), :] = exact_dot(order, packed_ref[:faces, :]).astype(jnp.int32)
    chosen_ref[...] = lax.dot_general(
        order.astype(BF16),
        one_hot(source, faces).astype(BF16),
        (((1,), (1,)), ((), ())),
        preferred_element_type=F32,
    )
    gather_traces(padded_ref[...], aligned_ref, 0, side_a_ref)


def far_message_kernel(held_ref, chosen_ref, side_a_ref, to_a_ref):
    faces = side_a_ref.shape[0]
    to_a_ref[:faces, :] = side_a_ref[...]
    to_a_ref[faces : 2 * faces, :] = exact_dot(chosen_ref[...], held_ref[...])
    to_a_ref[2 * faces :, :] = jnp.zeros_like(to_a_ref[2 * faces :, :])


def near_message_kernel(aligned_ref, padded_ref, to_a_ref, to_b_ref):
    faces = to_b_ref.shape[0] // 2
    to_b_ref[faces:, :] = to_a_ref[faces : 2 * faces, :]
    gather_traces(padded_ref[...], aligned_ref, faces, to_b_ref.at[:faces, :])


def near_traces_kernel(aligned_ref, image_ref, side_b_ref):
    gather_traces(image_ref[...], aligned_ref, side_b_ref.shape[0], side_b_ref)


def stiffness_kernel(pairs_ref, blocks_ref, field_ref, out_ref, pieces, sums):
    block_rows = field_ref.shape[0]
    size = blocks_ref.shape[1]
    count = pairs_ref.shape[1]
    high, low = halves(field_ref[...])
    pieces[...] = jnp.zeros_like(pieces)
    pieces[pl.ds(0, block_rows, stride=SUBLANES), :] = high
    pieces[pl.ds(1, block_rows, stride=SUBLANES), :] = low

    def times(row, block, contract):
        left = pieces[pl.ds(pl.multiple_of(row * SUBLANES, SUBLANES), SUBLANES), :]
        return lax.dot_general(
            left[:, :size].astype(BF16),
            block,
            (((1,), (contract,)), ((), ())),
            preferred_element_type=F32,
        )

    def add(row, value):
        place = pl.ds(pl.multiple_of(row * SUBLANES, SUBLANES), SUBLANES)
        sums[place, :size] = sums[place, :size] + value

    sums[...] = jnp.zeros_like(sums)
    for i in range(block_rows):
        sums[i * SUBLANES : (i + 1) * SUBLANES, :size] = times(i, blocks_ref[i], 1)
    for p in range(count):
        first = pairs_ref[0, p]
        other = pairs_ref[1, p]
        block = blocks_ref[block_rows + p]
        add(first, times(other, block, 1))
        add(other, times(first, block, 0))
    out_ref[...] = (
        sums[pl.ds(0, block_rows, stride=SUBLANES), :]
        + sums[pl.ds(1, block_rows, stride=SUBLANES), :]
    )


def spread_jumps(size, faces, rows_ref, rows_first, weights_ref, own_ref, arrived_ref, block_rows):
    dof_of = lax.broadcasted_iota(jnp.int32, (size, LANES), 0).astype(F32).astype(BF16)
    row_of = lax.broadcasted_iota(jnp.int32, (block_rows, LANES), 0).astype(F32).astype(BF16)
    none = jnp.zeros((), BF16)
    one = jnp.ones((), BF16)

    def widened(value, f, rows):
        slab = jnp.broadcast_to(value[f : f + 1, :], (2 * SUBLANES, LANES)).astype(BF16)
        return jnp.concatenate([slab] * (rows // (2 * SUBLANES)), axis=0)

    def step(k, total):
        lam = weights_ref[tile(k), :] * (own_ref[tile(k), :] - arrived_ref[tile(k), :])
        high, low = halves(lam)
        dof, row = split(rows_ref[tile(rows_first // SUBLANES + k), :], block_rows)
        dof = dof.astype(F32)
        row = row.astype(F32)
        left = []
        right = []
        for f in range(SUBLANES):
            here = row_of == widened(row, f, block_rows)
            left.append(
                jnp.concatenate(
                    [
                        jnp.where(here, widened(high, f, block_rows), none),
                        jnp.where(here, widened(low, f, block_rows), none),
                    ],
                    axis=0,
                )
            )
            right.append(jnp.where(dof_of == widened(dof, f, size), one, none))
        return total + lax.dot_general(
            jnp.concatenate(left, axis=1),
            jnp.concatenate(right, axis=1),
            (((1,), (1,)), ((), ())),
            preferred_element_type=F32,
        )

    total = lax.fori_loop(
        0, faces // SUBLANES, step, jnp.zeros((2 * block_rows, size), F32), unroll=8
    )
    return total[:block_rows] + total[block_rows:]


def near_kernel(size, aligned_ref, product_ref, to_ref, from_ref, partial_ref, weights_ref):
    block_rows = product_ref.shape[0]
    faces = weights_ref.shape[0]
    odd = lax.rem(lax.axis_index("sub"), 2) == 1
    weights_ref[...] = jnp.where(odd, from_ref[faces:, :], to_ref[faces:, :])
    partial_ref[...] = product_ref[...]
    partial_ref[:, :size] = partial_ref[:, :size] + spread_jumps(
        size, faces, aligned_ref, faces, weights_ref, to_ref, from_ref, block_rows
    )


def far_kernel(
    size,
    aligned_ref,
    partial_ref,
    to_ref,
    from_ref,
    image_ref,
    weights_ref,
    side_a_ref,
):
    block_rows = partial_ref.shape[0]
    faces = weights_ref.shape[0]
    odd = lax.rem(lax.axis_index("sub"), 2) == 1
    weights_ref[...] = jnp.where(
        odd, to_ref[faces : 2 * faces, :], from_ref[faces : 2 * faces, :]
    )
    image_ref[...] = partial_ref[...]
    image_ref[:, :size] = image_ref[:, :size] + spread_jumps(
        size, faces, aligned_ref, 0, weights_ref, to_ref, from_ref, block_rows
    )
    gather_traces(image_ref[...], aligned_ref, 0, side_a_ref.at[:faces, :])
    side_a_ref[faces:, :] = jnp.zeros_like(side_a_ref[faces:, :])


def column_sums(value):
    return jnp.sum(value, axis=0, keepdims=True)


def jump_sums(weights_ref, own_ref, arrived_ref, first_ref):
    faces = slice(0, weights_ref.shape[0])
    own = own_ref[faces, :]
    lam = weights_ref[...] * (own - arrived_ref[faces, :])
    return column_sums(lam * first_ref[faces, :]), column_sums(lam * own)


def near_sums_kernel(
    product_ref, weights_ref, own_ref, arrived_ref, first_ref, field_ref, image_ref, rows_ref
):
    field = field_ref[...]
    image = image_ref[...]
    product = product_ref[...]
    with_field, with_image = jump_sums(weights_ref, own_ref, arrived_ref, first_ref)
    parts = [
        column_sums(field * field),
        column_sums(field * image),
        column_sums(image * image),
        column_sums(field * product) + with_field,
        column_sums(image * product) + with_image,
    ]
    parts += [jnp.zeros_like(parts[0])] * (SUBLANES - len(parts))
    rows_ref[...] = jnp.concatenate(parts, axis=0)


def sums_kernel(rows_ref, weights_ref, own_ref, arrived_ref, first_ref, sums_ref):
    with_field, with_image = jump_sums(weights_ref, own_ref, arrived_ref, first_ref)
    row = lax.broadcasted_iota(jnp.int32, (SUBLANES, LANES), 0)
    rows = rows_ref[...] + jnp.where(row == 3, with_field, jnp.where(row == 4, with_image, 0.0))
    lane = lax.broadcasted_iota(jnp.int32, (SUBLANES, LANES), 1)
    whole = jnp.sum(rows, axis=1, keepdims=True)
    packed = column_sums(jnp.where(lane == row, whole, 0.0))
    sums_ref[...] = jnp.broadcast_to(packed[None], sums_ref.shape)


def second_kernel(
    size,
    aligned_ref,
    product_ref,
    weights_a_ref,
    weights_b_ref,
    side_a_ref,
    side_b_ref,
    from_a_ref,
    from_b_ref,
    second_ref,
):
    block_rows = product_ref.shape[0]
    faces = weights_a_ref.shape[0]
    second_ref[...] = product_ref[...]
    second_ref[:, :size] = (
        second_ref[:, :size]
        + spread_jumps(
            size, faces, aligned_ref, 0, weights_a_ref, side_a_ref, from_a_ref, block_rows
        )
        + spread_jumps(
            size, faces, aligned_ref, faces, weights_b_ref, side_b_ref, from_b_ref, block_rows
        )
    )


def final_kernel(field_ref, image_ref, second_ref, sums_ref, solution_ref, residual_ref):
    size = solution_ref.shape[1]
    row = jnp.sum(sums_ref[...], axis=0)
    lane = lax.broadcasted_iota(jnp.int32, (1, LANES), 1)

    def entry(k):
        return jnp.sum(jnp.where(lane == k, row, 0.0), axis=1, keepdims=True)

    bb, bq, qq, bw, qw = (entry(k) for k in range(5))
    field = field_ref[:, :size]
    image = image_ref[:, :size]
    second = second_ref[:, :size]
    alpha = bb / bq
    norm = bb - alpha * (2.0 * bq - alpha * qq)
    beta = norm / bb
    grown = 1.0 + beta
    energy = grown * (grown * bq - alpha * (bw + qq)) + alpha * alpha * qw
    alpha_next = norm / energy
    residual = field - alpha * image
    direction = residual + beta * field
    moved = (image - alpha * second) + beta * image
    solution_ref[...] = alpha * field + alpha_next * direction
    residual_ref[...] = residual - alpha_next * moved


def swap(value, odd):
    count = lax.axis_size("sub")
    pairs = []
    for first in range(odd, count, 2):
        second = (first + 1) % count
        pairs += [(first, second), (second, first)]
    return lax.ppermute(value, "sub", pairs)


def on_device(
    right_side, stiffness, block_pairs, trace_rows, partner_face, owner_list, mortar_weight
):
    field = right_side[0, 0].T
    block_rows, size = field.shape
    stored = stiffness[0, 0]
    blocks = stored.reshape(stored.shape[0], size, size)
    pairs = block_pairs[0, 0]
    rows = trace_rows[0, 0]
    partner = partner_face[0, 0]
    owners = owner_list[0, 0]
    faces = partner.shape[0]
    devices = lax.axis_size("sub") * lax.axis_size("blk")

    held = lax.all_to_all(mortar_weight[0, 0], "blk", split_axis=0, concat_axis=0, tiled=True)
    last = 2 * faces + block_rows

    def placed(value, first):
        below = last + SUBLANES - first - value.shape[0]
        return jnp.pad(value, ((first, below), (0, LANES - value.shape[1])))

    indices = placed(rows, 0) + placed(partner_face[0], last) + placed(owner_list[0], last + 1)
    packed = indices.astype(F32) + placed(field, 2 * faces)
    aligned, padded, chosen, side_a = call(
        functools.partial(first_kernel, owners.shape[0]),
        [
            shape(2 * faces, jnp.int32),
            shape(block_rows),
            jax.ShapeDtypeStruct((faces, faces), F32),
            shape(faces),
        ],
        [(packed, VMEM)],
    )
    (to_a,) = call(
        far_message_kernel,
        [shape(2 * faces + SUBLANES)],
        [(value, VMEM) for value in (held.reshape(faces, LANES), chosen, side_a)],
    )
    from_a = swap(to_a, 1)
    (to_b,) = call(
        near_message_kernel,
        [shape(2 * faces)],
        [(value, VMEM) for value in (aligned, padded, to_a)],
    )
    from_b = swap(to_b, 0)
    def stiff(vector):
        (product,) = call(
            stiffness_kernel,
            [shape(block_rows)],
            [(pairs, SMEM), (blocks, VMEM), (vector, VMEM)],
            scratch=[pltpu.VMEM((block_rows * SUBLANES, LANES), F32)] * 2,
        )
        return product

    partial, weights_b = call(
        functools.partial(near_kernel, size),
        [shape(block_rows), shape(faces)],
        [(value, VMEM) for value in (aligned, stiff(padded), to_b, from_b)],
        flops=1,
        moved=1,
    )
    image, weights_a, side_a = call(
        functools.partial(far_kernel, size),
        [shape(block_rows), shape(faces), shape(faces + SUBLANES)],
        [(value, VMEM) for value in (aligned, partial, to_a, from_a)],
    )
    from_a = swap(side_a, 1)
    (side_b,) = call(
        near_traces_kernel, [shape(faces)], [(aligned, VMEM), (image, VMEM)]
    )
    from_b = swap(side_b, 0)
    product = stiff(image)
    (sums,) = call(
        near_sums_kernel,
        [shape(SUBLANES)],
        [(value, VMEM) for value in (product, weights_b, side_b, from_b, to_b, padded, image)],
        flops=1,
        moved=1,
    )
    (sums,) = call(
        sums_kernel,
        [jax.ShapeDtypeStruct((devices, 1, LANES), F32)],
        [(value, VMEM) for value in (sums, weights_a, side_a, from_a, to_a)],
    )
    (second,) = call(
        functools.partial(second_kernel, size),
        [shape(block_rows)],
        [
            (value, VMEM)
            for value in (
                aligned, product, weights_a, weights_b, side_a, side_b, from_a, from_b
            )
        ],
        flops=1_000_000_000,
    )
    sums = lax.all_to_all(sums, ("sub", "blk"), split_axis=0, concat_axis=0, tiled=True)
    solution_field, residual = call(
        final_kernel,
        [jax.ShapeDtypeStruct((block_rows, size), F32)] * 2,
        [(padded, VMEM), (image, VMEM), (second, VMEM), (sums, VMEM)],
    )
    return (solution_field.T[None, None], residual.T[None, None])


def solution(mesh):
    in_specs = (
        P("sub", "blk", None, None),
        P("sub", "blk", None, None),
        P("sub", "blk", None, None),
        P("sub", "blk", None, None),
        P("sub", "blk", None),
        P("sub", "blk", None),
        P("sub", "blk", None, None, None),
    )
    out_specs = (P("sub", "blk", None, None), P("sub", "blk", None, None))
    return jax.shard_map(
        on_device, mesh=mesh, in_specs=in_specs, out_specs=out_specs, check_vma=False
    )
```

```python
import functools

import jax
import jax.numpy as jnp
from jax import lax
from jax.experimental import pallas as pl
from jax.experimental.pallas import tpu as pltpu
from jax.sharding import PartitionSpec as P

LANES = 128
SUBLANES = 8
VMEM = pl.BlockSpec(memory_space=pltpu.VMEM)
SMEM = pl.BlockSpec(memory_space=pltpu.SMEM)
F32 = jnp.float32
BF16 = jnp.bfloat16


def call(body, outs, inputs, scratch=(), flops=1_000_000, moved=1_000_000):
    return pl.pallas_call(
        body,
        out_shape=outs,
        in_specs=[spec for _, spec in inputs],
        out_specs=[VMEM] * len(outs),
        scratch_shapes=list(scratch),
        compiler_params=pltpu.CompilerParams(vmem_limit_bytes=32 * 1024 * 1024),
        cost_estimate=pl.CostEstimate(
            flops=flops, bytes_accessed=moved, transcendentals=0
        ),
    )(*[value for value, _ in inputs])


def shape(rows, dtype=F32):
    return jax.ShapeDtypeStruct((rows, LANES), dtype)


def halves(value):
    high = value.astype(BF16).astype(F32)
    return high, value - high


def gather_traces(field, rows_ref, rows_first, target):
    block_rows = field.shape[0]
    spread = [
        jnp.broadcast_to(field[i : i + 1, :], (SUBLANES, LANES)) for i in range(block_rows)
    ]
    for k in range(target.shape[0] // SUBLANES):
        index = rows_ref[rows_first + k * SUBLANES : rows_first + (k + 1) * SUBLANES, :]
        dof, row = split(index, block_rows)
        taken = jnp.zeros((SUBLANES, LANES), F32)
        for i in range(block_rows):
            here = jnp.take_along_axis(spread[i], dof, axis=1, mode="promise_in_bounds")
            taken = jnp.where(row == i, here, taken)
        target[k * SUBLANES : (k + 1) * SUBLANES, :] = taken


def tile(k):
    return pl.ds(pl.multiple_of(k * SUBLANES, SUBLANES), SUBLANES)


def split(index, block_rows):
    if block_rows & (block_rows - 1) == 0:
        shift = block_rows.bit_length() - 1
        return index >> shift, index & (block_rows - 1)
    return lax.div(index, block_rows), lax.rem(index, block_rows)


def one_hot(place, count):
    row = lax.broadcasted_iota(jnp.int32, (count, place.shape[1]), 0)
    return jnp.where(row == place, 1.0, 0.0)


def exact_dot(left, right):
    return jnp.dot(
        left, right, precision=lax.Precision.HIGHEST, preferred_element_type=F32
    )


def first_kernel(
    groups, packed_ref, aligned_ref, padded_ref, chosen_ref, side_a_ref
):
    faces = side_a_ref.shape[0]
    block_rows = padded_ref.shape[0]
    per_group = faces // groups
    slot = lax.axis_index("blk")
    parity = lax.rem(lax.axis_index("sub"), 2)
    east = pl.multiple_of((1 - parity) * faces, faces)
    west = pl.multiple_of(parity * faces, faces)
    padded_ref[...] = packed_ref[2 * faces : 2 * faces + block_rows, :]
    tail = packed_ref[2 * faces + block_rows :, :].astype(jnp.int32)
    partner = tail[:1, :faces]
    face = lax.broadcasted_iota(jnp.int32, (1, faces), 1)
    source = jnp.zeros((1, faces), jnp.int32)
    for g in range(groups):
        inside = face - g * per_group
        source = jnp.where(
            (inside >= 0) & (inside < per_group),
            (groups - 1 - (tail[1:2, g : g + 1] ^ slot)) * per_group + inside,
            source,
        )
    order = one_hot(partner, faces)
    aligned_ref[pl.ds(west, faces), :] = packed_ref[faces : 2 * faces, :].astype(jnp.int32)
    aligned_ref[pl.ds(east, faces), :] = exact_dot(order, packed_ref[:faces, :]).astype(jnp.int32)
    chosen_ref[...] = lax.dot_general(
        order.astype(BF16),
        one_hot(source, faces).astype(BF16),
        (((1,), (1,)), ((), ())),
        preferred_element_type=F32,
    )
    gather_traces(padded_ref[...], aligned_ref, 0, side_a_ref)


def blocks_kernel(weights_ref, *block_refs):
    slot = lax.axis_index("blk")
    for place, block_ref in enumerate(block_refs):
        block_ref[...] = weights_ref[slot ^ (len(block_refs) - 1 - place)]


def far_message_kernel(chosen_ref, side_a_ref, *refs):
    faces = side_a_ref.shape[0]
    *block_refs, to_a_ref = refs
    held = jnp.concatenate([block_ref[...] for block_ref in block_refs], axis=0)
    to_a_ref[:faces, :] = side_a_ref[...]
    to_a_ref[faces : 2 * faces, :] = exact_dot(chosen_ref[...], held)
    to_a_ref[2 * faces :, :] = jnp.zeros_like(to_a_ref[2 * faces :, :])


def near_message_kernel(aligned_ref, padded_ref, to_a_ref, to_b_ref):
    faces = to_b_ref.shape[0] // 2
    to_b_ref[faces:, :] = to_a_ref[faces : 2 * faces, :]
    gather_traces(padded_ref[...], aligned_ref, faces, to_b_ref.at[:faces, :])


def near_traces_kernel(aligned_ref, image_ref, side_b_ref):
    gather_traces(image_ref[...], aligned_ref, side_b_ref.shape[0], side_b_ref)


def stiffness_kernel(pairs_ref, blocks_ref, field_ref, out_ref, pieces, sums):
    block_rows = field_ref.shape[0]
    size = blocks_ref.shape[1]
    count = pairs_ref.shape[1]
    high, low = halves(field_ref[...])
    pieces[...] = jnp.zeros_like(pieces)
    pieces[pl.ds(0, block_rows, stride=SUBLANES), :] = high
    pieces[pl.ds(1, block_rows, stride=SUBLANES), :] = low

    def times(row, block, contract):
        left = pieces[pl.ds(pl.multiple_of(row * SUBLANES, SUBLANES), SUBLANES), :]
        return lax.dot_general(
            left[:, :size].astype(BF16),
            block,
            (((1,), (contract,)), ((), ())),
            preferred_element_type=F32,
        )

    def add(row, value):
        place = pl.ds(pl.multiple_of(row * SUBLANES, SUBLANES), SUBLANES)
        sums[place, :size] = sums[place, :size] + value

    sums[...] = jnp.zeros_like(sums)
    for i in range(block_rows):
        sums[i * SUBLANES : (i + 1) * SUBLANES, :size] = times(i, blocks_ref[i], 1)
    for p in range(count):
        first = pairs_ref[0, p]
        other = pairs_ref[1, p]
        block = blocks_ref[block_rows + p]
        add(first, times(other, block, 1))
        add(other, times(first, block, 0))
    out_ref[...] = (
        sums[pl.ds(0, block_rows, stride=SUBLANES), :]
        + sums[pl.ds(1, block_rows, stride=SUBLANES), :]
    )


def spread_jumps(size, faces, rows_ref, rows_first, weights_ref, own_ref, arrived_ref, block_rows):
    dof_of = lax.broadcasted_iota(jnp.int32, (size, LANES), 0).astype(F32).astype(BF16)
    row_of = lax.broadcasted_iota(jnp.int32, (block_rows, LANES), 0).astype(F32).astype(BF16)
    none = jnp.zeros((), BF16)
    one = jnp.ones((), BF16)

    def widened(value, f, rows):
        slab = jnp.broadcast_to(value[f : f + 1, :], (2 * SUBLANES, LANES)).astype(BF16)
        return jnp.concatenate([slab] * (rows // (2 * SUBLANES)), axis=0)

    def step(k, total):
        lam = weights_ref[tile(k), :] * (own_ref[tile(k), :] - arrived_ref[tile(k), :])
        high, low = halves(lam)
        dof, row = split(rows_ref[tile(rows_first // SUBLANES + k), :], block_rows)
        dof = dof.astype(F32)
        row = row.astype(F32)
        left = []
        right = []
        for f in range(SUBLANES):
            here = row_of == widened(row, f, block_rows)
            left.append(
                jnp.concatenate(
                    [
                        jnp.where(here, widened(high, f, block_rows), none),
                        jnp.where(here, widened(low, f, block_rows), none),
                    ],
                    axis=0,
                )
            )
            right.append(jnp.where(dof_of == widened(dof, f, size), one, none))
        return total + lax.dot_general(
            jnp.concatenate(left, axis=1),
            jnp.concatenate(right, axis=1),
            (((1,), (1,)), ((), ())),
            preferred_element_type=F32,
        )

    total = lax.fori_loop(
        0, faces // SUBLANES, step, jnp.zeros((2 * block_rows, size), F32), unroll=8
    )
    return total[:block_rows] + total[block_rows:]


def near_kernel(size, aligned_ref, product_ref, to_ref, from_ref, partial_ref, weights_ref):
    block_rows = product_ref.shape[0]
    faces = weights_ref.shape[0]
    odd = lax.rem(lax.axis_index("sub"), 2) == 1
    weights_ref[...] = jnp.where(odd, from_ref[faces:, :], to_ref[faces:, :])
    partial_ref[...] = product_ref[...]
    partial_ref[:, :size] = partial_ref[:, :size] + spread_jumps(
        size, faces, aligned_ref, faces, weights_ref, to_ref, from_ref, block_rows
    )


def far_kernel(
    size,
    aligned_ref,
    partial_ref,
    to_ref,
    from_ref,
    image_ref,
    weights_ref,
    side_a_ref,
):
    block_rows = partial_ref.shape[0]
    faces = weights_ref.shape[0]
    odd = lax.rem(lax.axis_index("sub"), 2) == 1
    weights_ref[...] = jnp.where(
        odd, to_ref[faces : 2 * faces, :], from_ref[faces : 2 * faces, :]
    )
    image_ref[...] = partial_ref[...]
    image_ref[:, :size] = image_ref[:, :size] + spread_jumps(
        size, faces, aligned_ref, 0, weights_ref, to_ref, from_ref, block_rows
    )
    gather_traces(image_ref[...], aligned_ref, 0, side_a_ref.at[:faces, :])
    side_a_ref[faces:, :] = jnp.zeros_like(side_a_ref[faces:, :])


def column_sums(value):
    return jnp.sum(value, axis=0, keepdims=True)


def jump_sums(weights_ref, own_ref, arrived_ref, first_ref):
    faces = slice(0, weights_ref.shape[0])
    own = own_ref[faces, :]
    lam = weights_ref[...] * (own - arrived_ref[faces, :])
    return column_sums(lam * first_ref[faces, :]), column_sums(lam * own)


def near_sums_kernel(
    product_ref, weights_ref, own_ref, arrived_ref, first_ref, field_ref, image_ref, rows_ref
):
    field = field_ref[...]
    image = image_ref[...]
    product = product_ref[...]
    with_field, with_image = jump_sums(weights_ref, own_ref, arrived_ref, first_ref)
    parts = [
        column_sums(field * field),
        column_sums(field * image),
        column_sums(image * image),
        column_sums(field * product) + with_field,
        column_sums(image * product) + with_image,
    ]
    parts += [jnp.zeros_like(parts[0])] * (SUBLANES - len(parts))
    rows_ref[...] = jnp.concatenate(parts, axis=0)


def sums_kernel(rows_ref, weights_ref, own_ref, arrived_ref, first_ref, sums_ref):
    with_field, with_image = jump_sums(weights_ref, own_ref, arrived_ref, first_ref)
    row = lax.broadcasted_iota(jnp.int32, (SUBLANES, LANES), 0)
    rows = rows_ref[...] + jnp.where(row == 3, with_field, jnp.where(row == 4, with_image, 0.0))
    lane = lax.broadcasted_iota(jnp.int32, (SUBLANES, LANES), 1)
    whole = jnp.sum(rows, axis=1, keepdims=True)
    packed = column_sums(jnp.where(lane == row, whole, 0.0))
    sums_ref[...] = jnp.broadcast_to(packed[None], sums_ref.shape)


def second_kernel(
    size,
    aligned_ref,
    product_ref,
    weights_a_ref,
    weights_b_ref,
    side_a_ref,
    side_b_ref,
    from_a_ref,
    from_b_ref,
    second_ref,
):
    block_rows = product_ref.shape[0]
    faces = weights_a_ref.shape[0]
    second_ref[...] = product_ref[...]
    second_ref[:, :size] = (
        second_ref[:, :size]
        + spread_jumps(
            size, faces, aligned_ref, 0, weights_a_ref, side_a_ref, from_a_ref, block_rows
        )
        + spread_jumps(
            size, faces, aligned_ref, faces, weights_b_ref, side_b_ref, from_b_ref, block_rows
        )
    )


def final_kernel(field_ref, image_ref, second_ref, sums_ref, solution_ref, residual_ref):
    size = solution_ref.shape[1]
    row = jnp.sum(sums_ref[...], axis=0)
    lane = lax.broadcasted_iota(jnp.int32, (1, LANES), 1)

    def entry(k):
        return jnp.sum(jnp.where(lane == k, row, 0.0), axis=1, keepdims=True)

    bb, bq, qq, bw, qw = (entry(k) for k in range(5))
    field = field_ref[:, :size]
    image = image_ref[:, :size]
    second = second_ref[:, :size]
    alpha = bb / bq
    norm = bb - alpha * (2.0 * bq - alpha * qq)
    beta = norm / bb
    grown = 1.0 + beta
    energy = grown * (grown * bq - alpha * (bw + qq)) + alpha * alpha * qw
    alpha_next = norm / energy
    residual = field - alpha * image
    direction = residual + beta * field
    moved = (image - alpha * second) + beta * image
    solution_ref[...] = alpha * field + alpha_next * direction
    residual_ref[...] = residual - alpha_next * moved


def swap(value, odd):
    count = lax.axis_size("sub")
    pairs = []
    for first in range(odd, count, 2):
        second = (first + 1) % count
        pairs += [(first, second), (second, first)]
    return lax.ppermute(value, "sub", pairs)


def swap_slots(value, k):
    count = lax.axis_size("blk")
    return lax.ppermute(value, "blk", [(slot, slot ^ k) for slot in range(count)])


def on_device(
    right_side, stiffness, block_pairs, trace_rows, partner_face, owner_list, mortar_weight
):
    field = right_side[0, 0].T
    block_rows, size = field.shape
    stored = stiffness[0, 0]
    blocks = stored.reshape(stored.shape[0], size, size)
    pairs = block_pairs[0, 0]
    rows = trace_rows[0, 0]
    partner = partner_face[0, 0]
    owners = owner_list[0, 0]
    faces = partner.shape[0]
    devices = lax.axis_size("sub") * lax.axis_size("blk")

    held = call(
        blocks_kernel,
        [shape(mortar_weight.shape[3])] * mortar_weight.shape[2],
        [(mortar_weight[0, 0], VMEM)],
    )
    held = [
        swap_slots(block, k) if k else block
        for k, block in zip(reversed(range(len(held))), held)
    ]
    last = 2 * faces + block_rows

    def placed(value, first):
        below = last + SUBLANES - first - value.shape[0]
        return jnp.pad(value, ((first, below), (0, LANES - value.shape[1])))

    indices = placed(rows, 0) + placed(partner_face[0], last) + placed(owner_list[0], last + 1)
    packed = indices.astype(F32) + placed(field, 2 * faces)
    aligned, padded, chosen, side_a = call(
        functools.partial(first_kernel, owners.shape[0]),
        [
            shape(2 * faces, jnp.int32),
            shape(block_rows),
            jax.ShapeDtypeStruct((faces, faces), F32),
            shape(faces),
        ],
        [(packed, VMEM)],
    )
    (to_a,) = call(
        far_message_kernel,
        [shape(2 * faces + SUBLANES)],
        [(value, VMEM) for value in (chosen, side_a, *held)],
    )
    from_a = swap(to_a, 1)
    (to_b,) = call(
        near_message_kernel,
        [shape(2 * faces)],
        [(value, VMEM) for value in (aligned, padded, to_a)],
    )
    from_b = swap(to_b, 0)
    def stiff(vector):
        (product,) = call(
            stiffness_kernel,
            [shape(block_rows)],
            [(pairs, SMEM), (blocks, VMEM), (vector, VMEM)],
            scratch=[pltpu.VMEM((block_rows * SUBLANES, LANES), F32)] * 2,
        )
        return product

    partial, weights_b = call(
        functools.partial(near_kernel, size),
        [shape(block_rows), shape(faces)],
        [(value, VMEM) for value in (aligned, stiff(padded), to_b, from_b)],
        flops=1,
        moved=1,
    )
    image, weights_a, side_a = call(
        functools.partial(far_kernel, size),
        [shape(block_rows), shape(faces), shape(faces + SUBLANES)],
        [(value, VMEM) for value in (aligned, partial, to_a, from_a)],
    )
    from_a = swap(side_a, 1)
    (side_b,) = call(
        near_traces_kernel, [shape(faces)], [(aligned, VMEM), (image, VMEM)]
    )
    from_b = swap(side_b, 0)
    product = stiff(image)
    (sums,) = call(
        near_sums_kernel,
        [shape(SUBLANES)],
        [(value, VMEM) for value in (product, weights_b, side_b, from_b, to_b, padded, image)],
        flops=1,
        moved=1,
    )
    (sums,) = call(
        sums_kernel,
        [jax.ShapeDtypeStruct((devices, 1, LANES), F32)],
        [(value, VMEM) for value in (sums, weights_a, side_a, from_a, to_a)],
    )
    (second,) = call(
        functools.partial(second_kernel, size),
        [shape(block_rows)],
        [
            (value, VMEM)
            for value in (
                aligned, product, weights_a, weights_b, side_a, side_b, from_a, from_b
            )
        ],
        flops=1_000_000_000,
    )
    sums = lax.all_to_all(sums, ("sub", "blk"), split_axis=0, concat_axis=0, tiled=True)
    solution_field, residual = call(
        final_kernel,
        [jax.ShapeDtypeStruct((block_rows, size), F32)] * 2,
        [(padded, VMEM), (image, VMEM), (second, VMEM), (sums, VMEM)],
    )
    return (solution_field.T[None, None], residual.T[None, None])


def solution(mesh):
    in_specs = (
        P("sub", "blk", None, None),
        P("sub", "blk", None, None),
        P("sub", "blk", None, None),
        P("sub", "blk", None, None),
        P("sub", "blk", None),
        P("sub", "blk", None),
        P("sub", "blk", None, None, None),
    )
    out_specs = (P("sub", "blk", None, None), P("sub", "blk", None, None))
    return jax.shard_map(
        on_device, mesh=mesh, in_specs=in_specs, out_specs=out_specs, check_vma=False
    )
```

```python
import functools

import jax
import jax.numpy as jnp
from jax import lax
from jax.experimental import pallas as pl
from jax.experimental.pallas import tpu as pltpu
from jax.sharding import PartitionSpec as P

LANES = 128
SUBLANES = 8
VMEM = pl.BlockSpec(memory_space=pltpu.VMEM)
SMEM = pl.BlockSpec(memory_space=pltpu.SMEM)
F32 = jnp.float32
BF16 = jnp.bfloat16


def call(body, outs, inputs, scratch=(), flops=1_000_000, moved=1_000_000):
    return pl.pallas_call(
        body,
        out_shape=outs,
        in_specs=[spec for _, spec in inputs],
        out_specs=[VMEM] * len(outs),
        scratch_shapes=list(scratch),
        compiler_params=pltpu.CompilerParams(vmem_limit_bytes=32 * 1024 * 1024),
        cost_estimate=pl.CostEstimate(
            flops=flops, bytes_accessed=moved, transcendentals=0
        ),
    )(*[value for value, _ in inputs])


def shape(rows, dtype=F32):
    return jax.ShapeDtypeStruct((rows, LANES), dtype)


def halves(value):
    high = value.astype(BF16).astype(F32)
    return high, value - high


def gather_traces(field, rows_ref, rows_first, target):
    block_rows = field.shape[0]
    spread = [
        jnp.broadcast_to(field[i : i + 1, :], (SUBLANES, LANES)) for i in range(block_rows)
    ]
    for k in range(target.shape[0] // SUBLANES):
        index = rows_ref[rows_first + k * SUBLANES : rows_first + (k + 1) * SUBLANES, :]
        dof, row = split(index, block_rows)
        taken = jnp.zeros((SUBLANES, LANES), F32)
        for i in range(block_rows):
            here = jnp.take_along_axis(spread[i], dof, axis=1, mode="promise_in_bounds")
            taken = jnp.where(row == i, here, taken)
        target[k * SUBLANES : (k + 1) * SUBLANES, :] = taken


def tile(k):
    return pl.ds(pl.multiple_of(k * SUBLANES, SUBLANES), SUBLANES)


def split(index, block_rows):
    if block_rows & (block_rows - 1) == 0:
        shift = block_rows.bit_length() - 1
        return index >> shift, index & (block_rows - 1)
    return lax.div(index, block_rows), lax.rem(index, block_rows)


def one_hot(place, count):
    row = lax.broadcasted_iota(jnp.int32, (count, place.shape[1]), 0)
    return jnp.where(row == place, 1.0, 0.0)


def exact_dot(left, right):
    return jnp.dot(
        left, right, precision=lax.Precision.HIGHEST, preferred_element_type=F32
    )


def first_kernel(
    groups, packed_ref, aligned_ref, padded_ref, chosen_ref, side_a_ref, side_b_ref
):
    faces = side_a_ref.shape[0]
    block_rows = padded_ref.shape[0]
    per_group = faces // groups
    slot = lax.axis_index("blk")
    parity = lax.rem(lax.axis_index("sub"), 2)
    east = pl.multiple_of((1 - parity) * faces, faces)
    west = pl.multiple_of(parity * faces, faces)
    padded_ref[...] = packed_ref[2 * faces : 2 * faces + block_rows, :]
    last = 2 * faces + block_rows
    tail = packed_ref[last : last + SUBLANES, :].astype(jnp.int32)
    partner = tail[:1, :faces]
    face = lax.broadcasted_iota(jnp.int32, (1, faces), 1)
    source = jnp.zeros((1, faces), jnp.int32)
    for g in range(groups):
        inside = face - g * per_group
        source = jnp.where(
            (inside >= 0) & (inside < per_group),
            (tail[1:2, g : g + 1] ^ slot) * per_group + inside,
            source,
        )
    order = one_hot(partner, faces)
    aligned_ref[pl.ds(west, faces), :] = packed_ref[faces : 2 * faces, :].astype(jnp.int32)
    aligned_ref[pl.ds(east, faces), :] = exact_dot(order, packed_ref[:faces, :]).astype(jnp.int32)
    chosen_ref[...] = lax.dot_general(
        order.astype(BF16),
        one_hot(source, faces).astype(BF16),
        (((1,), (1,)), ((), ())),
        preferred_element_type=F32,
    )
    gather_traces(padded_ref[...], aligned_ref, 0, side_a_ref)
    gather_traces(padded_ref[...], aligned_ref, faces, side_b_ref)


def message_kernel(first, packed_ref, chosen_ref, side_a_ref, side_b_ref, *refs):
    faces = side_a_ref.shape[0]
    *weight_refs, to_a_ref, to_b_ref = refs
    slot = lax.axis_index("blk")
    per_group = weight_refs[0].shape[1]
    kept = pl.ds(pl.multiple_of(first + slot * per_group, SUBLANES), per_group)
    held = jnp.concatenate(
        [packed_ref[kept, :]] + [weight_ref[slot] for weight_ref in weight_refs], axis=0
    )
    own = exact_dot(chosen_ref[...], held)
    for side_ref, to_ref in ((side_a_ref, to_a_ref), (side_b_ref, to_b_ref)):
        to_ref[:faces, :] = side_ref[...]
        to_ref[faces:, :] = own


def near_traces_kernel(aligned_ref, image_ref, side_b_ref):
    gather_traces(image_ref[...], aligned_ref, side_b_ref.shape[0], side_b_ref)


def stiffness_kernel(pairs_ref, blocks_ref, field_ref, out_ref, pieces, sums):
    block_rows = field_ref.shape[0]
    size = blocks_ref.shape[1]
    count = pairs_ref.shape[1]
    high, low = halves(field_ref[...])
    pieces[...] = jnp.zeros_like(pieces)
    pieces[pl.ds(0, block_rows, stride=SUBLANES), :] = high
    pieces[pl.ds(1, block_rows, stride=SUBLANES), :] = low

    def times(row, block, contract):
        left = pieces[pl.ds(pl.multiple_of(row * SUBLANES, SUBLANES), SUBLANES), :]
        return lax.dot_general(
            left[:, :size].astype(BF16),
            block,
            (((1,), (contract,)), ((), ())),
            preferred_element_type=F32,
        )

    def add(row, value):
        place = pl.ds(pl.multiple_of(row * SUBLANES, SUBLANES), SUBLANES)
        sums[place, :size] = sums[place, :size] + value

    sums[...] = jnp.zeros_like(sums)
    for i in range(block_rows):
        sums[i * SUBLANES : (i + 1) * SUBLANES, :size] = times(i, blocks_ref[i], 1)
    for p in range(count):
        first = pairs_ref[0, p]
        other = pairs_ref[1, p]
        block = blocks_ref[block_rows + p]
        add(first, times(other, block, 1))
        add(other, times(first, block, 0))
    out_ref[...] = (
        sums[pl.ds(0, block_rows, stride=SUBLANES), :]
        + sums[pl.ds(1, block_rows, stride=SUBLANES), :]
    )


def spread_jumps(size, faces, rows_ref, rows_first, weights_ref, own_ref, arrived_ref, block_rows):
    dof_of = lax.broadcasted_iota(jnp.int32, (size, LANES), 0).astype(F32).astype(BF16)
    row_of = lax.broadcasted_iota(jnp.int32, (block_rows, LANES), 0).astype(F32).astype(BF16)
    none = jnp.zeros((), BF16)
    one = jnp.ones((), BF16)

    def widened(value, f, rows):
        slab = jnp.broadcast_to(value[f : f + 1, :], (2 * SUBLANES, LANES)).astype(BF16)
        return jnp.concatenate([slab] * (rows // (2 * SUBLANES)), axis=0)

    def step(k, total):
        lam = weights_ref[tile(k), :] * (own_ref[tile(k), :] - arrived_ref[tile(k), :])
        high, low = halves(lam)
        dof, row = split(rows_ref[tile(rows_first // SUBLANES + k), :], block_rows)
        dof = dof.astype(F32)
        row = row.astype(F32)
        left = []
        right = []
        for f in range(SUBLANES):
            here = row_of == widened(row, f, block_rows)
            left.append(
                jnp.concatenate(
                    [
                        jnp.where(here, widened(high, f, block_rows), none),
                        jnp.where(here, widened(low, f, block_rows), none),
                    ],
                    axis=0,
                )
            )
            right.append(jnp.where(dof_of == widened(dof, f, size), one, none))
        return total + lax.dot_general(
            jnp.concatenate(left, axis=1),
            jnp.concatenate(right, axis=1),
            (((1,), (1,)), ((), ())),
            preferred_element_type=F32,
        )

    total = lax.fori_loop(
        0, faces // SUBLANES, step, jnp.zeros((2 * block_rows, size), F32), unroll=8
    )
    return total[:block_rows] + total[block_rows:]


def near_kernel(size, aligned_ref, product_ref, to_ref, from_ref, partial_ref, weights_ref):
    block_rows = product_ref.shape[0]
    faces = weights_ref.shape[0]
    odd = lax.rem(lax.axis_index("sub"), 2) == 1
    weights_ref[...] = jnp.where(odd, from_ref[faces:, :], to_ref[faces:, :])
    partial_ref[...] = product_ref[...]
    partial_ref[:, :size] = partial_ref[:, :size] + spread_jumps(
        size, faces, aligned_ref, faces, weights_ref, to_ref, from_ref, block_rows
    )


def far_kernel(
    size,
    aligned_ref,
    partial_ref,
    to_ref,
    from_ref,
    image_ref,
    weights_ref,
    side_a_ref,
):
    block_rows = partial_ref.shape[0]
    faces = weights_ref.shape[0]
    odd = lax.rem(lax.axis_index("sub"), 2) == 1
    weights_ref[...] = jnp.where(
        odd, to_ref[faces : 2 * faces, :], from_ref[faces : 2 * faces, :]
    )
    image_ref[...] = partial_ref[...]
    image_ref[:, :size] = image_ref[:, :size] + spread_jumps(
        size, faces, aligned_ref, 0, weights_ref, to_ref, from_ref, block_rows
    )
    gather_traces(image_ref[...], aligned_ref, 0, side_a_ref.at[:faces, :])
    side_a_ref[faces:, :] = jnp.zeros_like(side_a_ref[faces:, :])


def column_sums(value):
    return jnp.sum(value, axis=0, keepdims=True)


def jump_sums(weights_ref, own_ref, arrived_ref, first_ref):
    faces = slice(0, weights_ref.shape[0])
    own = own_ref[faces, :]
    lam = weights_ref[...] * (own - arrived_ref[faces, :])
    return column_sums(lam * first_ref[faces, :]), column_sums(lam * own)


def near_sums_kernel(
    product_ref, weights_ref, own_ref, arrived_ref, first_ref, field_ref, image_ref, rows_ref
):
    field = field_ref[...]
    image = image_ref[...]
    product = product_ref[...]
    with_field, with_image = jump_sums(weights_ref, own_ref, arrived_ref, first_ref)
    parts = [
        column_sums(field * field),
        column_sums(field * image),
        column_sums(image * image),
        column_sums(field * product) + with_field,
        column_sums(image * product) + with_image,
    ]
    parts += [jnp.zeros_like(parts[0])] * (SUBLANES - len(parts))
    rows_ref[...] = jnp.concatenate(parts, axis=0)


def sums_kernel(rows_ref, weights_ref, own_ref, arrived_ref, first_ref, sums_ref):
    with_field, with_image = jump_sums(weights_ref, own_ref, arrived_ref, first_ref)
    row = lax.broadcasted_iota(jnp.int32, (SUBLANES, LANES), 0)
    rows = rows_ref[...] + jnp.where(row == 3, with_field, jnp.where(row == 4, with_image, 0.0))
    lane = lax.broadcasted_iota(jnp.int32, (SUBLANES, LANES), 1)
    whole = jnp.sum(rows, axis=1, keepdims=True)
    packed = column_sums(jnp.where(lane == row, whole, 0.0))
    sums_ref[...] = jnp.broadcast_to(packed[None], sums_ref.shape)


def second_kernel(
    size,
    aligned_ref,
    product_ref,
    weights_a_ref,
    weights_b_ref,
    side_a_ref,
    side_b_ref,
    from_a_ref,
    from_b_ref,
    second_ref,
):
    block_rows = product_ref.shape[0]
    faces = weights_a_ref.shape[0]
    second_ref[...] = product_ref[...]
    second_ref[:, :size] = (
        second_ref[:, :size]
        + spread_jumps(
            size, faces, aligned_ref, 0, weights_a_ref, side_a_ref, from_a_ref, block_rows
        )
        + spread_jumps(
            size, faces, aligned_ref, faces, weights_b_ref, side_b_ref, from_b_ref, block_rows
        )
    )


def final_kernel(field_ref, image_ref, second_ref, sums_ref, solution_ref, residual_ref):
    size = solution_ref.shape[1]
    row = jnp.sum(sums_ref[...], axis=0)
    lane = lax.broadcasted_iota(jnp.int32, (1, LANES), 1)

    def entry(k):
        return jnp.sum(jnp.where(lane == k, row, 0.0), axis=1, keepdims=True)

    bb, bq, qq, bw, qw = (entry(k) for k in range(5))
    field = field_ref[:, :size]
    image = image_ref[:, :size]
    second = second_ref[:, :size]
    alpha = bb / bq
    norm = bb - alpha * (2.0 * bq - alpha * qq)
    beta = norm / bb
    grown = 1.0 + beta
    energy = grown * (grown * bq - alpha * (bw + qq)) + alpha * alpha * qw
    alpha_next = norm / energy
    residual = field - alpha * image
    direction = residual + beta * field
    moved = (image - alpha * second) + beta * image
    solution_ref[...] = alpha * field + alpha_next * direction
    residual_ref[...] = residual - alpha_next * moved


def swap(value, odd):
    count = lax.axis_size("sub")
    pairs = []
    for first in range(odd, count, 2):
        second = (first + 1) % count
        pairs += [(first, second), (second, first)]
    return lax.ppermute(value, "sub", pairs)


def swap_slots(value, k):
    count = lax.axis_size("blk")
    return lax.ppermute(value, "blk", [(slot, slot ^ k) for slot in range(count)])


def on_device(
    right_side, stiffness, block_pairs, trace_rows, partner_face, owner_list, mortar_weight
):
    field = right_side[0, 0].T
    block_rows, size = field.shape
    stored = stiffness[0, 0]
    blocks = stored.reshape(stored.shape[0], size, size)
    pairs = block_pairs[0, 0]
    rows = trace_rows[0, 0]
    partner = partner_face[0, 0]
    owners = owner_list[0, 0]
    faces = partner.shape[0]
    devices = lax.axis_size("sub") * lax.axis_size("blk")

    own_weights = mortar_weight[0, 0]
    held = [swap_slots(own_weights, k) for k in range(1, own_weights.shape[0])]
    last = 2 * faces + block_rows

    def placed(value, first):
        below = last + SUBLANES + faces - first - value.shape[0]
        return jnp.pad(value, ((first, below), (0, LANES - value.shape[1])))

    indices = placed(rows, 0) + placed(partner_face[0], last) + placed(owner_list[0], last + 1)
    packed = (
        indices.astype(F32)
        + placed(field, 2 * faces)
        + placed(own_weights.reshape(faces, LANES), last + SUBLANES)
    )
    aligned, padded, chosen, side_a, side_b = call(
        functools.partial(first_kernel, owners.shape[0]),
        [
            shape(2 * faces, jnp.int32),
            shape(block_rows),
            jax.ShapeDtypeStruct((faces, faces), F32),
            shape(faces),
            shape(faces),
        ],
        [(packed, VMEM)],
    )
    to_a, to_b = call(
        functools.partial(message_kernel, last + SUBLANES),
        [shape(2 * faces), shape(2 * faces)],
        [(value, VMEM) for value in (packed, chosen, side_a, side_b, *held)],
    )
    from_b = swap(to_b, 0)
    from_a = swap(to_a, 1)

    def stiff(vector):
        (product,) = call(
            stiffness_kernel,
            [shape(block_rows)],
            [(pairs, SMEM), (blocks, VMEM), (vector, VMEM)],
            scratch=[pltpu.VMEM((block_rows * SUBLANES, LANES), F32)] * 2,
        )
        return product

    partial, weights_b = call(
        functools.partial(near_kernel, size),
        [shape(block_rows), shape(faces)],
        [(value, VMEM) for value in (aligned, stiff(padded), to_b, from_b)],
        flops=1,
        moved=1,
    )
    image, weights_a, side_a = call(
        functools.partial(far_kernel, size),
        [shape(block_rows), shape(faces), shape(faces + SUBLANES)],
        [(value, VMEM) for value in (aligned, partial, to_a, from_a)],
    )
    from_a = swap(side_a, 1)
    (side_b,) = call(
        near_traces_kernel, [shape(faces)], [(aligned, VMEM), (image, VMEM)]
    )
    from_b = swap(side_b, 0)
    product = stiff(image)
    (sums,) = call(
        near_sums_kernel,
        [shape(SUBLANES)],
        [(value, VMEM) for value in (product, weights_b, side_b, from_b, to_b, padded, image)],
        flops=1,
        moved=1,
    )
    (sums,) = call(
        sums_kernel,
        [jax.ShapeDtypeStruct((devices, 1, LANES), F32)],
        [(value, VMEM) for value in (sums, weights_a, side_a, from_a, to_a)],
    )
    (second,) = call(
        functools.partial(second_kernel, size),
        [shape(block_rows)],
        [
            (value, VMEM)
            for value in (
                aligned, product, weights_a, weights_b, side_a, side_b, from_a, from_b
            )
        ],
        flops=1_000_000_000,
    )
    sums = lax.all_to_all(sums, ("sub", "blk"), split_axis=0, concat_axis=0, tiled=True)
    solution_field, residual = call(
        final_kernel,
        [jax.ShapeDtypeStruct((block_rows, size), F32)] * 2,
        [(padded, VMEM), (image, VMEM), (second, VMEM), (sums, VMEM)],
    )
    return (solution_field.T[None, None], residual.T[None, None])


def solution(mesh):
    in_specs = (
        P("sub", "blk", None, None),
        P("sub", "blk", None, None),
        P("sub", "blk", None, None),
        P("sub", "blk", None, None),
        P("sub", "blk", None),
        P("sub", "blk", None),
        P("sub", "blk", None, None, None),
    )
    out_specs = (P("sub", "blk", None, None), P("sub", "blk", None, None))
    return jax.shard_map(
        on_device, mesh=mesh, in_specs=in_specs, out_specs=out_specs, check_vma=False
    )
```

```python
import functools

import jax
import jax.numpy as jnp
from jax import lax
from jax.experimental import pallas as pl
from jax.experimental.pallas import tpu as pltpu
from jax.sharding import PartitionSpec as P

LANES = 128
SUBLANES = 8
VMEM = pl.BlockSpec(memory_space=pltpu.VMEM)
SMEM = pl.BlockSpec(memory_space=pltpu.SMEM)
F32 = jnp.float32
BF16 = jnp.bfloat16


def call(body, outs, inputs, scratch=(), flops=1_000_000, moved=1_000_000):
    return pl.pallas_call(
        body,
        out_shape=outs,
        in_specs=[spec for _, spec in inputs],
        out_specs=[VMEM] * len(outs),
        scratch_shapes=list(scratch),
        compiler_params=pltpu.CompilerParams(vmem_limit_bytes=32 * 1024 * 1024),
        cost_estimate=pl.CostEstimate(
            flops=flops, bytes_accessed=moved, transcendentals=0
        ),
    )(*[value for value, _ in inputs])


def shape(rows, dtype=F32):
    return jax.ShapeDtypeStruct((rows, LANES), dtype)


def halves(value):
    high = value.astype(BF16).astype(F32)
    return high, value - high


def gather_traces(field, rows_ref, rows_first, target):
    block_rows = field.shape[0]
    spread = [
        jnp.broadcast_to(field[i : i + 1, :], (SUBLANES, LANES)) for i in range(block_rows)
    ]
    for k in range(target.shape[0] // SUBLANES):
        index = rows_ref[rows_first + k * SUBLANES : rows_first + (k + 1) * SUBLANES, :]
        dof, row = split(index, block_rows)
        taken = jnp.zeros((SUBLANES, LANES), F32)
        for i in range(block_rows):
            here = jnp.take_along_axis(spread[i], dof, axis=1, mode="promise_in_bounds")
            taken = jnp.where(row == i, here, taken)
        target[k * SUBLANES : (k + 1) * SUBLANES, :] = taken


def tile(k):
    return pl.ds(pl.multiple_of(k * SUBLANES, SUBLANES), SUBLANES)


def split(index, block_rows):
    if block_rows & (block_rows - 1) == 0:
        shift = block_rows.bit_length() - 1
        return index >> shift, index & (block_rows - 1)
    return lax.div(index, block_rows), lax.rem(index, block_rows)


def one_hot(place, count):
    row = lax.broadcasted_iota(jnp.int32, (count, place.shape[1]), 0)
    return jnp.where(row == place, 1.0, 0.0)


def exact_dot(left, right):
    return jnp.dot(
        left, right, precision=lax.Precision.HIGHEST, preferred_element_type=F32
    )


def first_kernel(
    groups, packed_ref, aligned_ref, padded_ref, chosen_ref, side_a_ref, side_b_ref
):
    faces = side_a_ref.shape[0]
    block_rows = padded_ref.shape[0]
    per_group = faces // groups
    slot = lax.axis_index("blk")
    parity = lax.rem(lax.axis_index("sub"), 2)
    east = pl.multiple_of((1 - parity) * faces, faces)
    west = pl.multiple_of(parity * faces, faces)
    padded_ref[...] = packed_ref[2 * faces : 2 * faces + block_rows, :]
    last = 2 * faces + block_rows
    tail = packed_ref[last : last + SUBLANES, :].astype(jnp.int32)
    partner = tail[:1, :faces]
    face = lax.broadcasted_iota(jnp.int32, (1, faces), 1)
    source = jnp.zeros((1, faces), jnp.int32)
    for g in range(groups):
        inside = face - g * per_group
        source = jnp.where(
            (inside >= 0) & (inside < per_group),
            (tail[1:2, g : g + 1] ^ slot) * per_group + inside,
            source,
        )
    order = one_hot(partner, faces)
    aligned_ref[pl.ds(west, faces), :] = packed_ref[faces : 2 * faces, :].astype(jnp.int32)
    aligned_ref[pl.ds(east, faces), :] = exact_dot(order, packed_ref[:faces, :]).astype(jnp.int32)
    chosen_ref[...] = lax.dot_general(
        order.astype(BF16),
        one_hot(source, faces).astype(BF16),
        (((1,), (1,)), ((), ())),
        preferred_element_type=F32,
    )
    gather_traces(padded_ref[...], aligned_ref, 0, side_a_ref)
    gather_traces(padded_ref[...], aligned_ref, faces, side_b_ref)


def message_kernel(first, packed_ref, chosen_ref, side_a_ref, side_b_ref, *refs):
    faces = side_a_ref.shape[0]
    *weight_refs, to_a_ref, to_b_ref = refs
    slot = lax.axis_index("blk")
    per_group = weight_refs[0].shape[1]
    kept = pl.ds(pl.multiple_of(first + slot * per_group, SUBLANES), per_group)
    held = jnp.concatenate(
        [packed_ref[kept, :]] + [weight_ref[slot] for weight_ref in weight_refs], axis=0
    )
    own = exact_dot(chosen_ref[...], held)
    to_a_ref[2 * faces :, :] = jnp.zeros_like(to_a_ref[2 * faces :, :])
    for side_ref, to_ref in ((side_a_ref, to_a_ref), (side_b_ref, to_b_ref)):
        to_ref[:faces, :] = side_ref[...]
        to_ref[faces : 2 * faces, :] = own


def near_traces_kernel(aligned_ref, image_ref, side_b_ref):
    gather_traces(image_ref[...], aligned_ref, side_b_ref.shape[0], side_b_ref)


def stiffness_kernel(pairs_ref, blocks_ref, field_ref, out_ref, pieces, sums):
    block_rows = field_ref.shape[0]
    size = blocks_ref.shape[1]
    count = pairs_ref.shape[1]
    high, low = halves(field_ref[...])
    pieces[...] = jnp.zeros_like(pieces)
    pieces[pl.ds(0, block_rows, stride=SUBLANES), :] = high
    pieces[pl.ds(1, block_rows, stride=SUBLANES), :] = low

    def times(row, block, contract):
        left = pieces[pl.ds(pl.multiple_of(row * SUBLANES, SUBLANES), SUBLANES), :]
        return lax.dot_general(
            left[:, :size].astype(BF16),
            block,
            (((1,), (contract,)), ((), ())),
            preferred_element_type=F32,
        )

    def add(row, value):
        place = pl.ds(pl.multiple_of(row * SUBLANES, SUBLANES), SUBLANES)
        sums[place, :size] = sums[place, :size] + value

    sums[...] = jnp.zeros_like(sums)
    for i in range(block_rows):
        sums[i * SUBLANES : (i + 1) * SUBLANES, :size] = times(i, blocks_ref[i], 1)
    for p in range(count):
        first = pairs_ref[0, p]
        other = pairs_ref[1, p]
        block = blocks_ref[block_rows + p]
        add(first, times(other, block, 1))
        add(other, times(first, block, 0))
    out_ref[...] = (
        sums[pl.ds(0, block_rows, stride=SUBLANES), :]
        + sums[pl.ds(1, block_rows, stride=SUBLANES), :]
    )


def spread_jumps(size, faces, rows_ref, rows_first, weights_ref, own_ref, arrived_ref, block_rows):
    dof_of = lax.broadcasted_iota(jnp.int32, (size, LANES), 0).astype(F32).astype(BF16)
    row_of = lax.broadcasted_iota(jnp.int32, (block_rows, LANES), 0).astype(F32).astype(BF16)
    none = jnp.zeros((), BF16)
    one = jnp.ones((), BF16)

    def widened(value, f, rows):
        slab = jnp.broadcast_to(value[f : f + 1, :], (2 * SUBLANES, LANES)).astype(BF16)
        return jnp.concatenate([slab] * (rows // (2 * SUBLANES)), axis=0)

    def step(k, total):
        lam = weights_ref[tile(k), :] * (own_ref[tile(k), :] - arrived_ref[tile(k), :])
        high, low = halves(lam)
        dof, row = split(rows_ref[tile(rows_first // SUBLANES + k), :], block_rows)
        dof = dof.astype(F32)
        row = row.astype(F32)
        left = []
        right = []
        for f in range(SUBLANES):
            here = row_of == widened(row, f, block_rows)
            left.append(
                jnp.concatenate(
                    [
                        jnp.where(here, widened(high, f, block_rows), none),
                        jnp.where(here, widened(low, f, block_rows), none),
                    ],
                    axis=0,
                )
            )
            right.append(jnp.where(dof_of == widened(dof, f, size), one, none))
        return total + lax.dot_general(
            jnp.concatenate(right, axis=1),
            jnp.concatenate(left, axis=1),
            (((1,), (1,)), ((), ())),
            preferred_element_type=F32,
        )

    total = lax.fori_loop(
        0, faces // SUBLANES, step, jnp.zeros((size, 2 * block_rows), F32), unroll=8
    )
    total = total.T
    return total[:block_rows] + total[block_rows:]


def near_kernel(size, aligned_ref, product_ref, to_ref, from_ref, partial_ref, weights_ref):
    block_rows = product_ref.shape[0]
    faces = weights_ref.shape[0]
    odd = lax.rem(lax.axis_index("sub"), 2) == 1
    weights_ref[...] = jnp.where(odd, from_ref[faces:, :], to_ref[faces:, :])
    partial_ref[...] = product_ref[...]
    partial_ref[:, :size] = partial_ref[:, :size] + spread_jumps(
        size, faces, aligned_ref, faces, weights_ref, to_ref, from_ref, block_rows
    )


def far_kernel(
    size,
    aligned_ref,
    partial_ref,
    to_ref,
    from_ref,
    image_ref,
    weights_ref,
    side_a_ref,
):
    block_rows = partial_ref.shape[0]
    faces = weights_ref.shape[0]
    odd = lax.rem(lax.axis_index("sub"), 2) == 1
    weights_ref[...] = jnp.where(
        odd, to_ref[faces : 2 * faces, :], from_ref[faces : 2 * faces, :]
    )
    image_ref[...] = partial_ref[...]
    image_ref[:, :size] = image_ref[:, :size] + spread_jumps(
        size, faces, aligned_ref, 0, weights_ref, to_ref, from_ref, block_rows
    )
    gather_traces(image_ref[...], aligned_ref, 0, side_a_ref.at[:faces, :])
    side_a_ref[faces:, :] = jnp.zeros_like(side_a_ref[faces:, :])


def column_sums(value):
    return jnp.sum(value, axis=0, keepdims=True)


def jump_sums(weights_ref, own_ref, arrived_ref, first_ref):
    faces = slice(0, weights_ref.shape[0])
    own = own_ref[faces, :]
    lam = weights_ref[...] * (own - arrived_ref[faces, :])
    return column_sums(lam * first_ref[faces, :]), column_sums(lam * own)


def near_sums_kernel(
    product_ref, weights_ref, own_ref, arrived_ref, first_ref, field_ref, image_ref, rows_ref
):
    field = field_ref[...]
    image = image_ref[...]
    product = product_ref[...]
    with_field, with_image = jump_sums(weights_ref, own_ref, arrived_ref, first_ref)
    parts = [
        column_sums(field * field),
        column_sums(field * image),
        column_sums(image * image),
        column_sums(field * product) + with_field,
        column_sums(image * product) + with_image,
    ]
    parts += [jnp.zeros_like(parts[0])] * (SUBLANES - len(parts))
    rows_ref[...] = jnp.concatenate(parts, axis=0)


def sums_kernel(rows_ref, weights_ref, own_ref, arrived_ref, first_ref, sums_ref):
    with_field, with_image = jump_sums(weights_ref, own_ref, arrived_ref, first_ref)
    row = lax.broadcasted_iota(jnp.int32, (SUBLANES, LANES), 0)
    rows = rows_ref[...] + jnp.where(row == 3, with_field, jnp.where(row == 4, with_image, 0.0))
    lane = lax.broadcasted_iota(jnp.int32, (SUBLANES, LANES), 1)
    whole = jnp.sum(rows, axis=1, keepdims=True)
    packed = column_sums(jnp.where(lane == row, whole, 0.0))
    sums_ref[...] = jnp.broadcast_to(packed[None], sums_ref.shape)


def second_kernel(
    size,
    aligned_ref,
    product_ref,
    weights_a_ref,
    weights_b_ref,
    side_a_ref,
    side_b_ref,
    from_a_ref,
    from_b_ref,
    second_ref,
):
    block_rows = product_ref.shape[0]
    faces = weights_a_ref.shape[0]
    second_ref[...] = product_ref[...]
    second_ref[:, :size] = (
        second_ref[:, :size]
        + spread_jumps(
            size, faces, aligned_ref, 0, weights_a_ref, side_a_ref, from_a_ref, block_rows
        )
        + spread_jumps(
            size, faces, aligned_ref, faces, weights_b_ref, side_b_ref, from_b_ref, block_rows
        )
    )


def final_kernel(field_ref, image_ref, second_ref, sums_ref, solution_ref, residual_ref):
    size = solution_ref.shape[1]
    row = jnp.sum(sums_ref[...], axis=0)
    lane = lax.broadcasted_iota(jnp.int32, (1, LANES), 1)

    def entry(k):
        return jnp.sum(jnp.where(lane == k, row, 0.0), axis=1, keepdims=True)

    bb, bq, qq, bw, qw = (entry(k) for k in range(5))
    field = field_ref[:, :size]
    image = image_ref[:, :size]
    second = second_ref[:, :size]
    alpha = bb / bq
    norm = bb - alpha * (2.0 * bq - alpha * qq)
    beta = norm / bb
    grown = 1.0 + beta
    energy = grown * (grown * bq - alpha * (bw + qq)) + alpha * alpha * qw
    alpha_next = norm / energy
    residual = field - alpha * image
    direction = residual + beta * field
    moved = (image - alpha * second) + beta * image
    solution_ref[...] = alpha * field + alpha_next * direction
    residual_ref[...] = residual - alpha_next * moved


def swap(value, odd):
    count = lax.axis_size("sub")
    pairs = []
    for first in range(odd, count, 2):
        second = (first + 1) % count
        pairs += [(first, second), (second, first)]
    return lax.ppermute(value, "sub", pairs)


def swap_slots(value, k):
    count = lax.axis_size("blk")
    return lax.ppermute(value, "blk", [(slot, slot ^ k) for slot in range(count)])


def on_device(
    right_side, stiffness, block_pairs, trace_rows, partner_face, owner_list, mortar_weight
):
    field = right_side[0, 0].T
    block_rows, size = field.shape
    stored = stiffness[0, 0]
    blocks = stored.reshape(stored.shape[0], size, size)
    pairs = block_pairs[0, 0]
    rows = trace_rows[0, 0]
    partner = partner_face[0, 0]
    owners = owner_list[0, 0]
    faces = partner.shape[0]
    devices = lax.axis_size("sub") * lax.axis_size("blk")

    own_weights = mortar_weight[0, 0]
    held = [swap_slots(own_weights, k) for k in range(1, own_weights.shape[0])]
    last = 2 * faces + block_rows

    def placed(value, first):
        below = last + SUBLANES + faces - first - value.shape[0]
        return jnp.pad(value, ((first, below), (0, LANES - value.shape[1])))

    indices = placed(rows, 0) + placed(partner_face[0], last) + placed(owner_list[0], last + 1)
    packed = (
        indices.astype(F32)
        + placed(field, 2 * faces)
        + placed(own_weights.reshape(faces, LANES), last + SUBLANES)
    )
    aligned, padded, chosen, side_a, side_b = call(
        functools.partial(first_kernel, owners.shape[0]),
        [
            shape(2 * faces, jnp.int32),
            shape(block_rows),
            jax.ShapeDtypeStruct((faces, faces), F32),
            shape(faces),
            shape(faces),
        ],
        [(packed, VMEM)],
    )
    to_a, to_b = call(
        functools.partial(message_kernel, last + SUBLANES),
        [shape(2 * faces + SUBLANES), shape(2 * faces)],
        [(value, VMEM) for value in (packed, chosen, side_a, side_b, *held)],
    )
    from_b = swap(to_b, 0)
    from_a = swap(to_a, 1)

    def stiff(vector):
        (product,) = call(
            stiffness_kernel,
            [shape(block_rows)],
            [(pairs, SMEM), (blocks, VMEM), (vector, VMEM)],
            scratch=[pltpu.VMEM((block_rows * SUBLANES, LANES), F32)] * 2,
        )
        return product

    partial, weights_b = call(
        functools.partial(near_kernel, size),
        [shape(block_rows), shape(faces)],
        [(value, VMEM) for value in (aligned, stiff(padded), to_b, from_b)],
        flops=1,
        moved=1,
    )
    image, weights_a, side_a = call(
        functools.partial(far_kernel, size),
        [shape(block_rows), shape(faces), shape(faces + SUBLANES)],
        [(value, VMEM) for value in (aligned, partial, to_a, from_a)],
    )
    from_a = swap(side_a, 1)
    (side_b,) = call(
        near_traces_kernel, [shape(faces)], [(aligned, VMEM), (image, VMEM)]
    )
    from_b = swap(side_b, 0)
    product = stiff(image)
    (sums,) = call(
        near_sums_kernel,
        [shape(SUBLANES)],
        [(value, VMEM) for value in (product, weights_b, side_b, from_b, to_b, padded, image)],
        flops=1,
        moved=1,
    )
    (sums,) = call(
        sums_kernel,
        [jax.ShapeDtypeStruct((devices, 1, LANES), F32)],
        [(value, VMEM) for value in (sums, weights_a, side_a, from_a, to_a)],
    )
    (second,) = call(
        functools.partial(second_kernel, size),
        [shape(block_rows)],
        [
            (value, VMEM)
            for value in (
                aligned, product, weights_a, weights_b, side_a, side_b, from_a, from_b
            )
        ],
        flops=1_000_000_000,
    )
    sums = lax.all_to_all(sums, ("sub", "blk"), split_axis=0, concat_axis=0, tiled=True)
    solution_field, residual = call(
        final_kernel,
        [jax.ShapeDtypeStruct((block_rows, size), F32)] * 2,
        [(padded, VMEM), (image, VMEM), (second, VMEM), (sums, VMEM)],
    )
    return (solution_field.T[None, None], residual.T[None, None])


def solution(mesh):
    in_specs = (
        P("sub", "blk", None, None),
        P("sub", "blk", None, None),
        P("sub", "blk", None, None),
        P("sub", "blk", None, None),
        P("sub", "blk", None),
        P("sub", "blk", None),
        P("sub", "blk", None, None, None),
    )
    out_specs = (P("sub", "blk", None, None), P("sub", "blk", None, None))
    return jax.shard_map(
        on_device, mesh=mesh, in_specs=in_specs, out_specs=out_specs, check_vma=False
    )
```

```python
import functools

import jax
import jax.numpy as jnp
from jax import lax
from jax.experimental import pallas as pl
from jax.experimental.pallas import tpu as pltpu
from jax.sharding import PartitionSpec as P

LANES = 128
SUBLANES = 8
VMEM = pl.BlockSpec(memory_space=pltpu.VMEM)
SMEM = pl.BlockSpec(memory_space=pltpu.SMEM)
F32 = jnp.float32
BF16 = jnp.bfloat16


def call(body, outs, inputs, scratch=(), flops=1_000_000, moved=1_000_000):
    return pl.pallas_call(
        body,
        out_shape=outs,
        in_specs=[spec for _, spec in inputs],
        out_specs=[VMEM] * len(outs),
        scratch_shapes=list(scratch),
        compiler_params=pltpu.CompilerParams(vmem_limit_bytes=32 * 1024 * 1024),
        cost_estimate=pl.CostEstimate(
            flops=flops, bytes_accessed=moved, transcendentals=0
        ),
    )(*[value for value, _ in inputs])


def shape(rows, dtype=F32):
    return jax.ShapeDtypeStruct((rows, LANES), dtype)


def halves(value):
    high = value.astype(BF16).astype(F32)
    return high, value - high


def gather_traces(field, rows_ref, rows_first, target):
    block_rows = field.shape[0]
    spread = [
        jnp.broadcast_to(field[i : i + 1, :], (SUBLANES, LANES)) for i in range(block_rows)
    ]
    for k in range(target.shape[0] // SUBLANES):
        index = rows_ref[rows_first + k * SUBLANES : rows_first + (k + 1) * SUBLANES, :]
        dof, row = split(index, block_rows)
        taken = jnp.zeros((SUBLANES, LANES), F32)
        for i in range(block_rows):
            here = jnp.take_along_axis(spread[i], dof, axis=1, mode="promise_in_bounds")
            taken = jnp.where(row == i, here, taken)
        target[k * SUBLANES : (k + 1) * SUBLANES, :] = taken


def tile(k):
    return pl.ds(pl.multiple_of(k * SUBLANES, SUBLANES), SUBLANES)


def split(index, block_rows):
    if block_rows & (block_rows - 1) == 0:
        shift = block_rows.bit_length() - 1
        return index >> shift, index & (block_rows - 1)
    return lax.div(index, block_rows), lax.rem(index, block_rows)


def one_hot(place, count):
    row = lax.broadcasted_iota(jnp.int32, (count, place.shape[1]), 0)
    return jnp.where(row == place, 1.0, 0.0)


def exact_dot(left, right):
    return jnp.dot(
        left, right, precision=lax.Precision.HIGHEST, preferred_element_type=F32
    )


def block_place(k, groups):
    return jnp.where(k == 0, 0, groups - k)


def first_kernel(
    groups, packed_ref, aligned_ref, padded_ref, chosen_ref, side_a_ref, side_b_ref
):
    faces = side_a_ref.shape[0]
    block_rows = padded_ref.shape[0]
    per_group = faces // groups
    slot = lax.axis_index("blk")
    parity = lax.rem(lax.axis_index("sub"), 2)
    east = pl.multiple_of((1 - parity) * faces, faces)
    west = pl.multiple_of(parity * faces, faces)
    padded_ref[...] = packed_ref[2 * faces : 2 * faces + block_rows, :]
    last = 2 * faces + block_rows
    tail = packed_ref[last : last + SUBLANES, :].astype(jnp.int32)
    partner = tail[:1, :faces]
    face = lax.broadcasted_iota(jnp.int32, (1, faces), 1)
    source = jnp.zeros((1, faces), jnp.int32)
    for g in range(groups):
        inside = face - g * per_group
        source = jnp.where(
            (inside >= 0) & (inside < per_group),
            block_place(tail[1:2, g : g + 1] ^ slot, groups) * per_group + inside,
            source,
        )
    order = one_hot(partner, faces)
    aligned_ref[pl.ds(west, faces), :] = packed_ref[faces : 2 * faces, :].astype(jnp.int32)
    aligned_ref[pl.ds(east, faces), :] = exact_dot(order, packed_ref[:faces, :]).astype(jnp.int32)
    chosen_ref[...] = lax.dot_general(
        order.astype(BF16),
        one_hot(source, faces).astype(BF16),
        (((1,), (1,)), ((), ())),
        preferred_element_type=F32,
    )
    gather_traces(padded_ref[...], aligned_ref, 0, side_a_ref)
    gather_traces(padded_ref[...], aligned_ref, faces, side_b_ref)


def message_kernel(first, packed_ref, chosen_ref, side_a_ref, side_b_ref, *refs):
    faces = side_a_ref.shape[0]
    *weight_refs, odd_a_ref, odd_b_ref, even_a_ref, even_b_ref = refs
    slot = lax.axis_index("blk")
    per_group = weight_refs[0].shape[1]
    kept = pl.ds(pl.multiple_of(first + slot * per_group, SUBLANES), per_group)
    held = jnp.concatenate(
        [packed_ref[kept, :]] + [weight_ref[slot] for weight_ref in weight_refs], axis=0
    )
    own = exact_dot(chosen_ref[...], held)
    for side_ref, to_refs in (
        (side_a_ref, (odd_a_ref, even_a_ref)),
        (side_b_ref, (odd_b_ref, even_b_ref)),
    ):
        for to_ref in to_refs:
            to_ref[:faces, :] = side_ref[...]
    for to_ref in (odd_a_ref, odd_b_ref, even_b_ref):
        to_ref[faces : 2 * faces, :] = own
    for to_ref in (odd_a_ref, odd_b_ref):
        to_ref[2 * faces :, :] = jnp.zeros_like(to_ref[2 * faces :, :])


def stiffness_kernel(pairs_ref, blocks_ref, field_ref, out_ref, pieces, sums):
    block_rows = field_ref.shape[0]
    size = blocks_ref.shape[1]
    count = pairs_ref.shape[1]
    high, low = halves(field_ref[...])
    pieces[...] = jnp.zeros_like(pieces)
    pieces[pl.ds(0, block_rows, stride=SUBLANES), :] = high
    pieces[pl.ds(1, block_rows, stride=SUBLANES), :] = low

    def times(row, block, contract):
        left = pieces[pl.ds(pl.multiple_of(row * SUBLANES, SUBLANES), SUBLANES), :]
        return lax.dot_general(
            left[:, :size].astype(BF16),
            block,
            (((1,), (contract,)), ((), ())),
            preferred_element_type=F32,
        )

    def add(row, value):
        place = pl.ds(pl.multiple_of(row * SUBLANES, SUBLANES), SUBLANES)
        sums[place, :size] = sums[place, :size] + value

    sums[...] = jnp.zeros_like(sums)
    for i in range(block_rows):
        sums[i * SUBLANES : (i + 1) * SUBLANES, :size] = times(i, blocks_ref[i], 1)
    for p in range(count):
        first = pairs_ref[0, p]
        other = pairs_ref[1, p]
        block = blocks_ref[block_rows + p]
        add(first, times(other, block, 1))
        add(other, times(first, block, 0))
    out_ref[...] = (
        sums[pl.ds(0, block_rows, stride=SUBLANES), :]
        + sums[pl.ds(1, block_rows, stride=SUBLANES), :]
    )


def spread_jumps(size, block_rows, rows_ref, rows_first, jumps):
    dof_of = lax.broadcasted_iota(jnp.int32, (size, LANES), 0).astype(F32).astype(BF16)
    row_of = lax.broadcasted_iota(jnp.int32, (block_rows, LANES), 0).astype(F32).astype(BF16)
    none = jnp.zeros((), BF16)
    one = jnp.ones((), BF16)

    def widened(value, f, rows):
        slab = jnp.broadcast_to(value[f : f + 1, :], (2 * SUBLANES, LANES)).astype(BF16)
        return jnp.concatenate([slab] * (rows // (2 * SUBLANES)), axis=0)

    total = jnp.zeros((size, 2 * block_rows), F32)
    for k, lam in enumerate(jumps):
        high, low = halves(lam)
        place = slice(rows_first + k * SUBLANES, rows_first + (k + 1) * SUBLANES)
        dof, row = split(rows_ref[place, :], block_rows)
        dof = dof.astype(F32)
        row = row.astype(F32)
        left = []
        right = []
        for f in range(SUBLANES):
            here = row_of == widened(row, f, block_rows)
            left.append(
                jnp.concatenate(
                    [
                        jnp.where(here, widened(high, f, block_rows), none),
                        jnp.where(here, widened(low, f, block_rows), none),
                    ],
                    axis=0,
                )
            )
            right.append(jnp.where(dof_of == widened(dof, f, size), one, none))
        total = total + lax.dot_general(
            jnp.concatenate(right, axis=1),
            jnp.concatenate(left, axis=1),
            (((1,), (1,)), ((), ())),
            preferred_element_type=F32,
        )
    total = total.T
    return total[:block_rows] + total[block_rows:]


def weighted_jumps(faces, weights_ref, own_ref, *arrived_refs):
    odd = lax.rem(lax.axis_index("sub"), 2) == 1
    for k in range(0, faces, SUBLANES):
        place = slice(k, k + SUBLANES)
        arrived = arrived_refs[0][place, :]
        if len(arrived_refs) > 1:
            arrived = jnp.where(odd, arrived_refs[1][place, :], arrived)
        yield weights_ref[place, :] * (own_ref[place, :] - arrived)


def near_kernel(
    size,
    faces,
    aligned_ref,
    product_ref,
    to_ref,
    even_from_a_ref,
    even_from_b_ref,
    odd_from_b_ref,
    partial_ref,
    weights_a_ref,
    weights_b_ref,
    arrived_ref,
):
    odd = lax.rem(lax.axis_index("sub"), 2) == 1
    own = to_ref[faces : 2 * faces, :]
    weights_a_ref[...] = jnp.where(odd, own, even_from_a_ref[faces : 2 * faces, :])
    weights_b_ref[...] = jnp.where(odd, odd_from_b_ref[faces : 2 * faces, :], own)
    arrived_ref[...] = jnp.where(odd, odd_from_b_ref[:faces, :], even_from_b_ref[:faces, :])

    @pl.when(odd)
    def _():
        partial_ref[...] = product_ref[...]
        partial_ref[:, :size] = partial_ref[:, :size] + spread_jumps(
            size,
            product_ref.shape[0],
            aligned_ref,
            faces,
            weighted_jumps(faces, weights_b_ref, to_ref, arrived_ref),
        )


def odd_kernel(
    size,
    faces,
    aligned_ref,
    partial_ref,
    weights_ref,
    to_ref,
    from_ref,
    image_ref,
    side_a_ref,
    side_b_ref,
):
    @pl.when(lax.rem(lax.axis_index("sub"), 2) == 1)
    def _():
        image_ref[...] = partial_ref[...]
        image_ref[:, :size] = image_ref[:, :size] + spread_jumps(
            size,
            partial_ref.shape[0],
            aligned_ref,
            0,
            weighted_jumps(faces, weights_ref, to_ref, from_ref),
        )
        gather_traces(image_ref[...], aligned_ref, 0, side_a_ref.at[:faces, :])
        gather_traces(image_ref[...], aligned_ref, faces, side_b_ref)
        side_a_ref[faces:, :] = jnp.zeros_like(side_a_ref[faces:, :])


def even_kernel(
    size,
    faces,
    aligned_ref,
    product_ref,
    weights_a_ref,
    weights_b_ref,
    to_a_ref,
    to_b_ref,
    from_a_ref,
    from_b_ref,
    odd_image_ref,
    odd_a_ref,
    odd_b_ref,
    image_ref,
    side_a_ref,
    side_b_ref,
):
    odd = lax.rem(lax.axis_index("sub"), 2) == 1

    @pl.when(odd)
    def _():
        image_ref[...] = odd_image_ref[...]
        side_a_ref[...] = odd_a_ref[:faces, :]
        side_b_ref[...] = odd_b_ref[...]

    @pl.when(jnp.logical_not(odd))
    def _():
        image_ref[...] = product_ref[...]
        coupled = [
            spread_jumps(
                size,
                product_ref.shape[0],
                aligned_ref,
                first,
                weighted_jumps(faces, weights_ref, to_ref, from_ref),
            )
            for first, weights_ref, to_ref, from_ref in (
                (0, weights_a_ref, to_a_ref, from_a_ref),
                (faces, weights_b_ref, to_b_ref, from_b_ref),
            )
        ]
        image_ref[:, :size] = image_ref[:, :size] + (coupled[0] + coupled[1])
        gather_traces(image_ref[...], aligned_ref, 0, side_a_ref)
        gather_traces(image_ref[...], aligned_ref, faces, side_b_ref)


def column_sums(value):
    return jnp.sum(value, axis=0, keepdims=True)


def jump_sums(faces, weights_ref, own_ref, arrived_ref, first_ref, first_arrived_ref):
    even = lax.rem(lax.axis_index("sub"), 2) == 0
    place = slice(0, faces)
    jump = own_ref[place, :] - arrived_ref[place, :]
    first = first_ref[place, :] - first_arrived_ref[place, :]
    lam = weights_ref[...] * jump
    return tuple(
        jnp.where(even, column_sums(lam * value), 0.0) for value in (first, jump)
    )


def near_sums_kernel(
    faces,
    product_ref,
    weights_ref,
    own_ref,
    arrived_ref,
    first_ref,
    first_arrived_ref,
    field_ref,
    image_ref,
    rows_ref,
):
    field = field_ref[...]
    image = image_ref[...]
    product = product_ref[...]
    with_field, with_image = jump_sums(
        faces, weights_ref, own_ref, arrived_ref, first_ref, first_arrived_ref
    )
    parts = [
        column_sums(field * field),
        column_sums(field * image),
        column_sums(image * image),
        column_sums(field * product) + with_field,
        column_sums(image * product) + with_image,
    ]
    parts += [jnp.zeros_like(parts[0])] * (SUBLANES - len(parts))
    rows_ref[...] = jnp.concatenate(parts, axis=0)


def sums_kernel(
    faces, rows_ref, weights_ref, own_ref, arrived_ref, first_ref, first_arrived_ref, sums_ref
):
    with_field, with_image = jump_sums(
        faces, weights_ref, own_ref, arrived_ref, first_ref, first_arrived_ref
    )
    row = lax.broadcasted_iota(jnp.int32, (SUBLANES, LANES), 0)
    rows = rows_ref[...] + jnp.where(row == 3, with_field, jnp.where(row == 4, with_image, 0.0))
    lane = lax.broadcasted_iota(jnp.int32, (SUBLANES, LANES), 1)
    whole = jnp.sum(rows, axis=1, keepdims=True)
    packed = column_sums(jnp.where(lane == row, whole, 0.0))
    sums_ref[...] = jnp.broadcast_to(packed[None], sums_ref.shape)


def second_kernel(
    size,
    aligned_ref,
    product_ref,
    weights_a_ref,
    weights_b_ref,
    side_a_ref,
    side_b_ref,
    even_from_a_ref,
    even_from_b_ref,
    odd_from_a_ref,
    odd_from_b_ref,
    second_ref,
):
    block_rows = product_ref.shape[0]
    faces = side_a_ref.shape[0]
    second_ref[...] = product_ref[...]
    coupled = [
        spread_jumps(
            size,
            block_rows,
            aligned_ref,
            first,
            weighted_jumps(faces, weights_ref, own_ref, even_from_ref, odd_from_ref),
        )
        for first, weights_ref, own_ref, even_from_ref, odd_from_ref in (
            (0, weights_a_ref, side_a_ref, even_from_a_ref, odd_from_a_ref),
            (faces, weights_b_ref, side_b_ref, even_from_b_ref, odd_from_b_ref),
        )
    ]
    second_ref[:, :size] = second_ref[:, :size] + (coupled[0] + coupled[1])


def final_kernel(field_ref, image_ref, second_ref, sums_ref, solution_ref, residual_ref):
    size = solution_ref.shape[1]
    row = jnp.sum(sums_ref[...], axis=0)
    lane = lax.broadcasted_iota(jnp.int32, (1, LANES), 1)

    def entry(k):
        return jnp.sum(jnp.where(lane == k, row, 0.0), axis=1, keepdims=True)

    bb, bq, qq, bw, qw = (entry(k) for k in range(5))
    field = field_ref[:, :size]
    image = image_ref[:, :size]
    second = second_ref[:, :size]
    alpha = bb / bq
    norm = bb - alpha * (2.0 * bq - alpha * qq)
    beta = norm / bb
    grown = 1.0 + beta
    energy = grown * (grown * bq - alpha * (bw + qq)) + alpha * alpha * qw
    alpha_next = norm / energy
    residual = field - alpha * image
    direction = residual + beta * field
    moved = (image - alpha * second) + beta * image
    solution_ref[...] = alpha * field + alpha_next * direction
    residual_ref[...] = residual - alpha_next * moved


def across(value, parity, steps):
    count = lax.axis_size("sub")
    pairs = [(source, (source + steps) % count) for source in range(parity, count, 2)]
    return lax.ppermute(value, "sub", pairs)


def swap_slots(value, k):
    count = lax.axis_size("blk")
    return lax.ppermute(value, "blk", [(slot, slot ^ k) for slot in range(count)])


def on_device(
    right_side, stiffness, block_pairs, trace_rows, partner_face, owner_list, mortar_weight
):
    field = right_side[0, 0].T
    block_rows, size = field.shape
    stored = stiffness[0, 0]
    blocks = stored.reshape(stored.shape[0], size, size)
    pairs = block_pairs[0, 0]
    rows = trace_rows[0, 0]
    partner = partner_face[0, 0]
    owners = owner_list[0, 0]
    faces = partner.shape[0]
    devices = lax.axis_size("sub") * lax.axis_size("blk")

    own_weights = mortar_weight[0, 0]
    held = [swap_slots(own_weights, k) for k in range(own_weights.shape[0] - 1, 0, -1)]
    last = 2 * faces + block_rows

    def placed(value, first):
        below = last + SUBLANES + faces - first - value.shape[0]
        return jnp.pad(value, ((first, below), (0, LANES - value.shape[1])))

    indices = placed(rows, 0) + placed(partner_face[0], last) + placed(owner_list[0], last + 1)
    packed = (
        indices.astype(F32)
        + placed(field, 2 * faces)
        + placed(own_weights.reshape(faces, LANES), last + SUBLANES)
    )
    aligned, padded, chosen, side_a, side_b = call(
        functools.partial(first_kernel, owners.shape[0]),
        [
            shape(2 * faces, jnp.int32),
            shape(block_rows),
            jax.ShapeDtypeStruct((faces, faces), F32),
            shape(faces),
            shape(faces),
        ],
        [(packed, VMEM)],
    )
    to_a, to_b, even_a, even_b = call(
        functools.partial(message_kernel, last + SUBLANES),
        [
            shape(2 * faces + 2 * SUBLANES),
            shape(2 * faces + SUBLANES),
            shape(faces),
            shape(2 * faces),
        ],
        [(value, VMEM) for value in (packed, chosen, side_a, side_b, *held)],
    )
    even_from_a = across(to_a, 1, 1)
    even_from_b = across(to_b, 1, -1)
    odd_from_b = across(even_b, 0, 1)
    odd_from_a = across(even_a, 0, -1)

    def stiff(vector):
        (product,) = call(
            stiffness_kernel,
            [shape(block_rows)],
            [(pairs, SMEM), (blocks, VMEM), (vector, VMEM)],
            scratch=[pltpu.VMEM((block_rows * SUBLANES, LANES), F32)] * 2,
        )
        return product

    product = stiff(padded)
    partial, weights_a, weights_b, from_b = call(
        functools.partial(near_kernel, size, faces),
        [shape(block_rows)] + [shape(faces)] * 3,
        [
            (value, VMEM)
            for value in (aligned, product, to_b, even_from_a, even_from_b, odd_from_b)
        ],
        flops=1,
        moved=1,
    )
    odd_image, odd_a, odd_b = call(
        functools.partial(odd_kernel, size, faces),
        [shape(block_rows), shape(faces + SUBLANES), shape(faces)],
        [(value, VMEM) for value in (aligned, partial, weights_a, to_a, odd_from_a)],
        flops=1,
        moved=1,
    )
    second_from_a = across(odd_a, 1, 1)
    second_from_b = across(odd_b, 1, -1)
    image, side_a, side_b = call(
        functools.partial(even_kernel, size, faces),
        [shape(block_rows)] + [shape(faces)] * 2,
        [
            (value, VMEM)
            for value in (
                aligned,
                product,
                weights_a,
                weights_b,
                to_a,
                to_b,
                even_from_a,
                from_b,
                odd_image,
                odd_a,
                odd_b,
            )
        ],
        flops=1,
        moved=1,
    )
    third_from_b = across(side_b, 0, 1)
    third_from_a = across(side_a, 0, -1)
    product = stiff(image)
    (sums,) = call(
        functools.partial(near_sums_kernel, faces),
        [shape(SUBLANES)],
        [
            (value, VMEM)
            for value in (
                product, weights_b, side_b, second_from_b, to_b, from_b, padded, image
            )
        ],
        flops=1,
        moved=1,
    )
    (sums,) = call(
        functools.partial(sums_kernel, faces),
        [jax.ShapeDtypeStruct((devices, 1, LANES), F32)],
        [
            (value, VMEM)
            for value in (sums, weights_a, side_a, second_from_a, to_a, even_from_a)
        ],
    )
    (second,) = call(
        functools.partial(second_kernel, size),
        [shape(block_rows)],
        [
            (value, VMEM)
            for value in (
                aligned,
                product,
                weights_a,
                weights_b,
                side_a,
                side_b,
                second_from_a,
                second_from_b,
                third_from_a,
                third_from_b,
            )
        ],
        flops=1_000_000_000,
    )
    sums = lax.all_to_all(sums, ("sub", "blk"), split_axis=0, concat_axis=0, tiled=True)
    solution_field, residual = call(
        final_kernel,
        [jax.ShapeDtypeStruct((block_rows, size), F32)] * 2,
        [(padded, VMEM), (image, VMEM), (second, VMEM), (sums, VMEM)],
    )
    return (solution_field.T[None, None], residual.T[None, None])


def solution(mesh):
    in_specs = (
        P("sub", "blk", None, None),
        P("sub", "blk", None, None),
        P("sub", "blk", None, None),
        P("sub", "blk", None, None),
        P("sub", "blk", None),
        P("sub", "blk", None),
        P("sub", "blk", None, None, None),
    )
    out_specs = (P("sub", "blk", None, None), P("sub", "blk", None, None))
    return jax.shard_map(
        on_device, mesh=mesh, in_specs=in_specs, out_specs=out_specs, check_vma=False
    )
```

```python
import functools

import jax
import jax.numpy as jnp
from jax import lax
from jax.experimental import pallas as pl
from jax.experimental.pallas import tpu as pltpu
from jax.sharding import PartitionSpec as P

LANES = 128
SUBLANES = 8
VMEM = pl.BlockSpec(memory_space=pltpu.VMEM)
SMEM = pl.BlockSpec(memory_space=pltpu.SMEM)
F32 = jnp.float32
BF16 = jnp.bfloat16


def call(body, outs, inputs, scratch=(), flops=1_000_000, moved=1_000_000):
    return pl.pallas_call(
        body,
        out_shape=outs,
        in_specs=[spec for _, spec in inputs],
        out_specs=[VMEM] * len(outs),
        scratch_shapes=list(scratch),
        compiler_params=pltpu.CompilerParams(vmem_limit_bytes=32 * 1024 * 1024),
        cost_estimate=pl.CostEstimate(
            flops=flops, bytes_accessed=moved, transcendentals=0
        ),
    )(*[value for value, _ in inputs])


def shape(rows, dtype=F32):
    return jax.ShapeDtypeStruct((rows, LANES), dtype)


def halves(value):
    high = value.astype(BF16).astype(F32)
    return high, value - high


def gather_traces(field, rows_ref, rows_first, target):
    block_rows = field.shape[0]
    spread = [
        jnp.broadcast_to(field[i : i + 1, :], (SUBLANES, LANES)) for i in range(block_rows)
    ]
    for k in range(target.shape[0] // SUBLANES):
        index = rows_ref[rows_first + k * SUBLANES : rows_first + (k + 1) * SUBLANES, :]
        dof, row = split(index, block_rows)
        taken = jnp.zeros((SUBLANES, LANES), F32)
        for i in range(block_rows):
            here = jnp.take_along_axis(spread[i], dof, axis=1, mode="promise_in_bounds")
            taken = jnp.where(row == i, here, taken)
        target[k * SUBLANES : (k + 1) * SUBLANES, :] = taken


def tile(k):
    return pl.ds(pl.multiple_of(k * SUBLANES, SUBLANES), SUBLANES)


def split(index, block_rows):
    if block_rows & (block_rows - 1) == 0:
        shift = block_rows.bit_length() - 1
        return index >> shift, index & (block_rows - 1)
    return lax.div(index, block_rows), lax.rem(index, block_rows)


def one_hot(place, count):
    row = lax.broadcasted_iota(jnp.int32, (count, place.shape[1]), 0)
    return jnp.where(row == place, 1.0, 0.0)


def exact_dot(left, right):
    return jnp.dot(
        left, right, precision=lax.Precision.HIGHEST, preferred_element_type=F32
    )


def block_place(k, groups):
    return jnp.where(k == 0, 0, groups - k)


def first_kernel(
    groups, packed_ref, aligned_ref, padded_ref, choice_ref, to_a_ref, to_b_ref
):
    faces = aligned_ref.shape[0] // 2
    block_rows = padded_ref.shape[0]
    per_group = faces // groups
    slot = lax.axis_index("blk")
    parity = lax.rem(lax.axis_index("sub"), 2)
    east = pl.multiple_of((1 - parity) * faces, faces)
    west = pl.multiple_of(parity * faces, faces)
    padded_ref[...] = packed_ref[2 * faces : 2 * faces + block_rows, :]
    last = 2 * faces + block_rows
    tail = packed_ref[last : last + SUBLANES, :].astype(jnp.int32)
    partner = tail[:1, :faces]
    face = lax.broadcasted_iota(jnp.int32, (1, faces), 1)
    source = jnp.zeros((1, faces), jnp.int32)
    for g in range(groups):
        inside = face - g * per_group
        source = jnp.where(
            (inside >= 0) & (inside < per_group),
            block_place(tail[1:2, g : g + 1] ^ slot, groups) * per_group + inside,
            source,
        )
    order = one_hot(partner, faces)
    aligned_ref[pl.ds(west, faces), :] = packed_ref[faces : 2 * faces, :].astype(jnp.int32)
    aligned_ref[pl.ds(east, faces), :] = exact_dot(order, packed_ref[:faces, :]).astype(jnp.int32)
    choice_ref[...] = jnp.zeros_like(choice_ref)
    choice_ref[:1, :faces] = lax.dot_general(
        source.astype(F32).astype(BF16),
        order.astype(BF16),
        (((1,), (1,)), ((), ())),
        preferred_element_type=F32,
    )
    for first, to_ref in ((0, to_a_ref), (faces, to_b_ref)):
        gather_traces(padded_ref[...], aligned_ref, first, to_ref.at[:faces, :])
        to_ref[faces : faces + SUBLANES, :] = choice_ref[...]
    to_a_ref[faces + SUBLANES :, :] = jnp.zeros((SUBLANES, LANES), F32)


def blocks_kernel(first, packed_ref, last_ref, *block_refs):
    slot = lax.axis_index("blk")
    per_group = last_ref.shape[1]
    for place, block_ref in enumerate(block_refs):
        k = slot ^ (len(block_refs) - place)
        kept = pl.ds(pl.multiple_of(first + k * per_group, SUBLANES), per_group)
        block_ref[:per_group, :] = packed_ref[kept, :]
        block_ref[per_group:, :] = last_ref[k]


def near_traces_kernel(aligned_ref, image_ref, side_b_ref):
    gather_traces(image_ref[...], aligned_ref, side_b_ref.shape[0], side_b_ref)


def stiffness_kernel(pairs_ref, blocks_ref, field_ref, out_ref, pieces, sums):
    block_rows = field_ref.shape[0]
    size = blocks_ref.shape[1]
    count = pairs_ref.shape[1]
    high, low = halves(field_ref[...])
    pieces[...] = jnp.zeros_like(pieces)
    pieces[pl.ds(0, block_rows, stride=SUBLANES), :] = high
    pieces[pl.ds(1, block_rows, stride=SUBLANES), :] = low

    def times(row, block, contract):
        left = pieces[pl.ds(pl.multiple_of(row * SUBLANES, SUBLANES), SUBLANES), :]
        return lax.dot_general(
            left[:, :size].astype(BF16),
            block,
            (((1,), (contract,)), ((), ())),
            preferred_element_type=F32,
        )

    def add(row, value):
        place = pl.ds(pl.multiple_of(row * SUBLANES, SUBLANES), SUBLANES)
        sums[place, :size] = sums[place, :size] + value

    sums[...] = jnp.zeros_like(sums)
    for i in range(block_rows):
        sums[i * SUBLANES : (i + 1) * SUBLANES, :size] = times(i, blocks_ref[i], 1)
    for p in range(count):
        first = pairs_ref[0, p]
        other = pairs_ref[1, p]
        block = blocks_ref[block_rows + p]
        add(first, times(other, block, 1))
        add(other, times(first, block, 0))
    out_ref[...] = (
        sums[pl.ds(0, block_rows, stride=SUBLANES), :]
        + sums[pl.ds(1, block_rows, stride=SUBLANES), :]
    )


def spread_jumps(size, faces, rows_ref, rows_first, weights_ref, own_ref, arrived_ref, block_rows):
    dof_of = lax.broadcasted_iota(jnp.int32, (size, LANES), 0).astype(F32).astype(BF16)
    row_of = lax.broadcasted_iota(jnp.int32, (block_rows, LANES), 0).astype(F32).astype(BF16)
    none = jnp.zeros((), BF16)
    one = jnp.ones((), BF16)

    def widened(value, f, rows):
        slab = jnp.broadcast_to(value[f : f + 1, :], (2 * SUBLANES, LANES)).astype(BF16)
        return jnp.concatenate([slab] * (rows // (2 * SUBLANES)), axis=0)

    def step(k, total):
        lam = weights_ref[tile(k), :] * (own_ref[tile(k), :] - arrived_ref[tile(k), :])
        high, low = halves(lam)
        dof, row = split(rows_ref[tile(rows_first // SUBLANES + k), :], block_rows)
        dof = dof.astype(F32)
        row = row.astype(F32)
        left = []
        right = []
        for f in range(SUBLANES):
            here = row_of == widened(row, f, block_rows)
            left.append(
                jnp.concatenate(
                    [
                        jnp.where(here, widened(high, f, block_rows), none),
                        jnp.where(here, widened(low, f, block_rows), none),
                    ],
                    axis=0,
                )
            )
            right.append(jnp.where(dof_of == widened(dof, f, size), one, none))
        return total + lax.dot_general(
            jnp.concatenate(right, axis=1),
            jnp.concatenate(left, axis=1),
            (((1,), (1,)), ((), ())),
            preferred_element_type=F32,
        )

    total = lax.fori_loop(
        0, faces // SUBLANES, step, jnp.zeros((size, 2 * block_rows), F32), unroll=8
    )
    total = total.T
    return total[:block_rows] + total[block_rows:]


def image_kernel(
    size,
    first,
    packed_ref,
    last_ref,
    choice_ref,
    aligned_ref,
    product_ref,
    to_a_ref,
    to_b_ref,
    from_a_ref,
    from_b_ref,
    *refs,
):
    *block_refs, image_ref, weights_a_ref, weights_b_ref, side_a_ref = refs
    block_rows = product_ref.shape[0]
    faces = weights_a_ref.shape[0]
    per_group = last_ref.shape[1]
    slot = lax.axis_index("blk")
    odd = lax.rem(lax.axis_index("sub"), 2) == 1
    kept = pl.ds(pl.multiple_of(first + slot * per_group, SUBLANES), per_group)
    place = slice(faces, faces + SUBLANES)
    choice = jnp.where(odd, from_b_ref[place, :], from_a_ref[place, :])
    own, last = (
        lax.dot_general(
            one_hot(row[:1, :faces].astype(jnp.int32), faces),
            jnp.concatenate([block] + [block_ref[part, :] for block_ref in block_refs], axis=0),
            (((0,), (0,)), ((), ())),
            precision=lax.Precision.HIGHEST,
            preferred_element_type=F32,
        )
        for row, block, part in (
            (choice_ref[...], packed_ref[kept, :], slice(0, per_group)),
            (choice, last_ref[slot], slice(per_group, 2 * per_group)),
        )
    )
    weights_a_ref[...] = jnp.where(odd, own, last)
    weights_b_ref[...] = jnp.where(odd, last, own)
    image_ref[...] = product_ref[...]
    image_ref[:, :size] = (
        image_ref[:, :size]
        + spread_jumps(size, faces, aligned_ref, 0, weights_a_ref, to_a_ref, from_a_ref, block_rows)
        + spread_jumps(
            size, faces, aligned_ref, faces, weights_b_ref, to_b_ref, from_b_ref, block_rows
        )
    )
    gather_traces(image_ref[...], aligned_ref, 0, side_a_ref.at[:faces, :])
    side_a_ref[faces:, :] = jnp.zeros_like(side_a_ref[faces:, :])


def column_sums(value):
    return jnp.sum(value, axis=0, keepdims=True)


def jump_sums(weights_ref, own_ref, arrived_ref, first_ref):
    faces = slice(0, weights_ref.shape[0])
    own = own_ref[faces, :]
    lam = weights_ref[...] * (own - arrived_ref[faces, :])
    return column_sums(lam * first_ref[faces, :]), column_sums(lam * own)


def near_sums_kernel(
    product_ref, weights_ref, own_ref, arrived_ref, first_ref, field_ref, image_ref, rows_ref
):
    field = field_ref[...]
    image = image_ref[...]
    product = product_ref[...]
    with_field, with_image = jump_sums(weights_ref, own_ref, arrived_ref, first_ref)
    parts = [
        column_sums(field * field),
        column_sums(field * image),
        column_sums(image * image),
        column_sums(field * product) + with_field,
        column_sums(image * product) + with_image,
    ]
    parts += [jnp.zeros_like(parts[0])] * (SUBLANES - len(parts))
    rows_ref[...] = jnp.concatenate(parts, axis=0)


def sums_kernel(rows_ref, weights_ref, own_ref, arrived_ref, first_ref, sums_ref):
    with_field, with_image = jump_sums(weights_ref, own_ref, arrived_ref, first_ref)
    row = lax.broadcasted_iota(jnp.int32, (SUBLANES, LANES), 0)
    rows = rows_ref[...] + jnp.where(row == 3, with_field, jnp.where(row == 4, with_image, 0.0))
    lane = lax.broadcasted_iota(jnp.int32, (SUBLANES, LANES), 1)
    whole = jnp.sum(rows, axis=1, keepdims=True)
    packed = column_sums(jnp.where(lane == row, whole, 0.0))
    sums_ref[...] = jnp.broadcast_to(packed[None], sums_ref.shape)


def second_kernel(
    size,
    aligned_ref,
    product_ref,
    weights_a_ref,
    weights_b_ref,
    side_a_ref,
    side_b_ref,
    from_a_ref,
    from_b_ref,
    second_ref,
):
    block_rows = product_ref.shape[0]
    faces = weights_a_ref.shape[0]
    second_ref[...] = product_ref[...]
    second_ref[:, :size] = (
        second_ref[:, :size]
        + spread_jumps(
            size, faces, aligned_ref, 0, weights_a_ref, side_a_ref, from_a_ref, block_rows
        )
        + spread_jumps(
            size, faces, aligned_ref, faces, weights_b_ref, side_b_ref, from_b_ref, block_rows
        )
    )


def final_kernel(field_ref, image_ref, second_ref, sums_ref, solution_ref, residual_ref):
    size = solution_ref.shape[1]
    row = jnp.sum(sums_ref[...], axis=0)
    lane = lax.broadcasted_iota(jnp.int32, (1, LANES), 1)

    def entry(k):
        return jnp.sum(jnp.where(lane == k, row, 0.0), axis=1, keepdims=True)

    bb, bq, qq, bw, qw = (entry(k) for k in range(5))
    field = field_ref[:, :size]
    image = image_ref[:, :size]
    second = second_ref[:, :size]
    alpha = bb / bq
    norm = bb - alpha * (2.0 * bq - alpha * qq)
    beta = norm / bb
    grown = 1.0 + beta
    energy = grown * (grown * bq - alpha * (bw + qq)) + alpha * alpha * qw
    alpha_next = norm / energy
    residual = field - alpha * image
    direction = residual + beta * field
    moved = (image - alpha * second) + beta * image
    solution_ref[...] = alpha * field + alpha_next * direction
    residual_ref[...] = residual - alpha_next * moved


def swap(value, odd):
    count = lax.axis_size("sub")
    pairs = []
    for first in range(odd, count, 2):
        second = (first + 1) % count
        pairs += [(first, second), (second, first)]
    return lax.ppermute(value, "sub", pairs)


def from_behind(value, axis, steps):
    count = lax.axis_size(axis)
    pairs = [(source, (source + steps) % count) for source in range(count)]
    return lax.ppermute(value, axis, pairs)


def swap_slots(value, k):
    count = lax.axis_size("blk")
    return lax.ppermute(value, "blk", [(slot, slot ^ k) for slot in range(count)])


def on_device(
    right_side, stiffness, block_pairs, trace_rows, partner_face, owner_list, mortar_weight
):
    field = right_side[0, 0].T
    block_rows, size = field.shape
    stored = stiffness[0, 0]
    blocks = stored.reshape(stored.shape[0], size, size)
    pairs = block_pairs[0, 0]
    rows = trace_rows[0, 0]
    partner = partner_face[0, 0]
    owners = owner_list[0, 0]
    faces = partner.shape[0]
    devices = lax.axis_size("sub") * lax.axis_size("blk")

    own_weights = mortar_weight[0, 0]
    last_weights = from_behind(own_weights, "sub", 1)
    last = 2 * faces + block_rows

    def placed(value, first):
        below = last + SUBLANES + faces - first - value.shape[0]
        return jnp.pad(value, ((first, below), (0, LANES - value.shape[1])))

    indices = placed(rows, 0) + placed(partner_face[0], last) + placed(owner_list[0], last + 1)
    packed = (
        indices.astype(F32)
        + placed(field, 2 * faces)
        + placed(own_weights.reshape(faces, LANES), last + SUBLANES)
    )
    aligned, padded, choice, to_a, to_b = call(
        functools.partial(first_kernel, owners.shape[0]),
        [
            shape(2 * faces, jnp.int32),
            shape(block_rows),
            shape(SUBLANES),
            shape(faces + 2 * SUBLANES),
            shape(faces + SUBLANES),
        ],
        [(packed, VMEM)],
    )
    from_a = swap(to_a, 1)
    from_b = swap(to_b, 0)
    slots, per_group, _ = own_weights.shape
    blocks_to = call(
        functools.partial(blocks_kernel, last + SUBLANES),
        [shape(2 * per_group)] * (slots - 1),
        [(packed, VMEM), (last_weights, VMEM)],
        flops=1,
        moved=1,
    )
    blocks_from = [
        swap_slots(block, k) for k, block in zip(range(slots - 1, 0, -1), blocks_to)
    ]

    def stiff(vector):
        (product,) = call(
            stiffness_kernel,
            [shape(block_rows)],
            [(pairs, SMEM), (blocks, VMEM), (vector, VMEM)],
            scratch=[pltpu.VMEM((block_rows * SUBLANES, LANES), F32)] * 2,
        )
        return product

    image, weights_a, weights_b, side_a = call(
        functools.partial(image_kernel, size, last + SUBLANES),
        [shape(block_rows), shape(faces), shape(faces), shape(faces + SUBLANES)],
        [
            (value, VMEM)
            for value in (
                packed,
                last_weights,
                choice,
                aligned,
                stiff(padded),
                to_a,
                to_b,
                from_a,
                from_b,
                *blocks_from,
            )
        ],
    )
    from_a = swap(side_a, 1)
    (side_b,) = call(
        near_traces_kernel, [shape(faces)], [(aligned, VMEM), (image, VMEM)]
    )
    from_b = swap(side_b, 0)
    product = stiff(image)
    (sums,) = call(
        near_sums_kernel,
        [shape(SUBLANES)],
        [(value, VMEM) for value in (product, weights_b, side_b, from_b, to_b, padded, image)],
        flops=1,
        moved=1,
    )
    (sums,) = call(
        sums_kernel,
        [jax.ShapeDtypeStruct((devices, 1, LANES), F32)],
        [(value, VMEM) for value in (sums, weights_a, side_a, from_a, to_a)],
    )
    (second,) = call(
        functools.partial(second_kernel, size),
        [shape(block_rows)],
        [
            (value, VMEM)
            for value in (
                aligned, product, weights_a, weights_b, side_a, side_b, from_a, from_b
            )
        ],
        flops=1_000_000_000,
    )
    sums = lax.all_to_all(sums, ("sub", "blk"), split_axis=0, concat_axis=0, tiled=True)
    solution_field, residual = call(
        final_kernel,
        [jax.ShapeDtypeStruct((block_rows, size), F32)] * 2,
        [(padded, VMEM), (image, VMEM), (second, VMEM), (sums, VMEM)],
    )
    return (solution_field.T[None, None], residual.T[None, None])


def solution(mesh):
    in_specs = (
        P("sub", "blk", None, None),
        P("sub", "blk", None, None),
        P("sub", "blk", None, None),
        P("sub", "blk", None, None),
        P("sub", "blk", None),
        P("sub", "blk", None),
        P("sub", "blk", None, None, None),
    )
    out_specs = (P("sub", "blk", None, None), P("sub", "blk", None, None))
    return jax.shard_map(
        on_device, mesh=mesh, in_specs=in_specs, out_specs=out_specs, check_vma=False
    )
```

```python
import functools
import math

import jax
import jax.numpy as jnp
from jax import lax
from jax.experimental import pallas as pl
from jax.experimental.pallas import tpu as pltpu
from jax.sharding import PartitionSpec as P

LANES = 128
SUBLANES = 8
VMEM = pl.BlockSpec(memory_space=pltpu.VMEM)
F32 = jnp.float32
BF16 = jnp.bfloat16


def call(body, outs, inputs, scratch=(), flops=1_000_000, moved=1_000_000):
    return pl.pallas_call(
        body,
        out_shape=outs,
        in_specs=[spec for _, spec in inputs],
        out_specs=[VMEM] * len(outs),
        scratch_shapes=list(scratch),
        compiler_params=pltpu.CompilerParams(vmem_limit_bytes=32 * 1024 * 1024),
        cost_estimate=pl.CostEstimate(
            flops=flops, bytes_accessed=moved, transcendentals=0
        ),
    )(*[value for value, _ in inputs])


def shape(rows, dtype=F32):
    return jax.ShapeDtypeStruct((rows, LANES), dtype)


def halves(value):
    high = value.astype(BF16).astype(F32)
    return high, value - high


def gather_traces(field, rows_ref, rows_first, target):
    block_rows = field.shape[0]
    spread = [
        jnp.broadcast_to(field[i : i + 1, :], (SUBLANES, LANES)) for i in range(block_rows)
    ]
    for k in range(target.shape[0] // SUBLANES):
        index = rows_ref[rows_first + k * SUBLANES : rows_first + (k + 1) * SUBLANES, :]
        dof, row = split(index, block_rows)
        taken = jnp.zeros((SUBLANES, LANES), F32)
        for i in range(block_rows):
            here = jnp.take_along_axis(spread[i], dof, axis=1, mode="promise_in_bounds")
            taken = jnp.where(row == i, here, taken)
        target[k * SUBLANES : (k + 1) * SUBLANES, :] = taken


def tile(k):
    return pl.ds(pl.multiple_of(k * SUBLANES, SUBLANES), SUBLANES)


def split(index, block_rows):
    if block_rows & (block_rows - 1) == 0:
        shift = block_rows.bit_length() - 1
        return index >> shift, index & (block_rows - 1)
    return lax.div(index, block_rows), lax.rem(index, block_rows)


def one_hot(place, count):
    row = lax.broadcasted_iota(jnp.int32, (count, place.shape[1]), 0)
    return jnp.where(row == place, 1.0, 0.0)


def exact_dot(left, right):
    return jnp.dot(
        left, right, precision=lax.Precision.HIGHEST, preferred_element_type=F32
    )


def block_place(k, groups):
    return jnp.where(k == 0, 0, groups - k)


def first_kernel(
    groups, packed_ref, aligned_ref, padded_ref, choice_ref, to_a_ref, to_b_ref
):
    faces = aligned_ref.shape[0] // 2
    block_rows = padded_ref.shape[0]
    per_group = faces // groups
    slot = lax.axis_index("blk")
    parity = lax.rem(lax.axis_index("sub"), 2)
    east = pl.multiple_of((1 - parity) * faces, faces)
    west = pl.multiple_of(parity * faces, faces)
    padded_ref[...] = packed_ref[2 * faces : 2 * faces + block_rows, :]
    last = 2 * faces + block_rows
    tail = packed_ref[last : last + SUBLANES, :].astype(jnp.int32)
    partner = tail[:1, :faces]
    face = lax.broadcasted_iota(jnp.int32, (1, faces), 1)
    source = jnp.zeros((1, faces), jnp.int32)
    for g in range(groups):
        inside = face - g * per_group
        source = jnp.where(
            (inside >= 0) & (inside < per_group),
            block_place(tail[1:2, g : g + 1] ^ slot, groups) * per_group + inside,
            source,
        )
    order = one_hot(partner, faces)
    aligned_ref[pl.ds(west, faces), :] = packed_ref[faces : 2 * faces, :].astype(jnp.int32)
    aligned_ref[pl.ds(east, faces), :] = exact_dot(order, packed_ref[:faces, :]).astype(jnp.int32)
    choice_ref[...] = jnp.zeros_like(choice_ref)
    choice_ref[:1, :faces] = lax.dot_general(
        source.astype(F32).astype(BF16),
        order.astype(BF16),
        (((1,), (1,)), ((), ())),
        preferred_element_type=F32,
    )
    for first, to_ref in ((0, to_a_ref), (faces, to_b_ref)):
        gather_traces(padded_ref[...], aligned_ref, first, to_ref.at[:faces, :])
        to_ref[faces : faces + SUBLANES, :] = choice_ref[...]
    to_a_ref[faces + SUBLANES :, :] = jnp.zeros((SUBLANES, LANES), F32)


def blocks_kernel(first, packed_ref, last_ref, *block_refs):
    slot = lax.axis_index("blk")
    per_group = last_ref.shape[1]
    for place, block_ref in enumerate(block_refs):
        k = slot ^ (len(block_refs) - place)
        kept = pl.ds(pl.multiple_of(first + k * per_group, SUBLANES), per_group)
        block_ref[:per_group, :] = packed_ref[kept, :]
        block_ref[per_group:, :] = last_ref[k]


def near_traces_kernel(aligned_ref, image_ref, side_b_ref):
    gather_traces(image_ref[...], aligned_ref, side_b_ref.shape[0], side_b_ref)


def stiffness_kernel(size, pairs_ref, blocks_ref, field_ref, out_ref):
    block_rows = field_ref.shape[0]
    count = pairs_ref.shape[1]
    rows = block_rows + count
    width = math.lcm(size, LANES)
    tiles = width // LANES
    segments = width // size
    groups = size // segments
    batch = next(k for k in (4, 3, 2, 1) if groups % k == 0)

    def place(position):
        segment = sum(jnp.where(position >= k * size, 1, 0) for k in range(1, segments))
        return segment, position - segment * size

    def lanes_of(value, index):
        slabs = [
            jnp.take_along_axis(
                value[k : k + SUBLANES, :], index, axis=1, mode="promise_in_bounds"
            )
            for k in range(0, value.shape[0], SUBLANES)
        ]
        return jnp.concatenate(slabs, axis=0)

    field = field_ref[...]
    first_of, other_of = (one_hot(pairs_ref[k : k + 1, :], block_rows) for k in (0, 1))
    left, other = (
        lax.dot_general(
            ends,
            field,
            (((0,), (0,)), ((), ())),
            precision=lax.Precision.HIGHEST,
            preferred_element_type=F32,
        )
        for ends in (first_of, other_of)
    )
    right = jnp.concatenate([field, other], axis=0)
    lane = lax.broadcasted_iota(jnp.int32, (SUBLANES, LANES), 1)
    places = [place(lane + t * LANES) for t in range(tiles)]
    repeated = jnp.concatenate([lanes_of(right, inside) for _, inside in places], axis=1)
    segment, inside = place(lax.broadcasted_iota(jnp.int32, (width, LANES), 0))
    column = lax.broadcasted_iota(jnp.int32, (width, LANES), 1)
    add_segments = jnp.where(segment == column % segments, 1.0, 0.0).astype(BF16)
    fold = jnp.where(inside == column, 1.0, 0.0)
    dof_group = lax.broadcasted_iota(jnp.int32, (rows, LANES), 1) // segments
    total = jnp.zeros((rows, LANES), F32)
    turned = jnp.zeros((count, width), F32)
    for base in range(0, groups, batch):
        stack = []
        for g in range(base, base + batch):
            stored = blocks_ref[:, g * width : (g + 1) * width]
            product = stored * repeated
            high = product.astype(BF16)
            stack += [high, (product - high.astype(F32)).astype(BF16)]
            spread = [lanes_of(left, g * segments + segment) for segment, _ in places]
            turned = turned + stored[block_rows:] * jnp.concatenate(spread, axis=1)
        sums = jnp.dot(
            jnp.concatenate(stack, axis=0), add_segments, preferred_element_type=F32
        )
        for n in range(batch):
            both = sums[2 * n * rows : 2 * (n + 1) * rows]
            total = jnp.where(dof_group == base + n, both[:rows] + both[rows:], total)
    out_ref[...] = (
        total[:block_rows]
        + exact_dot(first_of, total[block_rows:])
        + exact_dot(other_of, exact_dot(turned, fold))
    )


def spread_jumps(size, faces, rows_ref, rows_first, weights_ref, own_ref, arrived_ref, block_rows):
    dof_of = lax.broadcasted_iota(jnp.int32, (size, LANES), 0).astype(F32).astype(BF16)
    row_of = lax.broadcasted_iota(jnp.int32, (block_rows, LANES), 0).astype(F32).astype(BF16)
    none = jnp.zeros((), BF16)
    one = jnp.ones((), BF16)

    def widened(value, f, rows):
        slab = jnp.broadcast_to(value[f : f + 1, :], (2 * SUBLANES, LANES)).astype(BF16)
        return jnp.concatenate([slab] * (rows // (2 * SUBLANES)), axis=0)

    def step(k, total):
        lam = weights_ref[tile(k), :] * (own_ref[tile(k), :] - arrived_ref[tile(k), :])
        high, low = halves(lam)
        dof, row = split(rows_ref[tile(rows_first // SUBLANES + k), :], block_rows)
        dof = dof.astype(F32)
        row = row.astype(F32)
        left = []
        right = []
        for f in range(SUBLANES):
            here = row_of == widened(row, f, block_rows)
            left.append(
                jnp.concatenate(
                    [
                        jnp.where(here, widened(high, f, block_rows), none),
                        jnp.where(here, widened(low, f, block_rows), none),
                    ],
                    axis=0,
                )
            )
            right.append(jnp.where(dof_of == widened(dof, f, size), one, none))
        return total + lax.dot_general(
            jnp.concatenate(right, axis=1),
            jnp.concatenate(left, axis=1),
            (((1,), (1,)), ((), ())),
            preferred_element_type=F32,
        )

    total = lax.fori_loop(
        0, faces // SUBLANES, step, jnp.zeros((size, 2 * block_rows), F32), unroll=8
    )
    total = total.T
    return total[:block_rows] + total[block_rows:]


def image_kernel(
    size,
    first,
    packed_ref,
    last_ref,
    choice_ref,
    aligned_ref,
    product_ref,
    to_a_ref,
    to_b_ref,
    from_a_ref,
    from_b_ref,
    *refs,
):
    *block_refs, image_ref, weights_a_ref, weights_b_ref, side_a_ref = refs
    block_rows = product_ref.shape[0]
    faces = weights_a_ref.shape[0]
    per_group = last_ref.shape[1]
    slot = lax.axis_index("blk")
    odd = lax.rem(lax.axis_index("sub"), 2) == 1
    kept = pl.ds(pl.multiple_of(first + slot * per_group, SUBLANES), per_group)
    place = slice(faces, faces + SUBLANES)
    choice = jnp.where(odd, from_b_ref[place, :], from_a_ref[place, :])
    own, last = (
        lax.dot_general(
            one_hot(row[:1, :faces].astype(jnp.int32), faces),
            jnp.concatenate([block] + [block_ref[part, :] for block_ref in block_refs], axis=0),
            (((0,), (0,)), ((), ())),
            precision=lax.Precision.HIGHEST,
            preferred_element_type=F32,
        )
        for row, block, part in (
            (choice_ref[...], packed_ref[kept, :], slice(0, per_group)),
            (choice, last_ref[slot], slice(per_group, 2 * per_group)),
        )
    )
    weights_a_ref[...] = jnp.where(odd, own, last)
    weights_b_ref[...] = jnp.where(odd, last, own)
    image_ref[...] = product_ref[...]
    image_ref[:, :size] = (
        image_ref[:, :size]
        + spread_jumps(size, faces, aligned_ref, 0, weights_a_ref, to_a_ref, from_a_ref, block_rows)
        + spread_jumps(
            size, faces, aligned_ref, faces, weights_b_ref, to_b_ref, from_b_ref, block_rows
        )
    )
    gather_traces(image_ref[...], aligned_ref, 0, side_a_ref.at[:faces, :])
    side_a_ref[faces:, :] = jnp.zeros_like(side_a_ref[faces:, :])


def column_sums(value):
    return jnp.sum(value, axis=0, keepdims=True)


def jump_sums(weights_ref, own_ref, arrived_ref, first_ref):
    faces = slice(0, weights_ref.shape[0])
    own = own_ref[faces, :]
    lam = weights_ref[...] * (own - arrived_ref[faces, :])
    return column_sums(lam * first_ref[faces, :]), column_sums(lam * own)


def near_sums_kernel(
    product_ref, weights_ref, own_ref, arrived_ref, first_ref, field_ref, image_ref, rows_ref
):
    field = field_ref[...]
    image = image_ref[...]
    product = product_ref[...]
    with_field, with_image = jump_sums(weights_ref, own_ref, arrived_ref, first_ref)
    parts = [
        column_sums(field * field),
        column_sums(field * image),
        column_sums(image * image),
        column_sums(field * product) + with_field,
        column_sums(image * product) + with_image,
    ]
    parts += [jnp.zeros_like(parts[0])] * (SUBLANES - len(parts))
    rows_ref[...] = jnp.concatenate(parts, axis=0)


def sums_kernel(rows_ref, weights_ref, own_ref, arrived_ref, first_ref, sums_ref):
    with_field, with_image = jump_sums(weights_ref, own_ref, arrived_ref, first_ref)
    row = lax.broadcasted_iota(jnp.int32, (SUBLANES, LANES), 0)
    rows = rows_ref[...] + jnp.where(row == 3, with_field, jnp.where(row == 4, with_image, 0.0))
    lane = lax.broadcasted_iota(jnp.int32, (SUBLANES, LANES), 1)
    whole = jnp.sum(rows, axis=1, keepdims=True)
    packed = column_sums(jnp.where(lane == row, whole, 0.0))
    sums_ref[...] = jnp.broadcast_to(packed[None], sums_ref.shape)


def second_kernel(
    size,
    aligned_ref,
    product_ref,
    weights_a_ref,
    weights_b_ref,
    side_a_ref,
    side_b_ref,
    from_a_ref,
    from_b_ref,
    second_ref,
):
    block_rows = product_ref.shape[0]
    faces = weights_a_ref.shape[0]
    second_ref[...] = product_ref[...]
    second_ref[:, :size] = (
        second_ref[:, :size]
        + spread_jumps(
            size, faces, aligned_ref, 0, weights_a_ref, side_a_ref, from_a_ref, block_rows
        )
        + spread_jumps(
            size, faces, aligned_ref, faces, weights_b_ref, side_b_ref, from_b_ref, block_rows
        )
    )


def final_kernel(field_ref, image_ref, second_ref, sums_ref, solution_ref, residual_ref):
    size = solution_ref.shape[1]
    row = jnp.sum(sums_ref[...], axis=0)
    lane = lax.broadcasted_iota(jnp.int32, (1, LANES), 1)

    def entry(k):
        return jnp.sum(jnp.where(lane == k, row, 0.0), axis=1, keepdims=True)

    bb, bq, qq, bw, qw = (entry(k) for k in range(5))
    field = field_ref[:, :size]
    image = image_ref[:, :size]
    second = second_ref[:, :size]
    alpha = bb / bq
    norm = bb - alpha * (2.0 * bq - alpha * qq)
    beta = norm / bb
    grown = 1.0 + beta
    energy = grown * (grown * bq - alpha * (bw + qq)) + alpha * alpha * qw
    alpha_next = norm / energy
    residual = field - alpha * image
    direction = residual + beta * field
    moved = (image - alpha * second) + beta * image
    solution_ref[...] = alpha * field + alpha_next * direction
    residual_ref[...] = residual - alpha_next * moved


def swap(value, odd):
    count = lax.axis_size("sub")
    pairs = []
    for first in range(odd, count, 2):
        second = (first + 1) % count
        pairs += [(first, second), (second, first)]
    return lax.ppermute(value, "sub", pairs)


def from_behind(value, axis, steps):
    count = lax.axis_size(axis)
    pairs = [(source, (source + steps) % count) for source in range(count)]
    return lax.ppermute(value, axis, pairs)


def swap_slots(value, k):
    count = lax.axis_size("blk")
    return lax.ppermute(value, "blk", [(slot, slot ^ k) for slot in range(count)])


def on_device(
    right_side, stiffness, block_pairs, trace_rows, partner_face, owner_list, mortar_weight
):
    field = right_side[0, 0].T
    block_rows, size = field.shape
    blocks = stiffness[0, 0].astype(F32)
    pairs = block_pairs[0, 0]
    rows = trace_rows[0, 0]
    partner = partner_face[0, 0]
    owners = owner_list[0, 0]
    faces = partner.shape[0]
    devices = lax.axis_size("sub") * lax.axis_size("blk")

    own_weights = mortar_weight[0, 0]
    last_weights = from_behind(own_weights, "sub", 1)
    last = 2 * faces + block_rows

    def placed(value, first):
        below = last + SUBLANES + faces - first - value.shape[0]
        return jnp.pad(value, ((first, below), (0, LANES - value.shape[1])))

    indices = placed(rows, 0) + placed(partner_face[0], last) + placed(owner_list[0], last + 1)
    packed = (
        indices.astype(F32)
        + placed(field, 2 * faces)
        + placed(own_weights.reshape(faces, LANES), last + SUBLANES)
    )
    aligned, padded, choice, to_a, to_b = call(
        functools.partial(first_kernel, owners.shape[0]),
        [
            shape(2 * faces, jnp.int32),
            shape(block_rows),
            shape(SUBLANES),
            shape(faces + 2 * SUBLANES),
            shape(faces + SUBLANES),
        ],
        [(packed, VMEM)],
    )
    from_a = swap(to_a, 1)
    from_b = swap(to_b, 0)
    slots, per_group, _ = own_weights.shape
    blocks_to = call(
        functools.partial(blocks_kernel, last + SUBLANES),
        [shape(2 * per_group)] * (slots - 1),
        [(packed, VMEM), (last_weights, VMEM)],
        flops=1,
        moved=1,
    )
    blocks_from = [
        swap_slots(block, k) for k, block in zip(range(slots - 1, 0, -1), blocks_to)
    ]

    def stiff(vector):
        (product,) = call(
            functools.partial(stiffness_kernel, size),
            [shape(block_rows)],
            [(pairs, VMEM), (blocks, VMEM), (vector, VMEM)],
        )
        return product

    image, weights_a, weights_b, side_a = call(
        functools.partial(image_kernel, size, last + SUBLANES),
        [shape(block_rows), shape(faces), shape(faces), shape(faces + SUBLANES)],
        [
            (value, VMEM)
            for value in (
                packed,
                last_weights,
                choice,
                aligned,
                stiff(padded),
                to_a,
                to_b,
                from_a,
                from_b,
                *blocks_from,
            )
        ],
    )
    from_a = swap(side_a, 1)
    (side_b,) = call(
        near_traces_kernel, [shape(faces)], [(aligned, VMEM), (image, VMEM)]
    )
    from_b = swap(side_b, 0)
    product = stiff(image)
    (sums,) = call(
        near_sums_kernel,
        [shape(SUBLANES)],
        [(value, VMEM) for value in (product, weights_b, side_b, from_b, to_b, padded, image)],
        flops=1,
        moved=1,
    )
    (sums,) = call(
        sums_kernel,
        [jax.ShapeDtypeStruct((devices, 1, LANES), F32)],
        [(value, VMEM) for value in (sums, weights_a, side_a, from_a, to_a)],
    )
    (second,) = call(
        functools.partial(second_kernel, size),
        [shape(block_rows)],
        [
            (value, VMEM)
            for value in (
                aligned, product, weights_a, weights_b, side_a, side_b, from_a, from_b
            )
        ],
        flops=1_000_000_000,
    )
    sums = lax.all_to_all(sums, ("sub", "blk"), split_axis=0, concat_axis=0, tiled=True)
    solution_field, residual = call(
        final_kernel,
        [jax.ShapeDtypeStruct((block_rows, size), F32)] * 2,
        [(padded, VMEM), (image, VMEM), (second, VMEM), (sums, VMEM)],
    )
    return (solution_field.T[None, None], residual.T[None, None])


def solution(mesh):
    in_specs = (
        P("sub", "blk", None, None),
        P("sub", "blk", None, None),
        P("sub", "blk", None, None),
        P("sub", "blk", None, None),
        P("sub", "blk", None),
        P("sub", "blk", None),
        P("sub", "blk", None, None, None),
    )
    out_specs = (P("sub", "blk", None, None), P("sub", "blk", None, None))
    return jax.shard_map(
        on_device, mesh=mesh, in_specs=in_specs, out_specs=out_specs, check_vma=False
    )
```

```python
import functools
import math

import jax
import jax.numpy as jnp
from jax import lax
from jax.experimental import pallas as pl
from jax.experimental.pallas import tpu as pltpu
from jax.sharding import PartitionSpec as P

LANES = 128
SUBLANES = 8
VMEM = pl.BlockSpec(memory_space=pltpu.VMEM)
F32 = jnp.float32
BF16 = jnp.bfloat16


def call(body, outs, inputs, scratch=(), flops=1_000_000, moved=1_000_000):
    return pl.pallas_call(
        body,
        out_shape=outs,
        in_specs=[spec for _, spec in inputs],
        out_specs=[VMEM] * len(outs),
        scratch_shapes=list(scratch),
        compiler_params=pltpu.CompilerParams(vmem_limit_bytes=32 * 1024 * 1024),
        cost_estimate=pl.CostEstimate(
            flops=flops, bytes_accessed=moved, transcendentals=0
        ),
    )(*[value for value, _ in inputs])


def shape(rows, dtype=F32):
    return jax.ShapeDtypeStruct((rows, LANES), dtype)


def halves(value):
    high = value.astype(BF16).astype(F32)
    return high, value - high


def gather_traces(field, rows_ref, rows_first, target):
    block_rows = field.shape[0]
    spread = [
        jnp.broadcast_to(field[i : i + 1, :], (SUBLANES, LANES)) for i in range(block_rows)
    ]
    for k in range(target.shape[0] // SUBLANES):
        index = rows_ref[rows_first + k * SUBLANES : rows_first + (k + 1) * SUBLANES, :]
        dof, row = split(index, block_rows)
        taken = jnp.zeros((SUBLANES, LANES), F32)
        for i in range(block_rows):
            here = jnp.take_along_axis(spread[i], dof, axis=1, mode="promise_in_bounds")
            taken = jnp.where(row == i, here, taken)
        target[k * SUBLANES : (k + 1) * SUBLANES, :] = taken


def tile(k):
    return pl.ds(pl.multiple_of(k * SUBLANES, SUBLANES), SUBLANES)


def split(index, block_rows):
    if block_rows & (block_rows - 1) == 0:
        shift = block_rows.bit_length() - 1
        return index >> shift, index & (block_rows - 1)
    return lax.div(index, block_rows), lax.rem(index, block_rows)


def one_hot(place, count):
    row = lax.broadcasted_iota(jnp.int32, (count, place.shape[1]), 0)
    return jnp.where(row == place, 1.0, 0.0)


def exact_dot(left, right):
    return jnp.dot(
        left, right, precision=lax.Precision.HIGHEST, preferred_element_type=F32
    )


def block_place(k, groups):
    return jnp.where(k == 0, 0, groups - k)


def first_kernel(
    groups, packed_ref, aligned_ref, padded_ref, choice_ref, to_a_ref, to_b_ref
):
    faces = aligned_ref.shape[0] // 2
    block_rows = padded_ref.shape[0]
    per_group = faces // groups
    slot = lax.axis_index("blk")
    parity = lax.rem(lax.axis_index("sub"), 2)
    east = pl.multiple_of((1 - parity) * faces, faces)
    west = pl.multiple_of(parity * faces, faces)
    padded_ref[...] = packed_ref[2 * faces : 2 * faces + block_rows, :]
    last = 2 * faces + block_rows
    tail = packed_ref[last : last + SUBLANES, :].astype(jnp.int32)
    partner = tail[:1, :faces]
    face = lax.broadcasted_iota(jnp.int32, (1, faces), 1)
    source = jnp.zeros((1, faces), jnp.int32)
    for g in range(groups):
        inside = face - g * per_group
        source = jnp.where(
            (inside >= 0) & (inside < per_group),
            block_place(tail[1:2, g : g + 1] ^ slot, groups) * per_group + inside,
            source,
        )
    order = one_hot(partner, faces)
    aligned_ref[pl.ds(west, faces), :] = packed_ref[faces : 2 * faces, :].astype(jnp.int32)
    aligned_ref[pl.ds(east, faces), :] = exact_dot(order, packed_ref[:faces, :]).astype(jnp.int32)
    choice_ref[...] = jnp.zeros_like(choice_ref)
    choice_ref[:1, :faces] = lax.dot_general(
        source.astype(F32).astype(BF16),
        order.astype(BF16),
        (((1,), (1,)), ((), ())),
        preferred_element_type=F32,
    )
    for first, to_ref in ((0, to_a_ref), (faces, to_b_ref)):
        gather_traces(padded_ref[...], aligned_ref, first, to_ref.at[:faces, :])
        to_ref[faces : faces + SUBLANES, :] = choice_ref[...]


def blocks_kernel(first, packed_ref, last_ref, *block_refs):
    slot = lax.axis_index("blk")
    per_group = last_ref.shape[1]
    for place, block_ref in enumerate(block_refs):
        k = slot ^ (len(block_refs) - place)
        kept = pl.ds(pl.multiple_of(first + k * per_group, SUBLANES), per_group)
        block_ref[:per_group, :] = packed_ref[kept, :]
        block_ref[per_group:, :] = last_ref[k]


def near_traces_kernel(aligned_ref, image_ref, side_b_ref):
    gather_traces(image_ref[...], aligned_ref, side_b_ref.shape[0], side_b_ref)


def stiffness_kernel(size, pairs_ref, blocks_ref, field_ref, out_ref):
    block_rows = field_ref.shape[0]
    count = pairs_ref.shape[1]
    rows = block_rows + count
    width = math.lcm(size, LANES)
    tiles = width // LANES
    segments = width // size
    groups = size // segments
    batch = next(k for k in (4, 3, 2, 1) if groups % k == 0)

    def place(position):
        segment = sum(jnp.where(position >= k * size, 1, 0) for k in range(1, segments))
        return segment, position - segment * size

    def lanes_of(value, index):
        slabs = [
            jnp.take_along_axis(
                value[k : k + SUBLANES, :], index, axis=1, mode="promise_in_bounds"
            )
            for k in range(0, value.shape[0], SUBLANES)
        ]
        return jnp.concatenate(slabs, axis=0)

    field = field_ref[...]
    first_of, other_of = (one_hot(pairs_ref[k : k + 1, :], block_rows) for k in (0, 1))
    left, other = (
        lax.dot_general(
            ends,
            field,
            (((0,), (0,)), ((), ())),
            precision=lax.Precision.HIGHEST,
            preferred_element_type=F32,
        )
        for ends in (first_of, other_of)
    )
    right = jnp.concatenate([field, other], axis=0)
    lane = lax.broadcasted_iota(jnp.int32, (SUBLANES, LANES), 1)
    places = [place(lane + t * LANES) for t in range(tiles)]
    repeated = jnp.concatenate([lanes_of(right, inside) for _, inside in places], axis=1)
    segment, inside = place(lax.broadcasted_iota(jnp.int32, (width, LANES), 0))
    column = lax.broadcasted_iota(jnp.int32, (width, LANES), 1)
    add_segments = jnp.where(segment == column % segments, 1.0, 0.0).astype(BF16)
    fold = jnp.where(inside == column, 1.0, 0.0)
    dof_group = lax.broadcasted_iota(jnp.int32, (rows, LANES), 1) // segments
    total = jnp.zeros((rows, LANES), F32)
    turned = jnp.zeros((count, width), F32)
    for base in range(0, groups, batch):
        stack = []
        for g in range(base, base + batch):
            stored = blocks_ref[:, g * width : (g + 1) * width]
            product = stored * repeated
            high = product.astype(BF16)
            stack += [high, (product - high.astype(F32)).astype(BF16)]
            spread = [lanes_of(left, g * segments + segment) for segment, _ in places]
            turned = turned + stored[block_rows:] * jnp.concatenate(spread, axis=1)
        sums = jnp.dot(
            jnp.concatenate(stack, axis=0), add_segments, preferred_element_type=F32
        )
        for n in range(batch):
            both = sums[2 * n * rows : 2 * (n + 1) * rows]
            total = jnp.where(dof_group == base + n, both[:rows] + both[rows:], total)
    out_ref[...] = (
        total[:block_rows]
        + exact_dot(first_of, total[block_rows:])
        + exact_dot(other_of, exact_dot(turned, fold))
    )


def spread_jumps(size, faces, rows_ref, rows_first, weights_ref, own_ref, arrived_ref, block_rows):
    dof_of = lax.broadcasted_iota(jnp.int32, (size, LANES), 0).astype(F32).astype(BF16)
    row_of = lax.broadcasted_iota(jnp.int32, (block_rows, LANES), 0).astype(F32).astype(BF16)
    none = jnp.zeros((), BF16)
    one = jnp.ones((), BF16)

    def widened(value, f, rows):
        slab = jnp.broadcast_to(value[f : f + 1, :], (2 * SUBLANES, LANES)).astype(BF16)
        return jnp.concatenate([slab] * (rows // (2 * SUBLANES)), axis=0)

    def step(k, total):
        lam = weights_ref[tile(k), :] * (own_ref[tile(k), :] - arrived_ref[tile(k), :])
        high, low = halves(lam)
        dof, row = split(rows_ref[tile(rows_first // SUBLANES + k), :], block_rows)
        dof = dof.astype(F32)
        row = row.astype(F32)
        left = []
        right = []
        for f in range(SUBLANES):
            here = row_of == widened(row, f, block_rows)
            left.append(
                jnp.concatenate(
                    [
                        jnp.where(here, widened(high, f, block_rows), none),
                        jnp.where(here, widened(low, f, block_rows), none),
                    ],
                    axis=0,
                )
            )
            right.append(jnp.where(dof_of == widened(dof, f, size), one, none))
        return total + lax.dot_general(
            jnp.concatenate(right, axis=1),
            jnp.concatenate(left, axis=1),
            (((1,), (1,)), ((), ())),
            preferred_element_type=F32,
        )

    total = lax.fori_loop(
        0, faces // SUBLANES, step, jnp.zeros((size, 2 * block_rows), F32), unroll=8
    )
    total = total.T
    return total[:block_rows] + total[block_rows:]


def image_kernel(
    size,
    first,
    packed_ref,
    last_ref,
    choice_ref,
    aligned_ref,
    product_ref,
    to_a_ref,
    to_b_ref,
    from_a_ref,
    from_b_ref,
    *refs,
):
    *block_refs, image_ref, weights_a_ref, weights_b_ref, side_a_ref = refs
    block_rows = product_ref.shape[0]
    faces = weights_a_ref.shape[0]
    per_group = last_ref.shape[1]
    slot = lax.axis_index("blk")
    odd = lax.rem(lax.axis_index("sub"), 2) == 1
    kept = pl.ds(pl.multiple_of(first + slot * per_group, SUBLANES), per_group)
    place = slice(faces, faces + SUBLANES)
    choice = jnp.where(odd, from_b_ref[place, :], from_a_ref[place, :])
    own, last = (
        lax.dot_general(
            one_hot(row[:1, :faces].astype(jnp.int32), faces),
            jnp.concatenate([block] + [block_ref[part, :] for block_ref in block_refs], axis=0),
            (((0,), (0,)), ((), ())),
            precision=lax.Precision.HIGHEST,
            preferred_element_type=F32,
        )
        for row, block, part in (
            (choice_ref[...], packed_ref[kept, :], slice(0, per_group)),
            (choice, last_ref[slot], slice(per_group, 2 * per_group)),
        )
    )
    weights_a_ref[...] = jnp.where(odd, own, last)
    weights_b_ref[...] = jnp.where(odd, last, own)
    image_ref[...] = product_ref[...]
    image_ref[:, :size] = (
        image_ref[:, :size]
        + spread_jumps(size, faces, aligned_ref, 0, weights_a_ref, to_a_ref, from_a_ref, block_rows)
        + spread_jumps(
            size, faces, aligned_ref, faces, weights_b_ref, to_b_ref, from_b_ref, block_rows
        )
    )
    gather_traces(image_ref[...], aligned_ref, 0, side_a_ref.at[:faces, :])
    side_a_ref[faces:, :] = jnp.zeros_like(side_a_ref[faces:, :])


def column_sums(value):
    return jnp.sum(value, axis=0, keepdims=True)


def jump_sums(weights_ref, own_ref, arrived_ref, first_ref):
    faces = slice(0, weights_ref.shape[0])
    own = own_ref[faces, :]
    lam = weights_ref[...] * (own - arrived_ref[faces, :])
    return column_sums(lam * first_ref[faces, :]), column_sums(lam * own)


def near_sums_kernel(
    product_ref, weights_ref, own_ref, arrived_ref, first_ref, field_ref, image_ref, rows_ref
):
    field = field_ref[...]
    image = image_ref[...]
    product = product_ref[...]
    with_field, with_image = jump_sums(weights_ref, own_ref, arrived_ref, first_ref)
    parts = [
        column_sums(field * field),
        column_sums(field * image),
        column_sums(image * image),
        column_sums(field * product) + with_field,
        column_sums(image * product) + with_image,
    ]
    parts += [jnp.zeros_like(parts[0])] * (SUBLANES - len(parts))
    rows_ref[...] = jnp.concatenate(parts, axis=0)


def sums_kernel(rows_ref, weights_ref, own_ref, arrived_ref, first_ref, sums_ref):
    with_field, with_image = jump_sums(weights_ref, own_ref, arrived_ref, first_ref)
    row = lax.broadcasted_iota(jnp.int32, (SUBLANES, LANES), 0)
    rows = rows_ref[...] + jnp.where(row == 3, with_field, jnp.where(row == 4, with_image, 0.0))
    lane = lax.broadcasted_iota(jnp.int32, (SUBLANES, LANES), 1)
    whole = jnp.sum(rows, axis=1, keepdims=True)
    packed = column_sums(jnp.where(lane == row, whole, 0.0))
    sums_ref[...] = jnp.broadcast_to(packed[None], sums_ref.shape)


def second_kernel(
    size,
    aligned_ref,
    product_ref,
    weights_a_ref,
    weights_b_ref,
    side_a_ref,
    side_b_ref,
    from_a_ref,
    from_b_ref,
    second_ref,
):
    block_rows = product_ref.shape[0]
    faces = weights_a_ref.shape[0]
    second_ref[...] = product_ref[...]
    second_ref[:, :size] = (
        second_ref[:, :size]
        + spread_jumps(
            size, faces, aligned_ref, 0, weights_a_ref, side_a_ref, from_a_ref, block_rows
        )
        + spread_jumps(
            size, faces, aligned_ref, faces, weights_b_ref, side_b_ref, from_b_ref, block_rows
        )
    )


def final_kernel(field_ref, image_ref, second_ref, sums_ref, solution_ref, residual_ref):
    size = solution_ref.shape[1]
    row = jnp.sum(sums_ref[...], axis=0)
    lane = lax.broadcasted_iota(jnp.int32, (1, LANES), 1)

    def entry(k):
        return jnp.sum(jnp.where(lane == k, row, 0.0), axis=1, keepdims=True)

    bb, bq, qq, bw, qw = (entry(k) for k in range(5))
    field = field_ref[:, :size]
    image = image_ref[:, :size]
    second = second_ref[:, :size]
    alpha = bb / bq
    norm = bb - alpha * (2.0 * bq - alpha * qq)
    beta = norm / bb
    grown = 1.0 + beta
    energy = grown * (grown * bq - alpha * (bw + qq)) + alpha * alpha * qw
    alpha_next = norm / energy
    residual = field - alpha * image
    direction = residual + beta * field
    moved = (image - alpha * second) + beta * image
    solution_ref[...] = alpha * field + alpha_next * direction
    residual_ref[...] = residual - alpha_next * moved


def swap(value, odd):
    count = lax.axis_size("sub")
    pairs = []
    for first in range(odd, count, 2):
        second = (first + 1) % count
        pairs += [(first, second), (second, first)]
    return lax.ppermute(value, "sub", pairs)


def from_behind(value, axis, steps):
    count = lax.axis_size(axis)
    pairs = [(source, (source + steps) % count) for source in range(count)]
    return lax.ppermute(value, axis, pairs)


def swap_slots(value, k):
    count = lax.axis_size("blk")
    return lax.ppermute(value, "blk", [(slot, slot ^ k) for slot in range(count)])


def on_device(
    right_side, stiffness, block_pairs, trace_rows, partner_face, owner_list, mortar_weight
):
    field = right_side[0, 0].T
    block_rows, size = field.shape
    blocks = stiffness[0, 0].astype(F32)
    pairs = block_pairs[0, 0]
    rows = trace_rows[0, 0]
    partner = partner_face[0, 0]
    owners = owner_list[0, 0]
    faces = partner.shape[0]
    devices = lax.axis_size("sub") * lax.axis_size("blk")

    own_weights = mortar_weight[0, 0]
    last_weights = from_behind(own_weights, "sub", 1)
    last = 2 * faces + block_rows

    def placed(value, first):
        below = last + SUBLANES + faces - first - value.shape[0]
        return jnp.pad(value, ((first, below), (0, LANES - value.shape[1])))

    indices = placed(rows, 0) + placed(partner_face[0], last) + placed(owner_list[0], last + 1)
    packed = (
        indices.astype(F32)
        + placed(field, 2 * faces)
        + placed(own_weights.reshape(faces, LANES), last + SUBLANES)
    )
    aligned, padded, choice, to_a, to_b = call(
        functools.partial(first_kernel, owners.shape[0]),
        [
            shape(2 * faces, jnp.int32),
            shape(block_rows),
            shape(SUBLANES),
            shape(faces + SUBLANES),
            shape(faces + SUBLANES),
        ],
        [(packed, VMEM)],
    )
    from_a = swap(to_a, 1)
    from_b = swap(to_b, 0)
    slots, per_group, _ = own_weights.shape
    blocks_to = call(
        functools.partial(blocks_kernel, last + SUBLANES),
        [shape(2 * per_group)] * (slots - 1),
        [(packed, VMEM), (last_weights, VMEM)],
        flops=1,
        moved=1,
    )
    blocks_from = [
        swap_slots(block, k) for k, block in zip(range(slots - 1, 0, -1), blocks_to)
    ]

    def stiff(vector):
        (product,) = call(
            functools.partial(stiffness_kernel, size),
            [shape(block_rows)],
            [(pairs, VMEM), (blocks, VMEM), (vector, VMEM)],
        )
        return product

    image, weights_a, weights_b, side_a = call(
        functools.partial(image_kernel, size, last + SUBLANES),
        [shape(block_rows), shape(faces), shape(faces), shape(faces + SUBLANES)],
        [
            (value, VMEM)
            for value in (
                packed,
                last_weights,
                choice,
                aligned,
                stiff(padded),
                to_a,
                to_b,
                from_a,
                from_b,
                *blocks_from,
            )
        ],
    )
    from_a = swap(side_a, 1)
    (side_b,) = call(
        near_traces_kernel, [shape(faces)], [(aligned, VMEM), (image, VMEM)]
    )
    from_b = swap(side_b, 0)
    product = stiff(image)
    (sums,) = call(
        near_sums_kernel,
        [shape(SUBLANES)],
        [(value, VMEM) for value in (product, weights_b, side_b, from_b, to_b, padded, image)],
        flops=1,
        moved=1,
    )
    (sums,) = call(
        sums_kernel,
        [jax.ShapeDtypeStruct((devices, 1, LANES), F32)],
        [(value, VMEM) for value in (sums, weights_a, side_a, from_a, to_a)],
    )
    (second,) = call(
        functools.partial(second_kernel, size),
        [shape(block_rows)],
        [
            (value, VMEM)
            for value in (
                aligned, product, weights_a, weights_b, side_a, side_b, from_a, from_b
            )
        ],
        flops=1_000_000_000,
    )
    sums = lax.all_to_all(sums, ("sub", "blk"), split_axis=0, concat_axis=0, tiled=True)
    solution_field, residual = call(
        final_kernel,
        [jax.ShapeDtypeStruct((block_rows, size), F32)] * 2,
        [(padded, VMEM), (image, VMEM), (second, VMEM), (sums, VMEM)],
    )
    return (solution_field.T[None, None], residual.T[None, None])


def solution(mesh):
    in_specs = (
        P("sub", "blk", None, None),
        P("sub", "blk", None, None),
        P("sub", "blk", None, None),
        P("sub", "blk", None, None),
        P("sub", "blk", None),
        P("sub", "blk", None),
        P("sub", "blk", None, None, None),
    )
    out_specs = (P("sub", "blk", None, None), P("sub", "blk", None, None))
    return jax.shard_map(
        on_device, mesh=mesh, in_specs=in_specs, out_specs=out_specs, check_vma=False
    )
```

```python
import functools
import math

import jax
import jax.numpy as jnp
from jax import lax
from jax.experimental import pallas as pl
from jax.experimental.pallas import tpu as pltpu
from jax.sharding import PartitionSpec as P

LANES = 128
SUBLANES = 8
VMEM = pl.BlockSpec(memory_space=pltpu.VMEM)
F32 = jnp.float32
BF16 = jnp.bfloat16


def call(body, outs, inputs, scratch=(), flops=1_000_000, moved=1_000_000):
    return pl.pallas_call(
        body,
        out_shape=outs,
        in_specs=[spec for _, spec in inputs],
        out_specs=[VMEM] * len(outs),
        scratch_shapes=list(scratch),
        compiler_params=pltpu.CompilerParams(vmem_limit_bytes=32 * 1024 * 1024),
        cost_estimate=pl.CostEstimate(
            flops=flops, bytes_accessed=moved, transcendentals=0
        ),
    )(*[value for value, _ in inputs])


def shape(rows, dtype=F32):
    return jax.ShapeDtypeStruct((rows, LANES), dtype)


def halves(value):
    high = value.astype(BF16).astype(F32)
    return high, value - high


def gather_traces(field, rows_ref, rows_first, target):
    block_rows = field.shape[0]
    spread = [
        jnp.broadcast_to(field[i : i + 1, :], (SUBLANES, LANES)) for i in range(block_rows)
    ]
    for k in range(target.shape[0] // SUBLANES):
        index = rows_ref[rows_first + k * SUBLANES : rows_first + (k + 1) * SUBLANES, :]
        dof, row = split(index, block_rows)
        taken = jnp.zeros((SUBLANES, LANES), F32)
        for i in range(block_rows):
            here = jnp.take_along_axis(spread[i], dof, axis=1, mode="promise_in_bounds")
            taken = jnp.where(row == i, here, taken)
        target[k * SUBLANES : (k + 1) * SUBLANES, :] = taken


def tile(k):
    return pl.ds(pl.multiple_of(k * SUBLANES, SUBLANES), SUBLANES)


def split(index, block_rows):
    if block_rows & (block_rows - 1) == 0:
        shift = block_rows.bit_length() - 1
        return index >> shift, index & (block_rows - 1)
    return lax.div(index, block_rows), lax.rem(index, block_rows)


def one_hot(place, count):
    row = lax.broadcasted_iota(jnp.int32, (count, place.shape[1]), 0)
    return jnp.where(row == place, 1.0, 0.0)


def exact_dot(left, right):
    return jnp.dot(
        left, right, precision=lax.Precision.HIGHEST, preferred_element_type=F32
    )


def block_place(k, groups):
    return jnp.where(k == 0, 0, groups - k)


def first_kernel(
    groups, packed_ref, aligned_ref, padded_ref, choice_ref, east_ref, west_ref, to_a_ref, to_b_ref
):
    faces = aligned_ref.shape[0] // 2
    block_rows = padded_ref.shape[0]
    per_group = faces // groups
    slot = lax.axis_index("blk")
    odd = lax.rem(lax.axis_index("sub"), 2) == 1
    padded_ref[...] = packed_ref[2 * faces : 2 * faces + block_rows, :]
    last = 2 * faces + block_rows
    tail = packed_ref[last : last + SUBLANES, :].astype(jnp.int32)
    partner = tail[:1, :faces]
    face = lax.broadcasted_iota(jnp.int32, (1, faces), 1)
    source = jnp.zeros((1, faces), jnp.int32)
    for g in range(groups):
        inside = face - g * per_group
        source = jnp.where(
            (inside >= 0) & (inside < per_group),
            block_place(tail[1:2, g : g + 1] ^ slot, groups) * per_group + inside,
            source,
        )
    order = one_hot(partner, faces)
    aligned_ref[faces:, :] = packed_ref[faces : 2 * faces, :].astype(jnp.int32)
    aligned_ref[:faces, :] = exact_dot(order, packed_ref[:faces, :]).astype(jnp.int32)
    choice_ref[...] = jnp.zeros_like(choice_ref)
    choice_ref[:1, :faces] = lax.dot_general(
        source.astype(F32).astype(BF16),
        order.astype(BF16),
        (((1,), (1,)), ((), ())),
        preferred_element_type=F32,
    )
    gather_traces(padded_ref[...], aligned_ref, 0, east_ref)
    gather_traces(padded_ref[...], aligned_ref, faces, west_ref)
    east = east_ref[...]
    west = west_ref[...]
    to_a_ref[:faces, :] = jnp.where(odd, east, west)
    to_b_ref[:faces, :] = jnp.where(odd, west, east)
    for to_ref in (to_a_ref, to_b_ref):
        to_ref[faces:, :] = choice_ref[...]


def blocks_kernel(first, packed_ref, last_ref, *block_refs):
    slot = lax.axis_index("blk")
    per_group = last_ref.shape[1]
    for place, block_ref in enumerate(block_refs):
        k = slot ^ (len(block_refs) - place)
        kept = pl.ds(pl.multiple_of(first + k * per_group, SUBLANES), per_group)
        block_ref[:per_group, :] = packed_ref[kept, :]
        block_ref[per_group:, :] = last_ref[k]


def west_traces_kernel(aligned_ref, image_ref, west_ref):
    gather_traces(image_ref[...], aligned_ref, west_ref.shape[0], west_ref)


def stiffness_kernel(size, pairs_ref, blocks_ref, field_ref, out_ref):
    block_rows = field_ref.shape[0]
    count = pairs_ref.shape[1]
    rows = block_rows + count
    width = math.lcm(size, LANES)
    tiles = width // LANES
    segments = width // size
    groups = size // segments
    batch = next(k for k in (4, 3, 2, 1) if groups % k == 0)

    def place(position):
        segment = sum(jnp.where(position >= k * size, 1, 0) for k in range(1, segments))
        return segment, position - segment * size

    def lanes_of(value, index):
        slabs = [
            jnp.take_along_axis(
                value[k : k + SUBLANES, :], index, axis=1, mode="promise_in_bounds"
            )
            for k in range(0, value.shape[0], SUBLANES)
        ]
        return jnp.concatenate(slabs, axis=0)

    field = field_ref[...]
    first_of, other_of = (one_hot(pairs_ref[k : k + 1, :], block_rows) for k in (0, 1))
    left, other = (
        lax.dot_general(
            ends,
            field,
            (((0,), (0,)), ((), ())),
            precision=lax.Precision.HIGHEST,
            preferred_element_type=F32,
        )
        for ends in (first_of, other_of)
    )
    right = jnp.concatenate([field, other], axis=0)
    lane = lax.broadcasted_iota(jnp.int32, (SUBLANES, LANES), 1)
    places = [place(lane + t * LANES) for t in range(tiles)]
    repeated = jnp.concatenate([lanes_of(right, inside) for _, inside in places], axis=1)
    segment, inside = place(lax.broadcasted_iota(jnp.int32, (width, LANES), 0))
    column = lax.broadcasted_iota(jnp.int32, (width, LANES), 1)
    add_segments = jnp.where(segment == column % segments, 1.0, 0.0).astype(BF16)
    fold = jnp.where(inside == column, 1.0, 0.0)
    dof_group = lax.broadcasted_iota(jnp.int32, (rows, LANES), 1) // segments
    total = jnp.zeros((rows, LANES), F32)
    turned = jnp.zeros((count, width), F32)
    for base in range(0, groups, batch):
        stack = []
        for g in range(base, base + batch):
            stored = blocks_ref[:, g * width : (g + 1) * width]
            product = stored * repeated
            high = product.astype(BF16)
            stack += [high, (product - high.astype(F32)).astype(BF16)]
            spread = [lanes_of(left, g * segments + segment) for segment, _ in places]
            turned = turned + stored[block_rows:] * jnp.concatenate(spread, axis=1)
        sums = jnp.dot(
            jnp.concatenate(stack, axis=0), add_segments, preferred_element_type=F32
        )
        for n in range(batch):
            both = sums[2 * n * rows : 2 * (n + 1) * rows]
            total = jnp.where(dof_group == base + n, both[:rows] + both[rows:], total)
    out_ref[...] = (
        total[:block_rows]
        + exact_dot(first_of, total[block_rows:])
        + exact_dot(other_of, exact_dot(turned, fold))
    )


def spread_jumps(size, rows_ref, rows_first, weighted, block_rows):
    dof_of = lax.broadcasted_iota(jnp.int32, (size, LANES), 0).astype(F32).astype(BF16)
    row_of = lax.broadcasted_iota(jnp.int32, (block_rows, LANES), 0).astype(F32).astype(BF16)
    none = jnp.zeros((), BF16)
    one = jnp.ones((), BF16)

    def widened(value, f, rows):
        slab = jnp.broadcast_to(value[f : f + 1, :], (2 * SUBLANES, LANES)).astype(BF16)
        return jnp.concatenate([slab] * (rows // (2 * SUBLANES)), axis=0)

    total = jnp.zeros((size, 2 * block_rows), F32)
    for k in range(0, weighted.shape[0], SUBLANES):
        high, low = halves(weighted[k : k + SUBLANES])
        dof, row = split(rows_ref[rows_first + k : rows_first + k + SUBLANES, :], block_rows)
        dof = dof.astype(F32)
        row = row.astype(F32)
        left = []
        right = []
        for f in range(SUBLANES):
            here = row_of == widened(row, f, block_rows)
            left.append(
                jnp.concatenate(
                    [
                        jnp.where(here, widened(high, f, block_rows), none),
                        jnp.where(here, widened(low, f, block_rows), none),
                    ],
                    axis=0,
                )
            )
            right.append(jnp.where(dof_of == widened(dof, f, size), one, none))
        total = total + lax.dot_general(
            jnp.concatenate(right, axis=1),
            jnp.concatenate(left, axis=1),
            (((1,), (1,)), ((), ())),
            preferred_element_type=F32,
        )
    total = total.T
    return total[:block_rows] + total[block_rows:]


def image_kernel(
    size,
    first,
    packed_ref,
    last_ref,
    choice_ref,
    aligned_ref,
    product_ref,
    east_ref,
    west_ref,
    from_a_ref,
    from_b_ref,
    *refs,
):
    *block_refs, image_ref, weights_east_ref, weights_west_ref, jump_ref, next_east_ref = refs
    block_rows = product_ref.shape[0]
    faces = weights_east_ref.shape[0]
    per_group = last_ref.shape[1]
    slot = lax.axis_index("blk")
    odd = lax.rem(lax.axis_index("sub"), 2) == 1
    kept = pl.ds(pl.multiple_of(first + slot * per_group, SUBLANES), per_group)
    from_west = jnp.where(odd, from_b_ref[...], from_a_ref[...])
    from_east = jnp.where(odd, from_a_ref[:faces, :], from_b_ref[:faces, :])
    for row, block, part, weights_ref in (
        (choice_ref[...], packed_ref[kept, :], slice(0, per_group), weights_east_ref),
        (from_west[faces:], last_ref[slot], slice(per_group, 2 * per_group), weights_west_ref),
    ):
        weights_ref[...] = lax.dot_general(
            one_hot(row[:1, :faces].astype(jnp.int32), faces),
            jnp.concatenate([block] + [block_ref[part, :] for block_ref in block_refs], axis=0),
            (((0,), (0,)), ((), ())),
            precision=lax.Precision.HIGHEST,
            preferred_element_type=F32,
        )
    jump_ref[...] = west_ref[...] - from_west[:faces]
    image_ref[...] = product_ref[...]
    image_ref[:, :size] = (
        image_ref[:, :size]
        + spread_jumps(
            size, aligned_ref, 0, weights_east_ref[...] * (east_ref[...] - from_east), block_rows
        )
        + spread_jumps(
            size, aligned_ref, faces, weights_west_ref[...] * jump_ref[...], block_rows
        )
    )
    gather_traces(image_ref[...], aligned_ref, 0, next_east_ref.at[:faces, :])
    next_east_ref[faces:, :] = jnp.zeros_like(next_east_ref[faces:, :])


def column_sums(value):
    return jnp.sum(value, axis=0, keepdims=True)


def sums_kernel(
    product_ref, weights_ref, own_ref, arrived_ref, jump_ref, field_ref, image_ref, sums_ref
):
    field = field_ref[...]
    image = image_ref[...]
    product = product_ref[...]
    jump = own_ref[...] - arrived_ref[: own_ref.shape[0], :]
    lam = weights_ref[...] * jump
    parts = [
        column_sums(field * field),
        column_sums(field * image),
        column_sums(image * image),
        column_sums(field * product) + column_sums(lam * jump_ref[...]),
        column_sums(image * product) + column_sums(lam * jump),
    ]
    parts += [jnp.zeros_like(parts[0])] * (SUBLANES - len(parts))
    whole = jnp.sum(jnp.concatenate(parts, axis=0), axis=1, keepdims=True)
    row = lax.broadcasted_iota(jnp.int32, (SUBLANES, LANES), 0)
    lane = lax.broadcasted_iota(jnp.int32, (SUBLANES, LANES), 1)
    packed = column_sums(jnp.where(lane == row, whole, 0.0))
    sums_ref[...] = jnp.broadcast_to(packed[None], sums_ref.shape)


def second_kernel(
    size,
    aligned_ref,
    product_ref,
    weights_east_ref,
    weights_west_ref,
    east_ref,
    west_ref,
    from_next_ref,
    from_last_ref,
    second_ref,
):
    block_rows = product_ref.shape[0]
    faces = west_ref.shape[0]
    second_ref[...] = product_ref[...]
    coupled = [
        spread_jumps(
            size,
            aligned_ref,
            first,
            weights_ref[...] * (own_ref[:faces, :] - arrived_ref[:faces, :]),
            block_rows,
        )
        for first, weights_ref, own_ref, arrived_ref in (
            (0, weights_east_ref, east_ref, from_next_ref),
            (faces, weights_west_ref, west_ref, from_last_ref),
        )
    ]
    second_ref[:, :size] = second_ref[:, :size] + (coupled[0] + coupled[1])


def final_kernel(field_ref, image_ref, second_ref, sums_ref, solution_ref, residual_ref):
    size = solution_ref.shape[1]
    row = jnp.sum(sums_ref[...], axis=0)
    lane = lax.broadcasted_iota(jnp.int32, (1, LANES), 1)

    def entry(k):
        return jnp.sum(jnp.where(lane == k, row, 0.0), axis=1, keepdims=True)

    bb, bq, qq, bw, qw = (entry(k) for k in range(5))
    field = field_ref[:, :size]
    image = image_ref[:, :size]
    second = second_ref[:, :size]
    alpha = bb / bq
    norm = bb - alpha * (2.0 * bq - alpha * qq)
    beta = norm / bb
    grown = 1.0 + beta
    energy = grown * (grown * bq - alpha * (bw + qq)) + alpha * alpha * qw
    alpha_next = norm / energy
    residual = field - alpha * image
    direction = residual + beta * field
    moved = (image - alpha * second) + beta * image
    solution_ref[...] = alpha * field + alpha_next * direction
    residual_ref[...] = residual - alpha_next * moved


def swap(value, odd):
    count = lax.axis_size("sub")
    pairs = []
    for first in range(odd, count, 2):
        second = (first + 1) % count
        pairs += [(first, second), (second, first)]
    return lax.ppermute(value, "sub", pairs)


def from_behind(value, axis, steps):
    count = lax.axis_size(axis)
    pairs = [(source, (source + steps) % count) for source in range(count)]
    return lax.ppermute(value, axis, pairs)


def swap_slots(value, k):
    count = lax.axis_size("blk")
    return lax.ppermute(value, "blk", [(slot, slot ^ k) for slot in range(count)])


def on_device(
    right_side, stiffness, block_pairs, trace_rows, partner_face, owner_list, mortar_weight
):
    field = right_side[0, 0].T
    block_rows, size = field.shape
    blocks = stiffness[0, 0].astype(F32)
    pairs = block_pairs[0, 0]
    rows = trace_rows[0, 0]
    partner = partner_face[0, 0]
    owners = owner_list[0, 0]
    faces = partner.shape[0]
    devices = lax.axis_size("sub") * lax.axis_size("blk")

    own_weights = mortar_weight[0, 0]
    last_weights = from_behind(own_weights, "sub", 1)
    last = 2 * faces + block_rows

    def placed(value, first):
        below = last + SUBLANES + faces - first - value.shape[0]
        return jnp.pad(value, ((first, below), (0, LANES - value.shape[1])))

    indices = placed(rows, 0) + placed(partner_face[0], last) + placed(owner_list[0], last + 1)
    packed = (
        indices.astype(F32)
        + placed(field, 2 * faces)
        + placed(own_weights.reshape(faces, LANES), last + SUBLANES)
    )
    aligned, padded, choice, east, west, to_a, to_b = call(
        functools.partial(first_kernel, owners.shape[0]),
        [
            shape(2 * faces, jnp.int32),
            shape(block_rows),
            shape(SUBLANES),
            shape(faces),
            shape(faces),
            shape(faces + SUBLANES),
            shape(faces + SUBLANES),
        ],
        [(packed, VMEM)],
    )
    from_a = swap(to_a, 1)
    from_b = swap(to_b, 0)
    slots, per_group, _ = own_weights.shape
    blocks_to = call(
        functools.partial(blocks_kernel, last + SUBLANES),
        [shape(2 * per_group)] * (slots - 1),
        [(packed, VMEM), (last_weights, VMEM)],
        flops=1,
        moved=1,
    )
    blocks_from = [
        swap_slots(block, k) for k, block in zip(range(slots - 1, 0, -1), blocks_to)
    ]

    def stiff(vector):
        (product,) = call(
            functools.partial(stiffness_kernel, size),
            [shape(block_rows)],
            [(pairs, VMEM), (blocks, VMEM), (vector, VMEM)],
        )
        return product

    image, weights_east, weights_west, jump, east = call(
        functools.partial(image_kernel, size, last + SUBLANES),
        [shape(block_rows)] + [shape(faces)] * 3 + [shape(faces + SUBLANES)],
        [
            (value, VMEM)
            for value in (
                packed,
                last_weights,
                choice,
                aligned,
                stiff(padded),
                east,
                west,
                from_a,
                from_b,
                *blocks_from,
            )
        ],
    )
    from_last = from_behind(east, "sub", 1)
    (west,) = call(west_traces_kernel, [shape(faces)], [(aligned, VMEM), (image, VMEM)])
    from_next = from_behind(west, "sub", -1)
    product = stiff(image)
    (sums,) = call(
        sums_kernel,
        [jax.ShapeDtypeStruct((devices, 1, LANES), F32)],
        [
            (value, VMEM)
            for value in (product, weights_west, west, from_last, jump, padded, image)
        ],
    )
    (second,) = call(
        functools.partial(second_kernel, size),
        [shape(block_rows)],
        [
            (value, VMEM)
            for value in (
                aligned, product, weights_east, weights_west, east, west, from_next, from_last
            )
        ],
        flops=1_000_000_000,
    )
    sums = lax.all_to_all(sums, ("sub", "blk"), split_axis=0, concat_axis=0, tiled=True)
    solution_field, residual = call(
        final_kernel,
        [jax.ShapeDtypeStruct((block_rows, size), F32)] * 2,
        [(padded, VMEM), (image, VMEM), (second, VMEM), (sums, VMEM)],
    )
    return (solution_field.T[None, None], residual.T[None, None])


def solution(mesh):
    in_specs = (
        P("sub", "blk", None, None),
        P("sub", "blk", None, None),
        P("sub", "blk", None, None),
        P("sub", "blk", None, None),
        P("sub", "blk", None),
        P("sub", "blk", None),
        P("sub", "blk", None, None, None),
    )
    out_specs = (P("sub", "blk", None, None), P("sub", "blk", None, None))
    return jax.shard_map(
        on_device, mesh=mesh, in_specs=in_specs, out_specs=out_specs, check_vma=False
    )
```

```python
import functools
import math

import jax
import jax.numpy as jnp
from jax import lax
from jax.experimental import pallas as pl
from jax.experimental.pallas import tpu as pltpu
from jax.sharding import PartitionSpec as P

LANES = 128
SUBLANES = 8
VMEM = pl.BlockSpec(memory_space=pltpu.VMEM)
F32 = jnp.float32
BF16 = jnp.bfloat16


def call(body, outs, inputs, scratch=(), flops=1_000_000, moved=1_000_000):
    return pl.pallas_call(
        body,
        out_shape=outs,
        in_specs=[spec for _, spec in inputs],
        out_specs=[VMEM] * len(outs),
        scratch_shapes=list(scratch),
        compiler_params=pltpu.CompilerParams(vmem_limit_bytes=32 * 1024 * 1024),
        cost_estimate=pl.CostEstimate(
            flops=flops, bytes_accessed=moved, transcendentals=0
        ),
    )(*[value for value, _ in inputs])


def shape(rows, dtype=F32):
    return jax.ShapeDtypeStruct((rows, LANES), dtype)


def halves(value):
    high = value.astype(BF16).astype(F32)
    return high, value - high


def gather_traces(field, rows_ref, rows_first, target):
    block_rows = field.shape[0]
    spread = [
        jnp.broadcast_to(field[i : i + 1, :], (SUBLANES, LANES)) for i in range(block_rows)
    ]
    for k in range(target.shape[0] // SUBLANES):
        index = rows_ref[rows_first + k * SUBLANES : rows_first + (k + 1) * SUBLANES, :]
        dof, row = split(index, block_rows)
        taken = jnp.zeros((SUBLANES, LANES), F32)
        for i in range(block_rows):
            here = jnp.take_along_axis(spread[i], dof, axis=1, mode="promise_in_bounds")
            taken = jnp.where(row == i, here, taken)
        target[k * SUBLANES : (k + 1) * SUBLANES, :] = taken


def tile(k):
    return pl.ds(pl.multiple_of(k * SUBLANES, SUBLANES), SUBLANES)


def split(index, block_rows):
    if block_rows & (block_rows - 1) == 0:
        shift = block_rows.bit_length() - 1
        return index >> shift, index & (block_rows - 1)
    return lax.div(index, block_rows), lax.rem(index, block_rows)


def one_hot(place, count):
    row = lax.broadcasted_iota(jnp.int32, (count, place.shape[1]), 0)
    return jnp.where(row == place, 1.0, 0.0)


def exact_dot(left, right):
    return jnp.dot(
        left, right, precision=lax.Precision.HIGHEST, preferred_element_type=F32
    )


def block_place(k, groups):
    return jnp.where(k == 0, 0, groups - k)


def first_kernel(
    groups, packed_ref, aligned_ref, padded_ref, choice_ref, east_ref, west_ref, to_a_ref, to_b_ref
):
    faces = aligned_ref.shape[0] // 2
    block_rows = padded_ref.shape[0]
    per_group = faces // groups
    slot = lax.axis_index("blk")
    odd = lax.rem(lax.axis_index("sub"), 2) == 1
    padded_ref[...] = packed_ref[2 * faces : 2 * faces + block_rows, :]
    last = 2 * faces + block_rows
    tail = packed_ref[last : last + SUBLANES, :].astype(jnp.int32)
    partner = tail[:1, :faces]
    face = lax.broadcasted_iota(jnp.int32, (1, faces), 1)
    source = jnp.zeros((1, faces), jnp.int32)
    for g in range(groups):
        inside = face - g * per_group
        source = jnp.where(
            (inside >= 0) & (inside < per_group),
            block_place(tail[1:2, g : g + 1] ^ slot, groups) * per_group + inside,
            source,
        )
    order = one_hot(partner, faces)
    aligned_ref[faces:, :] = packed_ref[faces : 2 * faces, :].astype(jnp.int32)
    aligned_ref[:faces, :] = exact_dot(order, packed_ref[:faces, :]).astype(jnp.int32)
    choice_ref[...] = jnp.zeros_like(choice_ref)
    choice_ref[:1, :faces] = lax.dot_general(
        source.astype(F32).astype(BF16),
        order.astype(BF16),
        (((1,), (1,)), ((), ())),
        preferred_element_type=F32,
    )
    gather_traces(padded_ref[...], aligned_ref, 0, east_ref)
    gather_traces(padded_ref[...], aligned_ref, faces, west_ref)
    east = east_ref[...]
    west = west_ref[...]
    to_a_ref[:faces, :] = jnp.where(odd, east, west)
    to_b_ref[:faces, :] = jnp.where(odd, west, east)
    for to_ref in (to_a_ref, to_b_ref):
        to_ref[faces:, :] = choice_ref[...]


def blocks_kernel(first, packed_ref, last_ref, *block_refs):
    slot = lax.axis_index("blk")
    per_group = last_ref.shape[1]
    for place, block_ref in enumerate(block_refs):
        k = slot ^ (len(block_refs) - place)
        kept = pl.ds(pl.multiple_of(first + k * per_group, SUBLANES), per_group)
        block_ref[:per_group, :] = packed_ref[kept, :]
        block_ref[per_group:, :] = last_ref[k]


def west_traces_kernel(aligned_ref, image_ref, west_ref):
    gather_traces(image_ref[...], aligned_ref, west_ref.shape[0], west_ref)


def stiffness_kernel(size, pairs_ref, blocks_ref, field_ref, out_ref):
    block_rows = field_ref.shape[0]
    count = pairs_ref.shape[1]
    rows = block_rows + count
    width = math.lcm(size, LANES)
    tiles = width // LANES
    segments = width // size
    groups = size // segments
    batch = next(k for k in (4, 3, 2, 1) if groups % k == 0)

    def place(position):
        segment = sum(jnp.where(position >= k * size, 1, 0) for k in range(1, segments))
        return segment, position - segment * size

    def lanes_of(value, index):
        slabs = [
            jnp.take_along_axis(
                value[k : k + SUBLANES, :], index, axis=1, mode="promise_in_bounds"
            )
            for k in range(0, value.shape[0], SUBLANES)
        ]
        return jnp.concatenate(slabs, axis=0)

    field = field_ref[...]
    first_of, other_of = (one_hot(pairs_ref[k : k + 1, :], block_rows) for k in (0, 1))
    left, other = (
        lax.dot_general(
            ends,
            field,
            (((0,), (0,)), ((), ())),
            precision=lax.Precision.HIGHEST,
            preferred_element_type=F32,
        )
        for ends in (first_of, other_of)
    )
    right = jnp.concatenate([field, other], axis=0)
    lane = lax.broadcasted_iota(jnp.int32, (SUBLANES, LANES), 1)
    places = [place(lane + t * LANES) for t in range(tiles)]
    repeated = jnp.concatenate([lanes_of(right, inside) for _, inside in places], axis=1)
    segment, inside = place(lax.broadcasted_iota(jnp.int32, (width, LANES), 0))
    column = lax.broadcasted_iota(jnp.int32, (width, LANES), 1)
    add_segments = jnp.where(segment == column % segments, 1.0, 0.0).astype(BF16)
    fold = jnp.where(inside == column, 1.0, 0.0)
    dof_group = lax.broadcasted_iota(jnp.int32, (rows, LANES), 1) // segments
    total = jnp.zeros((rows, LANES), F32)
    turned = jnp.zeros((count, width), F32)
    for base in range(0, groups, batch):
        stack = []
        for g in range(base, base + batch):
            stored = blocks_ref[:, g * width : (g + 1) * width]
            product = stored * repeated
            high = product.astype(BF16)
            stack += [high, (product - high.astype(F32)).astype(BF16)]
            spread = [lanes_of(left, g * segments + segment) for segment, _ in places]
            turned = turned + stored[block_rows:] * jnp.concatenate(spread, axis=1)
        sums = jnp.dot(
            jnp.concatenate(stack, axis=0), add_segments, preferred_element_type=F32
        )
        for n in range(batch):
            both = sums[2 * n * rows : 2 * (n + 1) * rows]
            total = jnp.where(dof_group == base + n, both[:rows] + both[rows:], total)
    out_ref[...] = (
        total[:block_rows]
        + exact_dot(first_of, total[block_rows:])
        + exact_dot(other_of, exact_dot(turned, fold))
    )


def spread_jumps(size, rows_ref, sides, block_rows):
    dof_of = lax.broadcasted_iota(jnp.int32, (size, LANES), 0).astype(F32).astype(BF16)
    row_of = lax.broadcasted_iota(jnp.int32, (block_rows, LANES), 0).astype(F32).astype(BF16)
    none = jnp.zeros((), BF16)
    one = jnp.ones((), BF16)

    def widened(value, f, rows):
        slab = jnp.broadcast_to(value[f : f + 1, :], (2 * SUBLANES, LANES)).astype(BF16)
        return jnp.concatenate([slab] * (rows // (2 * SUBLANES)), axis=0)

    total = jnp.zeros((size, 2 * block_rows), F32)
    for side, weighted in enumerate(sides):
        for k in range(0, weighted.shape[0], SUBLANES):
            high, low = halves(weighted[k : k + SUBLANES])
            first = side * weighted.shape[0] + k
            dof, row = split(rows_ref[first : first + SUBLANES, :], block_rows)
            dof = dof.astype(F32)
            row = row.astype(F32)
            left = []
            right = []
            for f in range(SUBLANES):
                here = row_of == widened(row, f, block_rows)
                left.append(
                    jnp.concatenate(
                        [
                            jnp.where(here, widened(high, f, block_rows), none),
                            jnp.where(here, widened(low, f, block_rows), none),
                        ],
                        axis=0,
                    )
                )
                right.append(jnp.where(dof_of == widened(dof, f, size), one, none))
            total = total + lax.dot_general(
                jnp.concatenate(right, axis=1),
                jnp.concatenate(left, axis=1),
                (((1,), (1,)), ((), ())),
                preferred_element_type=F32,
            )
    total = total.T
    return total[:block_rows] + total[block_rows:]


def pick_rows(choice, value):
    high, rest = halves(value)
    middle, low = halves(rest)
    pieces = jnp.concatenate([high, middle, low], axis=1).astype(BF16)
    picked = lax.dot_general(
        one_hot(choice, value.shape[0]).astype(BF16),
        pieces,
        (((0,), (0,)), ((), ())),
        preferred_element_type=F32,
    )
    return (
        picked[:, :LANES] + picked[:, LANES : 2 * LANES]
    ) + picked[:, 2 * LANES :]


def image_kernel(
    size,
    first,
    packed_ref,
    last_ref,
    choice_ref,
    aligned_ref,
    product_ref,
    east_ref,
    west_ref,
    from_a_ref,
    from_b_ref,
    *refs,
):
    *block_refs, image_ref, weights_east_ref, weights_west_ref, jump_ref, next_east_ref = refs
    block_rows = product_ref.shape[0]
    faces = weights_east_ref.shape[0]
    per_group = last_ref.shape[1]
    slot = lax.axis_index("blk")
    odd = lax.rem(lax.axis_index("sub"), 2) == 1
    kept = pl.ds(pl.multiple_of(first + slot * per_group, SUBLANES), per_group)
    from_west = jnp.where(odd, from_b_ref[...], from_a_ref[...])
    from_east = jnp.where(odd, from_a_ref[:faces, :], from_b_ref[:faces, :])
    for row, block, part, weights_ref in (
        (choice_ref[...], packed_ref[kept, :], slice(0, per_group), weights_east_ref),
        (from_west[faces:], last_ref[slot], slice(per_group, 2 * per_group), weights_west_ref),
    ):
        weights_ref[...] = pick_rows(
            row[:1, :faces].astype(jnp.int32),
            jnp.concatenate([block] + [block_ref[part, :] for block_ref in block_refs], axis=0),
        )
    jump_ref[...] = west_ref[...] - from_west[:faces]
    image_ref[...] = product_ref[...]
    image_ref[:, :size] = image_ref[:, :size] + spread_jumps(
        size,
        aligned_ref,
        (
            weights_east_ref[...] * (east_ref[...] - from_east),
            weights_west_ref[...] * jump_ref[...],
        ),
        block_rows,
    )
    gather_traces(image_ref[...], aligned_ref, 0, next_east_ref.at[:faces, :])
    next_east_ref[faces:, :] = jnp.zeros_like(next_east_ref[faces:, :])


def column_sums(value):
    return jnp.sum(value, axis=0, keepdims=True)


def sums_kernel(
    product_ref, weights_ref, own_ref, arrived_ref, jump_ref, field_ref, image_ref, sums_ref
):
    field = field_ref[...]
    image = image_ref[...]
    product = product_ref[...]
    jump = own_ref[...] - arrived_ref[: own_ref.shape[0], :]
    lam = weights_ref[...] * jump
    parts = [
        column_sums(field * field),
        column_sums(field * image),
        column_sums(image * image),
        column_sums(field * product) + column_sums(lam * jump_ref[...]),
        column_sums(image * product) + column_sums(lam * jump),
    ]
    parts += [jnp.zeros_like(parts[0])] * (SUBLANES - len(parts))
    whole = jnp.sum(jnp.concatenate(parts, axis=0), axis=1, keepdims=True)
    row = lax.broadcasted_iota(jnp.int32, (SUBLANES, LANES), 0)
    lane = lax.broadcasted_iota(jnp.int32, (SUBLANES, LANES), 1)
    packed = column_sums(jnp.where(lane == row, whole, 0.0))
    sums_ref[...] = jnp.broadcast_to(packed[None], sums_ref.shape)


def second_kernel(
    size,
    aligned_ref,
    product_ref,
    weights_east_ref,
    weights_west_ref,
    east_ref,
    west_ref,
    from_next_ref,
    from_last_ref,
    second_ref,
):
    block_rows = product_ref.shape[0]
    faces = west_ref.shape[0]
    second_ref[...] = product_ref[...]
    second_ref[:, :size] = second_ref[:, :size] + spread_jumps(
        size,
        aligned_ref,
        [
            weights_ref[...] * (own_ref[:faces, :] - arrived_ref[:faces, :])
            for weights_ref, own_ref, arrived_ref in (
                (weights_east_ref, east_ref, from_next_ref),
                (weights_west_ref, west_ref, from_last_ref),
            )
        ],
        block_rows,
    )


def final_kernel(field_ref, image_ref, second_ref, sums_ref, solution_ref, residual_ref):
    size = solution_ref.shape[1]
    row = jnp.sum(sums_ref[...], axis=0)
    lane = lax.broadcasted_iota(jnp.int32, (1, LANES), 1)

    def entry(k):
        return jnp.sum(jnp.where(lane == k, row, 0.0), axis=1, keepdims=True)

    bb, bq, qq, bw, qw = (entry(k) for k in range(5))
    field = field_ref[:, :size]
    image = image_ref[:, :size]
    second = second_ref[:, :size]
    alpha = bb / bq
    norm = bb - alpha * (2.0 * bq - alpha * qq)
    beta = norm / bb
    grown = 1.0 + beta
    energy = grown * (grown * bq - alpha * (bw + qq)) + alpha * alpha * qw
    alpha_next = norm / energy
    residual = field - alpha * image
    direction = residual + beta * field
    moved = (image - alpha * second) + beta * image
    solution_ref[...] = alpha * field + alpha_next * direction
    residual_ref[...] = residual - alpha_next * moved


def swap(value, odd):
    count = lax.axis_size("sub")
    pairs = []
    for first in range(odd, count, 2):
        second = (first + 1) % count
        pairs += [(first, second), (second, first)]
    return lax.ppermute(value, "sub", pairs)


def from_behind(value, axis, steps):
    count = lax.axis_size(axis)
    pairs = [(source, (source + steps) % count) for source in range(count)]
    return lax.ppermute(value, axis, pairs)


def swap_slots(value, k):
    count = lax.axis_size("blk")
    return lax.ppermute(value, "blk", [(slot, slot ^ k) for slot in range(count)])


def on_device(
    right_side, stiffness, block_pairs, trace_rows, partner_face, owner_list, mortar_weight
):
    field = right_side[0, 0].T
    block_rows, size = field.shape
    blocks = stiffness[0, 0].astype(F32)
    pairs = block_pairs[0, 0]
    rows = trace_rows[0, 0]
    partner = partner_face[0, 0]
    owners = owner_list[0, 0]
    faces = partner.shape[0]
    devices = lax.axis_size("sub") * lax.axis_size("blk")

    own_weights = mortar_weight[0, 0]
    last_weights = from_behind(own_weights, "sub", 1)
    last = 2 * faces + block_rows

    def placed(value, first):
        below = last + SUBLANES + faces - first - value.shape[0]
        return jnp.pad(value, ((first, below), (0, LANES - value.shape[1])))

    indices = placed(rows, 0) + placed(partner_face[0], last) + placed(owner_list[0], last + 1)
    packed = (
        indices.astype(F32)
        + placed(field, 2 * faces)
        + placed(own_weights.reshape(faces, LANES), last + SUBLANES)
    )
    aligned, padded, choice, east, west, to_a, to_b = call(
        functools.partial(first_kernel, owners.shape[0]),
        [
            shape(2 * faces, jnp.int32),
            shape(block_rows),
            shape(SUBLANES),
            shape(faces),
            shape(faces),
            shape(faces + SUBLANES),
            shape(faces + SUBLANES),
        ],
        [(packed, VMEM)],
    )
    from_a = swap(to_a, 1)
    from_b = swap(to_b, 0)
    slots, per_group, _ = own_weights.shape
    blocks_to = call(
        functools.partial(blocks_kernel, last + SUBLANES),
        [shape(2 * per_group)] * (slots - 1),
        [(packed, VMEM), (last_weights, VMEM)],
        flops=1,
        moved=1,
    )
    blocks_from = [
        swap_slots(block, k) for k, block in zip(range(slots - 1, 0, -1), blocks_to)
    ]

    def stiff(vector):
        (product,) = call(
            functools.partial(stiffness_kernel, size),
            [shape(block_rows)],
            [(pairs, VMEM), (blocks, VMEM), (vector, VMEM)],
        )
        return product

    image, weights_east, weights_west, jump, east = call(
        functools.partial(image_kernel, size, last + SUBLANES),
        [shape(block_rows)] + [shape(faces)] * 3 + [shape(faces + SUBLANES)],
        [
            (value, VMEM)
            for value in (
                packed,
                last_weights,
                choice,
                aligned,
                stiff(padded),
                east,
                west,
                from_a,
                from_b,
                *blocks_from,
            )
        ],
    )
    from_last = from_behind(east, "sub", 1)
    (west,) = call(west_traces_kernel, [shape(faces)], [(aligned, VMEM), (image, VMEM)])
    from_next = from_behind(west, "sub", -1)
    product = stiff(image)
    (sums,) = call(
        sums_kernel,
        [jax.ShapeDtypeStruct((devices, 1, LANES), F32)],
        [
            (value, VMEM)
            for value in (product, weights_west, west, from_last, jump, padded, image)
        ],
    )
    (second,) = call(
        functools.partial(second_kernel, size),
        [shape(block_rows)],
        [
            (value, VMEM)
            for value in (
                aligned, product, weights_east, weights_west, east, west, from_next, from_last
            )
        ],
        flops=1_000_000_000,
    )
    sums = lax.all_to_all(sums, ("sub", "blk"), split_axis=0, concat_axis=0, tiled=True)
    solution_field, residual = call(
        final_kernel,
        [jax.ShapeDtypeStruct((block_rows, size), F32)] * 2,
        [(padded, VMEM), (image, VMEM), (second, VMEM), (sums, VMEM)],
    )
    return (solution_field.T[None, None], residual.T[None, None])


def solution(mesh):
    in_specs = (
        P("sub", "blk", None, None),
        P("sub", "blk", None, None),
        P("sub", "blk", None, None),
        P("sub", "blk", None, None),
        P("sub", "blk", None),
        P("sub", "blk", None),
        P("sub", "blk", None, None, None),
    )
    out_specs = (P("sub", "blk", None, None), P("sub", "blk", None, None))
    return jax.shard_map(
        on_device, mesh=mesh, in_specs=in_specs, out_specs=out_specs, check_vma=False
    )
```

```python
import functools
import math

import jax
import jax.numpy as jnp
from jax import lax
from jax.experimental import pallas as pl
from jax.experimental.pallas import tpu as pltpu
from jax.sharding import PartitionSpec as P

LANES = 128
SUBLANES = 8
VMEM = pl.BlockSpec(memory_space=pltpu.VMEM)
F32 = jnp.float32
BF16 = jnp.bfloat16


def call(body, outs, inputs, scratch=(), flops=1_000_000, moved=1_000_000):
    return pl.pallas_call(
        body,
        out_shape=outs,
        in_specs=[spec for _, spec in inputs],
        out_specs=[VMEM] * len(outs),
        scratch_shapes=list(scratch),
        compiler_params=pltpu.CompilerParams(vmem_limit_bytes=32 * 1024 * 1024),
        cost_estimate=pl.CostEstimate(
            flops=flops, bytes_accessed=moved, transcendentals=0
        ),
    )(*[value for value, _ in inputs])


def shape(rows, dtype=F32):
    return jax.ShapeDtypeStruct((rows, LANES), dtype)


def halves(value):
    high = value.astype(BF16).astype(F32)
    return high, value - high


def gather_traces(field, rows_ref, rows_first, target):
    block_rows = field.shape[0]
    spread = [
        jnp.broadcast_to(field[i : i + 1, :], (SUBLANES, LANES)) for i in range(block_rows)
    ]
    for k in range(target.shape[0] // SUBLANES):
        index = rows_ref[rows_first + k * SUBLANES : rows_first + (k + 1) * SUBLANES, :]
        dof, row = split(index, block_rows)
        taken = jnp.zeros((SUBLANES, LANES), F32)
        for i in range(block_rows):
            here = jnp.take_along_axis(spread[i], dof, axis=1, mode="promise_in_bounds")
            taken = jnp.where(row == i, here, taken)
        target[k * SUBLANES : (k + 1) * SUBLANES, :] = taken


def tile(k):
    return pl.ds(pl.multiple_of(k * SUBLANES, SUBLANES), SUBLANES)


def split(index, block_rows):
    if block_rows & (block_rows - 1) == 0:
        shift = block_rows.bit_length() - 1
        return index >> shift, index & (block_rows - 1)
    return lax.div(index, block_rows), lax.rem(index, block_rows)


def one_hot(place, count):
    row = lax.broadcasted_iota(jnp.int32, (count, place.shape[1]), 0)
    return jnp.where(row == place, 1.0, 0.0)


def exact_dot(left, right):
    return jnp.dot(
        left, right, precision=lax.Precision.HIGHEST, preferred_element_type=F32
    )


def block_place(k, groups):
    return jnp.where(k == 0, 0, groups - k)


def first_kernel(
    groups, packed_ref, aligned_ref, padded_ref, choice_ref, east_ref, west_ref, to_a_ref, to_b_ref
):
    faces = aligned_ref.shape[0] // 2
    block_rows = padded_ref.shape[0]
    per_group = faces // groups
    slot = lax.axis_index("blk")
    odd = lax.rem(lax.axis_index("sub"), 2) == 1
    padded_ref[...] = packed_ref[2 * faces : 2 * faces + block_rows, :]
    last = 2 * faces + block_rows
    tail = packed_ref[last : last + SUBLANES, :].astype(jnp.int32)
    partner = tail[:1, :faces]
    face = lax.broadcasted_iota(jnp.int32, (1, faces), 1)
    source = jnp.zeros((1, faces), jnp.int32)
    for g in range(groups):
        inside = face - g * per_group
        source = jnp.where(
            (inside >= 0) & (inside < per_group),
            block_place(tail[1:2, g : g + 1] ^ slot, groups) * per_group + inside,
            source,
        )
    order = one_hot(partner, faces)
    aligned_ref[faces:, :] = packed_ref[faces : 2 * faces, :].astype(jnp.int32)
    aligned_ref[:faces, :] = exact_dot(order, packed_ref[:faces, :]).astype(jnp.int32)
    choice_ref[...] = jnp.zeros_like(choice_ref)
    choice_ref[:1, :faces] = lax.dot_general(
        source.astype(F32).astype(BF16),
        order.astype(BF16),
        (((1,), (1,)), ((), ())),
        preferred_element_type=F32,
    )
    gather_traces(padded_ref[...], aligned_ref, 0, east_ref)
    gather_traces(padded_ref[...], aligned_ref, faces, west_ref)
    east = east_ref[...]
    west = west_ref[...]
    to_a_ref[:faces, :] = jnp.where(odd, east, west)
    to_b_ref[:faces, :] = jnp.where(odd, west, east)
    for to_ref in (to_a_ref, to_b_ref):
        to_ref[faces:, :] = choice_ref[...]


def blocks_kernel(first, packed_ref, last_ref, *block_refs):
    slot = lax.axis_index("blk")
    per_group = last_ref.shape[1]
    for place, block_ref in enumerate(block_refs):
        k = slot ^ (len(block_refs) - place)
        kept = pl.ds(pl.multiple_of(first + k * per_group, SUBLANES), per_group)
        block_ref[:per_group, :] = packed_ref[kept, :]
        block_ref[per_group:, :] = last_ref[k]


def stiffness_kernel(size, pairs_ref, blocks_ref, field_ref, *refs):
    *aligned_refs, out_ref = refs[:1] if len(refs) == 1 else refs[:2]
    west_refs = refs[2:]
    block_rows = field_ref.shape[0]
    count = pairs_ref.shape[1]
    rows = block_rows + count
    width = math.lcm(size, LANES)
    tiles = width // LANES
    segments = width // size
    groups = size // segments
    batch = next(k for k in (4, 3, 2, 1) if groups % k == 0)

    def place(position):
        segment = sum(jnp.where(position >= k * size, 1, 0) for k in range(1, segments))
        return segment, position - segment * size

    def lanes_of(value, index):
        slabs = [
            jnp.take_along_axis(
                value[k : k + SUBLANES, :], index, axis=1, mode="promise_in_bounds"
            )
            for k in range(0, value.shape[0], SUBLANES)
        ]
        return jnp.concatenate(slabs, axis=0)

    field = field_ref[...]
    first_of, other_of = (one_hot(pairs_ref[k : k + 1, :], block_rows) for k in (0, 1))
    left, other = (
        lax.dot_general(
            ends,
            field,
            (((0,), (0,)), ((), ())),
            precision=lax.Precision.HIGHEST,
            preferred_element_type=F32,
        )
        for ends in (first_of, other_of)
    )
    right = jnp.concatenate([field, other], axis=0)
    lane = lax.broadcasted_iota(jnp.int32, (SUBLANES, LANES), 1)
    places = [place(lane + t * LANES) for t in range(tiles)]
    repeated = jnp.concatenate([lanes_of(right, inside) for _, inside in places], axis=1)
    segment, inside = place(lax.broadcasted_iota(jnp.int32, (width, LANES), 0))
    column = lax.broadcasted_iota(jnp.int32, (width, LANES), 1)
    add_segments = jnp.where(segment == column % segments, 1.0, 0.0).astype(BF16)
    fold = jnp.where(inside == column, 1.0, 0.0)
    dof_group = lax.broadcasted_iota(jnp.int32, (rows, LANES), 1) // segments
    total = jnp.zeros((rows, LANES), F32)
    turned = jnp.zeros((count, width), F32)
    for base in range(0, groups, batch):
        stack = []
        for g in range(base, base + batch):
            stored = blocks_ref[:, g * width : (g + 1) * width]
            product = stored * repeated
            high = product.astype(BF16)
            stack += [high, (product - high.astype(F32)).astype(BF16)]
            spread = [lanes_of(left, g * segments + segment) for segment, _ in places]
            turned = turned + stored[block_rows:] * jnp.concatenate(spread, axis=1)
        sums = jnp.dot(
            jnp.concatenate(stack, axis=0), add_segments, preferred_element_type=F32
        )
        for n in range(batch):
            both = sums[2 * n * rows : 2 * (n + 1) * rows]
            total = jnp.where(dof_group == base + n, both[:rows] + both[rows:], total)
    out_ref[...] = (
        total[:block_rows]
        + exact_dot(first_of, total[block_rows:])
        + exact_dot(other_of, exact_dot(turned, fold))
    )
    for aligned_ref, west_ref in zip(aligned_refs, west_refs):
        gather_traces(field, aligned_ref, west_ref.shape[0], west_ref)


def spread_jumps(size, rows_ref, sides, block_rows):
    dof_of = lax.broadcasted_iota(jnp.int32, (size, LANES), 0).astype(F32).astype(BF16)
    row_of = lax.broadcasted_iota(jnp.int32, (block_rows, LANES), 0).astype(F32).astype(BF16)
    none = jnp.zeros((), BF16)
    one = jnp.ones((), BF16)

    def widened(value, f, rows):
        slab = jnp.broadcast_to(value[f : f + 1, :], (2 * SUBLANES, LANES)).astype(BF16)
        return jnp.concatenate([slab] * (rows // (2 * SUBLANES)), axis=0)

    total = jnp.zeros((size, 2 * block_rows), F32)
    for side, weighted in enumerate(sides):
        for k in range(0, weighted.shape[0], SUBLANES):
            high, low = halves(weighted[k : k + SUBLANES])
            first = side * weighted.shape[0] + k
            dof, row = split(rows_ref[first : first + SUBLANES, :], block_rows)
            dof = dof.astype(F32)
            row = row.astype(F32)
            left = []
            right = []
            for f in range(SUBLANES):
                here = row_of == widened(row, f, block_rows)
                left.append(
                    jnp.concatenate(
                        [
                            jnp.where(here, widened(high, f, block_rows), none),
                            jnp.where(here, widened(low, f, block_rows), none),
                        ],
                        axis=0,
                    )
                )
                right.append(jnp.where(dof_of == widened(dof, f, size), one, none))
            total = total + lax.dot_general(
                jnp.concatenate(right, axis=1),
                jnp.concatenate(left, axis=1),
                (((1,), (1,)), ((), ())),
                preferred_element_type=F32,
            )
    total = total.T
    return total[:block_rows] + total[block_rows:]


def pick_rows(choice, value):
    high, rest = halves(value)
    middle, low = halves(rest)
    pieces = jnp.concatenate([high, middle, low], axis=1).astype(BF16)
    picked = lax.dot_general(
        one_hot(choice, value.shape[0]).astype(BF16),
        pieces,
        (((0,), (0,)), ((), ())),
        preferred_element_type=F32,
    )
    return (
        picked[:, :LANES] + picked[:, LANES : 2 * LANES]
    ) + picked[:, 2 * LANES :]


def image_kernel(
    size,
    first,
    packed_ref,
    last_ref,
    choice_ref,
    aligned_ref,
    product_ref,
    east_ref,
    west_ref,
    from_a_ref,
    from_b_ref,
    *refs,
):
    *block_refs, image_ref, weights_east_ref, weights_west_ref, jump_ref, next_east_ref = refs
    block_rows = product_ref.shape[0]
    faces = weights_east_ref.shape[0]
    per_group = last_ref.shape[1]
    slot = lax.axis_index("blk")
    odd = lax.rem(lax.axis_index("sub"), 2) == 1
    kept = pl.ds(pl.multiple_of(first + slot * per_group, SUBLANES), per_group)
    from_west = jnp.where(odd, from_b_ref[...], from_a_ref[...])
    from_east = jnp.where(odd, from_a_ref[:faces, :], from_b_ref[:faces, :])
    for row, block, part, weights_ref in (
        (choice_ref[...], packed_ref[kept, :], slice(0, per_group), weights_east_ref),
        (from_west[faces:], last_ref[slot], slice(per_group, 2 * per_group), weights_west_ref),
    ):
        weights_ref[...] = pick_rows(
            row[:1, :faces].astype(jnp.int32),
            jnp.concatenate([block] + [block_ref[part, :] for block_ref in block_refs], axis=0),
        )
    jump_ref[...] = west_ref[...] - from_west[:faces]
    image_ref[...] = product_ref[...]
    image_ref[:, :size] = image_ref[:, :size] + spread_jumps(
        size,
        aligned_ref,
        (
            weights_east_ref[...] * (east_ref[...] - from_east),
            weights_west_ref[...] * jump_ref[...],
        ),
        block_rows,
    )
    gather_traces(image_ref[...], aligned_ref, 0, next_east_ref.at[:faces, :])
    next_east_ref[faces:, :] = jnp.zeros_like(next_east_ref[faces:, :])


def column_sums(value):
    return jnp.sum(value, axis=0, keepdims=True)


def sums_kernel(
    product_ref, weights_ref, own_ref, arrived_ref, jump_ref, field_ref, image_ref, sums_ref
):
    field = field_ref[...]
    image = image_ref[...]
    product = product_ref[...]
    jump = own_ref[...] - arrived_ref[: own_ref.shape[0], :]
    lam = weights_ref[...] * jump
    parts = [
        column_sums(field * field),
        column_sums(field * image),
        column_sums(image * image),
        column_sums(field * product) + column_sums(lam * jump_ref[...]),
        column_sums(image * product) + column_sums(lam * jump),
    ]
    parts += [jnp.zeros_like(parts[0])] * (SUBLANES - len(parts))
    whole = jnp.sum(jnp.concatenate(parts, axis=0), axis=1, keepdims=True)
    row = lax.broadcasted_iota(jnp.int32, (SUBLANES, LANES), 0)
    lane = lax.broadcasted_iota(jnp.int32, (SUBLANES, LANES), 1)
    packed = column_sums(jnp.where(lane == row, whole, 0.0))
    sums_ref[...] = jnp.broadcast_to(packed[None], sums_ref.shape)


def second_kernel(
    size,
    aligned_ref,
    product_ref,
    weights_east_ref,
    weights_west_ref,
    east_ref,
    west_ref,
    from_next_ref,
    from_last_ref,
    second_ref,
):
    block_rows = product_ref.shape[0]
    faces = west_ref.shape[0]
    second_ref[...] = product_ref[...]
    second_ref[:, :size] = second_ref[:, :size] + spread_jumps(
        size,
        aligned_ref,
        [
            weights_ref[...] * (own_ref[:faces, :] - arrived_ref[:faces, :])
            for weights_ref, own_ref, arrived_ref in (
                (weights_east_ref, east_ref, from_next_ref),
                (weights_west_ref, west_ref, from_last_ref),
            )
        ],
        block_rows,
    )


def final_kernel(field_ref, image_ref, second_ref, sums_ref, solution_ref, residual_ref):
    size = solution_ref.shape[1]
    row = jnp.sum(sums_ref[...], axis=0)
    lane = lax.broadcasted_iota(jnp.int32, (1, LANES), 1)

    def entry(k):
        return jnp.sum(jnp.where(lane == k, row, 0.0), axis=1, keepdims=True)

    bb, bq, qq, bw, qw = (entry(k) for k in range(5))
    field = field_ref[:, :size]
    image = image_ref[:, :size]
    second = second_ref[:, :size]
    alpha = bb / bq
    norm = bb - alpha * (2.0 * bq - alpha * qq)
    beta = norm / bb
    grown = 1.0 + beta
    energy = grown * (grown * bq - alpha * (bw + qq)) + alpha * alpha * qw
    alpha_next = norm / energy
    residual = field - alpha * image
    direction = residual + beta * field
    moved = (image - alpha * second) + beta * image
    solution_ref[...] = alpha * field + alpha_next * direction
    residual_ref[...] = residual - alpha_next * moved


def swap(value, odd):
    count = lax.axis_size("sub")
    pairs = []
    for first in range(odd, count, 2):
        second = (first + 1) % count
        pairs += [(first, second), (second, first)]
    return lax.ppermute(value, "sub", pairs)


def from_behind(value, axis, steps):
    count = lax.axis_size(axis)
    pairs = [(source, (source + steps) % count) for source in range(count)]
    return lax.ppermute(value, axis, pairs)


def swap_slots(value, k):
    count = lax.axis_size("blk")
    return lax.ppermute(value, "blk", [(slot, slot ^ k) for slot in range(count)])


def on_device(
    right_side, stiffness, block_pairs, trace_rows, partner_face, owner_list, mortar_weight
):
    field = right_side[0, 0].T
    block_rows, size = field.shape
    blocks = stiffness[0, 0].astype(F32)
    pairs = block_pairs[0, 0]
    rows = trace_rows[0, 0]
    partner = partner_face[0, 0]
    owners = owner_list[0, 0]
    faces = partner.shape[0]
    devices = lax.axis_size("sub") * lax.axis_size("blk")

    own_weights = mortar_weight[0, 0]
    last_weights = from_behind(own_weights, "sub", 1)
    last = 2 * faces + block_rows

    def placed(value, first):
        below = last + SUBLANES + faces - first - value.shape[0]
        return jnp.pad(value, ((first, below), (0, LANES - value.shape[1])))

    indices = placed(rows, 0) + placed(partner_face[0], last) + placed(owner_list[0], last + 1)
    packed = (
        indices.astype(F32)
        + placed(field, 2 * faces)
        + placed(own_weights.reshape(faces, LANES), last + SUBLANES)
    )
    aligned, padded, choice, east, west, to_a, to_b = call(
        functools.partial(first_kernel, owners.shape[0]),
        [
            shape(2 * faces, jnp.int32),
            shape(block_rows),
            shape(SUBLANES),
            shape(faces),
            shape(faces),
            shape(faces + SUBLANES),
            shape(faces + SUBLANES),
        ],
        [(packed, VMEM)],
    )
    from_a = swap(to_a, 1)
    from_b = swap(to_b, 0)
    slots, per_group, _ = own_weights.shape
    blocks_to = call(
        functools.partial(blocks_kernel, last + SUBLANES),
        [shape(2 * per_group)] * (slots - 1),
        [(packed, VMEM), (last_weights, VMEM)],
        flops=1,
        moved=1,
    )
    blocks_from = [
        swap_slots(block, k) for k, block in zip(range(slots - 1, 0, -1), blocks_to)
    ]

    def stiff(vector, *ordered):
        return call(
            functools.partial(stiffness_kernel, size),
            [shape(block_rows)] + [shape(faces)] * len(ordered),
            [(value, VMEM) for value in (pairs, blocks, vector, *ordered)],
        )

    (product,) = stiff(padded)
    image, weights_east, weights_west, jump, east = call(
        functools.partial(image_kernel, size, last + SUBLANES),
        [shape(block_rows)] + [shape(faces)] * 3 + [shape(faces + SUBLANES)],
        [
            (value, VMEM)
            for value in (
                packed,
                last_weights,
                choice,
                aligned,
                product,
                east,
                west,
                from_a,
                from_b,
                *blocks_from,
            )
        ],
    )
    from_last = from_behind(east, "sub", 1)
    product, west = stiff(image, aligned)
    from_next = from_behind(west, "sub", -1)
    (sums,) = call(
        sums_kernel,
        [jax.ShapeDtypeStruct((devices, 1, LANES), F32)],
        [
            (value, VMEM)
            for value in (product, weights_west, west, from_last, jump, padded, image)
        ],
    )
    (second,) = call(
        functools.partial(second_kernel, size),
        [shape(block_rows)],
        [
            (value, VMEM)
            for value in (
                aligned, product, weights_east, weights_west, east, west, from_next, from_last
            )
        ],
        flops=1_000_000_000,
    )
    sums = lax.all_to_all(sums, ("sub", "blk"), split_axis=0, concat_axis=0, tiled=True)
    solution_field, residual = call(
        final_kernel,
        [jax.ShapeDtypeStruct((block_rows, size), F32)] * 2,
        [(padded, VMEM), (image, VMEM), (second, VMEM), (sums, VMEM)],
    )
    return (solution_field.T[None, None], residual.T[None, None])


def solution(mesh):
    in_specs = (
        P("sub", "blk", None, None),
        P("sub", "blk", None, None),
        P("sub", "blk", None, None),
        P("sub", "blk", None, None),
        P("sub", "blk", None),
        P("sub", "blk", None),
        P("sub", "blk", None, None, None),
    )
    out_specs = (P("sub", "blk", None, None), P("sub", "blk", None, None))
    return jax.shard_map(
        on_device, mesh=mesh, in_specs=in_specs, out_specs=out_specs, check_vma=False
    )
```

```python
import functools
import math

import jax
import jax.numpy as jnp
from jax import lax
from jax.experimental import pallas as pl
from jax.experimental.pallas import tpu as pltpu
from jax.sharding import PartitionSpec as P

LANES = 128
SUBLANES = 8
VMEM = pl.BlockSpec(memory_space=pltpu.VMEM)
F32 = jnp.float32
BF16 = jnp.bfloat16


def call(body, outs, inputs, scratch=(), flops=1_000_000, moved=1_000_000):
    return pl.pallas_call(
        body,
        out_shape=outs,
        in_specs=[spec for _, spec in inputs],
        out_specs=[VMEM] * len(outs),
        scratch_shapes=list(scratch),
        compiler_params=pltpu.CompilerParams(vmem_limit_bytes=32 * 1024 * 1024),
        cost_estimate=pl.CostEstimate(
            flops=flops, bytes_accessed=moved, transcendentals=0
        ),
    )(*[value for value, _ in inputs])


def shape(rows, dtype=F32):
    return jax.ShapeDtypeStruct((rows, LANES), dtype)


def halves(value):
    high = value.astype(BF16).astype(F32)
    return high, value - high


def gather_traces(field, rows_ref, rows_first, target):
    block_rows = field.shape[0]
    spread = [
        jnp.broadcast_to(field[i : i + 1, :], (SUBLANES, LANES)) for i in range(block_rows)
    ]
    for k in range(target.shape[0] // SUBLANES):
        index = rows_ref[rows_first + k * SUBLANES : rows_first + (k + 1) * SUBLANES, :]
        dof, row = split(index, block_rows)
        taken = jnp.zeros((SUBLANES, LANES), F32)
        for i in range(block_rows):
            here = jnp.take_along_axis(spread[i], dof, axis=1, mode="promise_in_bounds")
            taken = jnp.where(row == i, here, taken)
        target[k * SUBLANES : (k + 1) * SUBLANES, :] = taken


def tile(k):
    return pl.ds(pl.multiple_of(k * SUBLANES, SUBLANES), SUBLANES)


def split(index, block_rows):
    if block_rows & (block_rows - 1) == 0:
        shift = block_rows.bit_length() - 1
        return index >> shift, index & (block_rows - 1)
    return lax.div(index, block_rows), lax.rem(index, block_rows)


def one_hot(place, count):
    row = lax.broadcasted_iota(jnp.int32, (count, place.shape[1]), 0)
    return jnp.where(row == place, 1.0, 0.0)


def exact_dot(left, right):
    return jnp.dot(
        left, right, precision=lax.Precision.HIGHEST, preferred_element_type=F32
    )


def block_place(k, groups):
    return jnp.where(k == 0, 0, groups - k)


def first_kernel(
    groups, packed_ref, aligned_ref, padded_ref, choice_ref, east_ref, west_ref, to_a_ref, to_b_ref
):
    faces = aligned_ref.shape[0] // 2
    block_rows = padded_ref.shape[0]
    per_group = faces // groups
    slot = lax.axis_index("blk")
    odd = lax.rem(lax.axis_index("sub"), 2) == 1
    padded_ref[...] = packed_ref[2 * faces : 2 * faces + block_rows, :]
    last = 2 * faces + block_rows
    tail = packed_ref[last : last + SUBLANES, :].astype(jnp.int32)
    partner = tail[:1, :faces]
    face = lax.broadcasted_iota(jnp.int32, (1, faces), 1)
    source = jnp.zeros((1, faces), jnp.int32)
    for g in range(groups):
        inside = face - g * per_group
        source = jnp.where(
            (inside >= 0) & (inside < per_group),
            block_place(tail[1:2, g : g + 1] ^ slot, groups) * per_group + inside,
            source,
        )
    order = one_hot(partner, faces)
    east_rows = exact_dot(order, packed_ref[:faces, :])
    west_rows = packed_ref[faces : 2 * faces, :]
    aligned_ref[:faces, :] = east_rows.astype(jnp.int32)
    aligned_ref[faces:, :] = west_rows.astype(jnp.int32)
    choice_ref[...] = jnp.zeros_like(choice_ref)
    choice_ref[:1, :faces] = lax.dot_general(
        source.astype(F32).astype(BF16),
        order.astype(BF16),
        (((1,), (1,)), ((), ())),
        preferred_element_type=F32,
    )
    gather_traces(padded_ref[...], aligned_ref, 0, east_ref)
    gather_traces(padded_ref[...], aligned_ref, faces, west_ref)
    east = east_ref[...]
    west = west_ref[...]
    to_a_ref[:faces, :] = jnp.where(odd, east, west)
    to_b_ref[:faces, :] = jnp.where(odd, west, east)
    for to_ref in (to_a_ref, to_b_ref):
        to_ref[faces : faces + SUBLANES, :] = choice_ref[...]
    to_a_ref[faces + SUBLANES :, :] = jnp.where(odd, east_rows, west_rows)
    to_b_ref[faces + SUBLANES :, :] = jnp.where(odd, west_rows, east_rows)


def blocks_kernel(first, packed_ref, last_ref, *block_refs):
    slot = lax.axis_index("blk")
    per_group = last_ref.shape[1]
    for place, block_ref in enumerate(block_refs):
        k = slot ^ (len(block_refs) - place)
        kept = pl.ds(pl.multiple_of(first + k * per_group, SUBLANES), per_group)
        block_ref[:per_group, :] = packed_ref[kept, :]
        block_ref[per_group:, :] = last_ref[k]


def stiffness_kernel(size, pairs_ref, blocks_ref, field_ref, *refs):
    out_ref = refs[min(1, len(refs) - 1)]
    block_rows = field_ref.shape[0]
    count = pairs_ref.shape[1]
    rows = block_rows + count
    width = math.lcm(size, LANES)
    tiles = width // LANES
    segments = width // size
    groups = size // segments
    batch = next(k for k in (4, 3, 2, 1) if groups % k == 0)

    def place(position):
        segment = sum(jnp.where(position >= k * size, 1, 0) for k in range(1, segments))
        return segment, position - segment * size

    def lanes_of(value, index):
        slabs = [
            jnp.take_along_axis(
                value[k : k + SUBLANES, :], index, axis=1, mode="promise_in_bounds"
            )
            for k in range(0, value.shape[0], SUBLANES)
        ]
        return jnp.concatenate(slabs, axis=0)

    field = field_ref[...]
    first_of, other_of = (one_hot(pairs_ref[k : k + 1, :], block_rows) for k in (0, 1))
    left, other = (
        lax.dot_general(
            ends,
            field,
            (((0,), (0,)), ((), ())),
            precision=lax.Precision.HIGHEST,
            preferred_element_type=F32,
        )
        for ends in (first_of, other_of)
    )
    right = jnp.concatenate([field, other], axis=0)
    lane = lax.broadcasted_iota(jnp.int32, (SUBLANES, LANES), 1)
    places = [place(lane + t * LANES) for t in range(tiles)]
    repeated = jnp.concatenate([lanes_of(right, inside) for _, inside in places], axis=1)
    segment, inside = place(lax.broadcasted_iota(jnp.int32, (width, LANES), 0))
    column = lax.broadcasted_iota(jnp.int32, (width, LANES), 1)
    add_segments = jnp.where(segment == column % segments, 1.0, 0.0).astype(BF16)
    fold = jnp.where(inside == column, 1.0, 0.0)
    dof_group = lax.broadcasted_iota(jnp.int32, (rows, LANES), 1) // segments
    total = jnp.zeros((rows, LANES), F32)
    turned = jnp.zeros((count, width), F32)
    for base in range(0, groups, batch):
        stack = []
        for g in range(base, base + batch):
            stored = blocks_ref[:, g * width : (g + 1) * width]
            product = stored * repeated
            high = product.astype(BF16)
            stack += [high, (product - high.astype(F32)).astype(BF16)]
            spread = [lanes_of(left, g * segments + segment) for segment, _ in places]
            turned = turned + stored[block_rows:] * jnp.concatenate(spread, axis=1)
        sums = jnp.dot(
            jnp.concatenate(stack, axis=0), add_segments, preferred_element_type=F32
        )
        for n in range(batch):
            both = sums[2 * n * rows : 2 * (n + 1) * rows]
            total = jnp.where(dof_group == base + n, both[:rows] + both[rows:], total)
    out_ref[...] = (
        total[:block_rows]
        + exact_dot(first_of, total[block_rows:])
        + exact_dot(other_of, exact_dot(turned, fold))
    )
    if len(refs) > 1:
        aligned_ref, _, copy_ref, east_ref, west_ref = refs
        copy_ref[...] = field
        gather_traces(field, aligned_ref, 0, east_ref)
        gather_traces(field, aligned_ref, west_ref.shape[0], west_ref)


def spread_jumps(size, rows_ref, sides, block_rows):
    dof_of = lax.broadcasted_iota(jnp.int32, (size, LANES), 0).astype(F32).astype(BF16)
    row_of = lax.broadcasted_iota(jnp.int32, (block_rows, LANES), 0).astype(F32).astype(BF16)
    none = jnp.zeros((), BF16)
    one = jnp.ones((), BF16)

    def widened(value, f, rows):
        slab = jnp.broadcast_to(value[f : f + 1, :], (2 * SUBLANES, LANES)).astype(BF16)
        return jnp.concatenate([slab] * (rows // (2 * SUBLANES)), axis=0)

    total = jnp.zeros((size, 2 * block_rows), F32)
    for side, weighted in enumerate(sides):
        for k in range(0, weighted.shape[0], SUBLANES):
            high, low = halves(weighted[k : k + SUBLANES])
            first = side * weighted.shape[0] + k
            dof, row = split(rows_ref[first : first + SUBLANES, :], block_rows)
            dof = dof.astype(F32)
            row = row.astype(F32)
            left = []
            right = []
            for f in range(SUBLANES):
                here = row_of == widened(row, f, block_rows)
                left.append(
                    jnp.concatenate(
                        [
                            jnp.where(here, widened(high, f, block_rows), none),
                            jnp.where(here, widened(low, f, block_rows), none),
                        ],
                        axis=0,
                    )
                )
                right.append(jnp.where(dof_of == widened(dof, f, size), one, none))
            total = total + lax.dot_general(
                jnp.concatenate(right, axis=1),
                jnp.concatenate(left, axis=1),
                (((1,), (1,)), ((), ())),
                preferred_element_type=F32,
            )
    total = total.T
    return total[:block_rows] + total[block_rows:]


def pick_rows(choice, value):
    high, rest = halves(value)
    middle, low = halves(rest)
    pieces = jnp.concatenate([high, middle, low], axis=1).astype(BF16)
    picked = lax.dot_general(
        one_hot(choice, value.shape[0]).astype(BF16),
        pieces,
        (((0,), (0,)), ((), ())),
        preferred_element_type=F32,
    )
    return (
        picked[:, :LANES] + picked[:, LANES : 2 * LANES]
    ) + picked[:, 2 * LANES :]


def image_kernel(
    size,
    first,
    packed_ref,
    last_ref,
    choice_ref,
    aligned_ref,
    product_ref,
    east_ref,
    west_ref,
    from_a_ref,
    from_b_ref,
    *refs,
):
    *block_refs, image_ref, weights_east_ref, weights_west_ref, jump_ref = refs[:-2]
    next_rows_ref, last_rows_ref = refs[-2:]
    block_rows = product_ref.shape[0]
    faces = weights_east_ref.shape[0]
    per_group = last_ref.shape[1]
    slot = lax.axis_index("blk")
    odd = lax.rem(lax.axis_index("sub"), 2) == 1
    kept = pl.ds(pl.multiple_of(first + slot * per_group, SUBLANES), per_group)
    from_west = jnp.where(odd, from_b_ref[...], from_a_ref[...])
    from_east = jnp.where(odd, from_a_ref[...], from_b_ref[...])
    next_rows_ref[...] = from_east[faces + SUBLANES :].astype(jnp.int32)
    last_rows_ref[...] = from_west[faces + SUBLANES :].astype(jnp.int32)
    for row, block, part, weights_ref in (
        (choice_ref[...], packed_ref[kept, :], slice(0, per_group), weights_east_ref),
        (from_west[faces : faces + SUBLANES], last_ref[slot], slice(per_group, 2 * per_group), weights_west_ref),
    ):
        weights_ref[...] = pick_rows(
            row[:1, :faces].astype(jnp.int32),
            jnp.concatenate([block] + [block_ref[part, :] for block_ref in block_refs], axis=0),
        )
    jump_ref[...] = west_ref[...] - from_west[:faces]
    image_ref[...] = product_ref[...]
    image_ref[:, :size] = image_ref[:, :size] + spread_jumps(
        size,
        aligned_ref,
        (
            weights_east_ref[...] * (east_ref[...] - from_east[:faces]),
            weights_west_ref[...] * jump_ref[...],
        ),
        block_rows,
    )


def column_sums(value):
    return jnp.sum(value, axis=0, keepdims=True)


def sums_kernel(
    product_ref,
    weights_ref,
    own_ref,
    rows_ref,
    last_ref,
    jump_ref,
    field_ref,
    image_ref,
    sums_ref,
    arrived_ref,
):
    field = field_ref[...]
    image = image_ref[...]
    product = product_ref[...]
    gather_traces(last_ref[...], rows_ref, 0, arrived_ref)
    jump = own_ref[...] - arrived_ref[...]
    lam = weights_ref[...] * jump
    parts = [
        column_sums(field * field),
        column_sums(field * image),
        column_sums(image * image),
        column_sums(field * product) + column_sums(lam * jump_ref[...]),
        column_sums(image * product) + column_sums(lam * jump),
    ]
    parts += [jnp.zeros_like(parts[0])] * (SUBLANES - len(parts))
    whole = jnp.sum(jnp.concatenate(parts, axis=0), axis=1, keepdims=True)
    row = lax.broadcasted_iota(jnp.int32, (SUBLANES, LANES), 0)
    lane = lax.broadcasted_iota(jnp.int32, (SUBLANES, LANES), 1)
    packed = column_sums(jnp.where(lane == row, whole, 0.0))
    sums_ref[...] = jnp.broadcast_to(packed[None], sums_ref.shape)


def second_kernel(
    size,
    aligned_ref,
    product_ref,
    weights_east_ref,
    weights_west_ref,
    east_ref,
    west_ref,
    rows_ref,
    next_ref,
    from_last_ref,
    second_ref,
    from_next_ref,
):
    block_rows = product_ref.shape[0]
    gather_traces(next_ref[...], rows_ref, 0, from_next_ref)
    second_ref[...] = product_ref[...]
    second_ref[:, :size] = second_ref[:, :size] + spread_jumps(
        size,
        aligned_ref,
        [
            weights_ref[...] * (own_ref[...] - arrived_ref[...])
            for weights_ref, own_ref, arrived_ref in (
                (weights_east_ref, east_ref, from_next_ref),
                (weights_west_ref, west_ref, from_last_ref),
            )
        ],
        block_rows,
    )


def final_kernel(field_ref, image_ref, second_ref, sums_ref, solution_ref, residual_ref):
    size = solution_ref.shape[1]
    row = jnp.sum(sums_ref[...], axis=0)
    lane = lax.broadcasted_iota(jnp.int32, (1, LANES), 1)

    def entry(k):
        return jnp.sum(jnp.where(lane == k, row, 0.0), axis=1, keepdims=True)

    bb, bq, qq, bw, qw = (entry(k) for k in range(5))
    field = field_ref[:, :size]
    image = image_ref[:, :size]
    second = second_ref[:, :size]
    alpha = bb / bq
    norm = bb - alpha * (2.0 * bq - alpha * qq)
    beta = norm / bb
    grown = 1.0 + beta
    energy = grown * (grown * bq - alpha * (bw + qq)) + alpha * alpha * qw
    alpha_next = norm / energy
    residual = field - alpha * image
    direction = residual + beta * field
    moved = (image - alpha * second) + beta * image
    solution_ref[...] = alpha * field + alpha_next * direction
    residual_ref[...] = residual - alpha_next * moved


def swap(value, odd):
    count = lax.axis_size("sub")
    pairs = []
    for first in range(odd, count, 2):
        second = (first + 1) % count
        pairs += [(first, second), (second, first)]
    return lax.ppermute(value, "sub", pairs)


def from_behind(value, axis, steps):
    count = lax.axis_size(axis)
    pairs = [(source, (source + steps) % count) for source in range(count)]
    return lax.ppermute(value, axis, pairs)


def swap_slots(value, k):
    count = lax.axis_size("blk")
    return lax.ppermute(value, "blk", [(slot, slot ^ k) for slot in range(count)])


def on_device(
    right_side, stiffness, block_pairs, trace_rows, partner_face, owner_list, mortar_weight
):
    field = right_side[0, 0].T
    block_rows, size = field.shape
    blocks = stiffness[0, 0].astype(F32)
    pairs = block_pairs[0, 0]
    rows = trace_rows[0, 0]
    partner = partner_face[0, 0]
    owners = owner_list[0, 0]
    faces = partner.shape[0]
    devices = lax.axis_size("sub") * lax.axis_size("blk")

    own_weights = mortar_weight[0, 0]
    last_weights = from_behind(own_weights, "sub", 1)
    last = 2 * faces + block_rows

    def placed(value, first):
        below = last + SUBLANES + faces - first - value.shape[0]
        return jnp.pad(value, ((first, below), (0, LANES - value.shape[1])))

    indices = placed(rows, 0) + placed(partner_face[0], last) + placed(owner_list[0], last + 1)
    packed = (
        indices.astype(F32)
        + placed(field, 2 * faces)
        + placed(own_weights.reshape(faces, LANES), last + SUBLANES)
    )
    aligned, padded, choice, east, west, to_a, to_b = call(
        functools.partial(first_kernel, owners.shape[0]),
        [
            shape(2 * faces, jnp.int32),
            shape(block_rows),
            shape(SUBLANES),
            shape(faces),
            shape(faces),
            shape(2 * faces + SUBLANES),
            shape(2 * faces + SUBLANES),
        ],
        [(packed, VMEM)],
    )
    from_a = swap(to_a, 1)
    from_b = swap(to_b, 0)
    slots, per_group, _ = own_weights.shape
    blocks_to = call(
        functools.partial(blocks_kernel, last + SUBLANES),
        [shape(2 * per_group)] * (slots - 1),
        [(packed, VMEM), (last_weights, VMEM)],
        flops=1,
        moved=1,
    )
    blocks_from = [
        swap_slots(block, k) for k, block in zip(range(slots - 1, 0, -1), blocks_to)
    ]

    def stiff(vector, *ordered):
        return call(
            functools.partial(stiffness_kernel, size),
            [shape(block_rows)] * (1 + len(ordered)) + [shape(faces)] * (2 * len(ordered)),
            [(value, VMEM) for value in (pairs, blocks, vector, *ordered)],
        )

    (product,) = stiff(padded)
    image, weights_east, weights_west, jump, next_rows, last_rows = call(
        functools.partial(image_kernel, size, last + SUBLANES),
        [shape(block_rows)] + [shape(faces)] * 3 + [shape(faces, jnp.int32)] * 2,
        [
            (value, VMEM)
            for value in (
                packed,
                last_weights,
                choice,
                aligned,
                product,
                east,
                west,
                from_a,
                from_b,
                *blocks_from,
            )
        ],
    )
    from_last = from_behind(image, "sub", 1)
    product, copied, east, west = stiff(image, aligned)
    from_next = from_behind(copied, "sub", -1)
    sums, arrived = call(
        sums_kernel,
        [jax.ShapeDtypeStruct((devices, 1, LANES), F32), shape(faces)],
        [
            (value, VMEM)
            for value in (product, weights_west, west, last_rows, from_last, jump, padded, image)
        ],
    )
    (second,) = call(
        functools.partial(second_kernel, size),
        [shape(block_rows)],
        [
            (value, VMEM)
            for value in (
                aligned,
                product,
                weights_east,
                weights_west,
                east,
                west,
                next_rows,
                from_next,
                arrived,
            )
        ],
        scratch=[pltpu.VMEM((faces, LANES), F32)],
        flops=1_000_000_000,
    )
    sums = lax.all_to_all(sums, ("sub", "blk"), split_axis=0, concat_axis=0, tiled=True)
    solution_field, residual = call(
        final_kernel,
        [jax.ShapeDtypeStruct((block_rows, size), F32)] * 2,
        [(padded, VMEM), (image, VMEM), (second, VMEM), (sums, VMEM)],
    )
    return (solution_field.T[None, None], residual.T[None, None])


def solution(mesh):
    in_specs = (
        P("sub", "blk", None, None),
        P("sub", "blk", None, None),
        P("sub", "blk", None, None),
        P("sub", "blk", None, None),
        P("sub", "blk", None),
        P("sub", "blk", None),
        P("sub", "blk", None, None, None),
    )
    out_specs = (P("sub", "blk", None, None), P("sub", "blk", None, None))
    return jax.shard_map(
        on_device, mesh=mesh, in_specs=in_specs, out_specs=out_specs, check_vma=False
    )
```

```python
import functools
import math

import jax
import jax.numpy as jnp
from jax import lax
from jax.experimental import pallas as pl
from jax.experimental.pallas import tpu as pltpu
from jax.sharding import PartitionSpec as P

LANES = 128
SUBLANES = 8
VMEM = pl.BlockSpec(memory_space=pltpu.VMEM)
F32 = jnp.float32
BF16 = jnp.bfloat16


def call(body, outs, inputs, scratch=(), flops=1_000_000, moved=1_000_000):
    return pl.pallas_call(
        body,
        out_shape=outs,
        in_specs=[spec for _, spec in inputs],
        out_specs=[VMEM] * len(outs),
        scratch_shapes=list(scratch),
        compiler_params=pltpu.CompilerParams(vmem_limit_bytes=32 * 1024 * 1024),
        cost_estimate=pl.CostEstimate(
            flops=flops, bytes_accessed=moved, transcendentals=0
        ),
    )(*[value for value, _ in inputs])


def shape(rows, dtype=F32):
    return jax.ShapeDtypeStruct((rows, LANES), dtype)


def halves(value):
    high = value.astype(BF16).astype(F32)
    return high, value - high


def gather_traces(field, rows_ref, rows_first, target):
    block_rows = field.shape[0]
    spread = [
        jnp.broadcast_to(field[i : i + 1, :], (SUBLANES, LANES)) for i in range(block_rows)
    ]
    for k in range(target.shape[0] // SUBLANES):
        index = rows_ref[rows_first + k * SUBLANES : rows_first + (k + 1) * SUBLANES, :]
        dof, row = split(index, block_rows)
        taken = jnp.zeros((SUBLANES, LANES), F32)
        for i in range(block_rows):
            here = jnp.take_along_axis(spread[i], dof, axis=1, mode="promise_in_bounds")
            taken = jnp.where(row == i, here, taken)
        target[k * SUBLANES : (k + 1) * SUBLANES, :] = taken


def tile(k):
    return pl.ds(pl.multiple_of(k * SUBLANES, SUBLANES), SUBLANES)


def split(index, block_rows):
    if block_rows & (block_rows - 1) == 0:
        shift = block_rows.bit_length() - 1
        return index >> shift, index & (block_rows - 1)
    return lax.div(index, block_rows), lax.rem(index, block_rows)


def one_hot(place, count):
    row = lax.broadcasted_iota(jnp.int32, (count, place.shape[1]), 0)
    return jnp.where(row == place, 1.0, 0.0)


def exact_dot(left, right):
    return jnp.dot(
        left, right, precision=lax.Precision.HIGHEST, preferred_element_type=F32
    )


def block_place(k, groups):
    return jnp.where(k == 0, 0, groups - k)


def first_kernel(
    groups, packed_ref, aligned_ref, padded_ref, choice_ref, east_ref, west_ref, to_a_ref, to_b_ref
):
    faces = aligned_ref.shape[0] // 2
    block_rows = padded_ref.shape[0]
    per_group = faces // groups
    slot = lax.axis_index("blk")
    odd = lax.rem(lax.axis_index("sub"), 2) == 1
    padded_ref[...] = packed_ref[2 * faces : 2 * faces + block_rows, :]
    last = 2 * faces + block_rows
    tail = packed_ref[last : last + SUBLANES, :].astype(jnp.int32)
    partner = tail[:1, :faces]
    face = lax.broadcasted_iota(jnp.int32, (1, faces), 1)
    source = jnp.zeros((1, faces), jnp.int32)
    for g in range(groups):
        inside = face - g * per_group
        source = jnp.where(
            (inside >= 0) & (inside < per_group),
            block_place(tail[1:2, g : g + 1] ^ slot, groups) * per_group + inside,
            source,
        )
    order = one_hot(partner, faces)
    east_rows = exact_dot(order, packed_ref[:faces, :])
    west_rows = packed_ref[faces : 2 * faces, :]
    aligned_ref[:faces, :] = east_rows.astype(jnp.int32)
    aligned_ref[faces:, :] = west_rows.astype(jnp.int32)
    choice_ref[...] = jnp.zeros_like(choice_ref)
    choice_ref[:1, :faces] = lax.dot_general(
        source.astype(F32).astype(BF16),
        order.astype(BF16),
        (((1,), (1,)), ((), ())),
        preferred_element_type=F32,
    )
    gather_traces(padded_ref[...], aligned_ref, 0, east_ref)
    gather_traces(padded_ref[...], aligned_ref, faces, west_ref)
    east = east_ref[...]
    west = west_ref[...]
    to_a_ref[:faces, :] = jnp.where(odd, east, west)
    to_b_ref[:faces, :] = jnp.where(odd, west, east)
    for to_ref in (to_a_ref, to_b_ref):
        to_ref[faces : faces + SUBLANES, :] = choice_ref[...]
    to_a_ref[faces + SUBLANES :, :] = jnp.where(odd, east_rows, west_rows)
    to_b_ref[faces + SUBLANES :, :] = jnp.where(odd, west_rows, east_rows)


def blocks_kernel(first, packed_ref, last_ref, *block_refs):
    slot = lax.axis_index("blk")
    per_group = last_ref.shape[1]
    for place, block_ref in enumerate(block_refs):
        k = slot ^ (len(block_refs) - place)
        kept = pl.ds(pl.multiple_of(first + k * per_group, SUBLANES), per_group)
        block_ref[:per_group, :] = packed_ref[kept, :]
        block_ref[per_group:, :] = last_ref[k]


def thirds(value, axis):
    high, rest = halves(value)
    middle, low = halves(rest)
    return jnp.concatenate([high, middle, low], axis=axis).astype(BF16)


def sum_thirds(value, axis):
    size = value.shape[axis] // 3
    parts = [lax.slice_in_dim(value, k * size, (k + 1) * size, axis=axis) for k in range(3)]
    return (parts[0] + parts[1]) + parts[2]


def pick_rows(choice, value):
    picked = lax.dot_general(
        one_hot(choice, value.shape[0]).astype(BF16),
        thirds(value, 1),
        (((0,), (0,)), ((), ())),
        preferred_element_type=F32,
    )
    return sum_thirds(picked, 1)


def put_rows(choice, value, rows):
    put = jnp.dot(
        one_hot(choice, rows).astype(BF16), thirds(value, 1), preferred_element_type=F32
    )
    return sum_thirds(put, 1)


def stiffness_kernel(size, pairs_ref, blocks_ref, field_ref, *refs):
    out_ref = refs[min(1, len(refs) - 1)]
    block_rows = field_ref.shape[0]
    count = pairs_ref.shape[1]
    rows = block_rows + count
    width = math.lcm(size, LANES)
    tiles = width // LANES
    segments = width // size
    groups = size // segments
    batch = next(k for k in (4, 3, 2, 1) if groups % k == 0)

    def place(position):
        segment = sum(jnp.where(position >= k * size, 1, 0) for k in range(1, segments))
        return segment, position - segment * size

    def lanes_of(value, index):
        slabs = [
            jnp.take_along_axis(
                value[k : k + SUBLANES, :], index, axis=1, mode="promise_in_bounds"
            )
            for k in range(0, value.shape[0], SUBLANES)
        ]
        return jnp.concatenate(slabs, axis=0)

    field = field_ref[...]
    ends = jnp.concatenate([pairs_ref[:1, :], pairs_ref[1:, :]], axis=1)
    both = pick_rows(ends, field)
    left = both[:count]
    right = jnp.concatenate([field, both[count:]], axis=0)
    lane = lax.broadcasted_iota(jnp.int32, (SUBLANES, LANES), 1)
    places = [place(lane + t * LANES) for t in range(tiles)]
    repeated = jnp.concatenate([lanes_of(right, inside) for _, inside in places], axis=1)
    segment, inside = place(lax.broadcasted_iota(jnp.int32, (width, LANES), 0))
    column = lax.broadcasted_iota(jnp.int32, (width, LANES), 1)
    add_segments = jnp.where(segment == column % segments, 1.0, 0.0).astype(BF16)
    fold = jnp.where(inside == column, 1.0, 0.0).astype(BF16)
    dof_group = lax.broadcasted_iota(jnp.int32, (rows, LANES), 1) // segments
    total = jnp.zeros((rows, LANES), F32)
    turned = jnp.zeros((count, width), F32)
    for base in range(0, groups, batch):
        stack = []
        for g in range(base, base + batch):
            stored = blocks_ref[:, g * width : (g + 1) * width]
            product = stored * repeated
            high = product.astype(BF16)
            stack += [high, (product - high.astype(F32)).astype(BF16)]
            spread = [lanes_of(left, g * segments + segment) for segment, _ in places]
            turned = turned + stored[block_rows:] * jnp.concatenate(spread, axis=1)
        sums = jnp.dot(
            jnp.concatenate(stack, axis=0), add_segments, preferred_element_type=F32
        )
        for n in range(batch):
            part = sums[2 * n * rows : 2 * (n + 1) * rows]
            total = jnp.where(dof_group == base + n, part[:rows] + part[rows:], total)
    folded = sum_thirds(
        jnp.dot(thirds(turned, 0), fold, preferred_element_type=F32), 0
    )
    out_ref[...] = total[:block_rows] + put_rows(
        ends, jnp.concatenate([total[block_rows:], folded], axis=0), block_rows
    )
    if len(refs) > 1:
        aligned_ref, _, copy_ref, east_ref, west_ref = refs
        copy_ref[...] = field
        gather_traces(field, aligned_ref, 0, east_ref)
        gather_traces(field, aligned_ref, west_ref.shape[0], west_ref)


def spread_jumps(size, rows_ref, sides, block_rows):
    dof_of = lax.broadcasted_iota(jnp.int32, (size, LANES), 0).astype(F32).astype(BF16)
    row_of = lax.broadcasted_iota(jnp.int32, (block_rows, LANES), 0).astype(F32).astype(BF16)
    none = jnp.zeros((), BF16)
    one = jnp.ones((), BF16)

    def widened(value, f, rows):
        slab = jnp.broadcast_to(value[f : f + 1, :], (2 * SUBLANES, LANES)).astype(BF16)
        return jnp.concatenate([slab] * (rows // (2 * SUBLANES)), axis=0)

    total = jnp.zeros((size, 2 * block_rows), F32)
    for side, weighted in enumerate(sides):
        for k in range(0, weighted.shape[0], SUBLANES):
            high, low = halves(weighted[k : k + SUBLANES])
            first = side * weighted.shape[0] + k
            dof, row = split(rows_ref[first : first + SUBLANES, :], block_rows)
            dof = dof.astype(F32)
            row = row.astype(F32)
            left = []
            right = []
            for f in range(SUBLANES):
                here = row_of == widened(row, f, block_rows)
                left.append(
                    jnp.concatenate(
                        [
                            jnp.where(here, widened(high, f, block_rows), none),
                            jnp.where(here, widened(low, f, block_rows), none),
                        ],
                        axis=0,
                    )
                )
                right.append(jnp.where(dof_of == widened(dof, f, size), one, none))
            total = total + lax.dot_general(
                jnp.concatenate(right, axis=1),
                jnp.concatenate(left, axis=1),
                (((1,), (1,)), ((), ())),
                preferred_element_type=F32,
            )
    total = total.T
    return total[:block_rows] + total[block_rows:]


def image_kernel(
    size,
    first,
    packed_ref,
    last_ref,
    choice_ref,
    aligned_ref,
    product_ref,
    east_ref,
    west_ref,
    from_a_ref,
    from_b_ref,
    *refs,
):
    *block_refs, image_ref, weights_east_ref, weights_west_ref, jump_ref = refs[:-2]
    next_rows_ref, last_rows_ref = refs[-2:]
    block_rows = product_ref.shape[0]
    faces = weights_east_ref.shape[0]
    per_group = last_ref.shape[1]
    slot = lax.axis_index("blk")
    odd = lax.rem(lax.axis_index("sub"), 2) == 1
    kept = pl.ds(pl.multiple_of(first + slot * per_group, SUBLANES), per_group)
    from_west = jnp.where(odd, from_b_ref[...], from_a_ref[...])
    from_east = jnp.where(odd, from_a_ref[...], from_b_ref[...])
    next_rows_ref[...] = from_east[faces + SUBLANES :].astype(jnp.int32)
    last_rows_ref[...] = from_west[faces + SUBLANES :].astype(jnp.int32)
    for row, block, part, weights_ref in (
        (choice_ref[...], packed_ref[kept, :], slice(0, per_group), weights_east_ref),
        (from_west[faces : faces + SUBLANES], last_ref[slot], slice(per_group, 2 * per_group), weights_west_ref),
    ):
        weights_ref[...] = pick_rows(
            row[:1, :faces].astype(jnp.int32),
            jnp.concatenate([block] + [block_ref[part, :] for block_ref in block_refs], axis=0),
        )
    jump_ref[...] = west_ref[...] - from_west[:faces]
    image_ref[...] = product_ref[...]
    image_ref[:, :size] = image_ref[:, :size] + spread_jumps(
        size,
        aligned_ref,
        (
            weights_east_ref[...] * (east_ref[...] - from_east[:faces]),
            weights_west_ref[...] * jump_ref[...],
        ),
        block_rows,
    )


def column_sums(value):
    return jnp.sum(value, axis=0, keepdims=True)


def sums_kernel(
    product_ref,
    weights_ref,
    own_ref,
    rows_ref,
    last_ref,
    jump_ref,
    field_ref,
    image_ref,
    sums_ref,
    arrived_ref,
):
    field = field_ref[...]
    image = image_ref[...]
    product = product_ref[...]
    gather_traces(last_ref[...], rows_ref, 0, arrived_ref)
    jump = own_ref[...] - arrived_ref[...]
    lam = weights_ref[...] * jump
    parts = [
        column_sums(field * field),
        column_sums(field * image),
        column_sums(image * image),
        column_sums(field * product) + column_sums(lam * jump_ref[...]),
        column_sums(image * product) + column_sums(lam * jump),
    ]
    parts += [jnp.zeros_like(parts[0])] * (SUBLANES - len(parts))
    whole = jnp.sum(jnp.concatenate(parts, axis=0), axis=1, keepdims=True)
    row = lax.broadcasted_iota(jnp.int32, (SUBLANES, LANES), 0)
    lane = lax.broadcasted_iota(jnp.int32, (SUBLANES, LANES), 1)
    packed = column_sums(jnp.where(lane == row, whole, 0.0))
    sums_ref[...] = jnp.broadcast_to(packed[None], sums_ref.shape)


def second_kernel(
    size,
    aligned_ref,
    product_ref,
    weights_east_ref,
    weights_west_ref,
    east_ref,
    west_ref,
    rows_ref,
    next_ref,
    from_last_ref,
    second_ref,
    from_next_ref,
):
    block_rows = product_ref.shape[0]
    gather_traces(next_ref[...], rows_ref, 0, from_next_ref)
    second_ref[...] = product_ref[...]
    second_ref[:, :size] = second_ref[:, :size] + spread_jumps(
        size,
        aligned_ref,
        [
            weights_ref[...] * (own_ref[...] - arrived_ref[...])
            for weights_ref, own_ref, arrived_ref in (
                (weights_east_ref, east_ref, from_next_ref),
                (weights_west_ref, west_ref, from_last_ref),
            )
        ],
        block_rows,
    )


def final_kernel(field_ref, image_ref, second_ref, sums_ref, solution_ref, residual_ref):
    size = solution_ref.shape[1]
    row = jnp.sum(sums_ref[...], axis=0)
    lane = lax.broadcasted_iota(jnp.int32, (1, LANES), 1)

    def entry(k):
        return jnp.sum(jnp.where(lane == k, row, 0.0), axis=1, keepdims=True)

    bb, bq, qq, bw, qw = (entry(k) for k in range(5))
    field = field_ref[:, :size]
    image = image_ref[:, :size]
    second = second_ref[:, :size]
    alpha = bb / bq
    norm = bb - alpha * (2.0 * bq - alpha * qq)
    beta = norm / bb
    grown = 1.0 + beta
    energy = grown * (grown * bq - alpha * (bw + qq)) + alpha * alpha * qw
    alpha_next = norm / energy
    residual = field - alpha * image
    direction = residual + beta * field
    moved = (image - alpha * second) + beta * image
    solution_ref[...] = alpha * field + alpha_next * direction
    residual_ref[...] = residual - alpha_next * moved


def swap(value, odd):
    count = lax.axis_size("sub")
    pairs = []
    for first in range(odd, count, 2):
        second = (first + 1) % count
        pairs += [(first, second), (second, first)]
    return lax.ppermute(value, "sub", pairs)


def from_behind(value, axis, steps):
    count = lax.axis_size(axis)
    pairs = [(source, (source + steps) % count) for source in range(count)]
    return lax.ppermute(value, axis, pairs)


def swap_slots(value, k):
    count = lax.axis_size("blk")
    return lax.ppermute(value, "blk", [(slot, slot ^ k) for slot in range(count)])


def on_device(
    right_side, stiffness, block_pairs, trace_rows, partner_face, owner_list, mortar_weight
):
    field = right_side[0, 0].T
    block_rows, size = field.shape
    blocks = stiffness[0, 0].astype(F32)
    pairs = block_pairs[0, 0]
    rows = trace_rows[0, 0]
    partner = partner_face[0, 0]
    owners = owner_list[0, 0]
    faces = partner.shape[0]
    devices = lax.axis_size("sub") * lax.axis_size("blk")

    own_weights = mortar_weight[0, 0]
    last_weights = from_behind(own_weights, "sub", 1)
    last = 2 * faces + block_rows

    def placed(value, first):
        below = last + SUBLANES + faces - first - value.shape[0]
        return jnp.pad(value, ((first, below), (0, LANES - value.shape[1])))

    indices = placed(rows, 0) + placed(partner_face[0], last) + placed(owner_list[0], last + 1)
    packed = (
        indices.astype(F32)
        + placed(field, 2 * faces)
        + placed(own_weights.reshape(faces, LANES), last + SUBLANES)
    )
    aligned, padded, choice, east, west, to_a, to_b = call(
        functools.partial(first_kernel, owners.shape[0]),
        [
            shape(2 * faces, jnp.int32),
            shape(block_rows),
            shape(SUBLANES),
            shape(faces),
            shape(faces),
            shape(2 * faces + SUBLANES),
            shape(2 * faces + SUBLANES),
        ],
        [(packed, VMEM)],
    )
    from_a = swap(to_a, 1)
    from_b = swap(to_b, 0)
    slots, per_group, _ = own_weights.shape
    blocks_to = call(
        functools.partial(blocks_kernel, last + SUBLANES),
        [shape(2 * per_group)] * (slots - 1),
        [(packed, VMEM), (last_weights, VMEM)],
        flops=1,
        moved=1,
    )
    blocks_from = [
        swap_slots(block, k) for k, block in zip(range(slots - 1, 0, -1), blocks_to)
    ]

    def stiff(vector, *ordered):
        return call(
            functools.partial(stiffness_kernel, size),
            [shape(block_rows)] * (1 + len(ordered)) + [shape(faces)] * (2 * len(ordered)),
            [(value, VMEM) for value in (pairs, blocks, vector, *ordered)],
        )

    (product,) = stiff(padded)
    image, weights_east, weights_west, jump, next_rows, last_rows = call(
        functools.partial(image_kernel, size, last + SUBLANES),
        [shape(block_rows)] + [shape(faces)] * 3 + [shape(faces, jnp.int32)] * 2,
        [
            (value, VMEM)
            for value in (
                packed,
                last_weights,
                choice,
                aligned,
                product,
                east,
                west,
                from_a,
                from_b,
                *blocks_from,
            )
        ],
    )
    from_last = from_behind(image, "sub", 1)
    product, copied, east, west = stiff(image, aligned)
    from_next = from_behind(copied, "sub", -1)
    sums, arrived = call(
        sums_kernel,
        [jax.ShapeDtypeStruct((devices, 1, LANES), F32), shape(faces)],
        [
            (value, VMEM)
            for value in (product, weights_west, west, last_rows, from_last, jump, padded, image)
        ],
    )
    (second,) = call(
        functools.partial(second_kernel, size),
        [shape(block_rows)],
        [
            (value, VMEM)
            for value in (
                aligned,
                product,
                weights_east,
                weights_west,
                east,
                west,
                next_rows,
                from_next,
                arrived,
            )
        ],
        scratch=[pltpu.VMEM((faces, LANES), F32)],
        flops=1_000_000_000,
    )
    sums = lax.all_to_all(sums, ("sub", "blk"), split_axis=0, concat_axis=0, tiled=True)
    solution_field, residual = call(
        final_kernel,
        [jax.ShapeDtypeStruct((block_rows, size), F32)] * 2,
        [(padded, VMEM), (image, VMEM), (second, VMEM), (sums, VMEM)],
    )
    return (solution_field.T[None, None], residual.T[None, None])


def solution(mesh):
    in_specs = (
        P("sub", "blk", None, None),
        P("sub", "blk", None, None),
        P("sub", "blk", None, None),
        P("sub", "blk", None, None),
        P("sub", "blk", None),
        P("sub", "blk", None),
        P("sub", "blk", None, None, None),
    )
    out_specs = (P("sub", "blk", None, None), P("sub", "blk", None, None))
    return jax.shard_map(
        on_device, mesh=mesh, in_specs=in_specs, out_specs=out_specs, check_vma=False
    )
```

```python
import functools
import math

import jax
import jax.numpy as jnp
from jax import lax
from jax.experimental import pallas as pl
from jax.experimental.pallas import tpu as pltpu
from jax.sharding import PartitionSpec as P

LANES = 128
SUBLANES = 8
VMEM = pl.BlockSpec(memory_space=pltpu.VMEM)
F32 = jnp.float32
BF16 = jnp.bfloat16


def call(body, outs, inputs, scratch=(), flops=1_000_000, moved=1_000_000):
    return pl.pallas_call(
        body,
        out_shape=outs,
        in_specs=[spec for _, spec in inputs],
        out_specs=[VMEM] * len(outs),
        scratch_shapes=list(scratch),
        compiler_params=pltpu.CompilerParams(vmem_limit_bytes=32 * 1024 * 1024),
        cost_estimate=pl.CostEstimate(
            flops=flops, bytes_accessed=moved, transcendentals=0
        ),
    )(*[value for value, _ in inputs])


def shape(rows, dtype=F32):
    return jax.ShapeDtypeStruct((rows, LANES), dtype)


def halves(value):
    high = value.astype(BF16).astype(F32)
    return high, value - high


def gather_traces(field, rows_ref, rows_first, target):
    block_rows = field.shape[0]
    spread = [
        jnp.broadcast_to(field[i : i + 1, :], (SUBLANES, LANES)) for i in range(block_rows)
    ]
    for k in range(target.shape[0] // SUBLANES):
        index = rows_ref[rows_first + k * SUBLANES : rows_first + (k + 1) * SUBLANES, :]
        dof, row = split(index, block_rows)
        taken = jnp.zeros((SUBLANES, LANES), F32)
        for i in range(block_rows):
            here = jnp.take_along_axis(spread[i], dof, axis=1, mode="promise_in_bounds")
            taken = jnp.where(row == i, here, taken)
        target[k * SUBLANES : (k + 1) * SUBLANES, :] = taken


def tile(k):
    return pl.ds(pl.multiple_of(k * SUBLANES, SUBLANES), SUBLANES)


def split(index, block_rows):
    if block_rows & (block_rows - 1) == 0:
        shift = block_rows.bit_length() - 1
        return index >> shift, index & (block_rows - 1)
    return lax.div(index, block_rows), lax.rem(index, block_rows)


def one_hot(place, count):
    row = lax.broadcasted_iota(jnp.int32, (count, place.shape[1]), 0)
    return jnp.where(row == place, 1.0, 0.0)


def exact_dot(left, right):
    return jnp.dot(
        left, right, precision=lax.Precision.HIGHEST, preferred_element_type=F32
    )


def block_place(k, groups):
    return jnp.where(k == 0, 0, groups - k)


def first_kernel(
    groups, packed_ref, aligned_ref, padded_ref, choice_ref, east_ref, west_ref, to_a_ref, to_b_ref
):
    faces = aligned_ref.shape[0] // 2
    block_rows = padded_ref.shape[0]
    per_group = faces // groups
    slot = lax.axis_index("blk")
    odd = lax.rem(lax.axis_index("sub"), 2) == 1
    padded_ref[...] = packed_ref[2 * faces : 2 * faces + block_rows, :]
    last = 2 * faces + block_rows
    tail = packed_ref[last : last + SUBLANES, :].astype(jnp.int32)
    partner = tail[:1, :faces]
    face = lax.broadcasted_iota(jnp.int32, (1, faces), 1)
    source = jnp.zeros((1, faces), jnp.int32)
    for g in range(groups):
        inside = face - g * per_group
        source = jnp.where(
            (inside >= 0) & (inside < per_group),
            block_place(tail[1:2, g : g + 1] ^ slot, groups) * per_group + inside,
            source,
        )
    order = one_hot(partner, faces)
    east_rows = exact_dot(order, packed_ref[:faces, :])
    west_rows = packed_ref[faces : 2 * faces, :]
    aligned_ref[:faces, :] = east_rows.astype(jnp.int32)
    aligned_ref[faces:, :] = west_rows.astype(jnp.int32)
    choice_ref[...] = jnp.zeros_like(choice_ref)
    choice_ref[:1, :faces] = lax.dot_general(
        source.astype(F32).astype(BF16),
        order.astype(BF16),
        (((1,), (1,)), ((), ())),
        preferred_element_type=F32,
    )
    gather_traces(padded_ref[...], aligned_ref, 0, east_ref)
    gather_traces(padded_ref[...], aligned_ref, faces, west_ref)
    east = east_ref[...]
    west = west_ref[...]
    to_a_ref[:faces, :] = jnp.where(odd, east, west)
    to_b_ref[:faces, :] = jnp.where(odd, west, east)
    for to_ref in (to_a_ref, to_b_ref):
        to_ref[faces : faces + SUBLANES, :] = choice_ref[...]
    to_a_ref[faces + SUBLANES :, :] = jnp.where(odd, east_rows, west_rows)
    to_b_ref[faces + SUBLANES :, :] = jnp.where(odd, west_rows, east_rows)


def blocks_kernel(first, packed_ref, last_ref, *block_refs):
    slot = lax.axis_index("blk")
    per_group = last_ref.shape[1]
    for place, block_ref in enumerate(block_refs):
        k = slot ^ (len(block_refs) - place)
        kept = pl.ds(pl.multiple_of(first + k * per_group, SUBLANES), per_group)
        block_ref[:per_group, :] = packed_ref[kept, :]
        block_ref[per_group:, :] = last_ref[k]


def thirds(value, axis):
    high, rest = halves(value)
    middle, low = halves(rest)
    return jnp.concatenate([high, middle, low], axis=axis).astype(BF16)


def sum_thirds(value, axis):
    size = value.shape[axis] // 3
    parts = [lax.slice_in_dim(value, k * size, (k + 1) * size, axis=axis) for k in range(3)]
    return (parts[0] + parts[1]) + parts[2]


def pick_rows(choice, value):
    picked = lax.dot_general(
        one_hot(choice, value.shape[0]).astype(BF16),
        thirds(value, 1),
        (((0,), (0,)), ((), ())),
        preferred_element_type=F32,
    )
    return sum_thirds(picked, 1)


def put_rows(choice, value, rows):
    put = jnp.dot(
        one_hot(choice, rows).astype(BF16), thirds(value, 1), preferred_element_type=F32
    )
    return sum_thirds(put, 1)


def stiffness_kernel(size, pairs_ref, blocks_ref, field_ref, *refs):
    out_ref = refs[min(1, len(refs) - 1)]
    block_rows = field_ref.shape[0]
    count = pairs_ref.shape[1]
    rows = block_rows + count
    width = math.lcm(size, LANES)
    tiles = width // LANES
    segments = width // size
    groups = size // segments
    batch = next(k for k in (4, 3, 2, 1) if groups % k == 0)

    def place(position):
        segment = sum(jnp.where(position >= k * size, 1, 0) for k in range(1, segments))
        return segment, position - segment * size

    def lanes_of(value, index):
        slabs = [
            jnp.take_along_axis(
                value[k : k + SUBLANES, :], index, axis=1, mode="promise_in_bounds"
            )
            for k in range(0, value.shape[0], SUBLANES)
        ]
        return jnp.concatenate(slabs, axis=0)

    field = field_ref[...]
    ends = jnp.concatenate([pairs_ref[:1, :], pairs_ref[1:, :]], axis=1)
    both = pick_rows(ends, field)
    left = both[:count]
    right = jnp.concatenate([field, both[count:]], axis=0)
    lane = lax.broadcasted_iota(jnp.int32, (SUBLANES, LANES), 1)
    places = [place(lane + t * LANES) for t in range(tiles)]
    repeated = jnp.concatenate([lanes_of(right, inside) for _, inside in places], axis=1)
    segment, inside = place(lax.broadcasted_iota(jnp.int32, (width, LANES), 0))
    column = lax.broadcasted_iota(jnp.int32, (width, LANES), 1)
    add_segments = jnp.where(segment == column % segments, 1.0, 0.0).astype(BF16)
    fold = jnp.where(inside == column, 1.0, 0.0).astype(BF16)
    dof_group = lax.broadcasted_iota(jnp.int32, (rows, LANES), 1) // segments
    total = jnp.zeros((rows, LANES), F32)
    turned = jnp.zeros((count, width), F32)
    for base in range(0, groups, batch):
        stack = []
        for g in range(base, base + batch):
            stored = blocks_ref[:, g * width : (g + 1) * width]
            product = stored * repeated
            high = product.astype(BF16)
            stack += [high, (product - high.astype(F32)).astype(BF16)]
            spread = [lanes_of(left, g * segments + segment) for segment, _ in places]
            turned = turned + stored[block_rows:] * jnp.concatenate(spread, axis=1)
        sums = jnp.dot(
            jnp.concatenate(stack, axis=0), add_segments, preferred_element_type=F32
        )
        for n in range(batch):
            part = sums[2 * n * rows : 2 * (n + 1) * rows]
            total = jnp.where(dof_group == base + n, part[:rows] + part[rows:], total)
    folded = sum_thirds(
        jnp.dot(thirds(turned, 0), fold, preferred_element_type=F32), 0
    )
    out_ref[...] = total[:block_rows] + put_rows(
        ends, jnp.concatenate([total[block_rows:], folded], axis=0), block_rows
    )
    if len(refs) > 1:
        aligned_ref, _, copy_ref, west_ref = refs
        copy_ref[...] = field
        gather_traces(field, aligned_ref, west_ref.shape[0], west_ref)


def spread_jumps(size, rows_ref, sides, block_rows):
    dof_of = lax.broadcasted_iota(jnp.int32, (size, LANES), 0).astype(F32).astype(BF16)
    row_of = lax.broadcasted_iota(jnp.int32, (block_rows, LANES), 0).astype(F32).astype(BF16)
    none = jnp.zeros((), BF16)
    one = jnp.ones((), BF16)

    def widened(value, f, rows):
        slab = jnp.broadcast_to(value[f : f + 1, :], (2 * SUBLANES, LANES)).astype(BF16)
        return jnp.concatenate([slab] * (rows // (2 * SUBLANES)), axis=0)

    total = jnp.zeros((size, 2 * block_rows), F32)
    for side, weighted in enumerate(sides):
        for k in range(0, weighted.shape[0], SUBLANES):
            high, low = halves(weighted[k : k + SUBLANES])
            first = side * weighted.shape[0] + k
            dof, row = split(rows_ref[first : first + SUBLANES, :], block_rows)
            dof = dof.astype(F32)
            row = row.astype(F32)
            left = []
            right = []
            for f in range(SUBLANES):
                here = row_of == widened(row, f, block_rows)
                left.append(
                    jnp.concatenate(
                        [
                            jnp.where(here, widened(high, f, block_rows), none),
                            jnp.where(here, widened(low, f, block_rows), none),
                        ],
                        axis=0,
                    )
                )
                right.append(jnp.where(dof_of == widened(dof, f, size), one, none))
            total = total + lax.dot_general(
                jnp.concatenate(right, axis=1),
                jnp.concatenate(left, axis=1),
                (((1,), (1,)), ((), ())),
                preferred_element_type=F32,
            )
    total = total.T
    return total[:block_rows] + total[block_rows:]


def image_kernel(
    size,
    first,
    packed_ref,
    last_ref,
    choice_ref,
    aligned_ref,
    product_ref,
    east_ref,
    west_ref,
    from_a_ref,
    from_b_ref,
    *refs,
):
    *block_refs, image_ref, weights_east_ref, weights_west_ref, jump_ref = refs[:-2]
    next_rows_ref, last_rows_ref = refs[-2:]
    block_rows = product_ref.shape[0]
    faces = weights_east_ref.shape[0]
    per_group = last_ref.shape[1]
    slot = lax.axis_index("blk")
    odd = lax.rem(lax.axis_index("sub"), 2) == 1
    kept = pl.ds(pl.multiple_of(first + slot * per_group, SUBLANES), per_group)
    from_west = jnp.where(odd, from_b_ref[...], from_a_ref[...])
    from_east = jnp.where(odd, from_a_ref[...], from_b_ref[...])
    next_rows_ref[...] = from_east[faces + SUBLANES :].astype(jnp.int32)
    last_rows_ref[...] = from_west[faces + SUBLANES :].astype(jnp.int32)
    for row, block, part, weights_ref in (
        (choice_ref[...], packed_ref[kept, :], slice(0, per_group), weights_east_ref),
        (from_west[faces : faces + SUBLANES], last_ref[slot], slice(per_group, 2 * per_group), weights_west_ref),
    ):
        weights_ref[...] = pick_rows(
            row[:1, :faces].astype(jnp.int32),
            jnp.concatenate([block] + [block_ref[part, :] for block_ref in block_refs], axis=0),
        )
    jump_ref[...] = west_ref[...] - from_west[:faces]
    image_ref[...] = product_ref[...]
    image_ref[:, :size] = image_ref[:, :size] + spread_jumps(
        size,
        aligned_ref,
        (
            weights_east_ref[...] * (east_ref[...] - from_east[:faces]),
            weights_west_ref[...] * jump_ref[...],
        ),
        block_rows,
    )


def column_sums(value):
    return jnp.sum(value, axis=0, keepdims=True)


def sums_kernel(
    product_ref,
    weights_ref,
    own_ref,
    rows_ref,
    last_ref,
    jump_ref,
    field_ref,
    image_ref,
    sums_ref,
    arrived_ref,
):
    field = field_ref[...]
    image = image_ref[...]
    product = product_ref[...]
    gather_traces(last_ref[...], rows_ref, 0, arrived_ref)
    jump = own_ref[...] - arrived_ref[...]
    lam = weights_ref[...] * jump
    parts = [
        column_sums(field * field),
        column_sums(field * image),
        column_sums(image * image),
        column_sums(field * product) + column_sums(lam * jump_ref[...]),
        column_sums(image * product) + column_sums(lam * jump),
    ]
    parts += [jnp.zeros_like(parts[0])] * (SUBLANES - len(parts))
    whole = jnp.sum(jnp.concatenate(parts, axis=0), axis=1, keepdims=True)
    row = lax.broadcasted_iota(jnp.int32, (SUBLANES, LANES), 0)
    lane = lax.broadcasted_iota(jnp.int32, (SUBLANES, LANES), 1)
    packed = column_sums(jnp.where(lane == row, whole, 0.0))
    sums_ref[...] = jnp.broadcast_to(packed[None], sums_ref.shape)


def second_kernel(
    size,
    aligned_ref,
    product_ref,
    weights_east_ref,
    weights_west_ref,
    image_ref,
    west_ref,
    rows_ref,
    next_ref,
    from_last_ref,
    second_ref,
    east_ref,
    from_next_ref,
):
    block_rows = product_ref.shape[0]
    gather_traces(image_ref[...], aligned_ref, 0, east_ref)
    gather_traces(next_ref[...], rows_ref, 0, from_next_ref)
    second_ref[...] = product_ref[...]
    second_ref[:, :size] = second_ref[:, :size] + spread_jumps(
        size,
        aligned_ref,
        [
            weights_ref[...] * (own_ref[...] - arrived_ref[...])
            for weights_ref, own_ref, arrived_ref in (
                (weights_east_ref, east_ref, from_next_ref),
                (weights_west_ref, west_ref, from_last_ref),
            )
        ],
        block_rows,
    )


def final_kernel(field_ref, image_ref, second_ref, sums_ref, solution_ref, residual_ref):
    size = solution_ref.shape[1]
    row = jnp.broadcast_to(jnp.sum(sums_ref[...], axis=0), (SUBLANES, LANES))

    def entry(k):
        place = jnp.full((SUBLANES, LANES), k, jnp.int32)
        return jnp.take_along_axis(row, place, axis=1, mode="promise_in_bounds")[:1, :size]

    bb, bq, qq, bw, qw = (entry(k) for k in range(5))
    field = field_ref[:, :size]
    image = image_ref[:, :size]
    second = second_ref[:, :size]
    alpha = bb / bq
    norm = bb - alpha * (2.0 * bq - alpha * qq)
    beta = norm / bb
    grown = 1.0 + beta
    energy = grown * (grown * bq - alpha * (bw + qq)) + alpha * alpha * qw
    alpha_next = norm / energy
    residual = field - alpha * image
    direction = residual + beta * field
    moved = (image - alpha * second) + beta * image
    solution_ref[...] = alpha * field + alpha_next * direction
    residual_ref[...] = residual - alpha_next * moved


def swap(value, odd):
    count = lax.axis_size("sub")
    pairs = []
    for first in range(odd, count, 2):
        second = (first + 1) % count
        pairs += [(first, second), (second, first)]
    return lax.ppermute(value, "sub", pairs)


def from_behind(value, axis, steps):
    count = lax.axis_size(axis)
    pairs = [(source, (source + steps) % count) for source in range(count)]
    return lax.ppermute(value, axis, pairs)


def swap_slots(value, k):
    count = lax.axis_size("blk")
    return lax.ppermute(value, "blk", [(slot, slot ^ k) for slot in range(count)])


def on_device(
    right_side, stiffness, block_pairs, trace_rows, partner_face, owner_list, mortar_weight
):
    field = right_side[0, 0].T
    block_rows, size = field.shape
    blocks = stiffness[0, 0].astype(F32)
    pairs = block_pairs[0, 0]
    rows = trace_rows[0, 0]
    partner = partner_face[0, 0]
    owners = owner_list[0, 0]
    faces = partner.shape[0]
    devices = lax.axis_size("sub") * lax.axis_size("blk")

    own_weights = mortar_weight[0, 0]
    last_weights = from_behind(own_weights, "sub", 1)
    last = 2 * faces + block_rows

    def placed(value, first):
        below = last + SUBLANES + faces - first - value.shape[0]
        return jnp.pad(value, ((first, below), (0, LANES - value.shape[1])))

    indices = placed(rows, 0) + placed(partner_face[0], last) + placed(owner_list[0], last + 1)
    packed = (
        indices.astype(F32)
        + placed(field, 2 * faces)
        + placed(own_weights.reshape(faces, LANES), last + SUBLANES)
    )
    aligned, padded, choice, east, west, to_a, to_b = call(
        functools.partial(first_kernel, owners.shape[0]),
        [
            shape(2 * faces, jnp.int32),
            shape(block_rows),
            shape(SUBLANES),
            shape(faces),
            shape(faces),
            shape(2 * faces + SUBLANES),
            shape(2 * faces + SUBLANES),
        ],
        [(packed, VMEM)],
    )
    from_a = swap(to_a, 1)
    from_b = swap(to_b, 0)
    slots, per_group, _ = own_weights.shape
    blocks_to = call(
        functools.partial(blocks_kernel, last + SUBLANES),
        [shape(2 * per_group)] * (slots - 1),
        [(packed, VMEM), (last_weights, VMEM)],
        flops=1,
        moved=1,
    )
    blocks_from = [
        swap_slots(block, k) for k, block in zip(range(slots - 1, 0, -1), blocks_to)
    ]

    def stiff(vector, *ordered):
        return call(
            functools.partial(stiffness_kernel, size),
            [shape(block_rows)] * (1 + len(ordered)) + [shape(faces)] * len(ordered),
            [(value, VMEM) for value in (pairs, blocks, vector, *ordered)],
        )

    (product,) = stiff(padded)
    image, weights_east, weights_west, jump, next_rows, last_rows = call(
        functools.partial(image_kernel, size, last + SUBLANES),
        [shape(block_rows)] + [shape(faces)] * 3 + [shape(faces, jnp.int32)] * 2,
        [
            (value, VMEM)
            for value in (
                packed,
                last_weights,
                choice,
                aligned,
                product,
                east,
                west,
                from_a,
                from_b,
                *blocks_from,
            )
        ],
    )
    from_last = from_behind(image, "sub", 1)
    product, copied, west = stiff(image, aligned)
    from_next = from_behind(copied, "sub", -1)
    sums, arrived = call(
        sums_kernel,
        [jax.ShapeDtypeStruct((devices, 1, LANES), F32), shape(faces)],
        [
            (value, VMEM)
            for value in (product, weights_west, west, last_rows, from_last, jump, padded, image)
        ],
    )
    (second,) = call(
        functools.partial(second_kernel, size),
        [shape(block_rows)],
        [
            (value, VMEM)
            for value in (
                aligned,
                product,
                weights_east,
                weights_west,
                image,
                west,
                next_rows,
                from_next,
                arrived,
            )
        ],
        scratch=[pltpu.VMEM((faces, LANES), F32)] * 2,
        flops=1_000_000_000,
    )
    sums = lax.all_to_all(sums, ("sub", "blk"), split_axis=0, concat_axis=0, tiled=True)
    solution_field, residual = call(
        final_kernel,
        [jax.ShapeDtypeStruct((block_rows, size), F32)] * 2,
        [(padded, VMEM), (image, VMEM), (second, VMEM), (sums, VMEM)],
    )
    return (solution_field.T[None, None], residual.T[None, None])


def solution(mesh):
    in_specs = (
        P("sub", "blk", None, None),
        P("sub", "blk", None, None),
        P("sub", "blk", None, None),
        P("sub", "blk", None, None),
        P("sub", "blk", None),
        P("sub", "blk", None),
        P("sub", "blk", None, None, None),
    )
    out_specs = (P("sub", "blk", None, None), P("sub", "blk", None, None))
    return jax.shard_map(
        on_device, mesh=mesh, in_specs=in_specs, out_specs=out_specs, check_vma=False
    )
```

```python
import functools
import math

import jax
import jax.numpy as jnp
from jax import lax
from jax.experimental import pallas as pl
from jax.experimental.pallas import tpu as pltpu
from jax.sharding import PartitionSpec as P

LANES = 128
SUBLANES = 8
VMEM = pl.BlockSpec(memory_space=pltpu.VMEM)
MARK = 5
LARGE = 2.0**40
SMALL = 2.0**-40
SHRINK = 2.0**-60
F32 = jnp.float32
BF16 = jnp.bfloat16


def call(body, outs, inputs, scratch=(), flops=1_000_000, moved=1_000_000):
    return pl.pallas_call(
        body,
        out_shape=outs,
        in_specs=[spec for _, spec in inputs],
        out_specs=[VMEM] * len(outs),
        scratch_shapes=list(scratch),
        compiler_params=pltpu.CompilerParams(vmem_limit_bytes=32 * 1024 * 1024),
        cost_estimate=pl.CostEstimate(
            flops=flops, bytes_accessed=moved, transcendentals=0
        ),
    )(*[value for value, _ in inputs])


def shape(rows, dtype=F32):
    return jax.ShapeDtypeStruct((rows, LANES), dtype)


def halves(value):
    high = value.astype(BF16).astype(F32)
    return high, value - high


def gather_traces(field, rows_ref, rows_first, target):
    block_rows = field.shape[0]
    spread = [
        jnp.broadcast_to(field[i : i + 1, :], (SUBLANES, LANES)) for i in range(block_rows)
    ]
    for k in range(target.shape[0] // SUBLANES):
        index = rows_ref[rows_first + k * SUBLANES : rows_first + (k + 1) * SUBLANES, :]
        dof, row = split(index, block_rows)
        taken = jnp.zeros((SUBLANES, LANES), F32)
        for i in range(block_rows):
            here = jnp.take_along_axis(spread[i], dof, axis=1, mode="promise_in_bounds")
            taken = jnp.where(row == i, here, taken)
        target[k * SUBLANES : (k + 1) * SUBLANES, :] = taken


def tile(k):
    return pl.ds(pl.multiple_of(k * SUBLANES, SUBLANES), SUBLANES)


def split(index, block_rows):
    if block_rows & (block_rows - 1) == 0:
        shift = block_rows.bit_length() - 1
        return index >> shift, index & (block_rows - 1)
    return lax.div(index, block_rows), lax.rem(index, block_rows)


def one_hot(place, count):
    row = lax.broadcasted_iota(jnp.int32, (count, place.shape[1]), 0)
    return jnp.where(row == place, 1.0, 0.0)


def exact_dot(left, right):
    return jnp.dot(
        left, right, precision=lax.Precision.HIGHEST, preferred_element_type=F32
    )


def block_place(k, groups):
    return jnp.where(k == 0, 0, groups - k)


def first_kernel(
    groups, packed_ref, aligned_ref, padded_ref, choice_ref, east_ref, west_ref, to_a_ref, to_b_ref
):
    faces = aligned_ref.shape[0] // 2
    block_rows = padded_ref.shape[0]
    per_group = faces // groups
    slot = lax.axis_index("blk")
    odd = lax.rem(lax.axis_index("sub"), 2) == 1
    padded_ref[...] = packed_ref[2 * faces : 2 * faces + block_rows, :]
    last = 2 * faces + block_rows
    tail = packed_ref[last : last + SUBLANES, :].astype(jnp.int32)
    partner = tail[:1, :faces]
    face = lax.broadcasted_iota(jnp.int32, (1, faces), 1)
    source = jnp.zeros((1, faces), jnp.int32)
    for g in range(groups):
        inside = face - g * per_group
        source = jnp.where(
            (inside >= 0) & (inside < per_group),
            block_place(tail[1:2, g : g + 1] ^ slot, groups) * per_group + inside,
            source,
        )
    order = one_hot(partner, faces)
    east_rows = exact_dot(order, packed_ref[:faces, :])
    west_rows = packed_ref[faces : 2 * faces, :]
    aligned_ref[:faces, :] = east_rows.astype(jnp.int32)
    aligned_ref[faces:, :] = west_rows.astype(jnp.int32)
    choice_ref[...] = jnp.zeros_like(choice_ref)
    choice_ref[:1, :faces] = lax.dot_general(
        source.astype(F32).astype(BF16),
        order.astype(BF16),
        (((1,), (1,)), ((), ())),
        preferred_element_type=F32,
    )
    gather_traces(padded_ref[...], aligned_ref, 0, east_ref)
    gather_traces(padded_ref[...], aligned_ref, faces, west_ref)
    east = east_ref[...]
    west = west_ref[...]
    to_a_ref[:faces, :] = jnp.where(odd, east, west)
    to_b_ref[:faces, :] = jnp.where(odd, west, east)
    for to_ref in (to_a_ref, to_b_ref):
        to_ref[faces : faces + SUBLANES, :] = choice_ref[...]
    to_a_ref[faces + SUBLANES :, :] = jnp.where(odd, east_rows, west_rows)
    to_b_ref[faces + SUBLANES :, :] = jnp.where(odd, west_rows, east_rows)


def blocks_kernel(first, packed_ref, last_ref, *block_refs):
    slot = lax.axis_index("blk")
    per_group = last_ref.shape[1]
    for place, block_ref in enumerate(block_refs):
        k = slot ^ (len(block_refs) - place)
        kept = pl.ds(pl.multiple_of(first + k * per_group, SUBLANES), per_group)
        block_ref[:per_group, :] = packed_ref[kept, :]
        block_ref[per_group:, :] = last_ref[k]


def thirds(value, axis):
    high, rest = halves(value)
    middle, low = halves(rest)
    return jnp.concatenate([high, middle, low], axis=axis).astype(BF16)


def sum_thirds(value, axis):
    size = value.shape[axis] // 3
    parts = [lax.slice_in_dim(value, k * size, (k + 1) * size, axis=axis) for k in range(3)]
    return (parts[0] + parts[1]) + parts[2]


def pick_rows(choice, value):
    picked = lax.dot_general(
        one_hot(choice, value.shape[0]).astype(BF16),
        thirds(value, 1),
        (((0,), (0,)), ((), ())),
        preferred_element_type=F32,
    )
    return sum_thirds(picked, 1)


def put_rows(choice, value, rows):
    put = jnp.dot(
        one_hot(choice, rows).astype(BF16), thirds(value, 1), preferred_element_type=F32
    )
    return sum_thirds(put, 1)


def stiffness_kernel(size, pairs_ref, blocks_ref, field_ref, *refs):
    out_ref = refs[min(1, len(refs) - 1)]
    block_rows = field_ref.shape[0]
    count = pairs_ref.shape[1]
    rows = block_rows + count
    width = math.lcm(size, LANES)
    tiles = width // LANES
    segments = width // size
    groups = size // segments
    batch = next(k for k in (4, 3, 2, 1) if groups % k == 0)

    def place(position):
        segment = sum(jnp.where(position >= k * size, 1, 0) for k in range(1, segments))
        return segment, position - segment * size

    def lanes_of(value, index):
        slabs = [
            jnp.take_along_axis(
                value[k : k + SUBLANES, :], index, axis=1, mode="promise_in_bounds"
            )
            for k in range(0, value.shape[0], SUBLANES)
        ]
        return jnp.concatenate(slabs, axis=0)

    field = field_ref[...]
    ends = jnp.concatenate([pairs_ref[:1, :], pairs_ref[1:, :]], axis=1)
    both = pick_rows(ends, field)
    left = both[:count]
    right = jnp.concatenate([field, both[count:]], axis=0)
    lane = lax.broadcasted_iota(jnp.int32, (SUBLANES, LANES), 1)
    places = [place(lane + t * LANES) for t in range(tiles)]
    repeated = jnp.concatenate([lanes_of(right, inside) for _, inside in places], axis=1)
    segment, inside = place(lax.broadcasted_iota(jnp.int32, (width, LANES), 0))
    column = lax.broadcasted_iota(jnp.int32, (width, LANES), 1)
    add_segments = jnp.where(segment == column % segments, 1.0, 0.0).astype(BF16)
    fold = jnp.where(inside == column, 1.0, 0.0).astype(BF16)
    dof_group = lax.broadcasted_iota(jnp.int32, (rows, LANES), 1) // segments
    total = jnp.zeros((rows, LANES), F32)
    turned = jnp.zeros((count, width), F32)
    for base in range(0, groups, batch):
        stack = []
        for g in range(base, base + batch):
            stored = blocks_ref[:, g * width : (g + 1) * width]
            product = stored * repeated
            high = product.astype(BF16)
            stack += [high, (product - high.astype(F32)).astype(BF16)]
            spread = [lanes_of(left, g * segments + segment) for segment, _ in places]
            turned = turned + stored[block_rows:] * jnp.concatenate(spread, axis=1)
        sums = jnp.dot(
            jnp.concatenate(stack, axis=0), add_segments, preferred_element_type=F32
        )
        for n in range(batch):
            part = sums[2 * n * rows : 2 * (n + 1) * rows]
            total = jnp.where(dof_group == base + n, part[:rows] + part[rows:], total)
    folded = sum_thirds(
        jnp.dot(thirds(turned, 0), fold, preferred_element_type=F32), 0
    )
    out_ref[...] = total[:block_rows] + put_rows(
        ends, jnp.concatenate([total[block_rows:], folded], axis=0), block_rows
    )
    if len(refs) > 1:
        aligned_ref, _, copy_ref, west_ref = refs
        copy_ref[...] = field
        gather_traces(field, aligned_ref, west_ref.shape[0], west_ref)


def spread_jumps(size, rows_ref, sides, block_rows):
    dof_of = lax.broadcasted_iota(jnp.int32, (size, LANES), 0).astype(F32).astype(BF16)
    row_of = lax.broadcasted_iota(jnp.int32, (block_rows, LANES), 0).astype(F32).astype(BF16)
    none = jnp.zeros((), BF16)
    one = jnp.ones((), BF16)

    def widened(value, f, rows):
        slab = jnp.broadcast_to(value[f : f + 1, :], (2 * SUBLANES, LANES)).astype(BF16)
        return jnp.concatenate([slab] * (rows // (2 * SUBLANES)), axis=0)

    total = jnp.zeros((size, 2 * block_rows), F32)
    for side, weighted in enumerate(sides):
        for k in range(0, weighted.shape[0], SUBLANES):
            high, low = halves(weighted[k : k + SUBLANES])
            first = side * weighted.shape[0] + k
            dof, row = split(rows_ref[first : first + SUBLANES, :], block_rows)
            dof = dof.astype(F32)
            row = row.astype(F32)
            left = []
            right = []
            for f in range(SUBLANES):
                here = row_of == widened(row, f, block_rows)
                left.append(
                    jnp.concatenate(
                        [
                            jnp.where(here, widened(high, f, block_rows), none),
                            jnp.where(here, widened(low, f, block_rows), none),
                        ],
                        axis=0,
                    )
                )
                right.append(jnp.where(dof_of == widened(dof, f, size), one, none))
            total = total + lax.dot_general(
                jnp.concatenate(right, axis=1),
                jnp.concatenate(left, axis=1),
                (((1,), (1,)), ((), ())),
                preferred_element_type=F32,
            )
    total = total.T
    return total[:block_rows] + total[block_rows:]


def image_kernel(
    size,
    first,
    packed_ref,
    last_ref,
    choice_ref,
    aligned_ref,
    product_ref,
    east_ref,
    west_ref,
    from_a_ref,
    from_b_ref,
    *refs,
):
    *block_refs, image_ref, weights_east_ref, weights_west_ref, jump_ref = refs[:-2]
    next_rows_ref, last_rows_ref = refs[-2:]
    block_rows = product_ref.shape[0]
    faces = weights_east_ref.shape[0]
    per_group = last_ref.shape[1]
    slot = lax.axis_index("blk")
    odd = lax.rem(lax.axis_index("sub"), 2) == 1
    kept = pl.ds(pl.multiple_of(first + slot * per_group, SUBLANES), per_group)
    from_west = jnp.where(odd, from_b_ref[...], from_a_ref[...])
    from_east = jnp.where(odd, from_a_ref[...], from_b_ref[...])
    next_rows_ref[...] = from_east[faces + SUBLANES :].astype(jnp.int32)
    last_rows_ref[...] = from_west[faces + SUBLANES :].astype(jnp.int32)
    for row, block, part, weights_ref in (
        (choice_ref[...], packed_ref[kept, :], slice(0, per_group), weights_east_ref),
        (from_west[faces : faces + SUBLANES], last_ref[slot], slice(per_group, 2 * per_group), weights_west_ref),
    ):
        weights_ref[...] = pick_rows(
            row[:1, :faces].astype(jnp.int32),
            jnp.concatenate([block] + [block_ref[part, :] for block_ref in block_refs], axis=0),
        )
    jump_ref[...] = west_ref[...] - from_west[:faces]
    image_ref[...] = product_ref[...]
    image_ref[:, :size] = image_ref[:, :size] + spread_jumps(
        size,
        aligned_ref,
        (
            weights_east_ref[...] * (east_ref[...] - from_east[:faces]),
            weights_west_ref[...] * jump_ref[...],
        ),
        block_rows,
    )


def column_sums(value):
    return jnp.sum(value, axis=0, keepdims=True)


def sums_kernel(
    product_ref,
    weights_ref,
    own_ref,
    rows_ref,
    last_ref,
    jump_ref,
    field_ref,
    image_ref,
    sums_ref,
    arrived_ref,
):
    gather_traces(last_ref[...], rows_ref, 0, arrived_ref)
    largest = jnp.maximum(jnp.abs(field_ref[...]), jnp.abs(image_ref[...]))
    for value in (arrived_ref[...], jump_ref[...]):
        value = jnp.abs(value)
        for k in range(0, value.shape[0], largest.shape[0]):
            largest = jnp.maximum(largest, value[k : k + largest.shape[0]])
    largest = jnp.max(jnp.max(largest, axis=0, keepdims=True), axis=1, keepdims=True)
    level = jnp.where(largest > LARGE, 0, jnp.where(largest < SMALL, 2, 1))
    scale = jnp.where(largest > LARGE, SHRINK, jnp.where(largest < SMALL, 1.0 / SHRINK, 1.0))
    field = field_ref[...] * scale
    image = image_ref[...] * scale
    product = product_ref[...] * scale
    jump = own_ref[...] * scale - arrived_ref[...] * scale
    lam = weights_ref[...] * jump
    parts = [
        column_sums(field * field),
        column_sums(field * image),
        column_sums(image * image),
        column_sums(field * product) + column_sums(lam * (jump_ref[...] * scale)),
        column_sums(image * product) + column_sums(lam * jump),
    ]
    parts += [jnp.zeros_like(parts[0])] * (SUBLANES - len(parts))
    whole = jnp.sum(jnp.concatenate(parts, axis=0), axis=1, keepdims=True)
    row = lax.broadcasted_iota(jnp.int32, (SUBLANES, LANES), 0)
    lane = lax.broadcasted_iota(jnp.int32, (SUBLANES, LANES), 1)
    whole = jnp.where(row == MARK, 1.0, whole)
    packed = column_sums(jnp.where(lane == row + SUBLANES * level, whole, 0.0))
    sums_ref[...] = jnp.broadcast_to(packed[None], sums_ref.shape)


def second_kernel(
    size,
    aligned_ref,
    product_ref,
    weights_east_ref,
    weights_west_ref,
    image_ref,
    west_ref,
    rows_ref,
    next_ref,
    from_last_ref,
    second_ref,
    east_ref,
    from_next_ref,
):
    block_rows = product_ref.shape[0]
    gather_traces(image_ref[...], aligned_ref, 0, east_ref)
    gather_traces(next_ref[...], rows_ref, 0, from_next_ref)
    second_ref[...] = product_ref[...]
    second_ref[:, :size] = second_ref[:, :size] + spread_jumps(
        size,
        aligned_ref,
        [
            weights_ref[...] * (own_ref[...] - arrived_ref[...])
            for weights_ref, own_ref, arrived_ref in (
                (weights_east_ref, east_ref, from_next_ref),
                (weights_west_ref, west_ref, from_last_ref),
            )
        ],
        block_rows,
    )


def final_kernel(field_ref, image_ref, second_ref, sums_ref, solution_ref, residual_ref):
    size = solution_ref.shape[1]
    row = jnp.broadcast_to(jnp.sum(sums_ref[...], axis=0), (SUBLANES, LANES))

    def lane(k):
        place = jnp.full((SUBLANES, LANES), k, jnp.int32)
        return jnp.take_along_axis(row, place, axis=1, mode="promise_in_bounds")[:1, :size]

    large, plain = (lane(SUBLANES * level + MARK) > 0.0 for level in (0, 1))

    def entry(k):
        sums = [lane(SUBLANES * level + k) for level in range(3)]
        lower = SHRINK * SHRINK
        return jnp.where(
            large,
            sums[0] + sums[1] * lower,
            jnp.where(plain, sums[1] + sums[2] * lower, sums[2]),
        )

    bb, bq, qq, bw, qw = (entry(k) for k in range(5))
    field = field_ref[:, :size]
    image = image_ref[:, :size]
    second = second_ref[:, :size]
    alpha = bb / bq
    norm = bb - alpha * (2.0 * bq - alpha * qq)
    beta = norm / bb
    grown = 1.0 + beta
    energy = grown * (grown * bq - alpha * (bw + qq)) + alpha * alpha * qw
    alpha_next = norm / energy
    residual = field - alpha * image
    direction = residual + beta * field
    moved = (image - alpha * second) + beta * image
    solution_ref[...] = alpha * field + alpha_next * direction
    residual_ref[...] = residual - alpha_next * moved


def swap(value, odd):
    count = lax.axis_size("sub")
    pairs = []
    for first in range(odd, count, 2):
        second = (first + 1) % count
        pairs += [(first, second), (second, first)]
    return lax.ppermute(value, "sub", pairs)


def from_behind(value, axis, steps):
    count = lax.axis_size(axis)
    pairs = [(source, (source + steps) % count) for source in range(count)]
    return lax.ppermute(value, axis, pairs)


def swap_slots(value, k):
    count = lax.axis_size("blk")
    return lax.ppermute(value, "blk", [(slot, slot ^ k) for slot in range(count)])


def on_device(
    right_side, stiffness, block_pairs, trace_rows, partner_face, owner_list, mortar_weight
):
    field = right_side[0, 0].T
    block_rows, size = field.shape
    blocks = stiffness[0, 0].astype(F32)
    pairs = block_pairs[0, 0]
    rows = trace_rows[0, 0]
    partner = partner_face[0, 0]
    owners = owner_list[0, 0]
    faces = partner.shape[0]
    devices = lax.axis_size("sub") * lax.axis_size("blk")

    own_weights = mortar_weight[0, 0]
    last_weights = from_behind(own_weights, "sub", 1)
    last = 2 * faces + block_rows

    def placed(value, first):
        below = last + SUBLANES + faces - first - value.shape[0]
        return jnp.pad(value, ((first, below), (0, LANES - value.shape[1])))

    indices = placed(rows, 0) + placed(partner_face[0], last) + placed(owner_list[0], last + 1)
    packed = (
        indices.astype(F32)
        + placed(field, 2 * faces)
        + placed(own_weights.reshape(faces, LANES), last + SUBLANES)
    )
    aligned, padded, choice, east, west, to_a, to_b = call(
        functools.partial(first_kernel, owners.shape[0]),
        [
            shape(2 * faces, jnp.int32),
            shape(block_rows),
            shape(SUBLANES),
            shape(faces),
            shape(faces),
            shape(2 * faces + SUBLANES),
            shape(2 * faces + SUBLANES),
        ],
        [(packed, VMEM)],
    )
    from_a = swap(to_a, 1)
    from_b = swap(to_b, 0)
    slots, per_group, _ = own_weights.shape
    blocks_to = call(
        functools.partial(blocks_kernel, last + SUBLANES),
        [shape(2 * per_group)] * (slots - 1),
        [(packed, VMEM), (last_weights, VMEM)],
        flops=1,
        moved=1,
    )
    blocks_from = [
        swap_slots(block, k) for k, block in zip(range(slots - 1, 0, -1), blocks_to)
    ]

    def stiff(vector, *ordered):
        return call(
            functools.partial(stiffness_kernel, size),
            [shape(block_rows)] * (1 + len(ordered)) + [shape(faces)] * len(ordered),
            [(value, VMEM) for value in (pairs, blocks, vector, *ordered)],
        )

    (product,) = stiff(padded)
    image, weights_east, weights_west, jump, next_rows, last_rows = call(
        functools.partial(image_kernel, size, last + SUBLANES),
        [shape(block_rows)] + [shape(faces)] * 3 + [shape(faces, jnp.int32)] * 2,
        [
            (value, VMEM)
            for value in (
                packed,
                last_weights,
                choice,
                aligned,
                product,
                east,
                west,
                from_a,
                from_b,
                *blocks_from,
            )
        ],
    )
    from_last = from_behind(image, "sub", 1)
    product, copied, west = stiff(image, aligned)
    from_next = from_behind(copied, "sub", -1)
    sums, arrived = call(
        sums_kernel,
        [jax.ShapeDtypeStruct((devices, 1, LANES), F32), shape(faces)],
        [
            (value, VMEM)
            for value in (product, weights_west, west, last_rows, from_last, jump, padded, image)
        ],
    )
    (second,) = call(
        functools.partial(second_kernel, size),
        [shape(block_rows)],
        [
            (value, VMEM)
            for value in (
                aligned,
                product,
                weights_east,
                weights_west,
                image,
                west,
                next_rows,
                from_next,
                arrived,
            )
        ],
        scratch=[pltpu.VMEM((faces, LANES), F32)] * 2,
        flops=1_000_000_000,
    )
    sums = lax.all_to_all(sums, ("sub", "blk"), split_axis=0, concat_axis=0, tiled=True)
    solution_field, residual = call(
        final_kernel,
        [jax.ShapeDtypeStruct((block_rows, size), F32)] * 2,
        [(padded, VMEM), (image, VMEM), (second, VMEM), (sums, VMEM)],
    )
    return (solution_field.T[None, None], residual.T[None, None])


def solution(mesh):
    in_specs = (
        P("sub", "blk", None, None),
        P("sub", "blk", None, None),
        P("sub", "blk", None, None),
        P("sub", "blk", None, None),
        P("sub", "blk", None),
        P("sub", "blk", None),
        P("sub", "blk", None, None, None),
    )
    out_specs = (P("sub", "blk", None, None), P("sub", "blk", None, None))
    return jax.shard_map(
        on_device, mesh=mesh, in_specs=in_specs, out_specs=out_specs, check_vma=False
    )
```

```python
import functools
import math

import jax
import jax.numpy as jnp
from jax import lax
from jax.experimental import pallas as pl
from jax.experimental.pallas import tpu as pltpu
from jax.sharding import PartitionSpec as P

LANES = 128
SUBLANES = 8
VMEM = pl.BlockSpec(memory_space=pltpu.VMEM)
MARK = 5
LARGE = 2.0**40
SMALL = 2.0**-40
SHRINK = 2.0**-60
F32 = jnp.float32
BF16 = jnp.bfloat16


def call(body, outs, inputs, scratch=(), flops=1_000_000, moved=1_000_000):
    return pl.pallas_call(
        body,
        out_shape=outs,
        in_specs=[spec for _, spec in inputs],
        out_specs=[VMEM] * len(outs),
        scratch_shapes=list(scratch),
        compiler_params=pltpu.CompilerParams(vmem_limit_bytes=32 * 1024 * 1024),
        cost_estimate=pl.CostEstimate(
            flops=flops, bytes_accessed=moved, transcendentals=0
        ),
    )(*[value for value, _ in inputs])


def shape(rows, dtype=F32):
    return jax.ShapeDtypeStruct((rows, LANES), dtype)


def halves(value):
    high = value.astype(BF16).astype(F32)
    return high, value - high


def gather_traces(field, rows_ref, rows_first, target):
    block_rows = field.shape[0]
    spread = [
        jnp.broadcast_to(field[i : i + 1, :], (SUBLANES, LANES)) for i in range(block_rows)
    ]
    for k in range(target.shape[0] // SUBLANES):
        index = rows_ref[rows_first + k * SUBLANES : rows_first + (k + 1) * SUBLANES, :]
        dof, row = split(index, block_rows)
        taken = jnp.zeros((SUBLANES, LANES), F32)
        for i in range(block_rows):
            here = jnp.take_along_axis(spread[i], dof, axis=1, mode="promise_in_bounds")
            taken = jnp.where(row == i, here, taken)
        target[k * SUBLANES : (k + 1) * SUBLANES, :] = taken


def tile(k):
    return pl.ds(pl.multiple_of(k * SUBLANES, SUBLANES), SUBLANES)


def split(index, block_rows):
    if block_rows & (block_rows - 1) == 0:
        shift = block_rows.bit_length() - 1
        return index >> shift, index & (block_rows - 1)
    return lax.div(index, block_rows), lax.rem(index, block_rows)


def one_hot(place, count):
    row = lax.broadcasted_iota(jnp.int32, (count, place.shape[1]), 0)
    return jnp.where(row == place, 1.0, 0.0)


def exact_dot(left, right):
    return jnp.dot(
        left, right, precision=lax.Precision.HIGHEST, preferred_element_type=F32
    )


def block_place(k, groups):
    return jnp.where(k == 0, 0, groups - k)


def first_kernel(
    groups, packed_ref, aligned_ref, padded_ref, choice_ref, east_ref, west_ref, to_a_ref, to_b_ref
):
    faces = aligned_ref.shape[0] // 2
    block_rows = padded_ref.shape[0]
    per_group = faces // groups
    slot = lax.axis_index("blk")
    odd = lax.rem(lax.axis_index("sub"), 2) == 1
    padded_ref[...] = packed_ref[2 * faces : 2 * faces + block_rows, :]
    last = 2 * faces + block_rows
    tail = packed_ref[last : last + SUBLANES, :].astype(jnp.int32)
    partner = tail[:1, :faces]
    face = lax.broadcasted_iota(jnp.int32, (1, faces), 1)
    source = jnp.zeros((1, faces), jnp.int32)
    for g in range(groups):
        inside = face - g * per_group
        source = jnp.where(
            (inside >= 0) & (inside < per_group),
            block_place(tail[1:2, g : g + 1] ^ slot, groups) * per_group + inside,
            source,
        )
    order = one_hot(partner, faces)
    east_rows = exact_dot(order, packed_ref[:faces, :])
    west_rows = packed_ref[faces : 2 * faces, :]
    aligned_ref[:faces, :] = east_rows.astype(jnp.int32)
    aligned_ref[faces:, :] = west_rows.astype(jnp.int32)
    choice_ref[...] = jnp.zeros_like(choice_ref)
    choice_ref[:1, :faces] = lax.dot_general(
        source.astype(F32).astype(BF16),
        order.astype(BF16),
        (((1,), (1,)), ((), ())),
        preferred_element_type=F32,
    )
    gather_traces(padded_ref[...], aligned_ref, 0, east_ref)
    gather_traces(padded_ref[...], aligned_ref, faces, west_ref)
    east = east_ref[...]
    west = west_ref[...]
    to_a_ref[:faces, :] = jnp.where(odd, east, west)
    to_b_ref[:faces, :] = jnp.where(odd, west, east)
    for to_ref in (to_a_ref, to_b_ref):
        to_ref[faces : faces + SUBLANES, :] = choice_ref[...]
    to_a_ref[faces + SUBLANES :, :] = jnp.where(odd, east_rows, west_rows)
    to_b_ref[faces + SUBLANES :, :] = jnp.where(odd, west_rows, east_rows)


def blocks_kernel(first, packed_ref, last_ref, *block_refs):
    slot = lax.axis_index("blk")
    per_group = last_ref.shape[1]
    for place, block_ref in enumerate(block_refs):
        k = slot ^ (len(block_refs) - place)
        kept = pl.ds(pl.multiple_of(first + k * per_group, SUBLANES), per_group)
        block_ref[:per_group, :] = packed_ref[kept, :]
        block_ref[per_group:, :] = last_ref[k]


def thirds(value, axis):
    high, rest = halves(value)
    middle, low = halves(rest)
    return jnp.concatenate([high, middle, low], axis=axis).astype(BF16)


def sum_thirds(value, axis):
    size = value.shape[axis] // 3
    parts = [lax.slice_in_dim(value, k * size, (k + 1) * size, axis=axis) for k in range(3)]
    return (parts[0] + parts[1]) + parts[2]


def pick_rows(choice, value):
    picked = lax.dot_general(
        one_hot(choice, value.shape[0]).astype(BF16),
        thirds(value, 1),
        (((0,), (0,)), ((), ())),
        preferred_element_type=F32,
    )
    return sum_thirds(picked, 1)


def put_rows(choice, value, rows):
    put = jnp.dot(
        one_hot(choice, rows).astype(BF16), thirds(value, 1), preferred_element_type=F32
    )
    return sum_thirds(put, 1)


def stiffness_kernel(size, pairs_ref, blocks_ref, field_ref, *refs):
    out_ref = refs[min(1, len(refs) - 1)]
    block_rows = field_ref.shape[0]
    count = pairs_ref.shape[1]
    rows = block_rows + count
    width = math.lcm(size, LANES)
    tiles = width // LANES
    segments = width // size
    groups = size // segments
    batch = next(k for k in (4, 3, 2, 1) if groups % k == 0)

    def place(position):
        segment = sum(jnp.where(position >= k * size, 1, 0) for k in range(1, segments))
        return segment, position - segment * size

    def lanes_of(value, index):
        slabs = [
            jnp.take_along_axis(
                value[k : k + SUBLANES, :], index, axis=1, mode="promise_in_bounds"
            )
            for k in range(0, value.shape[0], SUBLANES)
        ]
        return jnp.concatenate(slabs, axis=0)

    field = field_ref[...]
    ends = jnp.concatenate([pairs_ref[:1, :], pairs_ref[1:, :]], axis=1)
    both = pick_rows(ends, field)
    left = both[:count]
    right = jnp.concatenate([field, both[count:]], axis=0)
    lane = lax.broadcasted_iota(jnp.int32, (SUBLANES, LANES), 1)
    places = [place(lane + t * LANES) for t in range(tiles)]
    repeated = jnp.concatenate([lanes_of(right, inside) for _, inside in places], axis=1)
    segment, inside = place(lax.broadcasted_iota(jnp.int32, (width, LANES), 0))
    column = lax.broadcasted_iota(jnp.int32, (width, LANES), 1)
    add_segments = jnp.where(segment == column % segments, 1.0, 0.0).astype(BF16)
    fold = jnp.where(inside == column, 1.0, 0.0).astype(BF16)
    dof_group = lax.broadcasted_iota(jnp.int32, (rows, LANES), 1) // segments
    total = jnp.zeros((rows, LANES), F32)
    turned = jnp.zeros((count, width), F32)
    for base in range(0, groups, batch):
        stack = []
        for g in range(base, base + batch):
            stored = blocks_ref[:, g * width : (g + 1) * width]
            product = stored * repeated
            high = product.astype(BF16)
            stack += [high, (product - high.astype(F32)).astype(BF16)]
            spread = [lanes_of(left, g * segments + segment) for segment, _ in places]
            turned = turned + stored[block_rows:] * jnp.concatenate(spread, axis=1)
        sums = jnp.dot(
            jnp.concatenate(stack, axis=0), add_segments, preferred_element_type=F32
        )
        for n in range(batch):
            part = sums[2 * n * rows : 2 * (n + 1) * rows]
            total = jnp.where(dof_group == base + n, part[:rows] + part[rows:], total)
    folded = sum_thirds(
        jnp.dot(thirds(turned, 0), fold, preferred_element_type=F32), 0
    )
    out_ref[...] = total[:block_rows] + put_rows(
        ends, jnp.concatenate([total[block_rows:], folded], axis=0), block_rows
    )
    if len(refs) > 1:
        aligned_ref, _, copy_ref, west_ref = refs
        copy_ref[...] = field
        gather_traces(field, aligned_ref, west_ref.shape[0], west_ref)


def spread_jumps(size, rows_ref, sides, block_rows):
    dof_of = lax.broadcasted_iota(jnp.int32, (size, LANES), 0).astype(F32).astype(BF16)
    row_of = lax.broadcasted_iota(jnp.int32, (block_rows, LANES), 0).astype(F32).astype(BF16)
    none = jnp.zeros((), BF16)
    one = jnp.ones((), BF16)

    def widened(value, f, rows):
        slab = jnp.broadcast_to(value[f : f + 1, :], (2 * SUBLANES, LANES)).astype(BF16)
        return jnp.concatenate([slab] * (rows // (2 * SUBLANES)), axis=0)

    total = jnp.zeros((size, 2 * block_rows), F32)
    for side, weighted in enumerate(sides):
        for k in range(0, weighted.shape[0], SUBLANES):
            high, low = halves(weighted[k : k + SUBLANES])
            first = side * weighted.shape[0] + k
            dof, row = split(rows_ref[first : first + SUBLANES, :], block_rows)
            dof = dof.astype(F32)
            row = row.astype(F32)
            left = []
            right = []
            for f in range(SUBLANES):
                here = row_of == widened(row, f, block_rows)
                left.append(
                    jnp.concatenate(
                        [
                            jnp.where(here, widened(high, f, block_rows), none),
                            jnp.where(here, widened(low, f, block_rows), none),
                        ],
                        axis=0,
                    )
                )
                right.append(jnp.where(dof_of == widened(dof, f, size), one, none))
            total = total + lax.dot_general(
                jnp.concatenate(right, axis=1),
                jnp.concatenate(left, axis=1),
                (((1,), (1,)), ((), ())),
                preferred_element_type=F32,
            )
    total = total.T
    return total[:block_rows] + total[block_rows:]


def image_kernel(
    size,
    first,
    packed_ref,
    last_ref,
    choice_ref,
    aligned_ref,
    product_ref,
    east_ref,
    west_ref,
    from_a_ref,
    from_b_ref,
    *refs,
):
    *block_refs, image_ref, weights_east_ref, weights_west_ref, jump_ref = refs[:-2]
    next_rows_ref, last_rows_ref = refs[-2:]
    block_rows = product_ref.shape[0]
    faces = weights_east_ref.shape[0]
    per_group = last_ref.shape[1]
    slot = lax.axis_index("blk")
    odd = lax.rem(lax.axis_index("sub"), 2) == 1
    kept = pl.ds(pl.multiple_of(first + slot * per_group, SUBLANES), per_group)
    from_west = jnp.where(odd, from_b_ref[...], from_a_ref[...])
    from_east = jnp.where(odd, from_a_ref[...], from_b_ref[...])
    next_rows_ref[...] = from_east[faces + SUBLANES :].astype(jnp.int32)
    last_rows_ref[...] = from_west[faces + SUBLANES :].astype(jnp.int32)
    for row, block, part, weights_ref in (
        (choice_ref[...], packed_ref[kept, :], slice(0, per_group), weights_east_ref),
        (from_west[faces : faces + SUBLANES], last_ref[slot], slice(per_group, 2 * per_group), weights_west_ref),
    ):
        weights_ref[...] = pick_rows(
            row[:1, :faces].astype(jnp.int32),
            jnp.concatenate([block] + [block_ref[part, :] for block_ref in block_refs], axis=0),
        )
    jump_ref[...] = west_ref[...] - from_west[:faces]
    image_ref[...] = product_ref[...]
    image_ref[:, :size] = image_ref[:, :size] + spread_jumps(
        size,
        aligned_ref,
        (
            weights_east_ref[...] * (east_ref[...] - from_east[:faces]),
            weights_west_ref[...] * jump_ref[...],
        ),
        block_rows,
    )


def column_sums(value):
    return jnp.sum(value, axis=0, keepdims=True)


def sums_kernel(
    product_ref,
    weights_ref,
    own_ref,
    rows_ref,
    last_ref,
    jump_ref,
    field_ref,
    image_ref,
    sums_ref,
    arrived_ref,
):
    gather_traces(last_ref[...], rows_ref, 0, arrived_ref)
    largest = jnp.maximum(jnp.abs(field_ref[...]), jnp.abs(image_ref[...]))
    for value in (arrived_ref[...], jump_ref[...]):
        value = jnp.abs(value)
        for k in range(0, value.shape[0], largest.shape[0]):
            largest = jnp.maximum(largest, value[k : k + largest.shape[0]])
    largest = jnp.max(jnp.max(largest, axis=0, keepdims=True), axis=1, keepdims=True)
    level = jnp.where(largest > LARGE, 0, jnp.where(largest < SMALL, 2, 1))
    parts = []
    for scale in (SHRINK, 1.0, 1.0 / SHRINK):
        field = field_ref[...] * scale
        image = image_ref[...] * scale
        product = product_ref[...] * scale
        jump = own_ref[...] * scale - arrived_ref[...] * scale
        lam = weights_ref[...] * jump
        parts += [
            column_sums(field * field),
            column_sums(field * image),
            column_sums(image * image),
            column_sums(field * product) + column_sums(lam * (jump_ref[...] * scale)),
            column_sums(image * product) + column_sums(lam * jump),
        ]
        parts += [jnp.zeros_like(parts[0])] * (SUBLANES - MARK)
    whole = jnp.sum(jnp.concatenate(parts, axis=0), axis=1, keepdims=True)
    row = lax.broadcasted_iota(jnp.int32, (len(parts), LANES), 0)
    lane = lax.broadcasted_iota(jnp.int32, (len(parts), LANES), 1)
    first = SUBLANES * level
    whole = jnp.where(row == first + MARK, 1.0, whole)
    chosen = (lane == row) & (row >= first) & (row < first + SUBLANES)
    packed = column_sums(jnp.where(chosen, whole, 0.0))
    sums_ref[...] = jnp.broadcast_to(packed[None], sums_ref.shape)


def second_kernel(
    size,
    aligned_ref,
    product_ref,
    weights_east_ref,
    weights_west_ref,
    image_ref,
    west_ref,
    rows_ref,
    next_ref,
    from_last_ref,
    second_ref,
    east_ref,
    from_next_ref,
):
    block_rows = product_ref.shape[0]
    gather_traces(image_ref[...], aligned_ref, 0, east_ref)
    gather_traces(next_ref[...], rows_ref, 0, from_next_ref)
    second_ref[...] = product_ref[...]
    second_ref[:, :size] = second_ref[:, :size] + spread_jumps(
        size,
        aligned_ref,
        [
            weights_ref[...] * (own_ref[...] - arrived_ref[...])
            for weights_ref, own_ref, arrived_ref in (
                (weights_east_ref, east_ref, from_next_ref),
                (weights_west_ref, west_ref, from_last_ref),
            )
        ],
        block_rows,
    )


def final_kernel(field_ref, image_ref, second_ref, sums_ref, solution_ref, residual_ref):
    size = solution_ref.shape[1]
    row = jnp.broadcast_to(jnp.sum(sums_ref[...], axis=0), (SUBLANES, LANES))

    def lane(k):
        place = jnp.full((SUBLANES, LANES), k, jnp.int32)
        return jnp.take_along_axis(row, place, axis=1, mode="promise_in_bounds")[:1, :size]

    large, plain = (lane(SUBLANES * level + MARK) > 0.0 for level in (0, 1))

    def entry(k):
        sums = [lane(SUBLANES * level + k) for level in range(3)]
        lower = SHRINK * SHRINK
        return jnp.where(
            large,
            sums[0] + sums[1] * lower,
            jnp.where(plain, sums[1] + sums[2] * lower, sums[2]),
        )

    bb, bq, qq, bw, qw = (entry(k) for k in range(5))
    field = field_ref[:, :size]
    image = image_ref[:, :size]
    second = second_ref[:, :size]
    alpha = bb / bq
    norm = bb - alpha * (2.0 * bq - alpha * qq)
    beta = norm / bb
    grown = 1.0 + beta
    energy = grown * (grown * bq - alpha * (bw + qq)) + alpha * alpha * qw
    alpha_next = norm / energy
    residual = field - alpha * image
    direction = residual + beta * field
    moved = (image - alpha * second) + beta * image
    solution_ref[...] = alpha * field + alpha_next * direction
    residual_ref[...] = residual - alpha_next * moved


def swap(value, odd):
    count = lax.axis_size("sub")
    pairs = []
    for first in range(odd, count, 2):
        second = (first + 1) % count
        pairs += [(first, second), (second, first)]
    return lax.ppermute(value, "sub", pairs)


def from_behind(value, axis, steps):
    count = lax.axis_size(axis)
    pairs = [(source, (source + steps) % count) for source in range(count)]
    return lax.ppermute(value, axis, pairs)


def swap_slots(value, k):
    count = lax.axis_size("blk")
    return lax.ppermute(value, "blk", [(slot, slot ^ k) for slot in range(count)])


def on_device(
    right_side, stiffness, block_pairs, trace_rows, partner_face, owner_list, mortar_weight
):
    field = right_side[0, 0].T
    block_rows, size = field.shape
    blocks = stiffness[0, 0].astype(F32)
    pairs = block_pairs[0, 0]
    rows = trace_rows[0, 0]
    partner = partner_face[0, 0]
    owners = owner_list[0, 0]
    faces = partner.shape[0]
    devices = lax.axis_size("sub") * lax.axis_size("blk")

    own_weights = mortar_weight[0, 0]
    last_weights = from_behind(own_weights, "sub", 1)
    last = 2 * faces + block_rows

    def placed(value, first):
        below = last + SUBLANES + faces - first - value.shape[0]
        return jnp.pad(value, ((first, below), (0, LANES - value.shape[1])))

    indices = placed(rows, 0) + placed(partner_face[0], last) + placed(owner_list[0], last + 1)
    packed = (
        indices.astype(F32)
        + placed(field, 2 * faces)
        + placed(own_weights.reshape(faces, LANES), last + SUBLANES)
    )
    aligned, padded, choice, east, west, to_a, to_b = call(
        functools.partial(first_kernel, owners.shape[0]),
        [
            shape(2 * faces, jnp.int32),
            shape(block_rows),
            shape(SUBLANES),
            shape(faces),
            shape(faces),
            shape(2 * faces + SUBLANES),
            shape(2 * faces + SUBLANES),
        ],
        [(packed, VMEM)],
    )
    from_a = swap(to_a, 1)
    from_b = swap(to_b, 0)
    slots, per_group, _ = own_weights.shape
    blocks_to = call(
        functools.partial(blocks_kernel, last + SUBLANES),
        [shape(2 * per_group)] * (slots - 1),
        [(packed, VMEM), (last_weights, VMEM)],
        flops=1,
        moved=1,
    )
    blocks_from = [
        swap_slots(block, k) for k, block in zip(range(slots - 1, 0, -1), blocks_to)
    ]

    def stiff(vector, *ordered):
        return call(
            functools.partial(stiffness_kernel, size),
            [shape(block_rows)] * (1 + len(ordered)) + [shape(faces)] * len(ordered),
            [(value, VMEM) for value in (pairs, blocks, vector, *ordered)],
        )

    (product,) = stiff(padded)
    image, weights_east, weights_west, jump, next_rows, last_rows = call(
        functools.partial(image_kernel, size, last + SUBLANES),
        [shape(block_rows)] + [shape(faces)] * 3 + [shape(faces, jnp.int32)] * 2,
        [
            (value, VMEM)
            for value in (
                packed,
                last_weights,
                choice,
                aligned,
                product,
                east,
                west,
                from_a,
                from_b,
                *blocks_from,
            )
        ],
    )
    from_last = from_behind(image, "sub", 1)
    product, copied, west = stiff(image, aligned)
    from_next = from_behind(copied, "sub", -1)
    sums, arrived = call(
        sums_kernel,
        [jax.ShapeDtypeStruct((devices, 1, LANES), F32), shape(faces)],
        [
            (value, VMEM)
            for value in (product, weights_west, west, last_rows, from_last, jump, padded, image)
        ],
    )
    (second,) = call(
        functools.partial(second_kernel, size),
        [shape(block_rows)],
        [
            (value, VMEM)
            for value in (
                aligned,
                product,
                weights_east,
                weights_west,
                image,
                west,
                next_rows,
                from_next,
                arrived,
            )
        ],
        scratch=[pltpu.VMEM((faces, LANES), F32)] * 2,
        flops=1_000_000_000,
    )
    sums = lax.all_to_all(sums, ("sub", "blk"), split_axis=0, concat_axis=0, tiled=True)
    solution_field, residual = call(
        final_kernel,
        [jax.ShapeDtypeStruct((block_rows, size), F32)] * 2,
        [(padded, VMEM), (image, VMEM), (second, VMEM), (sums, VMEM)],
    )
    return (solution_field.T[None, None], residual.T[None, None])


def solution(mesh):
    in_specs = (
        P("sub", "blk", None, None),
        P("sub", "blk", None, None),
        P("sub", "blk", None, None),
        P("sub", "blk", None, None),
        P("sub", "blk", None),
        P("sub", "blk", None),
        P("sub", "blk", None, None, None),
    )
    out_specs = (P("sub", "blk", None, None), P("sub", "blk", None, None))
    return jax.shard_map(
        on_device, mesh=mesh, in_specs=in_specs, out_specs=out_specs, check_vma=False
    )
```

```python
import functools
import math

import jax
import jax.numpy as jnp
from jax import lax
from jax.experimental import pallas as pl
from jax.experimental.pallas import tpu as pltpu
from jax.sharding import PartitionSpec as P

LANES = 128
SUBLANES = 8
VMEM = pl.BlockSpec(memory_space=pltpu.VMEM)
MARK = 5
LARGE = 2.0**40
SMALL = 2.0**-40
SHRINK = 2.0**-60
F32 = jnp.float32
BF16 = jnp.bfloat16


def call(body, outs, inputs, scratch=(), flops=1_000_000, moved=1_000_000):
    return pl.pallas_call(
        body,
        out_shape=outs,
        in_specs=[spec for _, spec in inputs],
        out_specs=[VMEM] * len(outs),
        scratch_shapes=list(scratch),
        compiler_params=pltpu.CompilerParams(vmem_limit_bytes=32 * 1024 * 1024),
        cost_estimate=pl.CostEstimate(
            flops=flops, bytes_accessed=moved, transcendentals=0
        ),
    )(*[value for value, _ in inputs])


def shape(rows, dtype=F32):
    return jax.ShapeDtypeStruct((rows, LANES), dtype)


def halves(value):
    high = value.astype(BF16).astype(F32)
    return high, value - high


def gather_traces(field, rows_ref, rows_first, target):
    block_rows = field.shape[0]
    spread = [
        jnp.broadcast_to(field[i : i + 1, :], (SUBLANES, LANES)) for i in range(block_rows)
    ]
    for k in range(target.shape[0] // SUBLANES):
        index = rows_ref[rows_first + k * SUBLANES : rows_first + (k + 1) * SUBLANES, :]
        dof, row = split(index, block_rows)
        bits = {}

        def pick(first, count):
            if count == 1:
                return jnp.take_along_axis(spread[first], dof, axis=1, mode="promise_in_bounds")
            half = 1 << ((count - 1).bit_length() - 1)
            if half not in bits:
                bits[half] = (row & half) != 0
            lower = pick(first, half)
            return jnp.where(bits[half], pick(first + half, count - half), lower)

        target[k * SUBLANES : (k + 1) * SUBLANES, :] = pick(0, block_rows)


def tile(k):
    return pl.ds(pl.multiple_of(k * SUBLANES, SUBLANES), SUBLANES)


def split(index, block_rows):
    if block_rows & (block_rows - 1) == 0:
        shift = block_rows.bit_length() - 1
        return index >> shift, index & (block_rows - 1)
    return lax.div(index, block_rows), lax.rem(index, block_rows)


def one_hot(place, count):
    row = lax.broadcasted_iota(jnp.int32, (count, place.shape[1]), 0)
    return jnp.where(row == place, 1.0, 0.0)


def exact_dot(left, right):
    return jnp.dot(
        left, right, precision=lax.Precision.HIGHEST, preferred_element_type=F32
    )


def block_place(k, groups):
    return jnp.where(k == 0, 0, groups - k)


def first_kernel(
    groups, packed_ref, aligned_ref, padded_ref, choice_ref, east_ref, west_ref, to_a_ref, to_b_ref
):
    faces = aligned_ref.shape[0] // 2
    block_rows = padded_ref.shape[0]
    per_group = faces // groups
    slot = lax.axis_index("blk")
    odd = lax.rem(lax.axis_index("sub"), 2) == 1
    padded_ref[...] = packed_ref[2 * faces : 2 * faces + block_rows, :]
    last = 2 * faces + block_rows
    tail = packed_ref[last : last + SUBLANES, :].astype(jnp.int32)
    partner = tail[:1, :faces]
    face = lax.broadcasted_iota(jnp.int32, (1, faces), 1)
    source = jnp.zeros((1, faces), jnp.int32)
    for g in range(groups):
        inside = face - g * per_group
        source = jnp.where(
            (inside >= 0) & (inside < per_group),
            block_place(tail[1:2, g : g + 1] ^ slot, groups) * per_group + inside,
            source,
        )
    order = one_hot(partner, faces)
    east_rows = exact_dot(order, packed_ref[:faces, :])
    west_rows = packed_ref[faces : 2 * faces, :]
    aligned_ref[:faces, :] = east_rows.astype(jnp.int32)
    aligned_ref[faces:, :] = west_rows.astype(jnp.int32)
    choice_ref[...] = jnp.zeros_like(choice_ref)
    choice_ref[:1, :faces] = lax.dot_general(
        source.astype(F32).astype(BF16),
        order.astype(BF16),
        (((1,), (1,)), ((), ())),
        preferred_element_type=F32,
    )
    gather_traces(padded_ref[...], aligned_ref, 0, east_ref)
    gather_traces(padded_ref[...], aligned_ref, faces, west_ref)
    east = east_ref[...]
    west = west_ref[...]
    to_a_ref[:faces, :] = jnp.where(odd, east, west)
    to_b_ref[:faces, :] = jnp.where(odd, west, east)
    for to_ref in (to_a_ref, to_b_ref):
        to_ref[faces : faces + SUBLANES, :] = choice_ref[...]
    to_a_ref[faces + SUBLANES :, :] = jnp.where(odd, east_rows, west_rows)
    to_b_ref[faces + SUBLANES :, :] = jnp.where(odd, west_rows, east_rows)


def blocks_kernel(first, packed_ref, last_ref, *block_refs):
    slot = lax.axis_index("blk")
    per_group = last_ref.shape[1]
    for place, block_ref in enumerate(block_refs):
        k = slot ^ (len(block_refs) - place)
        kept = pl.ds(pl.multiple_of(first + k * per_group, SUBLANES), per_group)
        block_ref[:per_group, :] = packed_ref[kept, :]
        block_ref[per_group:, :] = last_ref[k]


def thirds(value, axis):
    high, rest = halves(value)
    middle, low = halves(rest)
    return jnp.concatenate([high, middle, low], axis=axis).astype(BF16)


def sum_thirds(value, axis):
    size = value.shape[axis] // 3
    parts = [lax.slice_in_dim(value, k * size, (k + 1) * size, axis=axis) for k in range(3)]
    return (parts[0] + parts[1]) + parts[2]


def pick_rows(choice, value):
    picked = lax.dot_general(
        one_hot(choice, value.shape[0]).astype(BF16),
        thirds(value, 1),
        (((0,), (0,)), ((), ())),
        preferred_element_type=F32,
    )
    return sum_thirds(picked, 1)


def put_rows(choice, value, rows):
    put = jnp.dot(
        one_hot(choice, rows).astype(BF16), thirds(value, 1), preferred_element_type=F32
    )
    return sum_thirds(put, 1)


def stiffness_kernel(size, pairs_ref, blocks_ref, field_ref, *refs):
    out_ref = refs[min(1, len(refs) - 1)]
    block_rows = field_ref.shape[0]
    count = pairs_ref.shape[1]
    rows = block_rows + count
    width = math.lcm(size, LANES)
    tiles = width // LANES
    segments = width // size
    groups = size // segments
    batch = next(k for k in (4, 3, 2, 1) if groups % k == 0)

    def place(position):
        segment = sum(jnp.where(position >= k * size, 1, 0) for k in range(1, segments))
        return segment, position - segment * size

    def lanes_of(value, index):
        slabs = [
            jnp.take_along_axis(
                value[k : k + SUBLANES, :], index, axis=1, mode="promise_in_bounds"
            )
            for k in range(0, value.shape[0], SUBLANES)
        ]
        return jnp.concatenate(slabs, axis=0)

    field = field_ref[...]
    ends = jnp.concatenate([pairs_ref[:1, :], pairs_ref[1:, :]], axis=1)
    both = pick_rows(ends, field)
    left = both[:count]
    right = jnp.concatenate([field, both[count:]], axis=0)
    lane = lax.broadcasted_iota(jnp.int32, (SUBLANES, LANES), 1)
    places = [place(lane + t * LANES) for t in range(tiles)]
    repeated = jnp.concatenate([lanes_of(right, inside) for _, inside in places], axis=1)
    segment, inside = place(lax.broadcasted_iota(jnp.int32, (width, LANES), 0))
    column = lax.broadcasted_iota(jnp.int32, (width, LANES), 1)
    add_segments = jnp.where(segment == column % segments, 1.0, 0.0).astype(BF16)
    fold = jnp.where(inside == column, 1.0, 0.0).astype(BF16)
    dof_group = lax.broadcasted_iota(jnp.int32, (rows, LANES), 1) // segments
    total = jnp.zeros((rows, LANES), F32)
    turned = jnp.zeros((count, width), F32)
    for base in range(0, groups, batch):
        stack = []
        for g in range(base, base + batch):
            stored = blocks_ref[:, g * width : (g + 1) * width]
            product = stored * repeated
            high = product.astype(BF16)
            stack += [high, (product - high.astype(F32)).astype(BF16)]
            spread = [lanes_of(left, g * segments + segment) for segment, _ in places]
            turned = turned + stored[block_rows:] * jnp.concatenate(spread, axis=1)
        sums = jnp.dot(
            jnp.concatenate(stack, axis=0), add_segments, preferred_element_type=F32
        )
        for n in range(batch):
            part = sums[2 * n * rows : 2 * (n + 1) * rows]
            total = jnp.where(dof_group == base + n, part[:rows] + part[rows:], total)
    folded = sum_thirds(
        jnp.dot(thirds(turned, 0), fold, preferred_element_type=F32), 0
    )
    out_ref[...] = total[:block_rows] + put_rows(
        ends, jnp.concatenate([total[block_rows:], folded], axis=0), block_rows
    )
    if len(refs) > 1:
        aligned_ref, _, copy_ref, west_ref = refs
        copy_ref[...] = field
        gather_traces(field, aligned_ref, west_ref.shape[0], west_ref)


def spread_jumps(size, rows_ref, sides, block_rows):
    dof_of = lax.broadcasted_iota(jnp.int32, (size, LANES), 0).astype(F32).astype(BF16)
    row_of = lax.broadcasted_iota(jnp.int32, (block_rows, LANES), 0).astype(F32).astype(BF16)
    none = jnp.zeros((), BF16)
    one = jnp.ones((), BF16)

    def widened(value, f, rows):
        slab = jnp.broadcast_to(value[f : f + 1, :], (2 * SUBLANES, LANES)).astype(BF16)
        return jnp.concatenate([slab] * (rows // (2 * SUBLANES)), axis=0)

    total = jnp.zeros((size, 2 * block_rows), F32)
    for side, weighted in enumerate(sides):
        for k in range(0, weighted.shape[0], SUBLANES):
            high, low = halves(weighted[k : k + SUBLANES])
            first = side * weighted.shape[0] + k
            dof, row = split(rows_ref[first : first + SUBLANES, :], block_rows)
            dof = dof.astype(F32)
            row = row.astype(F32)
            left = []
            right = []
            for f in range(SUBLANES):
                here = row_of == widened(row, f, block_rows)
                left.append(
                    jnp.concatenate(
                        [
                            jnp.where(here, widened(high, f, block_rows), none),
                            jnp.where(here, widened(low, f, block_rows), none),
                        ],
                        axis=0,
                    )
                )
                right.append(jnp.where(dof_of == widened(dof, f, size), one, none))
            total = total + lax.dot_general(
                jnp.concatenate(right, axis=1),
                jnp.concatenate(left, axis=1),
                (((1,), (1,)), ((), ())),
                preferred_element_type=F32,
            )
    total = total.T
    return total[:block_rows] + total[block_rows:]


def image_kernel(
    size,
    first,
    packed_ref,
    last_ref,
    choice_ref,
    aligned_ref,
    product_ref,
    east_ref,
    west_ref,
    from_a_ref,
    from_b_ref,
    *refs,
):
    *block_refs, image_ref, weights_east_ref, weights_west_ref, jump_ref = refs[:-2]
    next_rows_ref, last_rows_ref = refs[-2:]
    block_rows = product_ref.shape[0]
    faces = weights_east_ref.shape[0]
    per_group = last_ref.shape[1]
    slot = lax.axis_index("blk")
    odd = lax.rem(lax.axis_index("sub"), 2) == 1
    kept = pl.ds(pl.multiple_of(first + slot * per_group, SUBLANES), per_group)
    from_west = jnp.where(odd, from_b_ref[...], from_a_ref[...])
    from_east = jnp.where(odd, from_a_ref[...], from_b_ref[...])
    next_rows_ref[...] = from_east[faces + SUBLANES :].astype(jnp.int32)
    last_rows_ref[...] = from_west[faces + SUBLANES :].astype(jnp.int32)
    for row, block, part, weights_ref in (
        (choice_ref[...], packed_ref[kept, :], slice(0, per_group), weights_east_ref),
        (from_west[faces : faces + SUBLANES], last_ref[slot], slice(per_group, 2 * per_group), weights_west_ref),
    ):
        weights_ref[...] = pick_rows(
            row[:1, :faces].astype(jnp.int32),
            jnp.concatenate([block] + [block_ref[part, :] for block_ref in block_refs], axis=0),
        )
    jump_ref[...] = west_ref[...] - from_west[:faces]
    image_ref[...] = product_ref[...]
    image_ref[:, :size] = image_ref[:, :size] + spread_jumps(
        size,
        aligned_ref,
        (
            weights_east_ref[...] * (east_ref[...] - from_east[:faces]),
            weights_west_ref[...] * jump_ref[...],
        ),
        block_rows,
    )


def column_sums(value):
    return jnp.sum(value, axis=0, keepdims=True)


def sums_kernel(
    product_ref,
    weights_ref,
    own_ref,
    rows_ref,
    last_ref,
    jump_ref,
    field_ref,
    image_ref,
    sums_ref,
    arrived_ref,
):
    gather_traces(last_ref[...], rows_ref, 0, arrived_ref)
    largest = jnp.maximum(jnp.abs(field_ref[...]), jnp.abs(image_ref[...]))
    for value in (arrived_ref[...], jump_ref[...]):
        value = jnp.abs(value)
        for k in range(0, value.shape[0], largest.shape[0]):
            largest = jnp.maximum(largest, value[k : k + largest.shape[0]])
    largest = jnp.max(jnp.max(largest, axis=0, keepdims=True), axis=1, keepdims=True)
    level = jnp.where(largest > LARGE, 0, jnp.where(largest < SMALL, 2, 1))
    parts = []
    for scale in (SHRINK, 1.0, 1.0 / SHRINK):
        field = field_ref[...] * scale
        image = image_ref[...] * scale
        product = product_ref[...] * scale
        jump = own_ref[...] * scale - arrived_ref[...] * scale
        lam = weights_ref[...] * jump
        parts += [
            column_sums(field * field),
            column_sums(field * image),
            column_sums(image * image),
            column_sums(field * product) + column_sums(lam * (jump_ref[...] * scale)),
            column_sums(image * product) + column_sums(lam * jump),
        ]
        parts += [jnp.zeros_like(parts[0])] * (SUBLANES - MARK)
    whole = jnp.sum(jnp.concatenate(parts, axis=0), axis=1, keepdims=True)
    row = lax.broadcasted_iota(jnp.int32, (len(parts), LANES), 0)
    lane = lax.broadcasted_iota(jnp.int32, (len(parts), LANES), 1)
    first = SUBLANES * level
    whole = jnp.where(row == first + MARK, 1.0, whole)
    chosen = (lane == row) & (row >= first) & (row < first + SUBLANES)
    packed = column_sums(jnp.where(chosen, whole, 0.0))
    sums_ref[...] = jnp.broadcast_to(packed[None], sums_ref.shape)


def second_kernel(
    size,
    aligned_ref,
    product_ref,
    weights_east_ref,
    weights_west_ref,
    image_ref,
    west_ref,
    rows_ref,
    next_ref,
    from_last_ref,
    second_ref,
    east_ref,
    from_next_ref,
):
    block_rows = product_ref.shape[0]
    gather_traces(image_ref[...], aligned_ref, 0, east_ref)
    gather_traces(next_ref[...], rows_ref, 0, from_next_ref)
    second_ref[...] = product_ref[...]
    second_ref[:, :size] = second_ref[:, :size] + spread_jumps(
        size,
        aligned_ref,
        [
            weights_ref[...] * (own_ref[...] - arrived_ref[...])
            for weights_ref, own_ref, arrived_ref in (
                (weights_east_ref, east_ref, from_next_ref),
                (weights_west_ref, west_ref, from_last_ref),
            )
        ],
        block_rows,
    )


def final_kernel(field_ref, image_ref, second_ref, sums_ref, solution_ref, residual_ref):
    size = solution_ref.shape[1]
    row = jnp.broadcast_to(jnp.sum(sums_ref[...], axis=0), (SUBLANES, LANES))

    def lane(k):
        place = jnp.full((SUBLANES, LANES), k, jnp.int32)
        return jnp.take_along_axis(row, place, axis=1, mode="promise_in_bounds")[:1, :size]

    large, plain = (lane(SUBLANES * level + MARK) > 0.0 for level in (0, 1))

    def entry(k):
        sums = [lane(SUBLANES * level + k) for level in range(3)]
        lower = SHRINK * SHRINK
        return jnp.where(
            large,
            sums[0] + sums[1] * lower,
            jnp.where(plain, sums[1] + sums[2] * lower, sums[2]),
        )

    bb, bq, qq, bw, qw = (entry(k) for k in range(5))
    field = field_ref[:, :size]
    image = image_ref[:, :size]
    second = second_ref[:, :size]
    alpha = bb / bq
    norm = bb - alpha * (2.0 * bq - alpha * qq)
    beta = norm / bb
    grown = 1.0 + beta
    energy = grown * (grown * bq - alpha * (bw + qq)) + alpha * alpha * qw
    alpha_next = norm / energy
    residual = field - alpha * image
    direction = residual + beta * field
    moved = (image - alpha * second) + beta * image
    solution_ref[...] = alpha * field + alpha_next * direction
    residual_ref[...] = residual - alpha_next * moved


def swap(value, odd):
    count = lax.axis_size("sub")
    pairs = []
    for first in range(odd, count, 2):
        second = (first + 1) % count
        pairs += [(first, second), (second, first)]
    return lax.ppermute(value, "sub", pairs)


def from_behind(value, axis, steps):
    count = lax.axis_size(axis)
    pairs = [(source, (source + steps) % count) for source in range(count)]
    return lax.ppermute(value, axis, pairs)


def swap_slots(value, k):
    count = lax.axis_size("blk")
    return lax.ppermute(value, "blk", [(slot, slot ^ k) for slot in range(count)])


def on_device(
    right_side, stiffness, block_pairs, trace_rows, partner_face, owner_list, mortar_weight
):
    field = right_side[0, 0].T
    block_rows, size = field.shape
    blocks = stiffness[0, 0].astype(F32)
    pairs = block_pairs[0, 0]
    rows = trace_rows[0, 0]
    partner = partner_face[0, 0]
    owners = owner_list[0, 0]
    faces = partner.shape[0]
    devices = lax.axis_size("sub") * lax.axis_size("blk")

    own_weights = mortar_weight[0, 0]
    last_weights = from_behind(own_weights, "sub", 1)
    last = 2 * faces + block_rows

    def placed(value, first):
        below = last + SUBLANES + faces - first - value.shape[0]
        return jnp.pad(value, ((first, below), (0, LANES - value.shape[1])))

    indices = placed(rows, 0) + placed(partner_face[0], last) + placed(owner_list[0], last + 1)
    packed = (
        indices.astype(F32)
        + placed(field, 2 * faces)
        + placed(own_weights.reshape(faces, LANES), last + SUBLANES)
    )
    aligned, padded, choice, east, west, to_a, to_b = call(
        functools.partial(first_kernel, owners.shape[0]),
        [
            shape(2 * faces, jnp.int32),
            shape(block_rows),
            shape(SUBLANES),
            shape(faces),
            shape(faces),
            shape(2 * faces + SUBLANES),
            shape(2 * faces + SUBLANES),
        ],
        [(packed, VMEM)],
    )
    from_a = swap(to_a, 1)
    from_b = swap(to_b, 0)
    slots, per_group, _ = own_weights.shape
    blocks_to = call(
        functools.partial(blocks_kernel, last + SUBLANES),
        [shape(2 * per_group)] * (slots - 1),
        [(packed, VMEM), (last_weights, VMEM)],
        flops=1,
        moved=1,
    )
    blocks_from = [
        swap_slots(block, k) for k, block in zip(range(slots - 1, 0, -1), blocks_to)
    ]

    def stiff(vector, *ordered):
        return call(
            functools.partial(stiffness_kernel, size),
            [shape(block_rows)] * (1 + len(ordered)) + [shape(faces)] * len(ordered),
            [(value, VMEM) for value in (pairs, blocks, vector, *ordered)],
        )

    (product,) = stiff(padded)
    image, weights_east, weights_west, jump, next_rows, last_rows = call(
        functools.partial(image_kernel, size, last + SUBLANES),
        [shape(block_rows)] + [shape(faces)] * 3 + [shape(faces, jnp.int32)] * 2,
        [
            (value, VMEM)
            for value in (
                packed,
                last_weights,
                choice,
                aligned,
                product,
                east,
                west,
                from_a,
                from_b,
                *blocks_from,
            )
        ],
    )
    from_last = from_behind(image, "sub", 1)
    product, copied, west = stiff(image, aligned)
    from_next = from_behind(copied, "sub", -1)
    sums, arrived = call(
        sums_kernel,
        [jax.ShapeDtypeStruct((devices, 1, LANES), F32), shape(faces)],
        [
            (value, VMEM)
            for value in (product, weights_west, west, last_rows, from_last, jump, padded, image)
        ],
    )
    (second,) = call(
        functools.partial(second_kernel, size),
        [shape(block_rows)],
        [
            (value, VMEM)
            for value in (
                aligned,
                product,
                weights_east,
                weights_west,
                image,
                west,
                next_rows,
                from_next,
                arrived,
            )
        ],
        scratch=[pltpu.VMEM((faces, LANES), F32)] * 2,
        flops=1_000_000_000,
    )
    sums = lax.all_to_all(sums, ("sub", "blk"), split_axis=0, concat_axis=0, tiled=True)
    solution_field, residual = call(
        final_kernel,
        [jax.ShapeDtypeStruct((block_rows, size), F32)] * 2,
        [(padded, VMEM), (image, VMEM), (second, VMEM), (sums, VMEM)],
    )
    return (solution_field.T[None, None], residual.T[None, None])


def solution(mesh):
    in_specs = (
        P("sub", "blk", None, None),
        P("sub", "blk", None, None),
        P("sub", "blk", None, None),
        P("sub", "blk", None, None),
        P("sub", "blk", None),
        P("sub", "blk", None),
        P("sub", "blk", None, None, None),
    )
    out_specs = (P("sub", "blk", None, None), P("sub", "blk", None, None))
    return jax.shard_map(
        on_device, mesh=mesh, in_specs=in_specs, out_specs=out_specs, check_vma=False
    )
```

```python
import functools
import math

import jax
import jax.numpy as jnp
from jax import lax
from jax.experimental import pallas as pl
from jax.experimental.pallas import tpu as pltpu
from jax.sharding import PartitionSpec as P

LANES = 128
SUBLANES = 8
VMEM = pl.BlockSpec(memory_space=pltpu.VMEM)
BATCH = 4
MARK = 5
LARGE = 2.0**40
SMALL = 2.0**-40
SHRINK = 2.0**-60
F32 = jnp.float32
BF16 = jnp.bfloat16


def call(body, outs, inputs, scratch=(), flops=1_000_000, moved=1_000_000):
    return pl.pallas_call(
        body,
        out_shape=outs,
        in_specs=[spec for _, spec in inputs],
        out_specs=[VMEM] * len(outs),
        scratch_shapes=list(scratch),
        compiler_params=pltpu.CompilerParams(vmem_limit_bytes=32 * 1024 * 1024),
        cost_estimate=pl.CostEstimate(
            flops=flops, bytes_accessed=moved, transcendentals=0
        ),
    )(*[value for value, _ in inputs])


def shape(rows, dtype=F32):
    return jax.ShapeDtypeStruct((rows, LANES), dtype)


def halves(value):
    high = value.astype(BF16).astype(F32)
    return high, value - high


def gather_traces(field, rows_ref, rows_first, target):
    block_rows = field.shape[0]
    spread = [
        jnp.broadcast_to(field[i : i + 1, :], (SUBLANES, LANES)) for i in range(block_rows)
    ]
    for k in range(target.shape[0] // SUBLANES):
        index = rows_ref[rows_first + k * SUBLANES : rows_first + (k + 1) * SUBLANES, :]
        dof, row = split(index, block_rows)
        bits = {}

        def pick(first, count):
            if count == 1:
                return jnp.take_along_axis(spread[first], dof, axis=1, mode="promise_in_bounds")
            half = 1 << ((count - 1).bit_length() - 1)
            if half not in bits:
                bits[half] = (row & half) != 0
            lower = pick(first, half)
            return jnp.where(bits[half], pick(first + half, count - half), lower)

        target[k * SUBLANES : (k + 1) * SUBLANES, :] = pick(0, block_rows)


def tile(k):
    return pl.ds(pl.multiple_of(k * SUBLANES, SUBLANES), SUBLANES)


def split(index, block_rows):
    if block_rows & (block_rows - 1) == 0:
        shift = block_rows.bit_length() - 1
        return index >> shift, index & (block_rows - 1)
    return lax.div(index, block_rows), lax.rem(index, block_rows)


def one_hot(place, count):
    row = lax.broadcasted_iota(jnp.int32, (count, place.shape[1]), 0)
    return jnp.where(row == place, 1.0, 0.0)


def exact_dot(left, right):
    return jnp.dot(
        left, right, precision=lax.Precision.HIGHEST, preferred_element_type=F32
    )


def block_place(k, groups):
    return jnp.where(k == 0, 0, groups - k)


def first_kernel(
    groups, packed_ref, aligned_ref, padded_ref, choice_ref, east_ref, west_ref, to_a_ref, to_b_ref
):
    faces = aligned_ref.shape[0] // 2
    block_rows = padded_ref.shape[0]
    per_group = faces // groups
    slot = lax.axis_index("blk")
    odd = lax.rem(lax.axis_index("sub"), 2) == 1
    padded_ref[...] = packed_ref[2 * faces : 2 * faces + block_rows, :]
    last = 2 * faces + block_rows
    tail = packed_ref[last : last + SUBLANES, :].astype(jnp.int32)
    partner = tail[:1, :faces]
    face = lax.broadcasted_iota(jnp.int32, (1, faces), 1)
    source = jnp.zeros((1, faces), jnp.int32)
    for g in range(groups):
        inside = face - g * per_group
        source = jnp.where(
            (inside >= 0) & (inside < per_group),
            block_place(tail[1:2, g : g + 1] ^ slot, groups) * per_group + inside,
            source,
        )
    order = one_hot(partner, faces)
    east_rows = exact_dot(order, packed_ref[:faces, :])
    west_rows = packed_ref[faces : 2 * faces, :]
    aligned_ref[:faces, :] = east_rows.astype(jnp.int32)
    aligned_ref[faces:, :] = west_rows.astype(jnp.int32)
    choice_ref[...] = jnp.zeros_like(choice_ref)
    choice_ref[:1, :faces] = lax.dot_general(
        source.astype(F32).astype(BF16),
        order.astype(BF16),
        (((1,), (1,)), ((), ())),
        preferred_element_type=F32,
    )
    gather_traces(padded_ref[...], aligned_ref, 0, east_ref)
    gather_traces(padded_ref[...], aligned_ref, faces, west_ref)
    east = east_ref[...]
    west = west_ref[...]
    to_a_ref[:faces, :] = jnp.where(odd, east, west)
    to_b_ref[:faces, :] = jnp.where(odd, west, east)
    for to_ref in (to_a_ref, to_b_ref):
        to_ref[faces : faces + SUBLANES, :] = choice_ref[...]
    to_a_ref[faces + SUBLANES :, :] = jnp.where(odd, east_rows, west_rows)
    to_b_ref[faces + SUBLANES :, :] = jnp.where(odd, west_rows, east_rows)


def blocks_kernel(first, packed_ref, last_ref, *block_refs):
    slot = lax.axis_index("blk")
    per_group = last_ref.shape[1]
    for place, block_ref in enumerate(block_refs):
        k = slot ^ (len(block_refs) - place)
        kept = pl.ds(pl.multiple_of(first + k * per_group, SUBLANES), per_group)
        block_ref[:per_group, :] = packed_ref[kept, :]
        block_ref[per_group:, :] = last_ref[k]


def thirds(value, axis):
    high, rest = halves(value)
    middle, low = halves(rest)
    return jnp.concatenate([high, middle, low], axis=axis).astype(BF16)


def sum_thirds(value, axis):
    size = value.shape[axis] // 3
    parts = [lax.slice_in_dim(value, k * size, (k + 1) * size, axis=axis) for k in range(3)]
    return (parts[0] + parts[1]) + parts[2]


def pick_rows(choice, value):
    picked = lax.dot_general(
        one_hot(choice, value.shape[0]).astype(BF16),
        thirds(value, 1),
        (((0,), (0,)), ((), ())),
        preferred_element_type=F32,
    )
    return sum_thirds(picked, 1)


def put_rows(choice, value, rows):
    put = jnp.dot(
        one_hot(choice, rows).astype(BF16), thirds(value, 1), preferred_element_type=F32
    )
    return sum_thirds(put, 1)


def stiffness_kernel(size, pairs_ref, blocks_ref, field_ref, *refs):
    out_ref = refs[min(1, len(refs) - 1)]
    block_rows = field_ref.shape[0]
    count = pairs_ref.shape[1]
    rows = block_rows + count
    width = math.lcm(size, LANES)
    tiles = width // LANES
    segments = width // size
    groups = size // segments
    batch = next(k for k in (4, 3, 2, 1) if groups % k == 0)

    def place(position):
        segment = sum(jnp.where(position >= k * size, 1, 0) for k in range(1, segments))
        return segment, position - segment * size

    def lanes_of(value, index):
        slabs = [
            jnp.take_along_axis(
                value[k : k + SUBLANES, :], index, axis=1, mode="promise_in_bounds"
            )
            for k in range(0, value.shape[0], SUBLANES)
        ]
        return jnp.concatenate(slabs, axis=0)

    field = field_ref[...]
    ends = jnp.concatenate([pairs_ref[:1, :], pairs_ref[1:, :]], axis=1)
    both = pick_rows(ends, field)
    left = both[:count]
    right = jnp.concatenate([field, both[count:]], axis=0)
    lane = lax.broadcasted_iota(jnp.int32, (SUBLANES, LANES), 1)
    places = [place(lane + t * LANES) for t in range(tiles)]
    repeated = jnp.concatenate([lanes_of(right, inside) for _, inside in places], axis=1)
    segment, inside = place(lax.broadcasted_iota(jnp.int32, (width, LANES), 0))
    column = lax.broadcasted_iota(jnp.int32, (width, LANES), 1)
    add_segments = jnp.where(segment == column % segments, 1.0, 0.0).astype(BF16)
    fold = jnp.where(inside == column, 1.0, 0.0).astype(BF16)
    dof_group = lax.broadcasted_iota(jnp.int32, (rows, LANES), 1) // segments
    total = jnp.zeros((rows, LANES), F32)
    turned = jnp.zeros((count, width), F32)
    for base in range(0, groups, batch):
        stack = []
        for g in range(base, base + batch):
            stored = blocks_ref[:, g * width : (g + 1) * width]
            product = stored * repeated
            high = product.astype(BF16)
            stack += [high, (product - high.astype(F32)).astype(BF16)]
            spread = [lanes_of(left, g * segments + segment) for segment, _ in places]
            turned = turned + stored[block_rows:] * jnp.concatenate(spread, axis=1)
        sums = jnp.dot(
            jnp.concatenate(stack, axis=0), add_segments, preferred_element_type=F32
        )
        for n in range(batch):
            part = sums[2 * n * rows : 2 * (n + 1) * rows]
            total = jnp.where(dof_group == base + n, part[:rows] + part[rows:], total)
    folded = sum_thirds(
        jnp.dot(thirds(turned, 0), fold, preferred_element_type=F32), 0
    )
    out_ref[...] = total[:block_rows] + put_rows(
        ends, jnp.concatenate([total[block_rows:], folded], axis=0), block_rows
    )
    if len(refs) > 1:
        aligned_ref, _, copy_ref, west_ref = refs
        copy_ref[...] = field
        gather_traces(field, aligned_ref, west_ref.shape[0], west_ref)


def spread_jumps(size, rows_ref, sides, block_rows):
    dof_of = lax.broadcasted_iota(jnp.int32, (size, LANES), 0).astype(F32).astype(BF16)
    row_of = lax.broadcasted_iota(jnp.int32, (block_rows, LANES), 0).astype(F32).astype(BF16)
    none = jnp.zeros((), BF16)
    one = jnp.ones((), BF16)

    def widened(value, f, rows):
        slab = jnp.broadcast_to(value[f : f + 1, :], (2 * SUBLANES, LANES)).astype(BF16)
        return jnp.concatenate([slab] * (rows // (2 * SUBLANES)), axis=0)

    total = jnp.zeros((size, 2 * block_rows), F32)
    for side, weighted in enumerate(sides):
        for k in range(0, weighted.shape[0], SUBLANES):
            high, low = halves(weighted[k : k + SUBLANES])
            first = side * weighted.shape[0] + k
            dof, row = split(rows_ref[first : first + SUBLANES, :], block_rows)
            dof = dof.astype(F32)
            row = row.astype(F32)
            for start in range(0, SUBLANES, BATCH):
                left = []
                right = []
                for f in range(start, start + BATCH):
                    here = row_of == widened(row, f, block_rows)
                    left.append(
                        jnp.concatenate(
                            [
                                jnp.where(here, widened(high, f, block_rows), none),
                                jnp.where(here, widened(low, f, block_rows), none),
                            ],
                            axis=0,
                        )
                    )
                    right.append(jnp.where(dof_of == widened(dof, f, size), one, none))
                total = total + lax.dot_general(
                    jnp.concatenate(right, axis=1),
                    jnp.concatenate(left, axis=1),
                    (((1,), (1,)), ((), ())),
                    preferred_element_type=F32,
                )
    total = total.T
    return total[:block_rows] + total[block_rows:]


def image_kernel(
    size,
    first,
    packed_ref,
    last_ref,
    choice_ref,
    aligned_ref,
    product_ref,
    east_ref,
    west_ref,
    from_a_ref,
    from_b_ref,
    *refs,
):
    *block_refs, image_ref, weights_east_ref, weights_west_ref, jump_ref = refs[:-2]
    next_rows_ref, last_rows_ref = refs[-2:]
    block_rows = product_ref.shape[0]
    faces = weights_east_ref.shape[0]
    per_group = last_ref.shape[1]
    slot = lax.axis_index("blk")
    odd = lax.rem(lax.axis_index("sub"), 2) == 1
    kept = pl.ds(pl.multiple_of(first + slot * per_group, SUBLANES), per_group)
    from_west = jnp.where(odd, from_b_ref[...], from_a_ref[...])
    from_east = jnp.where(odd, from_a_ref[...], from_b_ref[...])
    next_rows_ref[...] = from_east[faces + SUBLANES :].astype(jnp.int32)
    last_rows_ref[...] = from_west[faces + SUBLANES :].astype(jnp.int32)
    for row, block, part, weights_ref in (
        (choice_ref[...], packed_ref[kept, :], slice(0, per_group), weights_east_ref),
        (from_west[faces : faces + SUBLANES], last_ref[slot], slice(per_group, 2 * per_group), weights_west_ref),
    ):
        weights_ref[...] = pick_rows(
            row[:1, :faces].astype(jnp.int32),
            jnp.concatenate([block] + [block_ref[part, :] for block_ref in block_refs], axis=0),
        )
    jump_ref[...] = west_ref[...] - from_west[:faces]
    image_ref[...] = product_ref[...]
    image_ref[:, :size] = image_ref[:, :size] + spread_jumps(
        size,
        aligned_ref,
        (
            weights_east_ref[...] * (east_ref[...] - from_east[:faces]),
            weights_west_ref[...] * jump_ref[...],
        ),
        block_rows,
    )


def column_sums(value):
    return jnp.sum(value, axis=0, keepdims=True)


def sums_kernel(
    product_ref,
    weights_ref,
    own_ref,
    rows_ref,
    last_ref,
    jump_ref,
    field_ref,
    image_ref,
    sums_ref,
    arrived_ref,
):
    gather_traces(last_ref[...], rows_ref, 0, arrived_ref)
    largest = jnp.maximum(jnp.abs(field_ref[...]), jnp.abs(image_ref[...]))
    for value in (arrived_ref[...], jump_ref[...]):
        value = jnp.abs(value)
        for k in range(0, value.shape[0], largest.shape[0]):
            largest = jnp.maximum(largest, value[k : k + largest.shape[0]])
    largest = jnp.max(jnp.max(largest, axis=0, keepdims=True), axis=1, keepdims=True)
    level = jnp.where(largest > LARGE, 0, jnp.where(largest < SMALL, 2, 1))
    parts = []
    for scale in (SHRINK, 1.0, 1.0 / SHRINK):
        field = field_ref[...] * scale
        image = image_ref[...] * scale
        product = product_ref[...] * scale
        jump = own_ref[...] * scale - arrived_ref[...] * scale
        lam = weights_ref[...] * jump
        parts += [
            column_sums(field * field),
            column_sums(field * image),
            column_sums(image * image),
            column_sums(field * product) + column_sums(lam * (jump_ref[...] * scale)),
            column_sums(image * product) + column_sums(lam * jump),
        ]
        parts += [jnp.zeros_like(parts[0])] * (SUBLANES - MARK)
    whole = jnp.sum(jnp.concatenate(parts, axis=0), axis=1, keepdims=True)
    row = lax.broadcasted_iota(jnp.int32, (len(parts), LANES), 0)
    lane = lax.broadcasted_iota(jnp.int32, (len(parts), LANES), 1)
    first = SUBLANES * level
    whole = jnp.where(row == first + MARK, 1.0, whole)
    chosen = (lane == row) & (row >= first) & (row < first + SUBLANES)
    packed = column_sums(jnp.where(chosen, whole, 0.0))
    sums_ref[...] = jnp.broadcast_to(packed[None], sums_ref.shape)


def second_kernel(
    size,
    aligned_ref,
    product_ref,
    weights_east_ref,
    weights_west_ref,
    image_ref,
    west_ref,
    rows_ref,
    next_ref,
    from_last_ref,
    second_ref,
    east_ref,
    from_next_ref,
):
    block_rows = product_ref.shape[0]
    gather_traces(image_ref[...], aligned_ref, 0, east_ref)
    gather_traces(next_ref[...], rows_ref, 0, from_next_ref)
    second_ref[...] = product_ref[...]
    second_ref[:, :size] = second_ref[:, :size] + spread_jumps(
        size,
        aligned_ref,
        [
            weights_ref[...] * (own_ref[...] - arrived_ref[...])
            for weights_ref, own_ref, arrived_ref in (
                (weights_east_ref, east_ref, from_next_ref),
                (weights_west_ref, west_ref, from_last_ref),
            )
        ],
        block_rows,
    )


def final_kernel(field_ref, image_ref, second_ref, sums_ref, solution_ref, residual_ref):
    size = solution_ref.shape[1]
    row = jnp.broadcast_to(jnp.sum(sums_ref[...], axis=0), (SUBLANES, LANES))

    def lane(k):
        place = jnp.full((SUBLANES, LANES), k, jnp.int32)
        return jnp.take_along_axis(row, place, axis=1, mode="promise_in_bounds")[:1, :size]

    large, plain = (lane(SUBLANES * level + MARK) > 0.0 for level in (0, 1))

    def entry(k):
        sums = [lane(SUBLANES * level + k) for level in range(3)]
        lower = SHRINK * SHRINK
        return jnp.where(
            large,
            sums[0] + sums[1] * lower,
            jnp.where(plain, sums[1] + sums[2] * lower, sums[2]),
        )

    bb, bq, qq, bw, qw = (entry(k) for k in range(5))
    field = field_ref[:, :size]
    image = image_ref[:, :size]
    second = second_ref[:, :size]
    alpha = bb / bq
    norm = bb - alpha * (2.0 * bq - alpha * qq)
    beta = norm / bb
    grown = 1.0 + beta
    energy = grown * (grown * bq - alpha * (bw + qq)) + alpha * alpha * qw
    alpha_next = norm / energy
    residual = field - alpha * image
    direction = residual + beta * field
    moved = (image - alpha * second) + beta * image
    solution_ref[...] = alpha * field + alpha_next * direction
    residual_ref[...] = residual - alpha_next * moved


def swap(value, odd):
    count = lax.axis_size("sub")
    pairs = []
    for first in range(odd, count, 2):
        second = (first + 1) % count
        pairs += [(first, second), (second, first)]
    return lax.ppermute(value, "sub", pairs)


def from_behind(value, axis, steps):
    count = lax.axis_size(axis)
    pairs = [(source, (source + steps) % count) for source in range(count)]
    return lax.ppermute(value, axis, pairs)


def swap_slots(value, k):
    count = lax.axis_size("blk")
    return lax.ppermute(value, "blk", [(slot, slot ^ k) for slot in range(count)])


def on_device(
    right_side, stiffness, block_pairs, trace_rows, partner_face, owner_list, mortar_weight
):
    field = right_side[0, 0].T
    block_rows, size = field.shape
    blocks = stiffness[0, 0].astype(F32)
    pairs = block_pairs[0, 0]
    rows = trace_rows[0, 0]
    partner = partner_face[0, 0]
    owners = owner_list[0, 0]
    faces = partner.shape[0]
    devices = lax.axis_size("sub") * lax.axis_size("blk")

    own_weights = mortar_weight[0, 0]
    last_weights = from_behind(own_weights, "sub", 1)
    last = 2 * faces + block_rows

    def placed(value, first):
        below = last + SUBLANES + faces - first - value.shape[0]
        return jnp.pad(value, ((first, below), (0, LANES - value.shape[1])))

    indices = placed(rows, 0) + placed(partner_face[0], last) + placed(owner_list[0], last + 1)
    packed = (
        indices.astype(F32)
        + placed(field, 2 * faces)
        + placed(own_weights.reshape(faces, LANES), last + SUBLANES)
    )
    aligned, padded, choice, east, west, to_a, to_b = call(
        functools.partial(first_kernel, owners.shape[0]),
        [
            shape(2 * faces, jnp.int32),
            shape(block_rows),
            shape(SUBLANES),
            shape(faces),
            shape(faces),
            shape(2 * faces + SUBLANES),
            shape(2 * faces + SUBLANES),
        ],
        [(packed, VMEM)],
    )
    from_a = swap(to_a, 1)
    from_b = swap(to_b, 0)
    slots, per_group, _ = own_weights.shape
    blocks_to = call(
        functools.partial(blocks_kernel, last + SUBLANES),
        [shape(2 * per_group)] * (slots - 1),
        [(packed, VMEM), (last_weights, VMEM)],
        flops=1,
        moved=1,
    )
    blocks_from = [
        swap_slots(block, k) for k, block in zip(range(slots - 1, 0, -1), blocks_to)
    ]

    def stiff(vector, *ordered):
        return call(
            functools.partial(stiffness_kernel, size),
            [shape(block_rows)] * (1 + len(ordered)) + [shape(faces)] * len(ordered),
            [(value, VMEM) for value in (pairs, blocks, vector, *ordered)],
        )

    (product,) = stiff(padded)
    image, weights_east, weights_west, jump, next_rows, last_rows = call(
        functools.partial(image_kernel, size, last + SUBLANES),
        [shape(block_rows)] + [shape(faces)] * 3 + [shape(faces, jnp.int32)] * 2,
        [
            (value, VMEM)
            for value in (
                packed,
                last_weights,
                choice,
                aligned,
                product,
                east,
                west,
                from_a,
                from_b,
                *blocks_from,
            )
        ],
    )
    from_last = from_behind(image, "sub", 1)
    product, copied, west = stiff(image, aligned)
    from_next = from_behind(copied, "sub", -1)
    sums, arrived = call(
        sums_kernel,
        [jax.ShapeDtypeStruct((devices, 1, LANES), F32), shape(faces)],
        [
            (value, VMEM)
            for value in (product, weights_west, west, last_rows, from_last, jump, padded, image)
        ],
    )
    (second,) = call(
        functools.partial(second_kernel, size),
        [shape(block_rows)],
        [
            (value, VMEM)
            for value in (
                aligned,
                product,
                weights_east,
                weights_west,
                image,
                west,
                next_rows,
                from_next,
                arrived,
            )
        ],
        scratch=[pltpu.VMEM((faces, LANES), F32)] * 2,
        flops=1_000_000_000,
    )
    sums = lax.all_to_all(sums, ("sub", "blk"), split_axis=0, concat_axis=0, tiled=True)
    solution_field, residual = call(
        final_kernel,
        [jax.ShapeDtypeStruct((block_rows, size), F32)] * 2,
        [(padded, VMEM), (image, VMEM), (second, VMEM), (sums, VMEM)],
    )
    return (solution_field.T[None, None], residual.T[None, None])


def solution(mesh):
    in_specs = (
        P("sub", "blk", None, None),
        P("sub", "blk", None, None),
        P("sub", "blk", None, None),
        P("sub", "blk", None, None),
        P("sub", "blk", None),
        P("sub", "blk", None),
        P("sub", "blk", None, None, None),
    )
    out_specs = (P("sub", "blk", None, None), P("sub", "blk", None, None))
    return jax.shard_map(
        on_device, mesh=mesh, in_specs=in_specs, out_specs=out_specs, check_vma=False
    )
```

```python
import functools
import math

import jax
import jax.numpy as jnp
from jax import lax
from jax.experimental import pallas as pl
from jax.experimental.pallas import tpu as pltpu
from jax.sharding import PartitionSpec as P

LANES = 128
SUBLANES = 8
VMEM = pl.BlockSpec(memory_space=pltpu.VMEM)
BATCH = 16
MARK = 5
LARGE = 2.0**40
SMALL = 2.0**-40
SHRINK = 2.0**-60
F32 = jnp.float32
BF16 = jnp.bfloat16


def call(body, outs, inputs, scratch=(), flops=1_000_000, moved=1_000_000):
    return pl.pallas_call(
        body,
        out_shape=outs,
        in_specs=[spec for _, spec in inputs],
        out_specs=[VMEM] * len(outs),
        scratch_shapes=list(scratch),
        compiler_params=pltpu.CompilerParams(vmem_limit_bytes=32 * 1024 * 1024),
        cost_estimate=pl.CostEstimate(
            flops=flops, bytes_accessed=moved, transcendentals=0
        ),
    )(*[value for value, _ in inputs])


def shape(rows, dtype=F32):
    return jax.ShapeDtypeStruct((rows, LANES), dtype)


def halves(value):
    high = value.astype(BF16).astype(F32)
    return high, value - high


def gather_traces(field, rows_ref, rows_first, target):
    block_rows = field.shape[0]
    spread = [
        jnp.broadcast_to(field[i : i + 1, :], (SUBLANES, LANES)) for i in range(block_rows)
    ]
    for k in range(target.shape[0] // SUBLANES):
        index = rows_ref[rows_first + k * SUBLANES : rows_first + (k + 1) * SUBLANES, :]
        dof, row = split(index, block_rows)
        bits = {}

        def pick(first, count):
            if count == 1:
                return jnp.take_along_axis(spread[first], dof, axis=1, mode="promise_in_bounds")
            half = 1 << ((count - 1).bit_length() - 1)
            if half not in bits:
                bits[half] = (row & half) != 0
            lower = pick(first, half)
            return jnp.where(bits[half], pick(first + half, count - half), lower)

        target[k * SUBLANES : (k + 1) * SUBLANES, :] = pick(0, block_rows)


def tile(k):
    return pl.ds(pl.multiple_of(k * SUBLANES, SUBLANES), SUBLANES)


def split(index, block_rows):
    if block_rows & (block_rows - 1) == 0:
        shift = block_rows.bit_length() - 1
        return index >> shift, index & (block_rows - 1)
    return lax.div(index, block_rows), lax.rem(index, block_rows)


def one_hot(place, count):
    row = lax.broadcasted_iota(jnp.int32, (count, place.shape[1]), 0)
    return jnp.where(row == place, 1.0, 0.0)


def exact_dot(left, right):
    return jnp.dot(
        left, right, precision=lax.Precision.HIGHEST, preferred_element_type=F32
    )


def block_place(k, groups):
    return jnp.where(k == 0, 0, groups - k)


def first_kernel(
    groups, packed_ref, aligned_ref, padded_ref, choice_ref, east_ref, west_ref, to_a_ref, to_b_ref
):
    faces = aligned_ref.shape[0] // 2
    block_rows = padded_ref.shape[0]
    per_group = faces // groups
    slot = lax.axis_index("blk")
    odd = lax.rem(lax.axis_index("sub"), 2) == 1
    padded_ref[...] = packed_ref[2 * faces : 2 * faces + block_rows, :]
    last = 2 * faces + block_rows
    tail = packed_ref[last : last + SUBLANES, :].astype(jnp.int32)
    partner = tail[:1, :faces]
    face = lax.broadcasted_iota(jnp.int32, (1, faces), 1)
    source = jnp.zeros((1, faces), jnp.int32)
    for g in range(groups):
        inside = face - g * per_group
        source = jnp.where(
            (inside >= 0) & (inside < per_group),
            block_place(tail[1:2, g : g + 1] ^ slot, groups) * per_group + inside,
            source,
        )
    order = one_hot(partner, faces)
    east_rows = exact_dot(order, packed_ref[:faces, :])
    west_rows = packed_ref[faces : 2 * faces, :]
    aligned_ref[:faces, :] = east_rows.astype(jnp.int32)
    aligned_ref[faces:, :] = west_rows.astype(jnp.int32)
    choice_ref[...] = jnp.zeros_like(choice_ref)
    choice_ref[:1, :faces] = lax.dot_general(
        source.astype(F32).astype(BF16),
        order.astype(BF16),
        (((1,), (1,)), ((), ())),
        preferred_element_type=F32,
    )
    gather_traces(padded_ref[...], aligned_ref, 0, east_ref)
    gather_traces(padded_ref[...], aligned_ref, faces, west_ref)
    east = east_ref[...]
    west = west_ref[...]
    to_a_ref[:faces, :] = jnp.where(odd, east, west)
    to_b_ref[:faces, :] = jnp.where(odd, west, east)
    for to_ref in (to_a_ref, to_b_ref):
        to_ref[faces : faces + SUBLANES, :] = choice_ref[...]
    to_a_ref[faces + SUBLANES :, :] = jnp.where(odd, east_rows, west_rows)
    to_b_ref[faces + SUBLANES :, :] = jnp.where(odd, west_rows, east_rows)


def blocks_kernel(first, packed_ref, last_ref, *block_refs):
    slot = lax.axis_index("blk")
    per_group = last_ref.shape[1]
    for place, block_ref in enumerate(block_refs):
        k = slot ^ (len(block_refs) - place)
        kept = pl.ds(pl.multiple_of(first + k * per_group, SUBLANES), per_group)
        block_ref[:per_group, :] = packed_ref[kept, :]
        block_ref[per_group:, :] = last_ref[k]


def thirds(value, axis):
    high, rest = halves(value)
    middle, low = halves(rest)
    return jnp.concatenate([high, middle, low], axis=axis).astype(BF16)


def sum_thirds(value, axis):
    size = value.shape[axis] // 3
    parts = [lax.slice_in_dim(value, k * size, (k + 1) * size, axis=axis) for k in range(3)]
    return (parts[0] + parts[1]) + parts[2]


def pick_rows(choice, value):
    picked = lax.dot_general(
        one_hot(choice, value.shape[0]).astype(BF16),
        thirds(value, 1),
        (((0,), (0,)), ((), ())),
        preferred_element_type=F32,
    )
    return sum_thirds(picked, 1)


def put_rows(choice, value, rows):
    put = jnp.dot(
        one_hot(choice, rows).astype(BF16), thirds(value, 1), preferred_element_type=F32
    )
    return sum_thirds(put, 1)


def stiffness_kernel(size, pairs_ref, blocks_ref, field_ref, *refs):
    out_ref = refs[min(1, len(refs) - 1)]
    block_rows = field_ref.shape[0]
    count = pairs_ref.shape[1]
    rows = block_rows + count
    width = math.lcm(size, LANES)
    tiles = width // LANES
    segments = width // size
    groups = size // segments
    batch = next(k for k in (4, 3, 2, 1) if groups % k == 0)

    def place(position):
        segment = sum(jnp.where(position >= k * size, 1, 0) for k in range(1, segments))
        return segment, position - segment * size

    def lanes_of(value, index):
        slabs = [
            jnp.take_along_axis(
                value[k : k + SUBLANES, :], index, axis=1, mode="promise_in_bounds"
            )
            for k in range(0, value.shape[0], SUBLANES)
        ]
        return jnp.concatenate(slabs, axis=0)

    field = field_ref[...]
    ends = jnp.concatenate([pairs_ref[:1, :], pairs_ref[1:, :]], axis=1)
    both = pick_rows(ends, field)
    left = both[:count]
    right = jnp.concatenate([field, both[count:]], axis=0)
    lane = lax.broadcasted_iota(jnp.int32, (SUBLANES, LANES), 1)
    places = [place(lane + t * LANES) for t in range(tiles)]
    repeated = jnp.concatenate([lanes_of(right, inside) for _, inside in places], axis=1)
    segment, inside = place(lax.broadcasted_iota(jnp.int32, (width, LANES), 0))
    column = lax.broadcasted_iota(jnp.int32, (width, LANES), 1)
    add_segments = jnp.where(segment == column % segments, 1.0, 0.0).astype(BF16)
    fold = jnp.where(inside == column, 1.0, 0.0).astype(BF16)
    dof_group = lax.broadcasted_iota(jnp.int32, (rows, LANES), 1) // segments
    total = jnp.zeros((rows, LANES), F32)
    turned = jnp.zeros((count, width), F32)
    for base in range(0, groups, batch):
        stack = []
        for g in range(base, base + batch):
            stored = blocks_ref[:, g * width : (g + 1) * width]
            product = stored * repeated
            high = product.astype(BF16)
            stack += [high, (product - high.astype(F32)).astype(BF16)]
            spread = [lanes_of(left, g * segments + segment) for segment, _ in places]
            turned = turned + stored[block_rows:] * jnp.concatenate(spread, axis=1)
        sums = jnp.dot(
            jnp.concatenate(stack, axis=0), add_segments, preferred_element_type=F32
        )
        for n in range(batch):
            part = sums[2 * n * rows : 2 * (n + 1) * rows]
            total = jnp.where(dof_group == base + n, part[:rows] + part[rows:], total)
    folded = sum_thirds(
        jnp.dot(thirds(turned, 0), fold, preferred_element_type=F32), 0
    )
    out_ref[...] = total[:block_rows] + put_rows(
        ends, jnp.concatenate([total[block_rows:], folded], axis=0), block_rows
    )
    if len(refs) > 1:
        aligned_ref, _, copy_ref, west_ref = refs
        copy_ref[...] = field
        gather_traces(field, aligned_ref, west_ref.shape[0], west_ref)


def spread_jumps(size, rows_ref, sides, block_rows):
    dof_of = lax.broadcasted_iota(jnp.int32, (size, LANES), 0).astype(F32).astype(BF16)
    row_of = lax.broadcasted_iota(jnp.int32, (block_rows, LANES), 0).astype(F32).astype(BF16)
    none = jnp.zeros((), BF16)
    one = jnp.ones((), BF16)

    def widened(value, f, rows):
        slab = jnp.broadcast_to(value[f : f + 1, :], (2 * SUBLANES, LANES)).astype(BF16)
        return jnp.concatenate([slab] * (rows // (2 * SUBLANES)), axis=0)

    total = jnp.zeros((size, 2 * block_rows), F32)
    left, right = [], []
    for side, weighted in enumerate(sides):
        for k in range(0, weighted.shape[0], SUBLANES):
            high, low = halves(weighted[k : k + SUBLANES])
            first = side * weighted.shape[0] + k
            dof, row = split(rows_ref[first : first + SUBLANES, :], block_rows)
            dof = dof.astype(F32)
            row = row.astype(F32)
            for f in range(SUBLANES):
                here = row_of == widened(row, f, block_rows)
                left.append(
                    jnp.concatenate(
                        [
                            jnp.where(here, widened(high, f, block_rows), none),
                            jnp.where(here, widened(low, f, block_rows), none),
                        ],
                        axis=0,
                    )
                )
                right.append(jnp.where(dof_of == widened(dof, f, size), one, none))
            if len(left) < BATCH:
                continue
            total = total + lax.dot_general(
                jnp.concatenate(right, axis=1),
                jnp.concatenate(left, axis=1),
                (((1,), (1,)), ((), ())),
                preferred_element_type=F32,
            )
            left, right = [], []
    total = total.T
    return total[:block_rows] + total[block_rows:]


def image_kernel(
    size,
    first,
    packed_ref,
    last_ref,
    choice_ref,
    aligned_ref,
    product_ref,
    east_ref,
    west_ref,
    from_a_ref,
    from_b_ref,
    *refs,
):
    *block_refs, image_ref, weights_east_ref, weights_west_ref, jump_ref = refs[:-2]
    next_rows_ref, last_rows_ref = refs[-2:]
    block_rows = product_ref.shape[0]
    faces = weights_east_ref.shape[0]
    per_group = last_ref.shape[1]
    slot = lax.axis_index("blk")
    odd = lax.rem(lax.axis_index("sub"), 2) == 1
    kept = pl.ds(pl.multiple_of(first + slot * per_group, SUBLANES), per_group)
    from_west = jnp.where(odd, from_b_ref[...], from_a_ref[...])
    from_east = jnp.where(odd, from_a_ref[...], from_b_ref[...])
    next_rows_ref[...] = from_east[faces + SUBLANES :].astype(jnp.int32)
    last_rows_ref[...] = from_west[faces + SUBLANES :].astype(jnp.int32)
    for row, block, part, weights_ref in (
        (choice_ref[...], packed_ref[kept, :], slice(0, per_group), weights_east_ref),
        (from_west[faces : faces + SUBLANES], last_ref[slot], slice(per_group, 2 * per_group), weights_west_ref),
    ):
        weights_ref[...] = pick_rows(
            row[:1, :faces].astype(jnp.int32),
            jnp.concatenate([block] + [block_ref[part, :] for block_ref in block_refs], axis=0),
        )
    jump_ref[...] = west_ref[...] - from_west[:faces]
    image_ref[...] = product_ref[...]
    image_ref[:, :size] = image_ref[:, :size] + spread_jumps(
        size,
        aligned_ref,
        (
            weights_east_ref[...] * (east_ref[...] - from_east[:faces]),
            weights_west_ref[...] * jump_ref[...],
        ),
        block_rows,
    )


def column_sums(value):
    return jnp.sum(value, axis=0, keepdims=True)


def sums_kernel(
    product_ref,
    weights_ref,
    own_ref,
    rows_ref,
    last_ref,
    jump_ref,
    field_ref,
    image_ref,
    sums_ref,
    arrived_ref,
):
    gather_traces(last_ref[...], rows_ref, 0, arrived_ref)
    largest = jnp.maximum(jnp.abs(field_ref[...]), jnp.abs(image_ref[...]))
    for value in (arrived_ref[...], jump_ref[...]):
        value = jnp.abs(value)
        for k in range(0, value.shape[0], largest.shape[0]):
            largest = jnp.maximum(largest, value[k : k + largest.shape[0]])
    largest = jnp.max(jnp.max(largest, axis=0, keepdims=True), axis=1, keepdims=True)
    level = jnp.where(largest > LARGE, 0, jnp.where(largest < SMALL, 2, 1))
    parts = []
    for scale in (SHRINK, 1.0, 1.0 / SHRINK):
        field = field_ref[...] * scale
        image = image_ref[...] * scale
        product = product_ref[...] * scale
        jump = own_ref[...] * scale - arrived_ref[...] * scale
        lam = weights_ref[...] * jump
        parts += [
            column_sums(field * field),
            column_sums(field * image),
            column_sums(image * image),
            column_sums(field * product) + column_sums(lam * (jump_ref[...] * scale)),
            column_sums(image * product) + column_sums(lam * jump),
        ]
        parts += [jnp.zeros_like(parts[0])] * (SUBLANES - MARK)
    whole = jnp.sum(jnp.concatenate(parts, axis=0), axis=1, keepdims=True)
    row = lax.broadcasted_iota(jnp.int32, (len(parts), LANES), 0)
    lane = lax.broadcasted_iota(jnp.int32, (len(parts), LANES), 1)
    first = SUBLANES * level
    whole = jnp.where(row == first + MARK, 1.0, whole)
    chosen = (lane == row) & (row >= first) & (row < first + SUBLANES)
    packed = column_sums(jnp.where(chosen, whole, 0.0))
    sums_ref[...] = jnp.broadcast_to(packed[None], sums_ref.shape)


def second_kernel(
    size,
    aligned_ref,
    product_ref,
    weights_east_ref,
    weights_west_ref,
    image_ref,
    west_ref,
    rows_ref,
    next_ref,
    from_last_ref,
    second_ref,
    east_ref,
    from_next_ref,
):
    block_rows = product_ref.shape[0]
    gather_traces(image_ref[...], aligned_ref, 0, east_ref)
    gather_traces(next_ref[...], rows_ref, 0, from_next_ref)
    second_ref[...] = product_ref[...]
    second_ref[:, :size] = second_ref[:, :size] + spread_jumps(
        size,
        aligned_ref,
        [
            weights_ref[...] * (own_ref[...] - arrived_ref[...])
            for weights_ref, own_ref, arrived_ref in (
                (weights_east_ref, east_ref, from_next_ref),
                (weights_west_ref, west_ref, from_last_ref),
            )
        ],
        block_rows,
    )


def final_kernel(field_ref, image_ref, second_ref, sums_ref, solution_ref, residual_ref):
    size = solution_ref.shape[1]
    row = jnp.broadcast_to(jnp.sum(sums_ref[...], axis=0), (SUBLANES, LANES))

    def lane(k):
        place = jnp.full((SUBLANES, LANES), k, jnp.int32)
        return jnp.take_along_axis(row, place, axis=1, mode="promise_in_bounds")[:1, :size]

    large, plain = (lane(SUBLANES * level + MARK) > 0.0 for level in (0, 1))

    def entry(k):
        sums = [lane(SUBLANES * level + k) for level in range(3)]
        lower = SHRINK * SHRINK
        return jnp.where(
            large,
            sums[0] + sums[1] * lower,
            jnp.where(plain, sums[1] + sums[2] * lower, sums[2]),
        )

    bb, bq, qq, bw, qw = (entry(k) for k in range(5))
    field = field_ref[:, :size]
    image = image_ref[:, :size]
    second = second_ref[:, :size]
    alpha = bb / bq
    norm = bb - alpha * (2.0 * bq - alpha * qq)
    beta = norm / bb
    grown = 1.0 + beta
    energy = grown * (grown * bq - alpha * (bw + qq)) + alpha * alpha * qw
    alpha_next = norm / energy
    residual = field - alpha * image
    direction = residual + beta * field
    moved = (image - alpha * second) + beta * image
    solution_ref[...] = alpha * field + alpha_next * direction
    residual_ref[...] = residual - alpha_next * moved


def swap(value, odd):
    count = lax.axis_size("sub")
    pairs = []
    for first in range(odd, count, 2):
        second = (first + 1) % count
        pairs += [(first, second), (second, first)]
    return lax.ppermute(value, "sub", pairs)


def from_behind(value, axis, steps):
    count = lax.axis_size(axis)
    pairs = [(source, (source + steps) % count) for source in range(count)]
    return lax.ppermute(value, axis, pairs)


def swap_slots(value, k):
    count = lax.axis_size("blk")
    return lax.ppermute(value, "blk", [(slot, slot ^ k) for slot in range(count)])


def on_device(
    right_side, stiffness, block_pairs, trace_rows, partner_face, owner_list, mortar_weight
):
    field = right_side[0, 0].T
    block_rows, size = field.shape
    blocks = stiffness[0, 0].astype(F32)
    pairs = block_pairs[0, 0]
    rows = trace_rows[0, 0]
    partner = partner_face[0, 0]
    owners = owner_list[0, 0]
    faces = partner.shape[0]
    devices = lax.axis_size("sub") * lax.axis_size("blk")

    own_weights = mortar_weight[0, 0]
    last_weights = from_behind(own_weights, "sub", 1)
    last = 2 * faces + block_rows

    def placed(value, first):
        below = last + SUBLANES + faces - first - value.shape[0]
        return jnp.pad(value, ((first, below), (0, LANES - value.shape[1])))

    indices = placed(rows, 0) + placed(partner_face[0], last) + placed(owner_list[0], last + 1)
    packed = (
        indices.astype(F32)
        + placed(field, 2 * faces)
        + placed(own_weights.reshape(faces, LANES), last + SUBLANES)
    )
    aligned, padded, choice, east, west, to_a, to_b = call(
        functools.partial(first_kernel, owners.shape[0]),
        [
            shape(2 * faces, jnp.int32),
            shape(block_rows),
            shape(SUBLANES),
            shape(faces),
            shape(faces),
            shape(2 * faces + SUBLANES),
            shape(2 * faces + SUBLANES),
        ],
        [(packed, VMEM)],
    )
    from_a = swap(to_a, 1)
    from_b = swap(to_b, 0)
    slots, per_group, _ = own_weights.shape
    blocks_to = call(
        functools.partial(blocks_kernel, last + SUBLANES),
        [shape(2 * per_group)] * (slots - 1),
        [(packed, VMEM), (last_weights, VMEM)],
        flops=1,
        moved=1,
    )
    blocks_from = [
        swap_slots(block, k) for k, block in zip(range(slots - 1, 0, -1), blocks_to)
    ]

    def stiff(vector, *ordered):
        return call(
            functools.partial(stiffness_kernel, size),
            [shape(block_rows)] * (1 + len(ordered)) + [shape(faces)] * len(ordered),
            [(value, VMEM) for value in (pairs, blocks, vector, *ordered)],
        )

    (product,) = stiff(padded)
    image, weights_east, weights_west, jump, next_rows, last_rows = call(
        functools.partial(image_kernel, size, last + SUBLANES),
        [shape(block_rows)] + [shape(faces)] * 3 + [shape(faces, jnp.int32)] * 2,
        [
            (value, VMEM)
            for value in (
                packed,
                last_weights,
                choice,
                aligned,
                product,
                east,
                west,
                from_a,
                from_b,
                *blocks_from,
            )
        ],
    )
    from_last = from_behind(image, "sub", 1)
    product, copied, west = stiff(image, aligned)
    from_next = from_behind(copied, "sub", -1)
    sums, arrived = call(
        sums_kernel,
        [jax.ShapeDtypeStruct((devices, 1, LANES), F32), shape(faces)],
        [
            (value, VMEM)
            for value in (product, weights_west, west, last_rows, from_last, jump, padded, image)
        ],
    )
    (second,) = call(
        functools.partial(second_kernel, size),
        [shape(block_rows)],
        [
            (value, VMEM)
            for value in (
                aligned,
                product,
                weights_east,
                weights_west,
                image,
                west,
                next_rows,
                from_next,
                arrived,
            )
        ],
        scratch=[pltpu.VMEM((faces, LANES), F32)] * 2,
        flops=1_000_000_000,
    )
    sums = lax.all_to_all(sums, ("sub", "blk"), split_axis=0, concat_axis=0, tiled=True)
    solution_field, residual = call(
        final_kernel,
        [jax.ShapeDtypeStruct((block_rows, size), F32)] * 2,
        [(padded, VMEM), (image, VMEM), (second, VMEM), (sums, VMEM)],
    )
    return (solution_field.T[None, None], residual.T[None, None])


def solution(mesh):
    in_specs = (
        P("sub", "blk", None, None),
        P("sub", "blk", None, None),
        P("sub", "blk", None, None),
        P("sub", "blk", None, None),
        P("sub", "blk", None),
        P("sub", "blk", None),
        P("sub", "blk", None, None, None),
    )
    out_specs = (P("sub", "blk", None, None), P("sub", "blk", None, None))
    return jax.shard_map(
        on_device, mesh=mesh, in_specs=in_specs, out_specs=out_specs, check_vma=False
    )
```

```python
import functools
import math

import jax
import jax.numpy as jnp
from jax import lax
from jax.experimental import pallas as pl
from jax.experimental.pallas import tpu as pltpu
from jax.sharding import PartitionSpec as P

LANES = 128
SUBLANES = 8
VMEM = pl.BlockSpec(memory_space=pltpu.VMEM)
MARK = 5
LARGE = 2.0**40
SMALL = 2.0**-40
SHRINK = 2.0**-60
F32 = jnp.float32
BF16 = jnp.bfloat16


def call(body, outs, inputs, scratch=(), flops=1_000_000, moved=1_000_000):
    return pl.pallas_call(
        body,
        out_shape=outs,
        in_specs=[spec for _, spec in inputs],
        out_specs=[VMEM] * len(outs),
        scratch_shapes=list(scratch),
        compiler_params=pltpu.CompilerParams(vmem_limit_bytes=32 * 1024 * 1024),
        cost_estimate=pl.CostEstimate(
            flops=flops, bytes_accessed=moved, transcendentals=0
        ),
    )(*[value for value, _ in inputs])


def shape(rows, dtype=F32):
    return jax.ShapeDtypeStruct((rows, LANES), dtype)


def halves(value):
    high = value.astype(BF16).astype(F32)
    return high, value - high


def gather_traces(field, rows_ref, rows_first, target):
    block_rows = field.shape[0]
    spread = [
        jnp.broadcast_to(field[i : i + 1, :], (SUBLANES, LANES)) for i in range(block_rows)
    ]
    for k in range(target.shape[0] // SUBLANES):
        index = rows_ref[rows_first + k * SUBLANES : rows_first + (k + 1) * SUBLANES, :]
        dof, row = split(index, block_rows)
        bits = {}

        def pick(first, count):
            if count == 1:
                return jnp.take_along_axis(spread[first], dof, axis=1, mode="promise_in_bounds")
            half = 1 << ((count - 1).bit_length() - 1)
            if half not in bits:
                bits[half] = (row & half) != 0
            lower = pick(first, half)
            return jnp.where(bits[half], pick(first + half, count - half), lower)

        target[k * SUBLANES : (k + 1) * SUBLANES, :] = pick(0, block_rows)


def tile(k):
    return pl.ds(pl.multiple_of(k * SUBLANES, SUBLANES), SUBLANES)


def split(index, block_rows):
    if block_rows & (block_rows - 1) == 0:
        shift = block_rows.bit_length() - 1
        return index >> shift, index & (block_rows - 1)
    return lax.div(index, block_rows), lax.rem(index, block_rows)


def one_hot(place, count):
    row = lax.broadcasted_iota(jnp.int32, (count, place.shape[1]), 0)
    return jnp.where(row == place, 1.0, 0.0)


def exact_dot(left, right):
    return jnp.dot(
        left, right, precision=lax.Precision.HIGHEST, preferred_element_type=F32
    )


def block_place(k, groups):
    return jnp.where(k == 0, 0, groups - k)


def first_kernel(
    groups, packed_ref, aligned_ref, padded_ref, choice_ref, east_ref, west_ref, to_a_ref, to_b_ref
):
    faces = aligned_ref.shape[0] // 2
    block_rows = padded_ref.shape[0]
    per_group = faces // groups
    slot = lax.axis_index("blk")
    odd = lax.rem(lax.axis_index("sub"), 2) == 1
    padded_ref[...] = packed_ref[2 * faces : 2 * faces + block_rows, :]
    last = 2 * faces + block_rows
    tail = packed_ref[last : last + SUBLANES, :].astype(jnp.int32)
    partner = tail[:1, :faces]
    face = lax.broadcasted_iota(jnp.int32, (1, faces), 1)
    source = jnp.zeros((1, faces), jnp.int32)
    for g in range(groups):
        inside = face - g * per_group
        source = jnp.where(
            (inside >= 0) & (inside < per_group),
            block_place(tail[1:2, g : g + 1] ^ slot, groups) * per_group + inside,
            source,
        )
    order = one_hot(partner, faces)
    east_rows = exact_dot(order, packed_ref[:faces, :])
    west_rows = packed_ref[faces : 2 * faces, :]
    aligned_ref[:faces, :] = east_rows.astype(jnp.int32)
    aligned_ref[faces:, :] = west_rows.astype(jnp.int32)
    choice_ref[...] = jnp.zeros_like(choice_ref)
    choice_ref[:1, :faces] = lax.dot_general(
        source.astype(F32).astype(BF16),
        order.astype(BF16),
        (((1,), (1,)), ((), ())),
        preferred_element_type=F32,
    )
    gather_traces(padded_ref[...], aligned_ref, 0, east_ref)
    gather_traces(padded_ref[...], aligned_ref, faces, west_ref)
    east = east_ref[...]
    west = west_ref[...]
    to_a_ref[:faces, :] = jnp.where(odd, east, west)
    to_b_ref[:faces, :] = jnp.where(odd, west, east)
    for to_ref in (to_a_ref, to_b_ref):
        to_ref[faces : faces + SUBLANES, :] = choice_ref[...]
    to_a_ref[faces + SUBLANES :, :] = jnp.where(odd, east_rows, west_rows)
    to_b_ref[faces + SUBLANES :, :] = jnp.where(odd, west_rows, east_rows)


def blocks_kernel(first, packed_ref, last_ref, *block_refs):
    slot = lax.axis_index("blk")
    per_group = last_ref.shape[1]
    for place, block_ref in enumerate(block_refs):
        k = slot ^ (len(block_refs) - place)
        kept = pl.ds(pl.multiple_of(first + k * per_group, SUBLANES), per_group)
        block_ref[:per_group, :] = packed_ref[kept, :]
        block_ref[per_group:, :] = last_ref[k]


def thirds(value, axis):
    high, rest = halves(value)
    middle, low = halves(rest)
    return jnp.concatenate([high, middle, low], axis=axis).astype(BF16)


def sum_thirds(value, axis):
    size = value.shape[axis] // 3
    parts = [lax.slice_in_dim(value, k * size, (k + 1) * size, axis=axis) for k in range(3)]
    return (parts[0] + parts[1]) + parts[2]


def pick_rows(choice, value):
    picked = lax.dot_general(
        one_hot(choice, value.shape[0]).astype(BF16),
        thirds(value, 1),
        (((0,), (0,)), ((), ())),
        preferred_element_type=F32,
    )
    return sum_thirds(picked, 1)


def put_rows(choice, value, rows):
    put = jnp.dot(
        one_hot(choice, rows).astype(BF16), thirds(value, 1), preferred_element_type=F32
    )
    return sum_thirds(put, 1)


def stiffness_kernel(size, pairs_ref, blocks_ref, field_ref, *refs):
    out_ref = refs[min(1, len(refs) - 1)]
    block_rows = field_ref.shape[0]
    count = pairs_ref.shape[1]
    rows = block_rows + count
    width = math.lcm(size, LANES)
    tiles = width // LANES
    segments = width // size
    groups = size // segments
    batch = next(k for k in (8, 4, 3, 2, 1) if groups % k == 0)

    def place(position):
        segment = sum(jnp.where(position >= k * size, 1, 0) for k in range(1, segments))
        return segment, position - segment * size

    def lanes_of(value, index):
        slabs = [
            jnp.take_along_axis(
                value[k : k + SUBLANES, :], index, axis=1, mode="promise_in_bounds"
            )
            for k in range(0, value.shape[0], SUBLANES)
        ]
        return jnp.concatenate(slabs, axis=0)

    field = field_ref[...]
    ends = jnp.concatenate([pairs_ref[:1, :], pairs_ref[1:, :]], axis=1)
    both = pick_rows(ends, field)
    left = both[:count]
    right = jnp.concatenate([field, both[count:]], axis=0)
    lane = lax.broadcasted_iota(jnp.int32, (SUBLANES, LANES), 1)
    places = [place(lane + t * LANES) for t in range(tiles)]
    repeated = jnp.concatenate([lanes_of(right, inside) for _, inside in places], axis=1)
    segment, inside = place(lax.broadcasted_iota(jnp.int32, (width, LANES), 0))
    column = lax.broadcasted_iota(jnp.int32, (width, LANES), 1)
    add_segments = jnp.where(segment == column % segments, 1.0, 0.0).astype(BF16)
    fold = jnp.where(inside == column, 1.0, 0.0).astype(BF16)
    dof_group = lax.broadcasted_iota(jnp.int32, (rows, LANES), 1) // segments
    total = jnp.zeros((rows, LANES), F32)
    turned = jnp.zeros((count, width), F32)
    for base in range(0, groups, batch):
        stack = []
        for g in range(base, base + batch):
            stored = blocks_ref[:, g * width : (g + 1) * width]
            product = stored * repeated
            high = product.astype(BF16)
            stack += [high, (product - high.astype(F32)).astype(BF16)]
            spread = [lanes_of(left, g * segments + segment) for segment, _ in places]
            turned = turned + stored[block_rows:] * jnp.concatenate(spread, axis=1)
        sums = jnp.dot(
            jnp.concatenate(stack, axis=0), add_segments, preferred_element_type=F32
        )
        for n in range(batch):
            part = sums[2 * n * rows : 2 * (n + 1) * rows]
            total = jnp.where(dof_group == base + n, part[:rows] + part[rows:], total)
    folded = sum_thirds(
        jnp.dot(thirds(turned, 0), fold, preferred_element_type=F32), 0
    )
    out_ref[...] = total[:block_rows] + put_rows(
        ends, jnp.concatenate([total[block_rows:], folded], axis=0), block_rows
    )
    if len(refs) > 1:
        aligned_ref, _, copy_ref, west_ref = refs
        copy_ref[...] = field
        gather_traces(field, aligned_ref, west_ref.shape[0], west_ref)


def spread_jumps(size, rows_ref, sides, block_rows):
    dof_of = lax.broadcasted_iota(jnp.int32, (size, LANES), 0).astype(F32).astype(BF16)
    row_of = lax.broadcasted_iota(jnp.int32, (block_rows, LANES), 0).astype(F32).astype(BF16)
    none = jnp.zeros((), BF16)
    one = jnp.ones((), BF16)

    def widened(value, f, rows):
        slab = jnp.broadcast_to(value[f : f + 1, :], (2 * SUBLANES, LANES)).astype(BF16)
        return jnp.concatenate([slab] * (rows // (2 * SUBLANES)), axis=0)

    total = jnp.zeros((size, 2 * block_rows), F32)
    for side, weighted in enumerate(sides):
        for k in range(0, weighted.shape[0], SUBLANES):
            high, low = halves(weighted[k : k + SUBLANES])
            first = side * weighted.shape[0] + k
            dof, row = split(rows_ref[first : first + SUBLANES, :], block_rows)
            dof = dof.astype(F32)
            row = row.astype(F32)
            left = []
            right = []
            for f in range(SUBLANES):
                here = row_of == widened(row, f, block_rows)
                left.append(
                    jnp.concatenate(
                        [
                            jnp.where(here, widened(high, f, block_rows), none),
                            jnp.where(here, widened(low, f, block_rows), none),
                        ],
                        axis=0,
                    )
                )
                right.append(jnp.where(dof_of == widened(dof, f, size), one, none))
            total = total + lax.dot_general(
                jnp.concatenate(right, axis=1),
                jnp.concatenate(left, axis=1),
                (((1,), (1,)), ((), ())),
                preferred_element_type=F32,
            )
    total = total.T
    return total[:block_rows] + total[block_rows:]


def image_kernel(
    size,
    first,
    packed_ref,
    last_ref,
    choice_ref,
    aligned_ref,
    product_ref,
    east_ref,
    west_ref,
    from_a_ref,
    from_b_ref,
    *refs,
):
    *block_refs, image_ref, weights_east_ref, weights_west_ref, jump_ref = refs[:-2]
    next_rows_ref, last_rows_ref = refs[-2:]
    block_rows = product_ref.shape[0]
    faces = weights_east_ref.shape[0]
    per_group = last_ref.shape[1]
    slot = lax.axis_index("blk")
    odd = lax.rem(lax.axis_index("sub"), 2) == 1
    kept = pl.ds(pl.multiple_of(first + slot * per_group, SUBLANES), per_group)
    from_west = jnp.where(odd, from_b_ref[...], from_a_ref[...])
    from_east = jnp.where(odd, from_a_ref[...], from_b_ref[...])
    next_rows_ref[...] = from_east[faces + SUBLANES :].astype(jnp.int32)
    last_rows_ref[...] = from_west[faces + SUBLANES :].astype(jnp.int32)
    for row, block, part, weights_ref in (
        (choice_ref[...], packed_ref[kept, :], slice(0, per_group), weights_east_ref),
        (from_west[faces : faces + SUBLANES], last_ref[slot], slice(per_group, 2 * per_group), weights_west_ref),
    ):
        weights_ref[...] = pick_rows(
            row[:1, :faces].astype(jnp.int32),
            jnp.concatenate([block] + [block_ref[part, :] for block_ref in block_refs], axis=0),
        )
    jump_ref[...] = west_ref[...] - from_west[:faces]
    image_ref[...] = product_ref[...]
    image_ref[:, :size] = image_ref[:, :size] + spread_jumps(
        size,
        aligned_ref,
        (
            weights_east_ref[...] * (east_ref[...] - from_east[:faces]),
            weights_west_ref[...] * jump_ref[...],
        ),
        block_rows,
    )


def column_sums(value):
    return jnp.sum(value, axis=0, keepdims=True)


def sums_kernel(
    product_ref,
    weights_ref,
    own_ref,
    rows_ref,
    last_ref,
    jump_ref,
    field_ref,
    image_ref,
    sums_ref,
    arrived_ref,
):
    gather_traces(last_ref[...], rows_ref, 0, arrived_ref)
    largest = jnp.maximum(jnp.abs(field_ref[...]), jnp.abs(image_ref[...]))
    for value in (arrived_ref[...], jump_ref[...]):
        value = jnp.abs(value)
        for k in range(0, value.shape[0], largest.shape[0]):
            largest = jnp.maximum(largest, value[k : k + largest.shape[0]])
    largest = jnp.max(jnp.max(largest, axis=0, keepdims=True), axis=1, keepdims=True)
    level = jnp.where(largest > LARGE, 0, jnp.where(largest < SMALL, 2, 1))
    parts = []
    for scale in (SHRINK, 1.0, 1.0 / SHRINK):
        field = field_ref[...] * scale
        image = image_ref[...] * scale
        product = product_ref[...] * scale
        jump = own_ref[...] * scale - arrived_ref[...] * scale
        lam = weights_ref[...] * jump
        parts += [
            column_sums(field * field),
            column_sums(field * image),
            column_sums(image * image),
            column_sums(field * product) + column_sums(lam * (jump_ref[...] * scale)),
            column_sums(image * product) + column_sums(lam * jump),
        ]
        parts += [jnp.zeros_like(parts[0])] * (SUBLANES - MARK)
    whole = jnp.sum(jnp.concatenate(parts, axis=0), axis=1, keepdims=True)
    row = lax.broadcasted_iota(jnp.int32, (len(parts), LANES), 0)
    lane = lax.broadcasted_iota(jnp.int32, (len(parts), LANES), 1)
    first = SUBLANES * level
    whole = jnp.where(row == first + MARK, 1.0, whole)
    chosen = (lane == row) & (row >= first) & (row < first + SUBLANES)
    packed = column_sums(jnp.where(chosen, whole, 0.0))
    sums_ref[...] = jnp.broadcast_to(packed[None], sums_ref.shape)


def second_kernel(
    size,
    aligned_ref,
    product_ref,
    weights_east_ref,
    weights_west_ref,
    image_ref,
    west_ref,
    rows_ref,
    next_ref,
    from_last_ref,
    second_ref,
    east_ref,
    from_next_ref,
):
    block_rows = product_ref.shape[0]
    gather_traces(image_ref[...], aligned_ref, 0, east_ref)
    gather_traces(next_ref[...], rows_ref, 0, from_next_ref)
    second_ref[...] = product_ref[...]
    second_ref[:, :size] = second_ref[:, :size] + spread_jumps(
        size,
        aligned_ref,
        [
            weights_ref[...] * (own_ref[...] - arrived_ref[...])
            for weights_ref, own_ref, arrived_ref in (
                (weights_east_ref, east_ref, from_next_ref),
                (weights_west_ref, west_ref, from_last_ref),
            )
        ],
        block_rows,
    )


def final_kernel(field_ref, image_ref, second_ref, sums_ref, solution_ref, residual_ref):
    size = solution_ref.shape[1]
    row = jnp.broadcast_to(jnp.sum(sums_ref[...], axis=0), (SUBLANES, LANES))

    def lane(k):
        place = jnp.full((SUBLANES, LANES), k, jnp.int32)
        return jnp.take_along_axis(row, place, axis=1, mode="promise_in_bounds")[:1, :size]

    large, plain = (lane(SUBLANES * level + MARK) > 0.0 for level in (0, 1))

    def entry(k):
        sums = [lane(SUBLANES * level + k) for level in range(3)]
        lower = SHRINK * SHRINK
        return jnp.where(
            large,
            sums[0] + sums[1] * lower,
            jnp.where(plain, sums[1] + sums[2] * lower, sums[2]),
        )

    bb, bq, qq, bw, qw = (entry(k) for k in range(5))
    field = field_ref[:, :size]
    image = image_ref[:, :size]
    second = second_ref[:, :size]
    alpha = bb / bq
    norm = bb - alpha * (2.0 * bq - alpha * qq)
    beta = norm / bb
    grown = 1.0 + beta
    energy = grown * (grown * bq - alpha * (bw + qq)) + alpha * alpha * qw
    alpha_next = norm / energy
    residual = field - alpha * image
    direction = residual + beta * field
    moved = (image - alpha * second) + beta * image
    solution_ref[...] = alpha * field + alpha_next * direction
    residual_ref[...] = residual - alpha_next * moved


def swap(value, odd):
    count = lax.axis_size("sub")
    pairs = []
    for first in range(odd, count, 2):
        second = (first + 1) % count
        pairs += [(first, second), (second, first)]
    return lax.ppermute(value, "sub", pairs)


def from_behind(value, axis, steps):
    count = lax.axis_size(axis)
    pairs = [(source, (source + steps) % count) for source in range(count)]
    return lax.ppermute(value, axis, pairs)


def swap_slots(value, k):
    count = lax.axis_size("blk")
    return lax.ppermute(value, "blk", [(slot, slot ^ k) for slot in range(count)])


def on_device(
    right_side, stiffness, block_pairs, trace_rows, partner_face, owner_list, mortar_weight
):
    field = right_side[0, 0].T
    block_rows, size = field.shape
    blocks = stiffness[0, 0].astype(F32)
    pairs = block_pairs[0, 0]
    rows = trace_rows[0, 0]
    partner = partner_face[0, 0]
    owners = owner_list[0, 0]
    faces = partner.shape[0]
    devices = lax.axis_size("sub") * lax.axis_size("blk")

    own_weights = mortar_weight[0, 0]
    last_weights = from_behind(own_weights, "sub", 1)
    last = 2 * faces + block_rows

    def placed(value, first):
        below = last + SUBLANES + faces - first - value.shape[0]
        return jnp.pad(value, ((first, below), (0, LANES - value.shape[1])))

    indices = placed(rows, 0) + placed(partner_face[0], last) + placed(owner_list[0], last + 1)
    packed = (
        indices.astype(F32)
        + placed(field, 2 * faces)
        + placed(own_weights.reshape(faces, LANES), last + SUBLANES)
    )
    aligned, padded, choice, east, west, to_a, to_b = call(
        functools.partial(first_kernel, owners.shape[0]),
        [
            shape(2 * faces, jnp.int32),
            shape(block_rows),
            shape(SUBLANES),
            shape(faces),
            shape(faces),
            shape(2 * faces + SUBLANES),
            shape(2 * faces + SUBLANES),
        ],
        [(packed, VMEM)],
    )
    from_a = swap(to_a, 1)
    from_b = swap(to_b, 0)
    slots, per_group, _ = own_weights.shape
    blocks_to = call(
        functools.partial(blocks_kernel, last + SUBLANES),
        [shape(2 * per_group)] * (slots - 1),
        [(packed, VMEM), (last_weights, VMEM)],
        flops=1,
        moved=1,
    )
    blocks_from = [
        swap_slots(block, k) for k, block in zip(range(slots - 1, 0, -1), blocks_to)
    ]

    def stiff(vector, *ordered):
        return call(
            functools.partial(stiffness_kernel, size),
            [shape(block_rows)] * (1 + len(ordered)) + [shape(faces)] * len(ordered),
            [(value, VMEM) for value in (pairs, blocks, vector, *ordered)],
        )

    (product,) = stiff(padded)
    image, weights_east, weights_west, jump, next_rows, last_rows = call(
        functools.partial(image_kernel, size, last + SUBLANES),
        [shape(block_rows)] + [shape(faces)] * 3 + [shape(faces, jnp.int32)] * 2,
        [
            (value, VMEM)
            for value in (
                packed,
                last_weights,
                choice,
                aligned,
                product,
                east,
                west,
                from_a,
                from_b,
                *blocks_from,
            )
        ],
    )
    from_last = from_behind(image, "sub", 1)
    product, copied, west = stiff(image, aligned)
    from_next = from_behind(copied, "sub", -1)
    sums, arrived = call(
        sums_kernel,
        [jax.ShapeDtypeStruct((devices, 1, LANES), F32), shape(faces)],
        [
            (value, VMEM)
            for value in (product, weights_west, west, last_rows, from_last, jump, padded, image)
        ],
    )
    (second,) = call(
        functools.partial(second_kernel, size),
        [shape(block_rows)],
        [
            (value, VMEM)
            for value in (
                aligned,
                product,
                weights_east,
                weights_west,
                image,
                west,
                next_rows,
                from_next,
                arrived,
            )
        ],
        scratch=[pltpu.VMEM((faces, LANES), F32)] * 2,
        flops=1_000_000_000,
    )
    sums = lax.all_to_all(sums, ("sub", "blk"), split_axis=0, concat_axis=0, tiled=True)
    solution_field, residual = call(
        final_kernel,
        [jax.ShapeDtypeStruct((block_rows, size), F32)] * 2,
        [(padded, VMEM), (image, VMEM), (second, VMEM), (sums, VMEM)],
    )
    return (solution_field.T[None, None], residual.T[None, None])


def solution(mesh):
    in_specs = (
        P("sub", "blk", None, None),
        P("sub", "blk", None, None),
        P("sub", "blk", None, None),
        P("sub", "blk", None, None),
        P("sub", "blk", None),
        P("sub", "blk", None),
        P("sub", "blk", None, None, None),
    )
    out_specs = (P("sub", "blk", None, None), P("sub", "blk", None, None))
    return jax.shard_map(
        on_device, mesh=mesh, in_specs=in_specs, out_specs=out_specs, check_vma=False
    )
```
